128 devices in a mesh: dp: 16 (over x_hi, y, core), tensor: 8 (over z, x_lo).
Axes of the slice: x: 4 (x_hi: 2, x_lo: 2; x = x_hi * 2 + x_lo), y: 4, z: 4, core: 2. Of those that a mesh axis runs over, the one named last changes fastest.
Arguments:
- hidden: bfloat16 [2, 16, 512, 1536], P(None, 'dp', 'tensor'), may hold values from -6 to 6
- condition: bfloat16 [2, 16, 1024], P(None, 'dp'), may hold values from -6 to 6
- caption: bfloat16 [2, 16, 256, 4096], P(None, 'dp'), may hold values from -6 to 6
- lengths: int32 [2, 16], P(None, 'dp'), may hold values from 128 to 512, as said below
- frames: int32 [2, 16], P(None, 'dp'), may hold values from 1 to 4
- widths: int32 [2, 16], P(None, 'dp'), may hold values from 8 to 32
- caption_lens: int32 [2, 16], P(None, 'dp'), may hold values from 32 to 256, as said below
- cotangent: bfloat16 [2, 16, 512, 1536], P(None, 'dp', 'tensor'), may hold values from -6 to 6
- ada_weight: bfloat16 [1024, 6144], P('dp', 'tensor'), may hold values from -0.1875 to 0.1875
- ada_bias: bfloat16 [6144], P('dp'), may hold values from -3 to 3
- norm_gains: bfloat16 [4, 1536], P(None, 'dp'), may hold values from 0.25 to 1.75
- qkv_weight: bfloat16 [3, 1536, 1536], P(None, 'dp', 'tensor'), may hold values from -0.15625 to 0.15625
- head_gains: bfloat16 [3, 64], replicated, may hold values from 0.25 to 1.75
- caption_weight: bfloat16 [2, 4096, 1536], P(None, 'dp', 'tensor'), may hold values from -0.09375 to 0.09375
- head_gate: bfloat16 [24], replicated, may hold values from -1.5 to 1.5
- out_weight: bfloat16 [1536, 1536], P('tensor', 'dp'), may hold values from -0.15625 to 0.15625
- ffn_weight: bfloat16 [2, 1536, 4096], P(None, 'dp', 'tensor'), may hold values from -0.15625 to 0.15625
- down_weight: bfloat16 [4096, 1536], P('tensor', 'dp'), may hold values from -0.09375 to 0.09375
Outputs:
- layer_out: bfloat16 [2, 16, 512, 1536], P(None, 'dp', 'tensor')
- grad_hidden: float32 [2, 16, 512, 1536], P(None, 'dp', 'tensor')
- grad_ada_weight: float32 [1024, 6144], P('dp', 'tensor')
- grad_ada_bias: float32 [6144], P('dp')
- grad_norm_gains: float32 [4, 1536], P(None, 'dp')
- grad_qkv_weight: float32 [3, 1536, 1536], P(None, 'dp', 'tensor')
- grad_head_gains: float32 [3, 64], replicated
- grad_caption_weight: float32 [2, 4096, 1536], P(None, 'dp', 'tensor')
- grad_head_gate: float32 [24], replicated
- grad_out_weight: float32 [1536, 1536], P('tensor', 'dp')
- grad_ffn_weight: float32 [2, 1536, 4096], P(None, 'dp', 'tensor')
- grad_down_weight: float32 [4096, 1536], P('tensor', 'dp')
The draws below stay inside these ranges and needn't reach their ends.
Inputs may be any that keep to these rules, and one draw needn't show every extreme that they name: `lengths`: for every item index, one of the 2 micro-batches holds an item with all 512 slots live. `caption_lens`: for every item index, one of the 2 micro-batches holds an item with all 256 caption slots live.
All inputs are finite; a program needn't handle non-finite values.
Results may differ from the reference program's by a relative error of at most 0.023.
Values may be sent and summed in bfloat16 or wider, within the bound.
A program may use at most 192 MiB of HBM per device.

```python
import jax
import jax.numpy as jnp
from jax import lax

D = 1536
H = 24
HD = 64
FF = 4096
CTX = 4096
CD = 1024
TXT = 256
MB = 2
ITEMS = 16
SEQ = 512


def one_full(key, lowest, highest):
    first_key, second_key = jax.random.split(key)
    counts = jax.random.randint(first_key, (MB, ITEMS), lowest, highest + 1)
    chosen = jax.random.randint(second_key, (ITEMS,), 0, MB)
    picked = jnp.arange(MB, dtype=jnp.int32)[:, None] == chosen[None, :]
    return jnp.where(picked, highest, counts).astype(jnp.int32)


def draw_lengths(key, part):
    key = jax.random.fold_in(key, 5)
    return one_full(key, SEQ // 4, SEQ)


def draw_caption_lens(key, part):
    key = jax.random.fold_in(key, 9)
    return one_full(key, TXT // 8, TXT)


def place_ends(values, rng, smallest, high):
    dims = values.shape
    place = [jax.random.randint(jax.random.fold_in(rng, axis), (), 0, dims[axis]) for axis in range(len(dims))]
    values = values.at[tuple(place)].set(smallest)
    longest = dims.index(max(dims))
    place[longest] = (place[longest] + 1) % dims[longest]
    return values.at[tuple(place)].set(high)


def level_of(rng, shape, cuts, low, high):
    level = 1.0
    for dim, parts in cuts:
        heights = jax.random.uniform(jax.random.fold_in(jax.random.fold_in(rng, 6), dim), (parts,), jnp.float32, low / len(cuts), high / len(cuts))
        level = level * jnp.repeat(jnp.exp(heights), shape[dim] // parts).reshape((-1,) + (1,) * (len(shape) - 1 - dim))
    return level


def bell_draw(key, extent, scale, limit, cuts=(), kind=jnp.bfloat16):
    drawn = jax.random.normal(key, extent, jnp.float32) * scale
    if len(cuts) > 0:
        drawn = level_of(key, extent, cuts, -0.22, 0.18) * drawn
    return jnp.clip(drawn, min=-limit, max=limit).astype(kind)


def setup_inputs(seed: int = 0) -> dict:
    arg_keys = jax.random.split(jax.random.key(seed), 19)
    hidden = bell_draw(arg_keys[0], (MB, ITEMS, SEQ, D), 1.0, 6.0, ((1, 16), (2, 8)))
    condition = bell_draw(arg_keys[1], (MB, ITEMS, CD), 1.0, 6.0, ((1, 16),))
    caption = bell_draw(arg_keys[2], (MB, ITEMS, TXT, CTX), 1.0, 6.0, ((1, 16),))
    lengths = draw_lengths(jax.random.fold_in(arg_keys[18], 71), 0)
    frames = place_ends(jax.random.randint(arg_keys[4], (MB, ITEMS), 1, 5), jax.random.fold_in(arg_keys[4], 1), 1, 4).astype(jnp.int32)
    widths = place_ends(jax.random.randint(arg_keys[5], (MB, ITEMS), 8, 33), jax.random.fold_in(arg_keys[5], 1), 8, 32).astype(jnp.int32)
    caption_lens = draw_caption_lens(jax.random.fold_in(arg_keys[18], 71), 0)
    cotangent = bell_draw(arg_keys[7], (MB, ITEMS, SEQ, D), 1.0, 6.0, ((1, 16), (2, 8)))
    ada_weight = bell_draw(arg_keys[8], (CD, 4 * D), CD ** -0.5, 0.1875, ((0, 16), (1, 8)))
    ada_bias = bell_draw(arg_keys[9], (4 * D,), 0.5, 3.0, ((0, 16),))
    norm_gains = jnp.clip(1.0 + 0.15 * jax.random.normal(arg_keys[10], (4, D), jnp.float32), 0.25, 1.75).astype(jnp.bfloat16)
    qkv_weight = bell_draw(arg_keys[11], (3, D, D), D ** -0.5, 0.15625, ((1, 16), (2, 8)))
    head_gains = jnp.clip(1.0 + 0.15 * jax.random.normal(arg_keys[12], (3, HD), jnp.float32), 0.25, 1.75).astype(jnp.bfloat16)
    caption_weight = bell_draw(arg_keys[13], (2, CTX, D), CTX ** -0.5, 0.09375, ((1, 16), (2, 8)))
    head_gate = jnp.clip(jax.random.uniform(arg_keys[14], (H,), jnp.float32, -1.5, 1.5), -1.5, 1.5).astype(jnp.bfloat16)
    out_weight = bell_draw(arg_keys[15], (D, D), D ** -0.5, 0.15625, ((0, 8), (1, 16)))
    ffn_weight = bell_draw(arg_keys[16], (2, D, FF), D ** -0.5, 0.15625, ((1, 16), (2, 8)))
    down_weight = bell_draw(arg_keys[17], (FF, D), FF ** -0.5, 0.09375, ((0, 8), (1, 16)))
    return dict(hidden=hidden, condition=condition, caption=caption, lengths=lengths, frames=frames, widths=widths, caption_lens=caption_lens, cotangent=cotangent, ada_weight=ada_weight, ada_bias=ada_bias, norm_gains=norm_gains, qkv_weight=qkv_weight, head_gains=head_gains, caption_weight=caption_weight, head_gate=head_gate, out_weight=out_weight, ffn_weight=ffn_weight, down_weight=down_weight)


EPSILON = 1e-05
NEGATIVE = -1e+30
PRECISE = lax.Precision.HIGHEST

@jax.custom_vjp
def low(v):
    return lax.optimization_barrier(v.astype(jnp.bfloat16)).astype(jnp.float32)

@jax.custom_vjp
def low_back(v):
    return v

def low_keep(v):
    return (low(v), None)

def low_pass(kept, grad):
    return (grad,)

def back_keep(v):
    return (v, None)

def back_low(kept, grad):
    return (low(grad),)
low.defvjp(low_keep, low_pass)
low_back.defvjp(back_keep, back_low)

def matmul(left, right):
    return jnp.dot(left, right, precision=PRECISE, preferred_element_type=jnp.float32)

def rms_norm(values, gain):
    return values * lax.rsqrt(lax.optimization_barrier(jnp.mean(values * values, axis=-1, keepdims=True)) + EPSILON) * gain

def swish(values):
    return values * jax.nn.sigmoid(values)

def rope_tables(length, frames, width, total, head_size):
    position = jnp.arange(total, dtype=jnp.int32)
    per_frame = (length + frames - 1) // frames
    frame_pos = position // per_frame
    within = position - frame_pos * per_frame
    row_pos = within // width
    col_pos = within - row_pos * width
    half_size = head_size // 2
    time_pairs = head_size // 8
    space_pairs = (half_size - time_pairs) // 2
    pair = jnp.arange(half_size, dtype=jnp.int32)
    in_row = pair >= time_pairs
    in_col = pair >= time_pairs + space_pairs
    offset = jnp.where(in_col, time_pairs + space_pairs, jnp.where(in_row, time_pairs, 0))
    group_size = jnp.where(in_row, space_pairs, time_pairs)
    freq = 10000.0 ** (-(pair - offset).astype(jnp.float32) / group_size.astype(jnp.float32))
    chosen = jnp.where(in_col[None, :], col_pos[:, None], jnp.where(in_row[None, :], row_pos[:, None], frame_pos[:, None]))
    angle = chosen.astype(jnp.float32) * freq[None, :]
    return (jnp.cos(angle), jnp.sin(angle))

def rotate(values, cosine, sine_table):
    half_size = values.shape[-1] // 2
    first_half = values[..., :half_size]
    second_half = values[..., half_size:]
    cos_rows = cosine[:, None, :]
    sin_rows = sine_table[:, None, :]
    return jnp.concatenate([first_half * cos_rows - second_half * sin_rows, first_half * sin_rows + second_half * cos_rows], axis=-1)

def softmax_rows(scores):
    top_score = lax.optimization_barrier(jnp.max(scores, axis=-1, keepdims=True))
    exponent = jnp.exp(scores - top_score)
    return exponent / lax.optimization_barrier(jnp.sum(exponent, axis=-1, keepdims=True))

def layer(hidden_in, caption_in, condition_in, length, frames, width, caption_len, ada_weight, ada_bias, norm_gains, qkv_weight, head_gains, caption_weight, head_gate, out_weight, ffn_weight, down_weight):
    scaling = HD ** (-0.5)
    modulation = matmul(low(swish(condition_in))[None, :], ada_weight)[0] + ada_bias
    scales = modulation.reshape(4, D)
    slots = jnp.arange(SEQ, dtype=jnp.int32)
    live_rows = (slots < length).astype(jnp.float32)[:, None]
    key_live = slots < length
    text_live = jnp.arange(TXT, dtype=jnp.int32) < caption_len
    cosine, sine_table = rope_tables(length, frames, width, SEQ, HD)
    first_in = low(rms_norm(hidden_in, norm_gains[0]) * (1.0 + scales[0]))
    q_raw = low_back(matmul(first_in, qkv_weight[0])).reshape(SEQ, H, HD)
    k_raw = low_back(matmul(first_in, qkv_weight[1])).reshape(SEQ, H, HD)
    values = low(low_back(matmul(first_in, qkv_weight[2]))).reshape(SEQ, H, HD)
    queries = low(rotate(rms_norm(q_raw, head_gains[0]), cosine, sine_table))
    keys = low(rotate(rms_norm(k_raw, head_gains[1]), cosine, sine_table))
    text_raw = low_back(matmul(caption_in, caption_weight[0])).reshape(TXT, H, HD)
    text_keys = low(rms_norm(text_raw, head_gains[2]))
    text_values = low(low_back(matmul(caption_in, caption_weight[1]))).reshape(TXT, H, HD)
    block_rows = min(512, SEQ)

    def attend(query_block):
        scores = low_back(jnp.einsum('qhd,khd->hqk', query_block, keys, precision=PRECISE) * scaling)
        scores = jnp.where(key_live[None, None, :], scores, NEGATIVE)
        probs = softmax_rows(scores)
        own = jnp.einsum('hqk,khd->qhd', low(probs), values, precision=PRECISE)
        text_scores = low_back(jnp.einsum('qhd,khd->hqk', query_block, text_keys, precision=PRECISE) * scaling)
        text_scores = jnp.where(text_live[None, None, :], text_scores, NEGATIVE)
        text_probs = softmax_rows(text_scores)
        other = low_back(jnp.einsum('hqk,khd->qhd', low(text_probs), text_values, precision=PRECISE))
        return own + jnp.tanh(head_gate)[None, :, None] * other
    mixed = lax.map(jax.checkpoint(attend), queries.reshape(SEQ // block_rows, block_rows, H, HD))
    combined = low_back(low(mixed.reshape(SEQ, D)))
    attn = low_back(matmul(combined, out_weight))
    mid = hidden_in + live_rows * jnp.tanh(scales[1]) * rms_norm(attn, norm_gains[1])
    second_in = low(rms_norm(mid, norm_gains[2]) * (1.0 + scales[2]))
    gate_pre = low_back(matmul(second_in, ffn_weight[0]))
    up_pre = low_back(matmul(second_in, ffn_weight[1]))
    activated = low(swish(gate_pre) * up_pre)
    ffn_sum = low_back(matmul(activated, down_weight))
    return mid + live_rows * jnp.tanh(scales[3]) * rms_norm(ffn_sum, norm_gains[3])

def reference(hidden, condition, caption, lengths, frames, widths, caption_lens, cotangent, ada_weight, ada_bias, norm_gains, qkv_weight, head_gains, caption_weight, head_gate, out_weight, ffn_weight, down_weight):
    weights = tuple((w.astype(jnp.float32) for w in (ada_weight, ada_bias, norm_gains, qkv_weight, head_gains, caption_weight, head_gate, out_weight, ffn_weight, down_weight)))
    total_items = MB * ITEMS
    items = (hidden.reshape(total_items, SEQ, D), caption.reshape(total_items, TXT, CTX), condition.reshape(total_items, CD), lengths.reshape(total_items), frames.reshape(total_items), widths.reshape(total_items), caption_lens.reshape(total_items), cotangent.reshape(total_items, SEQ, D))

    def one_item(totals, item):
        seq_hidden, seq_caption, seq_condition, length, frame_count, width, caption_len, seq_grad = item

        def forward(hidden_in, *params):
            return layer(hidden_in, seq_caption.astype(jnp.float32), seq_condition.astype(jnp.float32), length, frame_count, width, caption_len, *params)
        result, pull = jax.vjp(forward, seq_hidden.astype(jnp.float32), *weights)
        grads = pull(seq_grad.astype(jnp.float32))
        return (tuple((left + right for left, right in zip(totals, grads[1:]))), (result.astype(jnp.bfloat16), grads[0]))
    totals, (results, grad_rows) = lax.scan(one_item, tuple((jnp.zeros_like(w) for w in weights)), items)
    shape = (MB, ITEMS, SEQ, D)
    return (results.reshape(shape), grad_rows.reshape(shape), totals[0], totals[1], totals[2], totals[3], totals[4], totals[5], totals[6], totals[7], totals[8], totals[9])
```

```python
import functools

import jax
import jax.numpy as jnp
from jax import lax
from jax.experimental import pallas as pl
from jax.experimental.pallas import tpu as pltpu
from jax.sharding import PartitionSpec as P

D = 1536
H = 24
HD = 64
EPSILON = 1e-05
NEGATIVE = -1e30
MESH = pl.DeviceIdType.MESH
VMEM = pltpu.VMEM
F32 = jnp.float32
BF16 = jnp.bfloat16


def coords():
    dp = lax.axis_index("dp")
    t = lax.axis_index("tensor")
    return dp // 8, t % 2, (dp // 2) % 4, t // 2, dp % 2


def device_of(x, y, z, c):
    return ((x // 2) * 8 + y * 2 + c, z * 2 + x % 2)


def greet(devices):
    barrier = pltpu.get_barrier_semaphore()
    for device in devices:
        pl.semaphore_signal(barrier, inc=1, device_id=device, device_id_type=MESH)
    pl.semaphore_wait(barrier, len(devices))


class Sender:
    def __init__(self, send_sem, recv_sem):
        self.send_sem = send_sem
        self.recv_sem = recv_sem
        self.copies = []

    def __call__(self, src, dst, device):
        k = len(self.copies)
        copy = pltpu.make_async_remote_copy(
            src_ref=src,
            dst_ref=dst,
            send_sem=self.send_sem.at[k],
            recv_sem=self.recv_sem.at[k],
            device_id=device,
            device_id_type=MESH,
        )
        copy.start()
        self.copies.append(copy)
        return copy

    def drain(self):
        for copy in self.copies:
            copy.wait_send()


def dma_sems(n):
    return [pltpu.SemaphoreType.DMA((n,)), pltpu.SemaphoreType.DMA((n,))]


def kernel_call(body, inputs, out_shape, cid, scratch, in_space=VMEM, out_space=VMEM, name=None):
    single = not isinstance(out_shape, (tuple, list))
    spec = pl.BlockSpec(memory_space=out_space)
    return pl.pallas_call(
        body,
        out_shape=out_shape,
        in_specs=[pl.BlockSpec(memory_space=in_space)] * len(inputs),
        out_specs=spec if single else [spec] * len(out_shape),
        scratch_shapes=scratch,
        compiler_params=pltpu.CompilerParams(
            collective_id=cid, has_side_effects=True, vmem_limit_bytes=56 * 2**20
        ),
        name=name,
    )(*inputs)


def mod_kernel(msg_ref, ada_ref, bias_ref, got1, got3, sent, got2, s1, r1, s2, r2, s3, r3):
    dp = lax.axis_index("dp")
    t = lax.axis_index("tensor")
    dp_peers = [((dp + k) % 16, t) for k in range(1, 16)]
    t_peers = [(dp, (t + k) % 8) for k in range(1, 8)]
    greet(dp_peers + t_peers)
    first = Sender(s1, r1)
    for peer in dp_peers:
        first(msg_ref.at[peer[0]], got1.at[dp], peer)
    got1[dp] = msg_ref[dp]
    for copy in first.copies:
        copy.wait_recv()
    rows = got1[...].reshape(128, 128).astype(BF16)
    part = jnp.dot(rows, ada_ref[...], preferred_element_type=F32) + bias_ref[...]
    sent[...] = part.reshape(16, 8, 768)
    second = Sender(s2, r2)
    for peer in dp_peers:
        second(sent.at[peer[0]], got2.at[dp], peer)
    got2[dp] = sent[dp]
    for copy in second.copies:
        copy.wait_recv()
    got3[t] = jnp.sum(got2[...], axis=0)
    third = Sender(s3, r3)
    for peer in t_peers:
        third(got3.at[t], got3.at[t], peer)
    for copy in third.copies:
        copy.wait_recv()
    for sender in (first, second, third):
        sender.drain()


def hidden_kernel(hid_ref, cot_ref, all_ref, cot_out, ss, rs):
    xh, xl, y, z, c = coords()
    pair = device_of(2 * xh + 1 - xl, y, z, c)
    right = device_of(2 * xh + xl, y, (z + 1) % 4, c)
    left = device_of(2 * xh + xl, y, (z + 3) % 4, c)
    greet([pair, right, left])
    send = Sender(ss, rs)
    swap = send(hid_ref.at[1 - xl], all_ref.at[z, xl], pair)
    all_ref[z, xl] = hid_ref[xl]
    cot_swap = send(cot_ref.at[1 - xl], cot_out.at[xl], pair)
    cot_out[xl] = cot_ref[xl]
    swap.wait_recv()
    zl = (z + 3) % 4
    zr = (z + 1) % 4
    to_right = send(all_ref.at[z], all_ref.at[z], right)
    to_left = send(all_ref.at[z], all_ref.at[z], left)
    to_right.wait_recv()
    on_right = send(all_ref.at[zl, 0], all_ref.at[zl, 0], right)
    to_left.wait_recv()
    on_left = send(all_ref.at[zr, 1], all_ref.at[zr, 1], left)
    on_right.wait_recv()
    on_left.wait_recv()
    cot_swap.wait_recv()
    send.drain()


def swap_kernel(out_ref, grad_ref, out_got, grad_got, ss, rs):
    xh, xl, y, z, c = coords()
    pair = device_of(2 * xh + 1 - xl, y, z, c)
    greet([pair])
    send = Sender(ss, rs)
    a = send(out_ref.at[1 - xl], out_got.at[xl], pair)
    b = send(grad_ref.at[1 - xl], grad_got.at[xl], pair)
    a.wait_recv()
    b.wait_recv()
    send.drain()


def z_gather_kernel(x_ref, all_ref, ss, rs):
    xh, xl, y, z, c = coords()
    right = device_of(2 * xh + xl, y, (z + 1) % 4, c)
    left = device_of(2 * xh + xl, y, (z + 3) % 4, c)
    greet([left, right])
    send = Sender(ss, rs)
    to_right = send(x_ref, all_ref.at[z], right)
    to_left = send(x_ref, all_ref.at[z], left)
    all_ref[z] = x_ref[...]
    zl = (z + 3) % 4
    zr = (z + 1) % 4
    lower, upper = pl.ds(0, 64), pl.ds(64, 64)
    to_right.wait_recv()
    on_right = send(all_ref.at[zl, lower], all_ref.at[zl, lower], right)
    to_left.wait_recv()
    on_left = send(all_ref.at[zr, upper], all_ref.at[zr, upper], left)
    on_right.wait_recv()
    on_left.wait_recv()
    send.drain()


def z_scatter_kernel(x_ref, sum_ref, relay_r, relay_l, sum_r, sum_l, got_r, got_l, ss, rs):
    xh, xl, y, z, c = coords()
    right = device_of(2 * xh + xl, y, (z + 1) % 4, c)
    left = device_of(2 * xh + xl, y, (z + 3) % 4, c)
    greet([left, right])
    send = Sender(ss, rs)
    zl = (z + 3) % 4
    zr = (z + 1) % 4
    zo = (z + 2) % 4
    lower, upper = pl.ds(0, 64), pl.ds(64, 64)
    relay1 = send(x_ref.at[zo, lower], relay_r, right)
    relay2 = send(x_ref.at[zo, upper], relay_l, left)
    near1 = send(x_ref.at[zr, upper], got_r.at[upper], right)
    near2 = send(x_ref.at[zl, lower], got_l.at[lower], left)
    relay1.wait_recv()
    sum_r[...] = (relay_r[...].astype(F32) + x_ref[zr, lower].astype(F32)).astype(BF16)
    far1 = send(sum_r, got_r.at[lower], right)
    relay2.wait_recv()
    sum_l[...] = (relay_l[...].astype(F32) + x_ref[zl, upper].astype(F32)).astype(BF16)
    far2 = send(sum_l, got_l.at[upper], left)
    for copy in (near1, near2, far1, far2):
        copy.wait_recv()
    sum_ref[...] = x_ref[z].astype(F32) + got_r[...].astype(F32) + got_l[...].astype(F32)
    send.drain()


def z_gather(x, cid):
    return kernel_call(
        z_gather_kernel,
        [x],
        jax.ShapeDtypeStruct((4, 128, D), BF16),
        cid,
        dma_sems(4),
        name="z_gather%d" % cid,
    ).reshape(512, D)


def z_scatter(x, cid):
    half = VMEM((64, D), BF16)
    full = VMEM((128, D), BF16)
    return kernel_call(
        z_scatter_kernel,
        [x.reshape(4, 128, D)],
        jax.ShapeDtypeStruct((128, D), F32),
        cid,
        [half, half, half, half, full, full] + dma_sems(6),
        name="z_scatter%d" % cid,
    )


def plane_peers():
    xh, xl, y, z, c = coords()
    x = 2 * xh + xl
    xr, xq = (x + 1) % 4, (x + 3) % 4
    yr, yq = (y + 1) % 4, (y + 3) % 4
    peers = [
        device_of(xr, y, z, c),
        device_of(xq, y, z, c),
        device_of(x, yr, z, c),
        device_of(x, yq, z, c),
        device_of(x, y, z, 1 - c),
    ]
    return x, y, c, xr, xq, yr, yq, peers


def plane_gather_kernel(rows, cols, w_ref, all_ref, ss, rs, local_sem):
    x, y, c, xr, xq, yr, yq, peers = plane_peers()
    go_xr, go_xq, go_yr, go_yq, sibling = peers
    greet(peers)
    send = Sender(ss, rs)
    half = rows // 2
    top, low = pl.ds(0, half), pl.ds(half, half)

    def at(xx, yy, *rest):
        return all_ref.at[(xx % 2, xx // 2, yy, c) + rest]

    def same(ref, device):
        return send(ref, ref, device)

    local = pltpu.make_async_copy(w_ref, at(x, y), local_sem)
    local.start()
    a_r = send(w_ref.at[top], at(x, y, top), go_xr)
    a_l = send(w_ref.at[top], at(x, y, top), go_xq)
    b_r = send(w_ref.at[low], at(x, y, low), go_yr)
    b_l = send(w_ref.at[low], at(x, y, low), go_yq)
    own = send(w_ref, at(x, y), sibling)
    if rows == 96:
        left_half, right_half = pl.ds(0, cols // 2), pl.ds(cols // 2, cols // 2)
        qa = [(top, left_half), (top, right_half)]
        qb = [(low, left_half), (low, right_half)]
    else:
        q = half // 2
        qa = [(pl.ds(0, q),), (pl.ds(q, q),)]
        qb = [(pl.ds(2 * q, q),), (pl.ds(3 * q, q),)]
    a_r.wait_recv()
    f1 = same(at(xq, y, *qa[0]), go_xr)
    a_l.wait_recv()
    f2 = same(at(xr, y, *qa[1]), go_xq)
    b_r.wait_recv()
    f3 = same(at(x, yq, *qb[0]), go_yr)
    b_l.wait_recv()
    f4 = same(at(x, yr, *qb[1]), go_yq)
    for copy in (f1, f2, f3, f4):
        copy.wait_recv()
    local.wait()
    every = slice(None)
    block = all_ref.at[:, :, y, c, top]
    g_r = same(block, go_yr)
    g_l = same(block, go_yq)
    block = all_ref.at[x % 2, x // 2, :, c, low]
    h_r = same(block, go_xr)
    h_l = same(block, go_xq)
    g_r.wait_recv()
    f1 = same(all_ref.at[0, :, yq, c, top], go_yr)
    g_l.wait_recv()
    f2 = same(all_ref.at[1, :, yr, c, top], go_yq)
    h_r.wait_recv()
    f3 = same(all_ref.at[xq % 2, xq // 2, pl.ds(0, 2), c, low], go_xr)
    h_l.wait_recv()
    f4 = same(all_ref.at[xr % 2, xr // 2, pl.ds(2, 2), c, low], go_xq)
    for copy in (f1, f2, f3, f4):
        copy.wait_recv()
    late = []
    for k in range(1, 4):
        xx = (x + k) % 4
        late.append(same(all_ref.at[xx % 2, xx // 2, :, c], sibling))
    for k in range(1, 4):
        late.append(same(at(x, (y + k) % 4), sibling))
    for copy in late:
        copy.wait_recv()
    own.wait_recv()
    send.drain()


def plane_gather(w, cid):
    rows, cols = w.shape
    return kernel_call(
        functools.partial(plane_gather_kernel, rows, cols),
        [w],
        jax.ShapeDtypeStruct((2, 2, 4, 2, rows, cols), BF16),
        cid,
        dma_sems(24) + [pltpu.SemaphoreType.DMA],
        pl.ANY,
        pl.ANY,
        name="plane_gather%d" % cid,
    ).reshape(2, 16 * rows, cols)


def add_low(a, b):
    return (a.astype(F32) + b.astype(F32)).astype(BF16)


def plane_scatter_kernel(rows, cols, g_ref, out_ref, sib, ra, rb, ga, gb, pa, pb, qa, qb, ss, rs):
    x, y, c, xr, xq, yr, yq, peers = plane_peers()
    go_xr, go_xq, go_yr, go_yq, sibling = peers
    greet(peers)
    send = Sender(ss, rs)
    half = rows // 2
    top, low = pl.ds(0, half), pl.ds(half, half)
    xo, yo = (x + 2) % 4, (y + 2) % 4
    parts = []
    for k in range(4):
        parts.append(
            send(g_ref.at[k % 2, k // 2, :, 1 - c], sib.at[k % 2, k // 2], sibling)
        )
    for k in range(4):
        parts[k].wait_recv()

        def add_sibling(j, carry, k=k):
            sib[k % 2, k // 2, j] = add_low(sib[k % 2, k // 2, j], g_ref[k % 2, k // 2, j, c])
            return carry

        lax.fori_loop(0, 4, add_sibling, 0)
    t1 = send(sib.at[0, :, yo, top], ra.at[0], go_yr)
    t2 = send(sib.at[1, :, yo, top], ra.at[1], go_yq)
    l1 = send(sib.at[xo % 2, xo // 2, pl.ds(0, 2), low], rb.at[0], go_xr)
    l2 = send(sib.at[xo % 2, xo // 2, pl.ds(2, 2), low], rb.at[1], go_xq)
    t1.wait_recv()
    for j in range(2):
        sib[0, j, yr, top] = add_low(sib[0, j, yr, top], ra[0, j])
    t2.wait_recv()
    for j in range(2):
        sib[1, j, yq, top] = add_low(sib[1, j, yq, top], ra[1, j])
    t3 = send(sib.at[:, :, yr, top], ga.at[0], go_yr)
    t4 = send(sib.at[:, :, yq, top], ga.at[1], go_yq)
    l1.wait_recv()
    for j in range(2):
        sib[xr % 2, xr // 2, j, low] = add_low(sib[xr % 2, xr // 2, j, low], rb[0, j])
    l2.wait_recv()
    for j in range(2):
        sib[xq % 2, xq // 2, 2 + j, low] = add_low(sib[xq % 2, xq // 2, 2 + j, low], rb[1, j])
    l3 = send(sib.at[xr % 2, xr // 2, :, low], gb.at[0], go_xr)
    l4 = send(sib.at[xq % 2, xq // 2, :, low], gb.at[1], go_xq)
    t3.wait_recv()
    t4.wait_recv()
    for i in range(2):
        for j in range(2):
            total = (
                sib[i, j, y, top].astype(F32) + ga[0, i, j].astype(F32) + ga[1, i, j].astype(F32)
            )
            pa[i, j] = total.astype(BF16)
    q = half // 2
    q0, q1 = pl.ds(0, q), pl.ds(q, q)
    if rows == 96:
        q0 = (slice(None), pl.ds(0, cols // 2))
        q1 = (slice(None), pl.ds(cols // 2, cols // 2))
        shape0 = (half, cols // 2)
    else:
        q0, q1 = (pl.ds(0, q),), (pl.ds(q, q),)
        shape0 = (q, cols)
    e1 = send(pa.at[(xo % 2, xo // 2) + q0], qa.at[0], go_xr)
    e2 = send(pa.at[(xo % 2, xo // 2) + q1], qa.at[1], go_xq)
    l3.wait_recv()
    l4.wait_recv()
    for j in range(4):
        total = (
            sib[x % 2, x // 2, j, low].astype(F32) + gb[0, j].astype(F32) + gb[1, j].astype(F32)
        )
        pb[j] = total.astype(BF16)
    m1 = send(pb.at[(yo,) + q0], qb.at[0], go_yr)
    m2 = send(pb.at[(yo,) + q1], qb.at[1], go_yq)
    e1.wait_recv()
    ir = (xr % 2, xr // 2)
    iq = (xq % 2, xq // 2)
    pa[ir + q0] = add_low(pa[ir + q0], qa[0])
    e2.wait_recv()
    pa[iq + q1] = add_low(pa[iq + q1], qa[1])
    e3 = send(pa.at[ir], ga.at[0, 0, 0], go_xr)
    e4 = send(pa.at[iq], ga.at[1, 0, 0], go_xq)
    m1.wait_recv()
    pb[(yr,) + q0] = add_low(pb[(yr,) + q0], qb[0])
    m2.wait_recv()
    pb[(yq,) + q1] = add_low(pb[(yq,) + q1], qb[1])
    m3 = send(pb.at[yr], gb.at[0, 0], go_yr)
    m4 = send(pb.at[yq], gb.at[1, 0], go_yq)
    e3.wait_recv()
    e4.wait_recv()
    out_ref[top] = (
        pa[x % 2, x // 2].astype(F32) + ga[0, 0, 0].astype(F32) + ga[1, 0, 0].astype(F32)
    )
    m3.wait_recv()
    m4.wait_recv()
    out_ref[low] = pb[y].astype(F32) + gb[0, 0].astype(F32) + gb[1, 0].astype(F32)
    send.drain()


def plane_scatter(g, cid):
    _, total_rows, cols = g.shape
    rows = total_rows // 16
    half = rows // 2
    quarter = (half, cols // 2) if rows == 96 else (half // 2, cols)
    return kernel_call(
        functools.partial(plane_scatter_kernel, rows, cols),
        [g.reshape(2, 2, 4, 2, rows, cols)],
        jax.ShapeDtypeStruct((rows, cols), F32),
        cid,
        [
            VMEM((2, 2, 4, rows, cols), BF16),
            VMEM((2, 2, half, cols), BF16),
            VMEM((2, 2, half, cols), BF16),
            VMEM((2, 2, 2, half, cols), BF16),
            VMEM((2, 4, half, cols), BF16),
            VMEM((2, 2, half, cols), BF16),
            VMEM((4, half, cols), BF16),
            VMEM((2,) + quarter, BF16),
            VMEM((2,) + quarter, BF16),
        ]
        + dma_sems(20),
        name="plane_scatter%d" % cid,
    )


def small_kernel(mod_ref, gain_ref, g_all, gain_out, bias_all, gt, gg, gsum, s1, r1, s2, r2, s3, r3, s4, r4, s5, r5):
    dp = lax.axis_index("dp")
    t = lax.axis_index("tensor")
    dp_peers = [((dp + k) % 16, t) for k in range(1, 16)]
    t_peers = [(dp, (t + k) % 8) for k in range(1, 8)]
    greet(dp_peers + t_peers)
    first = Sender(s1, r1)
    for peer in t_peers:
        first(mod_ref.at[peer[1]], gt.at[t], peer)
    gains = Sender(s2, r2)
    for peer in dp_peers:
        gains(gain_ref.at[peer[0]], gg.at[dp], peer)
    gt[t] = mod_ref[t]
    gg[dp] = gain_ref[dp]
    for copy in first.copies:
        copy.wait_recv()
    g_all[dp, 0] = gt[0] + gt[2] + gt[4] + gt[6]
    g_all[dp, 1] = gt[1] + gt[3] + gt[5] + gt[7]
    second = Sender(s3, r3)
    for peer in dp_peers:
        second(g_all.at[dp], g_all.at[dp], peer)
    for copy in gains.copies:
        copy.wait_recv()
    gsum[t] = jnp.sum(gg[...], axis=0)
    third = Sender(s4, r4)
    for peer in t_peers:
        third(gsum.at[t], gsum.at[t], peer)
    for copy in second.copies:
        copy.wait_recv()
    bias_all[t] = jnp.sum(g_all[...], axis=(0, 1))
    fourth = Sender(s5, r5)
    for peer in t_peers:
        fourth(bias_all.at[t], bias_all.at[t], peer)
    for copy in third.copies:
        copy.wait_recv()
    gain_out[...] = jnp.sum(gsum[...], axis=0)
    for copy in fourth.copies:
        copy.wait_recv()
    for sender in (first, gains, second, third, fourth):
        sender.drain()


def normalize(values):
    inverse = lax.rsqrt(jnp.mean(values * values, axis=-1, keepdims=True) + EPSILON)
    return (values * inverse, inverse)


def norm_back(unit_values, inverse, gradient):
    return inverse * (
        gradient - unit_values * jnp.mean(gradient * unit_values, axis=-1, keepdims=True)
    )


def swish(values):
    return values * jax.nn.sigmoid(values)


def rope_tables(length, frames, width, total, head_size):
    position = jnp.arange(total, dtype=jnp.int32)
    per_frame = (length + frames - 1) // frames
    frame_pos = position // per_frame
    within = position - frame_pos * per_frame
    row_pos = within // width
    col_pos = within - row_pos * width
    half_size = head_size // 2
    time_pairs = head_size // 8
    space_pairs = (half_size - time_pairs) // 2
    pair = jnp.arange(half_size, dtype=jnp.int32)
    in_row = pair >= time_pairs
    in_col = pair >= time_pairs + space_pairs
    offset = jnp.where(in_col, time_pairs + space_pairs, jnp.where(in_row, time_pairs, 0))
    group_size = jnp.where(in_row, space_pairs, time_pairs)
    freq = 10000.0 ** (-(pair - offset).astype(jnp.float32) / group_size.astype(jnp.float32))
    chosen = jnp.where(
        in_col[None, :],
        col_pos[:, None],
        jnp.where(in_row[None, :], row_pos[:, None], frame_pos[:, None]),
    )
    angle = chosen.astype(jnp.float32) * freq[None, :]
    return (jnp.cos(angle), jnp.sin(angle))


def rotate(values, cosine, sine_table):
    half_size = values.shape[-1] // 2
    first_half = values[..., :half_size]
    second_half = values[..., half_size:]
    cos_rows = cosine[:, None, :]
    sin_rows = sine_table[:, None, :]
    return jnp.concatenate(
        [
            first_half * cos_rows - second_half * sin_rows,
            first_half * sin_rows + second_half * cos_rows,
        ],
        axis=-1,
    )


def rotate_back(gradient, cosine, sine_table):
    return rotate(gradient, cosine, -sine_table)


def pick(array, index):
    return lax.dynamic_index_in_dim(array, index, 0, keepdims=False)


def dot(spec, a, b):
    return jnp.einsum(spec, a, b, preferred_element_type=F32)


def on_device(
    hidden,
    condition,
    caption,
    lengths,
    frames,
    widths,
    caption_lens,
    cotangent,
    ada_weight,
    ada_bias,
    norm_gains,
    qkv_weight,
    head_gains,
    caption_weight,
    head_gate,
    out_weight,
    ffn_weight,
    down_weight,
):
    S = jax.ShapeDtypeStruct
    dp = lax.axis_index("dp")
    t = lax.axis_index("tensor")
    z = t // 2
    xl = t % 2
    scaling = HD ** (-0.5)
    d_shard = jnp.concatenate(
        [
            qkv_weight[0],
            qkv_weight[1],
            qkv_weight[2],
            out_weight.T,
            ffn_weight[0],
            ffn_weight[1],
            down_weight.T,
        ],
        axis=1,
    )
    c_shard = jnp.concatenate([caption_weight[0], caption_weight[1]], axis=1)
    unit_rows = swish(condition[:, 0].astype(F32)).astype(BF16)
    unit_msg = jnp.transpose(unit_rows.astype(F32).reshape(2, 16, 64), (1, 0, 2))
    unit_msg = jnp.pad(unit_msg, ((0, 0), (0, 2), (0, 64)))
    gain_msg = jnp.broadcast_to(jnp.pad(norm_gains.astype(F32), ((0, 0), (0, 32)))[None], (16, 4, 128))
    msg = jnp.concatenate([unit_msg, gain_msg], axis=1)
    ada_pad = jnp.pad(ada_weight, ((0, 64), (0, 0)))
    bias_f = ada_bias.astype(F32)
    bias_row = jnp.where(
        t == dp // 2,
        jnp.where(
            dp % 2 == 0,
            jnp.concatenate([bias_f, jnp.zeros((384,), F32)]),
            jnp.concatenate([jnp.zeros((384,), F32), bias_f]),
        ),
        0.0,
    )[None]
    got1, got3 = kernel_call(
        mod_kernel,
        [msg, ada_pad, bias_row],
        [S((16, 8, 128), F32), S((8, 8, 768), F32)],
        1,
        [VMEM((16, 8, 768), F32), VMEM((16, 8, 768), F32)]
        + dma_sems(15)
        + dma_sems(15)
        + dma_sems(7),
        name="modulation",
    )
    units = got1[:, 0:2, :64].reshape(32, 64)
    gains = jnp.transpose(got1[:, 4:8, :96], (1, 0, 2)).reshape(4, D)
    mod_rows = jnp.where(xl == 0, got3[:, 0], got3[:, 1]).reshape(4, D)
    scale_attn, gate_attn, scale_ffn, gate_ffn = (mod_rows[i] for i in range(4))
    hid_all, cot = kernel_call(
        hidden_kernel,
        [hidden[:, 0], cotangent[:, 0]],
        [S((4, 2, 64, D), BF16), S((2, 64, D), BF16)],
        2,
        dma_sems(6),
        name="hidden_gather",
    )
    resid = pick(hid_all, z).reshape(128, D).astype(F32)
    grad_top = cot.reshape(128, D).astype(F32)
    w_d = plane_gather(d_shard, 3)
    w_c = plane_gather(c_shard, 4)

    length = pick(lengths[:, 0], xl)
    frame_count = pick(frames[:, 0], xl)
    width = pick(widths[:, 0], xl)
    text_len = pick(caption_lens[:, 0], xl)
    cap = pick(caption[:, 0], xl)
    slot_rows = z * 128 + jnp.arange(128, dtype=jnp.int32)
    live_rows = (slot_rows < length).astype(F32)[:, None]
    key_live = jnp.arange(512, dtype=jnp.int32) < length
    text_live = jnp.arange(256, dtype=jnp.int32) < text_len
    cosine, sine_table = rope_tables(length, frame_count, width, 512, HD)
    head_scales = head_gains.astype(F32)
    gate_values = jnp.tanh(lax.dynamic_slice_in_dim(head_gate.astype(F32), z * 6, 6, 0))

    unit_all, _ = normalize(hid_all.reshape(512, D).astype(F32))
    first_all = (unit_all * gains[0] * (1.0 + scale_attn)).astype(BF16)
    unit_one, inverse_one = normalize(resid)
    w_q, w_k, w_v, w_o = (w_d[:, :, i * 192 : (i + 1) * 192] for i in range(4))
    w_g, w_u, w_dn = (w_d[:, :, 768 + i * 512 : 768 + (i + 1) * 512] for i in range(3))
    w_ck, w_cv = w_c[:, :, :192], w_c[:, :, 192:]
    hs = (512, 6, HD)
    ts = (256, 6, HD)
    q_raw, k_raw, v_raw = (dot("sd,xdk->sxk", first_all, w).reshape(hs) for w in (w_q, w_k, w_v))
    query_unit, query_inverse = normalize(q_raw)
    key_unit, key_inverse = normalize(k_raw)
    queries = rotate(query_unit * head_scales[0], cosine, sine_table).astype(BF16)
    keys = rotate(key_unit * head_scales[1], cosine, sine_table).astype(BF16)
    values = v_raw.astype(BF16)
    text_raw = dot("td,xdk->txk", cap, w_ck).reshape(ts)
    text_unit, text_inverse = normalize(text_raw)
    text_keys = (text_unit * head_scales[2]).astype(BF16)
    text_values = dot("td,xdk->txk", cap, w_cv).reshape(ts).astype(BF16)

    def softmax(scores, live):
        masked = jnp.where(live[None, None, :], scores, NEGATIVE)
        top = jnp.max(masked, axis=-1, keepdims=True)
        e = jnp.exp(masked - top)
        return e / jnp.sum(e, axis=-1, keepdims=True)

    probs = softmax(dot("qhd,khd->hqk", queries, keys) * scaling, key_live)
    own = dot("hqk,khd->qhd", probs.astype(BF16), values)
    text_probs = softmax(dot("qhd,khd->hqk", queries, text_keys) * scaling, text_live)
    other = dot("hqk,khd->qhd", text_probs.astype(BF16), text_values)
    combined = (own + gate_values[None, :, None] * other).astype(BF16).reshape(512, 2, 192)
    attn = z_scatter(dot("sxk,xdk->sd", combined, w_o).astype(BF16), 5)
    unit_two, inverse_two = normalize(attn)
    gate_a = jnp.tanh(gate_attn)
    middle = resid + live_rows * gate_a * unit_two * gains[1]
    unit_three, inverse_three = normalize(middle)
    second_in = (unit_three * gains[2] * (1.0 + scale_ffn)).astype(BF16)
    second_all = z_gather(second_in, 6)
    pre_g = dot("sd,xdf->sxf", second_all, w_g)
    pre_u = dot("sd,xdf->sxf", second_all, w_u)
    sigma = jax.nn.sigmoid(pre_g)
    activated = (pre_g * sigma * pre_u).astype(BF16)
    ffn_total = z_scatter(dot("sxf,xdf->sd", activated, w_dn).astype(BF16), 7)
    unit_four, inverse_four = normalize(ffn_total)
    gate_f = jnp.tanh(gate_ffn)
    layer_out = (middle + live_rows * gate_f * unit_four * gains[3]).astype(BF16)

    weighted = grad_top * live_rows
    gain_four = jnp.sum(weighted * gate_f * unit_four, axis=0)
    gate_ffn_grad = jnp.sum(weighted * unit_four * gains[3], axis=0) * (1.0 - gate_f * gate_f)
    grad_ffn_in = norm_back(unit_four, inverse_four, weighted * gate_f * gains[3]).astype(BF16)
    grad_two = z_gather(grad_ffn_in, 8)
    grad_act = dot("sd,xdf->sxf", grad_two, w_dn)
    down_grad = dot("sd,sxf->xdf", grad_two, activated)
    grad_g = (grad_act * pre_u * sigma * (1.0 + pre_g * (1.0 - sigma))).astype(BF16)
    grad_u = (grad_act * pre_g * sigma).astype(BF16)
    gate_grad = dot("sd,sxf->xdf", second_all, grad_g)
    up_grad = dot("sd,sxf->xdf", second_all, grad_u)
    grad_second = z_scatter(
        (dot("sxf,xdf->sd", grad_g, w_g) + dot("sxf,xdf->sd", grad_u, w_u)).astype(BF16), 9
    )
    scale_ffn_grad = jnp.sum(grad_second * unit_three * gains[2], axis=0)
    gain_three = jnp.sum(grad_second * (1.0 + scale_ffn) * unit_three, axis=0)
    grad_middle = grad_top + norm_back(
        unit_three, inverse_three, grad_second * (1.0 + scale_ffn) * gains[2]
    )
    weighted_mid = grad_middle * live_rows
    gain_two = jnp.sum(weighted_mid * gate_a * unit_two, axis=0)
    gate_attn_grad = jnp.sum(weighted_mid * unit_two * gains[1], axis=0) * (1.0 - gate_a * gate_a)
    grad_attn_in = norm_back(unit_two, inverse_two, weighted_mid * gate_a * gains[1]).astype(BF16)
    grad_one = z_gather(grad_attn_in, 10)
    grad_combined = dot("sd,xdk->sxk", grad_one, w_o).astype(BF16)
    out_grad = dot("sd,sxk->xdk", grad_one, combined)
    grad_heads = grad_combined.reshape(hs)
    gate_local = jnp.sum(grad_heads.astype(F32) * other, axis=(0, 2)) * (
        1.0 - gate_values * gate_values
    )
    grad_text_heads = (gate_values[None, :, None] * grad_heads.astype(F32)).astype(BF16)

    def back(p, grad, vals):
        grad_values = dot("hqk,qhd->khd", p.astype(BF16), grad)
        grad_probs = dot("qhd,khd->hqk", grad, vals)
        grad_scores = p * (grad_probs - jnp.sum(p * grad_probs, axis=-1, keepdims=True))
        return grad_values, grad_scores.astype(BF16)

    grad_values, grad_scores = back(probs, grad_heads, values)
    grad_text_values, grad_text_scores = back(text_probs, grad_text_heads, text_values)
    grad_query = (
        dot("hqk,khd->qhd", grad_scores, keys) + dot("hqk,khd->qhd", grad_text_scores, text_keys)
    ) * scaling
    grad_keys = dot("hqk,qhd->khd", grad_scores, queries) * scaling
    grad_text_keys = dot("hqk,qhd->khd", grad_text_scores, queries) * scaling
    grad_query_rot = rotate_back(grad_query, cosine, sine_table)
    grad_key_rot = rotate_back(grad_keys, cosine, sine_table)
    head_query = jnp.sum(grad_query_rot * query_unit, axis=(0, 1))
    head_key = jnp.sum(grad_key_rot * key_unit, axis=(0, 1))
    head_text = jnp.sum(grad_text_keys * text_unit, axis=(0, 1))
    shape = (512, 2, 192)
    grad_q = norm_back(query_unit, query_inverse, grad_query_rot * head_scales[0])
    grad_k = norm_back(key_unit, key_inverse, grad_key_rot * head_scales[1])
    grad_q = grad_q.astype(BF16).reshape(shape)
    grad_k = grad_k.astype(BF16).reshape(shape)
    grad_v = grad_values.astype(BF16).reshape(shape)
    grad_tk = norm_back(text_unit, text_inverse, grad_text_keys * head_scales[2])
    grad_tk = grad_tk.astype(BF16).reshape(256, 2, 192)
    grad_tv = grad_text_values.astype(BF16).reshape(256, 2, 192)
    grad_first = z_scatter(
        (
            dot("sxk,xdk->sd", grad_q, w_q)
            + dot("sxk,xdk->sd", grad_k, w_k)
            + dot("sxk,xdk->sd", grad_v, w_v)
        ).astype(BF16),
        11,
    )
    scale_attn_grad = jnp.sum(grad_first * unit_one * gains[0], axis=0)
    gain_one = jnp.sum(grad_first * (1.0 + scale_attn) * unit_one, axis=0)
    grad_hidden = grad_middle + norm_back(
        unit_one, inverse_one, grad_first * (1.0 + scale_attn) * gains[0]
    )
    d_grad = jnp.concatenate(
        [
            dot("sd,sxk->xdk", first_all, grad_q).astype(BF16),
            dot("sd,sxk->xdk", first_all, grad_k).astype(BF16),
            dot("sd,sxk->xdk", first_all, grad_v).astype(BF16),
            out_grad.astype(BF16),
            gate_grad.astype(BF16),
            up_grad.astype(BF16),
            down_grad.astype(BF16),
        ],
        axis=2,
    )
    c_grad = jnp.concatenate(
        [
            dot("td,txk->xdk", cap, grad_tk).astype(BF16),
            dot("td,txk->xdk", cap, grad_tv).astype(BF16),
        ],
        axis=2,
    )
    d_out = plane_scatter(d_grad, 12)
    c_out = plane_scatter(c_grad, 13)
    out_half = layer_out.reshape(2, 64, D)
    grad_half = grad_hidden.reshape(2, 64, D)
    out_got, grad_got = kernel_call(
        swap_kernel,
        [out_half, grad_half],
        [S((2, 64, D), BF16), S((2, 64, D), F32)],
        14,
        dma_sems(2),
        name="swap_back",
    )
    mine = jnp.arange(2)[:, None, None] == xl
    layer_final = jnp.where(mine, pick(out_half, xl)[None], pick(out_got, 1 - xl)[None])
    grad_final = jnp.where(mine, pick(grad_half, xl)[None], pick(grad_got, 1 - xl)[None])

    mod_grad = jnp.stack([scale_attn_grad, gate_attn_grad, scale_ffn_grad, gate_ffn_grad])
    mod_msg = jnp.pad(mod_grad.reshape(8, 6, 128), ((0, 0), (0, 2), (0, 0)))
    gain_grad = jnp.stack([gain_one, gain_two, gain_three, gain_four])
    gain_part = jnp.pad(
        jnp.transpose(gain_grad.reshape(4, 16, 96), (1, 0, 2)), ((0, 0), (0, 0), (0, 32))
    )
    gate_part = lax.dynamic_update_slice_in_dim(jnp.zeros((64,), F32), gate_local, z * 6, 0)
    head_part = jnp.concatenate([head_query, head_key, head_text, gate_part]).reshape(2, 128)
    head_part = jnp.broadcast_to(jnp.pad(head_part, ((0, 2), (0, 0)))[None], (16, 4, 128))
    gain_msg = jnp.concatenate([gain_part, head_part], axis=1)
    g_all, gain_out, bias_all = kernel_call(
        small_kernel,
        [mod_msg, gain_msg],
        [S((16, 2, 8, 128), F32), S((8, 128), F32), S((8, 8, 128), F32)],
        15,
        [VMEM((8, 8, 128), F32), VMEM((16, 8, 128), F32), VMEM((8, 8, 128), F32)]
        + dma_sems(7)
        + dma_sems(15)
        + dma_sems(15)
        + dma_sems(7)
        + dma_sems(7),
        name="small_sums",
    )
    g_items = g_all[:, :, :6].reshape(32, 768)
    ada_grad = jnp.einsum("mc,mk->ck", units, g_items, precision=lax.Precision.HIGHEST)
    bias_block = pick(bias_all, dp // 2)[:6].reshape(2, 384)
    bias_grad = pick(bias_block, dp % 2)
    heads = gain_out[4:6].reshape(256)
    return (
        layer_final[:, None],
        grad_final[:, None],
        ada_grad,
        bias_grad,
        gain_out[:4, :96],
        jnp.stack([d_out[:, :192], d_out[:, 192:384], d_out[:, 384:576]]),
        heads[:192].reshape(3, 64),
        jnp.stack([c_out[:, :192], c_out[:, 192:]]),
        heads[192:216],
        d_out[:, 576:768].T,
        jnp.stack([d_out[:, 768:1280], d_out[:, 1280:1792]]),
        d_out[:, 1792:].T,
    )


def solution(mesh):
    return jax.shard_map(
        on_device,
        mesh=mesh,
        in_specs=(
            P(None, "dp", "tensor", None),
            P(None, "dp", None),
            P(None, "dp", None, None),
            P(None, "dp"),
            P(None, "dp"),
            P(None, "dp"),
            P(None, "dp"),
            P(None, "dp", "tensor", None),
            P("dp", "tensor"),
            P("dp"),
            P(None, "dp"),
            P(None, "dp", "tensor"),
            P(),
            P(None, "dp", "tensor"),
            P(),
            P("tensor", "dp"),
            P(None, "dp", "tensor"),
            P("tensor", "dp"),
        ),
        out_specs=(
            P(None, "dp", "tensor", None),
            P(None, "dp", "tensor", None),
            P("dp", "tensor"),
            P("dp"),
            P(None, "dp"),
            P(None, "dp", "tensor"),
            P(),
            P(None, "dp", "tensor"),
            P(),
            P("tensor", "dp"),
            P(None, "dp", "tensor"),
            P("tensor", "dp"),
        ),
        check_vma=False,
    )
```

```python
import functools

import jax
import jax.numpy as jnp
from jax import lax
from jax.experimental import pallas as pl
from jax.experimental.pallas import tpu as pltpu
from jax.sharding import PartitionSpec as P

D = 1536
H = 24
HD = 64
EPSILON = 1e-05
NEGATIVE = -1e30
MESH = pl.DeviceIdType.MESH
VMEM = pltpu.VMEM
F32 = jnp.float32
BF16 = jnp.bfloat16


def coords():
    dp = lax.axis_index("dp")
    t = lax.axis_index("tensor")
    return dp // 8, t % 2, (dp // 2) % 4, t // 2, dp % 2


def device_of(x, y, z, c):
    return ((x // 2) * 8 + y * 2 + c, z * 2 + x % 2)


def greet(devices):
    barrier = pltpu.get_barrier_semaphore()
    for device in devices:
        pl.semaphore_signal(barrier, inc=1, device_id=device, device_id_type=MESH)
    pl.semaphore_wait(barrier, len(devices))


class Sender:
    def __init__(self, send_sem, recv_sem):
        self.send_sem = send_sem
        self.recv_sem = recv_sem
        self.copies = []

    def __call__(self, src, dst, device):
        k = len(self.copies)
        copy = pltpu.make_async_remote_copy(
            src_ref=src,
            dst_ref=dst,
            send_sem=self.send_sem.at[k],
            recv_sem=self.recv_sem.at[k],
            device_id=device,
            device_id_type=MESH,
        )
        copy.start()
        self.copies.append(copy)
        return copy

    def drain(self):
        for copy in self.copies:
            copy.wait_send()


def dma_sems(n):
    return [pltpu.SemaphoreType.DMA((n,)), pltpu.SemaphoreType.DMA((n,))]


def kernel_call(body, inputs, out_shape, cid, scratch, in_space=VMEM, out_space=VMEM, name=None):
    single = not isinstance(out_shape, (tuple, list))
    spec = pl.BlockSpec(memory_space=out_space)
    return pl.pallas_call(
        body,
        out_shape=out_shape,
        in_specs=[pl.BlockSpec(memory_space=in_space)] * len(inputs),
        out_specs=spec if single else [spec] * len(out_shape),
        scratch_shapes=scratch,
        compiler_params=pltpu.CompilerParams(
            collective_id=cid, has_side_effects=True, vmem_limit_bytes=56 * 2**20
        ),
        name=name,
    )(*inputs)


def mod_kernel(msg_ref, ada_ref, bias_ref, got1, got3, sent, got2, s1, r1, s2, r2, s3, r3):
    dp = lax.axis_index("dp")
    t = lax.axis_index("tensor")
    dp_peers = [((dp + k) % 16, t) for k in range(1, 16)]
    t_peers = [(dp, (t + k) % 8) for k in range(1, 8)]
    greet(dp_peers + t_peers)
    first = Sender(s1, r1)
    for peer in dp_peers:
        first(msg_ref.at[peer[0]], got1.at[dp], peer)
    got1[dp] = msg_ref[dp]
    for copy in first.copies:
        copy.wait_recv()
    rows = got1[...].reshape(128, 128).astype(BF16)
    part = jnp.dot(rows, ada_ref[...], preferred_element_type=F32) + bias_ref[...]
    sent[...] = part.reshape(16, 8, 768)
    second = Sender(s2, r2)
    for peer in dp_peers:
        second(sent.at[peer[0]], got2.at[dp], peer)
    got2[dp] = sent[dp]
    for copy in second.copies:
        copy.wait_recv()
    got3[t] = jnp.sum(got2[...], axis=0)
    third = Sender(s3, r3)
    for peer in t_peers:
        third(got3.at[t], got3.at[t], peer)
    for copy in third.copies:
        copy.wait_recv()
    for sender in (first, second, third):
        sender.drain()


def hidden_kernel(hid_ref, cot_ref, all_ref, cot_out, ss, rs):
    xh, xl, y, z, c = coords()
    pair = device_of(2 * xh + 1 - xl, y, z, c)
    right = device_of(2 * xh + xl, y, (z + 1) % 4, c)
    left = device_of(2 * xh + xl, y, (z + 3) % 4, c)
    greet([pair, right, left])
    send = Sender(ss, rs)
    swap = send(hid_ref.at[1 - xl], all_ref.at[z, xl], pair)
    all_ref[z, xl] = hid_ref[xl]
    cot_swap = send(cot_ref.at[1 - xl], cot_out.at[xl], pair)
    cot_out[xl] = cot_ref[xl]
    swap.wait_recv()
    zl = (z + 3) % 4
    zr = (z + 1) % 4
    to_right = send(all_ref.at[z], all_ref.at[z], right)
    to_left = send(all_ref.at[z], all_ref.at[z], left)
    to_right.wait_recv()
    on_right = send(all_ref.at[zl, 0], all_ref.at[zl, 0], right)
    to_left.wait_recv()
    on_left = send(all_ref.at[zr, 1], all_ref.at[zr, 1], left)
    on_right.wait_recv()
    on_left.wait_recv()
    cot_swap.wait_recv()
    send.drain()


def swap_kernel(out_ref, grad_ref, out_got, grad_got, ss, rs):
    xh, xl, y, z, c = coords()
    pair = device_of(2 * xh + 1 - xl, y, z, c)
    greet([pair])
    send = Sender(ss, rs)
    a = send(out_ref.at[1 - xl], out_got.at[xl], pair)
    b = send(grad_ref.at[1 - xl], grad_got.at[xl], pair)
    a.wait_recv()
    b.wait_recv()
    send.drain()


def z_gather_kernel(x_ref, all_ref, ss, rs):
    xh, xl, y, z, c = coords()
    right = device_of(2 * xh + xl, y, (z + 1) % 4, c)
    left = device_of(2 * xh + xl, y, (z + 3) % 4, c)
    greet([left, right])
    send = Sender(ss, rs)
    to_right = send(x_ref, all_ref.at[z], right)
    to_left = send(x_ref, all_ref.at[z], left)
    all_ref[z] = x_ref[...]
    zl = (z + 3) % 4
    zr = (z + 1) % 4
    lower, upper = pl.ds(0, 64), pl.ds(64, 64)
    to_right.wait_recv()
    on_right = send(all_ref.at[zl, lower], all_ref.at[zl, lower], right)
    to_left.wait_recv()
    on_left = send(all_ref.at[zr, upper], all_ref.at[zr, upper], left)
    on_right.wait_recv()
    on_left.wait_recv()
    send.drain()


def z_scatter_kernel(x_ref, sum_ref, relay_r, relay_l, sum_r, sum_l, got_r, got_l, ss, rs):
    xh, xl, y, z, c = coords()
    right = device_of(2 * xh + xl, y, (z + 1) % 4, c)
    left = device_of(2 * xh + xl, y, (z + 3) % 4, c)
    greet([left, right])
    send = Sender(ss, rs)
    zl = (z + 3) % 4
    zr = (z + 1) % 4
    zo = (z + 2) % 4
    lower, upper = pl.ds(0, 64), pl.ds(64, 64)
    relay1 = send(x_ref.at[zo, lower], relay_r, right)
    relay2 = send(x_ref.at[zo, upper], relay_l, left)
    near1 = send(x_ref.at[zr, upper], got_r.at[upper], right)
    near2 = send(x_ref.at[zl, lower], got_l.at[lower], left)
    relay1.wait_recv()
    sum_r[...] = (relay_r[...].astype(F32) + x_ref[zr, lower].astype(F32)).astype(BF16)
    far1 = send(sum_r, got_r.at[lower], right)
    relay2.wait_recv()
    sum_l[...] = (relay_l[...].astype(F32) + x_ref[zl, upper].astype(F32)).astype(BF16)
    far2 = send(sum_l, got_l.at[upper], left)
    for copy in (near1, near2, far1, far2):
        copy.wait_recv()
    sum_ref[...] = x_ref[z].astype(F32) + got_r[...].astype(F32) + got_l[...].astype(F32)
    send.drain()


def z_gather(x, cid):
    return kernel_call(
        z_gather_kernel,
        [x],
        jax.ShapeDtypeStruct((4, 128, D), BF16),
        cid,
        dma_sems(4),
        name="z_gather%d" % cid,
    ).reshape(512, D)


def z_scatter(x, cid):
    half = VMEM((64, D), BF16)
    full = VMEM((128, D), BF16)
    return kernel_call(
        z_scatter_kernel,
        [x.reshape(4, 128, D)],
        jax.ShapeDtypeStruct((128, D), F32),
        cid,
        [half, half, half, half, full, full] + dma_sems(6),
        name="z_scatter%d" % cid,
    )


def plane_peers():
    xh, xl, y, z, c = coords()
    x = 2 * xh + xl
    xr, xq = (x + 1) % 4, (x + 3) % 4
    yr, yq = (y + 1) % 4, (y + 3) % 4
    peers = [
        device_of(xr, y, z, c),
        device_of(xq, y, z, c),
        device_of(x, yr, z, c),
        device_of(x, yq, z, c),
        device_of(x, y, z, 1 - c),
    ]
    return x, y, c, xr, xq, yr, yq, peers


def plane_gather_kernel(rows, cols, w_ref, all_ref, ss, rs, local_sem):
    x, y, c, xr, xq, yr, yq, peers = plane_peers()
    go_xr, go_xq, go_yr, go_yq, sibling = peers
    greet(peers)
    send = Sender(ss, rs)
    half = rows // 2
    top, low = pl.ds(0, half), pl.ds(half, half)

    def at(xx, yy, *rest):
        return all_ref.at[(xx % 2, xx // 2, yy, c) + rest]

    def same(ref, device):
        return send(ref, ref, device)

    local = pltpu.make_async_copy(w_ref, at(x, y), local_sem)
    local.start()
    a_r = send(w_ref.at[top], at(x, y, top), go_xr)
    a_l = send(w_ref.at[top], at(x, y, top), go_xq)
    b_r = send(w_ref.at[low], at(x, y, low), go_yr)
    b_l = send(w_ref.at[low], at(x, y, low), go_yq)
    own = send(w_ref, at(x, y), sibling)
    if rows == 96:
        left_half, right_half = pl.ds(0, cols // 2), pl.ds(cols // 2, cols // 2)
        qa = [(top, left_half), (top, right_half)]
        qb = [(low, left_half), (low, right_half)]
    else:
        q = half // 2
        qa = [(pl.ds(0, q),), (pl.ds(q, q),)]
        qb = [(pl.ds(2 * q, q),), (pl.ds(3 * q, q),)]
    a_r.wait_recv()
    f1 = same(at(xq, y, *qa[0]), go_xr)
    a_l.wait_recv()
    f2 = same(at(xr, y, *qa[1]), go_xq)
    b_r.wait_recv()
    f3 = same(at(x, yq, *qb[0]), go_yr)
    b_l.wait_recv()
    f4 = same(at(x, yr, *qb[1]), go_yq)
    for copy in (f1, f2, f3, f4):
        copy.wait_recv()
    local.wait()
    every = slice(None)
    block = all_ref.at[:, :, y, c, top]
    g_r = same(block, go_yr)
    g_l = same(block, go_yq)
    block = all_ref.at[x % 2, x // 2, :, c, low]
    h_r = same(block, go_xr)
    h_l = same(block, go_xq)
    g_r.wait_recv()
    f1 = same(all_ref.at[0, :, yq, c, top], go_yr)
    g_l.wait_recv()
    f2 = same(all_ref.at[1, :, yr, c, top], go_yq)
    h_r.wait_recv()
    f3 = same(all_ref.at[xq % 2, xq // 2, pl.ds(0, 2), c, low], go_xr)
    h_l.wait_recv()
    f4 = same(all_ref.at[xr % 2, xr // 2, pl.ds(2, 2), c, low], go_xq)
    for copy in (f1, f2, f3, f4):
        copy.wait_recv()
    late = []
    for k in range(1, 4):
        xx = (x + k) % 4
        late.append(same(all_ref.at[xx % 2, xx // 2, :, c], sibling))
    for k in range(1, 4):
        late.append(same(at(x, (y + k) % 4), sibling))
    for copy in late:
        copy.wait_recv()
    own.wait_recv()
    send.drain()


def plane_gather(w, cid):
    rows, cols = w.shape
    return kernel_call(
        functools.partial(plane_gather_kernel, rows, cols),
        [w],
        jax.ShapeDtypeStruct((2, 2, 4, 2, rows, cols), BF16),
        cid,
        dma_sems(24) + [pltpu.SemaphoreType.DMA],
        pl.ANY,
        pl.ANY,
        name="plane_gather%d" % cid,
    ).reshape(2, 16 * rows, cols)


def add_low(a, b):
    return (a.astype(F32) + b.astype(F32)).astype(BF16)


def plane_scatter_kernel(rows, cols, g_ref, out_ref, sib, ra, rb, ga, gb, pa, pb, qa, qb, ss, rs):
    x, y, c, xr, xq, yr, yq, peers = plane_peers()
    go_xr, go_xq, go_yr, go_yq, sibling = peers
    greet(peers)
    send = Sender(ss, rs)
    half = rows // 2
    top, low = pl.ds(0, half), pl.ds(half, half)
    xo, yo = (x + 2) % 4, (y + 2) % 4
    parts = []
    for k in range(4):
        parts.append(
            send(g_ref.at[k % 2, k // 2, :, 1 - c], sib.at[k % 2, k // 2], sibling)
        )
    for k in range(4):
        parts[k].wait_recv()

        def add_sibling(j, carry, k=k):
            sib[k % 2, k // 2, j] = add_low(sib[k % 2, k // 2, j], g_ref[k % 2, k // 2, j, c])
            return carry

        lax.fori_loop(0, 4, add_sibling, 0)
    t1 = send(sib.at[0, :, yo, top], ra.at[0], go_yr)
    t2 = send(sib.at[1, :, yo, top], ra.at[1], go_yq)
    l1 = send(sib.at[xo % 2, xo // 2, pl.ds(0, 2), low], rb.at[0], go_xr)
    l2 = send(sib.at[xo % 2, xo // 2, pl.ds(2, 2), low], rb.at[1], go_xq)
    t1.wait_recv()
    for j in range(2):
        sib[0, j, yr, top] = add_low(sib[0, j, yr, top], ra[0, j])
    t2.wait_recv()
    for j in range(2):
        sib[1, j, yq, top] = add_low(sib[1, j, yq, top], ra[1, j])
    t3 = send(sib.at[:, :, yr, top], ga.at[0], go_yr)
    t4 = send(sib.at[:, :, yq, top], ga.at[1], go_yq)
    l1.wait_recv()
    for j in range(2):
        sib[xr % 2, xr // 2, j, low] = add_low(sib[xr % 2, xr // 2, j, low], rb[0, j])
    l2.wait_recv()
    for j in range(2):
        sib[xq % 2, xq // 2, 2 + j, low] = add_low(sib[xq % 2, xq // 2, 2 + j, low], rb[1, j])
    l3 = send(sib.at[xr % 2, xr // 2, :, low], gb.at[0], go_xr)
    l4 = send(sib.at[xq % 2, xq // 2, :, low], gb.at[1], go_xq)
    t3.wait_recv()
    t4.wait_recv()
    for i in range(2):
        for j in range(2):
            total = (
                sib[i, j, y, top].astype(F32) + ga[0, i, j].astype(F32) + ga[1, i, j].astype(F32)
            )
            pa[i, j] = total.astype(BF16)
    q = half // 2
    q0, q1 = pl.ds(0, q), pl.ds(q, q)
    if rows == 96:
        q0 = (slice(None), pl.ds(0, cols // 2))
        q1 = (slice(None), pl.ds(cols // 2, cols // 2))
        shape0 = (half, cols // 2)
    else:
        q0, q1 = (pl.ds(0, q),), (pl.ds(q, q),)
        shape0 = (q, cols)
    e1 = send(pa.at[(xo % 2, xo // 2) + q0], qa.at[0], go_xr)
    e2 = send(pa.at[(xo % 2, xo // 2) + q1], qa.at[1], go_xq)
    l3.wait_recv()
    l4.wait_recv()
    for j in range(4):
        total = (
            sib[x % 2, x // 2, j, low].astype(F32) + gb[0, j].astype(F32) + gb[1, j].astype(F32)
        )
        pb[j] = total.astype(BF16)
    m1 = send(pb.at[(yo,) + q0], qb.at[0], go_yr)
    m2 = send(pb.at[(yo,) + q1], qb.at[1], go_yq)
    e1.wait_recv()
    ir = (xr % 2, xr // 2)
    iq = (xq % 2, xq // 2)
    pa[ir + q0] = add_low(pa[ir + q0], qa[0])
    e2.wait_recv()
    pa[iq + q1] = add_low(pa[iq + q1], qa[1])
    e3 = send(pa.at[ir], ga.at[0, 0, 0], go_xr)
    e4 = send(pa.at[iq], ga.at[1, 0, 0], go_xq)
    m1.wait_recv()
    pb[(yr,) + q0] = add_low(pb[(yr,) + q0], qb[0])
    m2.wait_recv()
    pb[(yq,) + q1] = add_low(pb[(yq,) + q1], qb[1])
    m3 = send(pb.at[yr], gb.at[0, 0], go_yr)
    m4 = send(pb.at[yq], gb.at[1, 0], go_yq)
    e3.wait_recv()
    e4.wait_recv()
    out_ref[top] = (
        pa[x % 2, x // 2].astype(F32) + ga[0, 0, 0].astype(F32) + ga[1, 0, 0].astype(F32)
    )
    m3.wait_recv()
    m4.wait_recv()
    out_ref[low] = pb[y].astype(F32) + gb[0, 0].astype(F32) + gb[1, 0].astype(F32)
    send.drain()


def plane_scatter(g, cid):
    _, total_rows, cols = g.shape
    rows = total_rows // 16
    half = rows // 2
    quarter = (half, cols // 2) if rows == 96 else (half // 2, cols)
    return kernel_call(
        functools.partial(plane_scatter_kernel, rows, cols),
        [g.reshape(2, 2, 4, 2, rows, cols)],
        jax.ShapeDtypeStruct((rows, cols), F32),
        cid,
        [
            VMEM((2, 2, 4, rows, cols), BF16),
            VMEM((2, 2, half, cols), BF16),
            VMEM((2, 2, half, cols), BF16),
            VMEM((2, 2, 2, half, cols), BF16),
            VMEM((2, 4, half, cols), BF16),
            VMEM((2, 2, half, cols), BF16),
            VMEM((4, half, cols), BF16),
            VMEM((2,) + quarter, BF16),
            VMEM((2,) + quarter, BF16),
        ]
        + dma_sems(20),
        name="plane_scatter%d" % cid,
    )


def small_kernel(mod_ref, gain_ref, g_all, gain_out, bias_all, gt, gg, gsum, s1, r1, s2, r2, s3, r3, s4, r4, s5, r5):
    dp = lax.axis_index("dp")
    t = lax.axis_index("tensor")
    dp_peers = [((dp + k) % 16, t) for k in range(1, 16)]
    t_peers = [(dp, (t + k) % 8) for k in range(1, 8)]
    greet(dp_peers + t_peers)
    first = Sender(s1, r1)
    for peer in t_peers:
        first(mod_ref.at[peer[1]], gt.at[t], peer)
    gains = Sender(s2, r2)
    for peer in dp_peers:
        gains(gain_ref.at[peer[0]], gg.at[dp], peer)
    gt[t] = mod_ref[t]
    gg[dp] = gain_ref[dp]
    for copy in first.copies:
        copy.wait_recv()
    g_all[dp, 0] = gt[0] + gt[2] + gt[4] + gt[6]
    g_all[dp, 1] = gt[1] + gt[3] + gt[5] + gt[7]
    second = Sender(s3, r3)
    for peer in dp_peers:
        second(g_all.at[dp], g_all.at[dp], peer)
    for copy in gains.copies:
        copy.wait_recv()
    gsum[t] = jnp.sum(gg[...], axis=0)
    third = Sender(s4, r4)
    for peer in t_peers:
        third(gsum.at[t], gsum.at[t], peer)
    for copy in second.copies:
        copy.wait_recv()
    bias_all[t] = jnp.sum(g_all[...], axis=(0, 1))
    fourth = Sender(s5, r5)
    for peer in t_peers:
        fourth(bias_all.at[t], bias_all.at[t], peer)
    for copy in third.copies:
        copy.wait_recv()
    gain_out[...] = jnp.sum(gsum[...], axis=0)
    for copy in fourth.copies:
        copy.wait_recv()
    for sender in (first, gains, second, third, fourth):
        sender.drain()


def normalize(values):
    inverse = lax.rsqrt(jnp.mean(values * values, axis=-1, keepdims=True) + EPSILON)
    return (values * inverse, inverse)


def norm_back(unit_values, inverse, gradient):
    return inverse * (
        gradient - unit_values * jnp.mean(gradient * unit_values, axis=-1, keepdims=True)
    )


def swish(values):
    return values * jax.nn.sigmoid(values)


def rope_tables(length, frames, width, total, head_size):
    position = jnp.arange(total, dtype=jnp.int32)
    per_frame = (length + frames - 1) // frames
    frame_pos = position // per_frame
    within = position - frame_pos * per_frame
    row_pos = within // width
    col_pos = within - row_pos * width
    half_size = head_size // 2
    time_pairs = head_size // 8
    space_pairs = (half_size - time_pairs) // 2
    pair = jnp.arange(half_size, dtype=jnp.int32)
    in_row = pair >= time_pairs
    in_col = pair >= time_pairs + space_pairs
    offset = jnp.where(in_col, time_pairs + space_pairs, jnp.where(in_row, time_pairs, 0))
    group_size = jnp.where(in_row, space_pairs, time_pairs)
    freq = 10000.0 ** (-(pair - offset).astype(jnp.float32) / group_size.astype(jnp.float32))
    chosen = jnp.where(
        in_col[None, :],
        col_pos[:, None],
        jnp.where(in_row[None, :], row_pos[:, None], frame_pos[:, None]),
    )
    angle = chosen.astype(jnp.float32) * freq[None, :]
    return (jnp.cos(angle), jnp.sin(angle))


def rotate(values, cosine, sine_table):
    half_size = values.shape[-1] // 2
    first_half = values[..., :half_size]
    second_half = values[..., half_size:]
    cos_rows = cosine[:, None, :]
    sin_rows = sine_table[:, None, :]
    return jnp.concatenate(
        [
            first_half * cos_rows - second_half * sin_rows,
            first_half * sin_rows + second_half * cos_rows,
        ],
        axis=-1,
    )


def rotate_back(gradient, cosine, sine_table):
    return rotate(gradient, cosine, -sine_table)


def z_ring():
    xh, xl, y, z, c = coords()
    x = 2 * xh + xl
    return z, device_of(x, y, (z + 1) % 4, c), device_of(x, y, (z + 3) % 4, c)


class ZGather:
    def __init__(self, send, own, every, right, left):
        self.send, self.every, self.right, self.left = send, every, right, left
        self.from_left = send(own, every.at[1], right)
        self.from_right = send(own, every.at[2], left)

    def near(self):
        self.from_left.wait_recv()
        every = self.every
        half = every.shape[1] // 2
        lower, upper = pl.ds(0, half), pl.ds(half, half)
        self.far_low = self.send(every.at[1, lower], every.at[3, lower], self.right)
        self.from_right.wait_recv()
        self.far_up = self.send(every.at[2, upper], every.at[3, upper], self.left)

    def far(self):
        self.far_low.wait_recv()
        self.far_up.wait_recv()


class ZScatter:
    def __init__(self, send, part, relay, got, right, left):
        self.send, self.part, self.relay, self.got = send, part, relay, got
        self.right, self.left = right, left
        half = part.shape[1] // 2
        self.lower, self.upper = pl.ds(0, half), pl.ds(half, half)

    def near(self):
        part, got = self.part, self.got
        self.near_r = self.send(part.at[2, self.upper], got.at[0, self.upper], self.right)
        self.near_l = self.send(part.at[1, self.lower], got.at[1, self.lower], self.left)

    def far(self):
        part, relay = self.part, self.relay
        self.relay_r = self.send(part.at[3, self.lower], relay.at[0], self.right)
        self.relay_l = self.send(part.at[3, self.upper], relay.at[1], self.left)

    def pass_on(self):
        part, relay, got = self.part, self.relay, self.got
        self.relay_r.wait_recv()
        part[2, self.lower] = add_low(part[2, self.lower], relay[0])
        self.last_r = self.send(part.at[2, self.lower], got.at[0, self.lower], self.right)
        self.relay_l.wait_recv()
        part[1, self.upper] = add_low(part[1, self.upper], relay[1])
        self.last_l = self.send(part.at[1, self.upper], got.at[1, self.upper], self.left)

    def total(self):
        for copy in (self.near_r, self.near_l, self.last_r, self.last_l):
            copy.wait_recv()
        got = self.got
        return self.part[0].astype(F32) + got[0].astype(F32) + got[1].astype(F32)


def mm(a, b):
    return lax.dot_general(a, b, (((1,), (0,)), ((), ())), preferred_element_type=F32)


def mm_t(a, b):
    return lax.dot_general(a, b, (((1,), (1,)), ((), ())), preferred_element_type=F32)


def tile(j, size=256):
    return pl.ds(pl.multiple_of(j * size, size), size)


def transpose_into(src, dst):
    def column(j, carry):
        cols = tile(j, 128)
        for slot in range(4):
            dst[cols, slot * 128 : (slot + 1) * 128] = src[slot, :, cols].T
        return carry

    lax.fori_loop(0, D // 128, column, 0)


class PlaneGather:
    def __init__(self, send, shard, every):
        self.send, self.shard, self.every = send, shard, every
        rows, cols = shard.shape
        half = rows // 2
        self.top, self.low = pl.ds(0, half), pl.ds(half, half)
        if rows == 96:
            left, right = pl.ds(0, cols // 2), pl.ds(cols // 2, cols // 2)
            self.qa = [(self.top, left), (self.top, right)]
            self.qb = [(self.low, left), (self.low, right)]
        else:
            q = half // 2
            self.qa = [(pl.ds(0, q),), (pl.ds(q, q),)]
            self.qb = [(pl.ds(2 * q, q),), (pl.ds(3 * q, q),)]
        self.late = []

    def at(self, xx, yy, *rest):
        return self.every.at[(xx % 2, xx // 2, yy, self.c) + rest]

    def same(self, ref, device):
        return self.send(ref, ref, device)

    def to_sibling(self, ref):
        self.late.append(self.send(ref, ref, self.sibling))

    def start(self, local_sem):
        x, y, c, xr, xq, yr, yq, peers = plane_peers()
        self.x, self.y, self.c = x, y, c
        self.xr, self.xq, self.yr, self.yq = xr, xq, yr, yq
        self.go_xr, self.go_xq, self.go_yr, self.go_yq, self.sibling = peers
        shard, top, low = self.shard, self.top, self.low
        self.a_r = self.send(shard.at[top], self.at(x, y, top), self.go_xr)
        self.a_l = self.send(shard.at[top], self.at(x, y, top), self.go_xq)
        self.b_r = self.send(shard.at[low], self.at(x, y, low), self.go_yr)
        self.b_l = self.send(shard.at[low], self.at(x, y, low), self.go_yq)
        self.late.append(self.send(shard, self.at(x, y), self.sibling))
        self.local = pltpu.make_async_copy(shard, self.at(x, y), local_sem)
        self.local.start()

    def step2(self):
        x, y = self.x, self.y
        self.a_r.wait_recv()
        self.f1 = self.same(self.at(self.xq, y, *self.qa[0]), self.go_xr)
        self.a_l.wait_recv()
        self.f2 = self.same(self.at(self.xr, y, *self.qa[1]), self.go_xq)
        self.b_r.wait_recv()
        self.f3 = self.same(self.at(x, self.yq, *self.qb[0]), self.go_yr)
        self.b_l.wait_recv()
        self.f4 = self.same(self.at(x, self.yr, *self.qb[1]), self.go_yq)

    def step3(self):
        x, y, c = self.x, self.y, self.c
        every, top, low = self.every, self.top, self.low
        self.local.wait()
        self.f1.wait_recv()
        self.f2.wait_recv()
        block = every.at[:, :, y, c, top]
        self.g_r = self.same(block, self.go_yr)
        self.g_l = self.same(block, self.go_yq)
        self.f3.wait_recv()
        self.f4.wait_recv()
        block = every.at[x % 2, x // 2, :, c, low]
        self.h_r = self.same(block, self.go_xr)
        self.h_l = self.same(block, self.go_xq)
        for k in range(1, 4):
            self.to_sibling(self.at((x + k) % 4, y, top))
            self.to_sibling(self.at(x, (y + k) % 4, low))

    def step4(self):
        c, every, top, low = self.c, self.every, self.top, self.low
        xr, xq, yr, yq = self.xr, self.xq, self.yr, self.yq
        self.g_r.wait_recv()
        self.f1 = self.same(every.at[0, :, yq, c, top], self.go_yr)
        self.g_l.wait_recv()
        self.f2 = self.same(every.at[1, :, yr, c, top], self.go_yq)
        self.h_r.wait_recv()
        self.f3 = self.same(every.at[xq % 2, xq // 2, pl.ds(0, 2), c, low], self.go_xr)
        self.h_l.wait_recv()
        self.f4 = self.same(every.at[xr % 2, xr // 2, pl.ds(2, 2), c, low], self.go_xq)
        self.to_sibling(every.at[:, :, yq, c, top])
        self.to_sibling(every.at[:, :, yr, c, top])
        self.to_sibling(every.at[xq % 2, xq // 2, :, c, low])
        self.to_sibling(every.at[xr % 2, xr // 2, :, c, low])

    def step5(self):
        c, every, top, low = self.c, self.every, self.top, self.low
        xo, yo = (self.x + 2) % 4, (self.y + 2) % 4
        for copy in (self.f1, self.f2, self.f3, self.f4):
            copy.wait_recv()
        self.to_sibling(every.at[:, :, yo, c, top])
        self.to_sibling(every.at[xo % 2, xo // 2, :, c, low])

    def finish(self):
        for copy in self.late:
            copy.wait_recv()


OFFSETS = (0, 3, 1, 2)


def lanes(shape):
    return lax.broadcasted_iota(jnp.int32, shape, len(shape) - 1)


def head_block():
    row = lax.broadcasted_iota(jnp.int32, (128, 128), 0) // 64
    col = lax.broadcasted_iota(jnp.int32, (128, 128), 1) // 64
    return jnp.where(row == col, 1.0 / 64.0, 0.0).astype(BF16)


def head_mean(values, block):
    high = values.astype(BF16)
    low = (values - high.astype(F32)).astype(BF16)
    return mm(high, block) + mm(low, block)


def swap_quarters(values):
    second = (lanes(values.shape) % 64) >= 32
    return jnp.where(second, pltpu.roll(values, 32, 1), pltpu.roll(values, 96, 1))


def pick_scalar(ref, xl):
    return jnp.where(xl == 0, ref[0, 0], ref[1, 0])


def key_bias(total, z, length):
    lane = lanes((1, total))
    if total == 512:
        slot = lane // 128
        block = jnp.where(slot == 0, z, jnp.where(slot == 1, z + 3, jnp.where(slot == 2, z + 1, z + 2)))
        position = (block % 4) * 128 + lane % 128
    else:
        position = lane
    return jnp.where(position < length, 0.0, NEGATIVE)


def fill_rope(cos_ref, sin_ref, z, length, frames, width):
    lane = lanes((128, 128))
    pair = lane % 32
    offset = jnp.where(pair >= 20, 20, jnp.where(pair >= 8, 8, 0))
    size = jnp.where(pair >= 8, 12.0, 8.0)
    freq = jnp.exp((pair - offset).astype(F32) / size * (-9.210340371976184))
    sign = jnp.where(lane % 64 >= 32, 1.0, -1.0)
    ones = jnp.ones((128, 128), F32)
    count = ones * length.astype(F32)
    frame_count = ones * frames.astype(F32)
    row_size = ones * width.astype(F32)
    per_frame = jnp.floor((count + frame_count - 0.5) / frame_count)
    row = lax.broadcasted_iota(jnp.int32, (128, 128), 0).astype(F32)
    for slot in range(4):
        start = (((z + OFFSETS[slot]) % 4) * 128).astype(F32)
        position = row + start
        frame = jnp.floor((position + 0.5) / per_frame)
        within = position - frame * per_frame
        row_pos = jnp.floor((within + 0.5) / row_size)
        col_pos = within - row_pos * row_size
        chosen = jnp.where(pair >= 20, col_pos, jnp.where(pair >= 8, row_pos, frame))
        angle = chosen * freq
        cos_ref[slot] = jnp.cos(angle)
        sin_ref[slot] = jnp.sin(angle) * sign


def attention_kernel(
    hid_ref,
    cot_ref,
    cond_ref,
    gain_in,
    bias_in,
    ada_ref,
    qkv_ref,
    out_t_ref,
    ffn_w_ref,
    down_t_ref,
    cap_w_ref,
    cap_hbm,
    hg_ref,
    gate_ref,
    len_ref,
    frame_ref,
    width_ref,
    tlen_ref,
    w_a,
    w_f,
    first,
    resid_ref,
    cot_out,
    q8,
    kk,
    vv,
    qr,
    kr,
    tk,
    tv,
    tkr,
    other_ref,
    lse_ref,
    cw,
    attn_ref,
    mid_ref,
    second_ref,
    mod_ref,
    gains_ref,
    got1,
    cos_ref,
    sin_ref,
    live_ref,
    sh_a,
    sh_f,
    sh_c,
    w_c,
    cap,
    hid_all,
    hid_own,
    msg,
    sent2,
    got2,
    got3,
    mixed,
    text_acc,
    part,
    relay,
    got,
    local_sems,
    ss,
    rs,
):
    dp = lax.axis_index("dp")
    t = lax.axis_index("tensor")
    xh, xl, y, z, c = coords()
    _, right, left = z_ring()
    pair = device_of(2 * xh + 1 - xl, y, z, c)
    dp_peers = [((dp + k) % 16, t) for k in range(1, 16)]
    t_peers = [(dp, (t + k) % 8) for k in range(1, 8)]
    outer_x = device_of((2 * xh + xl + 3 - 2 * xl) % 4, y, z, c)
    barrier = pltpu.get_barrier_semaphore()
    everyone = dp_peers + t_peers + [outer_x]
    for device in everyone:
        pl.semaphore_signal(barrier, inc=1, device_id=device, device_id_type=MESH)
    load_cap = pltpu.make_async_copy(cap_hbm.at[xl], cap, local_sems.at[0])
    load_cap.start()
    qs, ks, vs = qkv_ref[0], qkv_ref[1], qkv_ref[2]
    os = out_t_ref[...]
    sh_a[...] = jnp.concatenate(
        [
            qs,
            ks[:, 128:192],
            ks[:, 0:128],
            vs,
            os[:, 128:192],
            os[:, 0:128],
        ],
        axis=1,
    )
    ck, cv = cap_w_ref[0], cap_w_ref[1]
    sh_c[...] = jnp.concatenate([ck, cv[:, 128:192], cv[:, 0:128]], axis=1)
    unit = swish(cond_ref[...].astype(F32)).astype(BF16).astype(F32)
    msg[...] = jnp.zeros((16, 8, 128), F32)
    gain_rows = gain_in[...].astype(F32)
    for d in range(16):
        msg[d, 0:2, 0:64] = unit[:, d * 64 : (d + 1) * 64]
        msg[d, 4:8, 0:96] = gain_rows
    pl.semaphore_wait(barrier, len(everyone))

    send = Sender(ss, rs)
    swap = send(hid_ref.at[1 - xl], hid_own.at[xl], pair)
    cot_swap = send(cot_ref.at[1 - xl], cot_out.at[xl], pair)
    round1 = [send(msg.at[p[0]], got1.at[dp], p) for p in dp_peers]
    ga = PlaneGather(send, sh_a, w_a)
    gc = PlaneGather(send, sh_c, w_c)
    gf = PlaneGather(send, sh_f, w_f)
    ga.start(local_sems.at[1])
    hid_own[xl] = hid_ref[xl]
    cot_out[xl] = cot_ref[xl]
    got1[dp] = msg[dp]
    sh_f[:, 0:512] = ffn_w_ref[0]
    sh_f[:, 512:1024] = ffn_w_ref[1]
    sh_f[:, 1024:1536] = down_t_ref[...]
    length = pick_scalar(len_ref, xl)
    text_len = pick_scalar(tlen_ref, xl)
    swap.wait_recv()
    tokens = ZGather(send, hid_own, hid_all, right, left)
    hid_all[0] = hid_own[...]
    gc.start(local_sems.at[2])
    for copy in round1:
        copy.wait_recv()
    rows = got1[...].reshape(128, 128)[:, :64].astype(BF16)
    bias = bias_in[...].astype(F32)
    here = t == dp // 2
    low_bias = jnp.where(jnp.logical_and(here, dp % 2 == 0), 1.0, 0.0)
    high_bias = jnp.where(jnp.logical_and(here, dp % 2 == 1), 1.0, 0.0)
    terms = mm(rows, ada_ref[...])
    terms = terms + jnp.concatenate([bias * low_bias, bias * high_bias], axis=1)
    sent2[...] = jnp.zeros((16, 16, 128), F32)
    for d in range(16):
        for j in range(6):
            sent2[d, 2 * j : 2 * j + 2, :] = terms[8 * d : 8 * d + 2, 128 * j : 128 * j + 128]
    round2 = [send(sent2.at[p[0]], got2.at[dp], p) for p in dp_peers]
    got2[dp] = sent2[dp]
    ga.step2()
    fill_rope(cos_ref, sin_ref, z, length, pick_scalar(frame_ref, xl), pick_scalar(width_ref, xl))
    gc.step2()
    ga.step3()
    tokens.near()
    for copy in round2:
        copy.wait_recv()
    got3[t] = jnp.sum(got2[...], axis=0)
    round3 = [send(got3.at[t], got3.at[t], p) for p in t_peers]
    for d in range(16):
        gains_ref[0:4, d * 96 : (d + 1) * 96] = got1[d, 4:8, 0:96]
    gains_ref[4:8, :] = jnp.zeros((4, D), F32)
    slot_row = lax.broadcasted_iota(jnp.int32, (128, 128), 0) + z * 128
    live_ref[...] = jnp.where(slot_row < length, 1.0, 0.0)
    gc.step3()
    ga.step4()
    gf.start(local_sems.at[3])
    for copy in round3:
        copy.wait_recv()
    for i in range(4):
        for h in range(2):
            block = got3[2 * i + h]
            for j in range(6):
                lo = h * 768 + j * 128
                mod_ref[i : i + 1, lo : lo + 128] = jnp.where(
                    xl == 0, block[2 * j : 2 * j + 1], block[2 * j + 1 : 2 * j + 2]
                )
    mod_ref[4:8, :] = jnp.zeros((4, D), F32)
    factor = gains_ref[0:1, :] * (1.0 + mod_ref[0:1, :])
    tokens.far()

    def scale_rows(slot, carry):
        unit_rows, _ = normalize(hid_all[slot].reshape(128, D).astype(F32))
        first[slot] = (unit_rows * factor).astype(BF16)
        return carry

    lax.fori_loop(0, 4, scale_rows, 0)
    resid_ref[...] = hid_all[0].reshape(128, D)
    gc.step4()
    ga.step5()
    gf.step2()
    ga.finish()

    x_rows = first[...].reshape(512, D)
    low_head = lanes((512, 128)) < 64
    w_flat = w_a

    def project(xx, cols):
        w_cols = w_flat[xx, :, :, :, :, cols].reshape(D, cols.stop - cols.start)
        return mm(x_rows, w_cols)

    for xx in range(2):
        p = project(xx, slice(0, 256))
        qr[xx] = p[:, :128].reshape(4, 128, 128)
        mixed[0, xx] = p[:, 128:]
        p = project(xx, slice(256, 512))
        kr[xx] = p[:, :128].reshape(4, 128, 128)
        vv[xx] = p[:, 128:].astype(BF16).reshape(4, 128, 128)
        mixed[1, xx] = project(xx, slice(512, 640))
    x0, x1 = mixed[0, 0], mixed[0, 1]
    qr[2] = jnp.where(low_head, x0, pltpu.roll(x1, 64, 1)).reshape(4, 128, 128)
    kr[2] = jnp.where(low_head, pltpu.roll(x0, 64, 1), x1).reshape(4, 128, 128)
    x0, x1 = mixed[1, 0], mixed[1, 1]
    vv[2] = jnp.where(low_head, x0, pltpu.roll(x1, 64, 1)).astype(BF16).reshape(4, 128, 128)
    gc.step5()
    gf.step3()
    block = head_block()
    cos = cos_ref[...].reshape(512, 128)
    sin = sin_ref[...].reshape(512, 128)

    def turned(raw, gain):
        raw = raw.reshape(512, 128)
        v = raw * lax.rsqrt(head_mean(raw * raw, block) + EPSILON) * gain
        return v * cos + swap_quarters(v) * sin

    for p in range(3):
        q = turned(qr[p], hg_ref[0:1, :]).astype(BF16)
        q8[p] = (q.astype(F32) * 0.125).astype(BF16).reshape(4, 128, 128)
        kk[p] = turned(kr[p], hg_ref[1:2, :]).astype(BF16).reshape(4, 128, 128)
    load_cap.wait()
    gc.finish()
    text_acc[...] = jnp.zeros((2, 256, 384), F32)

    def text_step(i, carry):
        xx = i // 8
        j = i % 8
        w_cols = w_c[xx, j // 4, j % 4].reshape(512, 384)
        text_acc[xx] += mm(cap[:, tile(j, 512)], w_cols)
        return carry

    lax.fori_loop(0, 16, text_step, 0)
    gf.step4()
    low_text = lanes((256, 128)) < 64
    for xx in range(2):
        tkr[xx] = text_acc[xx, :, 0:128]
        tv[xx] = text_acc[xx, :, 256:384].astype(BF16)
    x0, x1 = text_acc[0, :, 128:256], text_acc[1, :, 128:256]
    tkr[2] = jnp.where(low_text, x0, pltpu.roll(x1, 64, 1))
    tv[2] = jnp.where(low_text, pltpu.roll(x0, 64, 1), x1).astype(BF16)
    for p in range(3):
        raw = tkr[p]
        tk[p] = (raw * lax.rsqrt(head_mean(raw * raw, block) + EPSILON) * hg_ref[2:3, :]).astype(BF16)

    self_bias = key_bias(512, z, length)
    text_bias = key_bias(256, z, text_len)
    lse_ref[...] = jnp.zeros((4, 128, 128), F32)

    def attend(p):
        def rows_step(b, carry):
            slots = pl.ds(b * 2, 2)
            q = q8[p, slots].reshape(256, 128)
            low_rows = lanes((256, 128)) < 64
            own = jnp.zeros((256, 128), F32)
            other = jnp.zeros((256, 128), F32)
            for head in range(2):
                keep = low_rows if head == 0 else jnp.logical_not(low_rows)
                qm = jnp.where(keep, q, jnp.zeros_like(q))
                for text in range(2):
                    k = tk[p] if text else kk[p].reshape(512, 128)
                    v = tv[p] if text else vv[p].reshape(512, 128)
                    scores = mm_t(qm, k) + (text_bias if text else self_bias)
                    top = jnp.max(scores, axis=-1, keepdims=True)
                    e = jnp.exp(scores - top)
                    total = jnp.sum(e, axis=-1, keepdims=True)
                    probs = (e * (1.0 / total)).astype(BF16)
                    mix = jnp.where(keep, mm(probs, v), 0.0)
                    lane = p * 2 + head + 8 * text
                    lse_ref[slots, :, lane : lane + 1] = (top + jnp.log(total)).reshape(2, 128, 1)
                    if text:
                        other = other + mix
                    else:
                        own = own + mix
            other_ref[p, slots] = other.reshape(2, 128, 128)
            both = own + gate_ref[p : p + 1, :] * other
            if p < 2:
                cw[p, slots, :, 128:256] = both.astype(BF16).reshape(2, 128, 128)
            else:
                moved = pltpu.roll(both, 64, 1)
                zero = jnp.zeros_like(both)
                cw[0, slots, :, 0:128] = jnp.where(low_rows, zero, moved).astype(BF16).reshape(2, 128, 128)
                cw[1, slots, :, 0:128] = jnp.where(low_rows, zero, both).astype(BF16).reshape(2, 128, 128)
            return carry

        lax.fori_loop(0, 2, rows_step, 0)

    attend(0)
    gf.step5()
    attend(1)
    attend(2)

    def out_rows(lo, count):
        n = count * 128
        a0 = cw[0, lo : lo + count].reshape(n, 256)
        a1 = cw[1, lo : lo + count].reshape(n, 256)
        for xb in range(2):
            cols = slice(xb * 768, xb * 768 + 768)
            b0 = w_a[0, xb, :, :, :, 512:768].reshape(768, 256)
            b1 = w_a[1, xb, :, :, :, 512:768].reshape(768, 256)
            total = mm_t(a0, b0) + mm_t(a1, b1)
            part[lo : lo + count, :, cols] = total.astype(BF16).reshape(count, 128, 768)

    sums = ZScatter(send, part, relay, got, right, left)
    out_rows(1, 2)
    sums.near()
    out_rows(3, 1)
    sums.far()
    out_rows(0, 1)
    sums.pass_on()
    attn = sums.total()
    attn_ref[...] = attn
    unit_two, _ = normalize(attn)
    live = live_ref[...][:, :1]
    middle = resid_ref[...].astype(F32) + live * jnp.tanh(mod_ref[1:2, :]) * unit_two * gains_ref[1:2, :]
    mid_ref[...] = middle
    unit_three, _ = normalize(middle)
    second_ref[...] = (unit_three * gains_ref[2:3, :] * (1.0 + mod_ref[2:3, :])).astype(BF16)
    cot_swap.wait_recv()
    gf.finish()
    send.drain()


def attention_call(args, cid):
    S = jax.ShapeDtypeStruct
    vm = pl.BlockSpec(memory_space=VMEM)
    sm = pl.BlockSpec(memory_space=pltpu.SMEM)
    any_ = pl.BlockSpec(memory_space=pl.ANY)
    pair = (3, 4, 128, 128)
    outs = [
        S((2, 2, 4, 2, 96, 768), BF16),
        S((2, 2, 4, 2, 96, D), BF16),
        S((4, 128, D), BF16),
        S((128, D), BF16),
        S((2, 64, D), BF16),
        S(pair, BF16),
        S(pair, BF16),
        S(pair, BF16),
        S(pair, F32),
        S(pair, F32),
        S((3, 256, 128), BF16),
        S((3, 256, 128), BF16),
        S((3, 256, 128), F32),
        S(pair, F32),
        S((4, 128, 128), F32),
        S((2, 4, 128, 256), BF16),
        S((128, D), F32),
        S((128, D), F32),
        S((128, D), BF16),
        S((8, D), F32),
        S((8, D), F32),
        S((16, 8, 128), F32),
        S((4, 128, 128), F32),
        S((4, 128, 128), F32),
        S((128, 128), F32),
    ]
    return pl.pallas_call(
        attention_kernel,
        out_shape=outs,
        in_specs=[vm] * 11 + [any_] + [vm] * 2 + [sm] * 4,
        out_specs=[vm, any_] + [vm] * (len(outs) - 2),
        scratch_shapes=[
            VMEM((96, 768), BF16),
            VMEM((96, D), BF16),
            VMEM((256, 384), BF16),
            VMEM((2, 2, 4, 2, 256, 384), BF16),
            VMEM((256, 4096), BF16),
            VMEM((4, 2, 64, D), BF16),
            VMEM((2, 64, D), BF16),
            VMEM((16, 8, 128), F32),
            VMEM((16, 16, 128), F32),
            VMEM((16, 16, 128), F32),
            VMEM((8, 16, 128), F32),
            VMEM((2, 2, 512, 128), F32),
            VMEM((2, 256, 384), F32),
            VMEM((4, 128, D), BF16),
            VMEM((2, 64, D), BF16),
            VMEM((2, 128, D), BF16),
            pltpu.SemaphoreType.DMA((4,)),
        ]
        + dma_sems(160),
        compiler_params=pltpu.CompilerParams(
            collective_id=cid, has_side_effects=True, vmem_limit_bytes=56 * 2**20
        ),
        name="attention",
    )(*args)


def ffn_kernel(
    x_ref,
    w_hbm,
    mid_ref,
    attn_ref,
    cot_ref,
    mod_ref,
    gain_ref,
    live_ref,
    out_ref,
    gmid_ref,
    gattn_ref,
    sums_ref,
    dw_ref,
    w,
    x_all,
    g_all,
    act,
    dgate,
    dup,
    gpre,
    part1,
    part2,
    relay1,
    relay2,
    got1,
    got2,
    flip,
    own_g,
    w_sem,
    ss,
    rs,
):
    z, right, left = z_ring()
    load = pltpu.make_async_copy(w_hbm, w, w_sem)
    load.start()
    greet([right, left])
    send = Sender(ss, rs)
    one = ZGather(send, x_ref, x_all, right, left)
    x_all[0] = x_ref[...]
    load.wait()

    def pre(lo, count):
        rows = count * 128
        x = x_all[lo : lo + count].reshape(rows, D)
        for xx in range(2):

            def column(j, carry, xx=xx):
                g = mm(x, w[xx, :, tile(j)])
                u = mm(x, w[xx, :, tile(j + 2)])
                s = jax.nn.sigmoid(g)
                gs = g * s
                act[xx, lo : lo + count, :, tile(j)] = (gs * u).astype(BF16).reshape(count, 128, 256)
                dgate[xx, lo : lo + count, :, tile(j)] = (u * s * (1.0 + g * (1.0 - s))).reshape(count, 128, 256)
                dup[xx, lo : lo + count, :, tile(j)] = gs.reshape(count, 128, 256)
                return carry

            lax.fori_loop(0, 2, column, 0)

    def down(lo, count):
        rows = count * 128
        a0 = act[0, lo : lo + count].reshape(rows, 512)
        a1 = act[1, lo : lo + count].reshape(rows, 512)

        def column(j, carry):
            cols = tile(j)
            total = mm_t(a0, w[0, cols, 1024:1536]) + mm_t(a1, w[1, cols, 1024:1536])
            part1[lo : lo + count, :, cols] = total.astype(BF16).reshape(count, 128, 256)
            return carry

        lax.fori_loop(0, D // 256, column, 0)

    sum1 = ZScatter(send, part1, relay1, got1, right, left)
    pre(0, 1)
    one.near()
    pre(1, 2)
    down(1, 2)
    sum1.near()
    one.far()
    pre(3, 1)
    down(3, 1)
    sum1.far()
    down(0, 1)
    transpose_into(x_all, flip)
    sum1.pass_on()
    ffn_total = sum1.total()

    live = live_ref[...][:, :1]
    mod = mod_ref[...]
    gains = gain_ref[...]
    gate_f = jnp.tanh(mod[3:4])
    middle = mid_ref[...]
    unit_four, inverse_four = normalize(ffn_total)
    out_ref[...] = (middle + live * gate_f * unit_four * gains[3:4]).astype(BF16)
    grad_top = cot_ref[...].astype(F32)
    weighted = grad_top * live
    part_four = jnp.sum(weighted * unit_four, axis=0, keepdims=True)
    own_g[...] = norm_back(unit_four, inverse_four, weighted * gate_f * gains[3:4]).astype(BF16)
    two = ZGather(send, own_g, g_all, right, left)
    g_all[0] = own_g[...]
    sums_ref[3:4, :] = part_four * gains[3:4] * (1.0 - gate_f * gate_f)
    sums_ref[7:8, :] = part_four * gate_f

    def back(lo, count):
        rows = count * 128
        g = g_all[lo : lo + count].reshape(rows, D)
        for xx in range(2):

            def column(j, carry, xx=xx):
                ga = mm(g, w[xx, :, tile(j + 4)])
                dg = dgate[xx, lo : lo + count, :, tile(j)].reshape(rows, 256)
                du = dup[xx, lo : lo + count, :, tile(j)].reshape(rows, 256)
                gpre[xx, lo : lo + count, :, tile(j)] = (ga * dg).astype(BF16).reshape(count, 128, 256)
                gpre[xx, lo : lo + count, :, tile(j + 2)] = (ga * du).astype(BF16).reshape(count, 128, 256)
                return carry

            lax.fori_loop(0, 2, column, 0)

    def back_in(lo, count):
        rows = count * 128
        a0 = gpre[0, lo : lo + count].reshape(rows, 1024)
        a1 = gpre[1, lo : lo + count].reshape(rows, 1024)

        def column(j, carry):
            cols = tile(j)
            total = mm_t(a0, w[0, cols, 0:1024]) + mm_t(a1, w[1, cols, 0:1024])
            part2[lo : lo + count, :, cols] = total.astype(BF16).reshape(count, 128, 256)
            return carry

        lax.fori_loop(0, D // 256, column, 0)

    sum2 = ZScatter(send, part2, relay2, got2, right, left)
    back(0, 1)
    two.near()
    back(1, 2)
    back_in(1, 2)
    sum2.near()
    two.far()
    back(3, 1)
    back_in(3, 1)
    sum2.far()
    back_in(0, 1)

    def weight_grad(right_of, first, count):
        def column(i, carry):
            xx = i // count
            j = i % count
            b = right_of(xx, j).reshape(512, 256)
            for r in range(0, D, 512):
                dw_ref[xx, r : r + 512, tile(j + first)] = mm(flip[r : r + 512, :], b).astype(BF16)
            return carry

        lax.fori_loop(0, 2 * count, column, 0)

    weight_grad(lambda xx, j: gpre[xx, :, :, tile(j)], 0, 4)
    sum2.pass_on()
    transpose_into(g_all, flip)
    weight_grad(lambda xx, j: act[xx, :, :, tile(j)], 4, 2)
    grad_second = sum2.total()

    scale_f = mod[2:3]
    unit_three, inverse_three = normalize(middle)
    sum_three = jnp.sum(grad_second * unit_three, axis=0, keepdims=True)
    sums_ref[2:3, :] = sum_three * gains[2:3]
    sums_ref[6:7, :] = sum_three * (1.0 + scale_f)
    grad_middle = grad_top + norm_back(
        unit_three, inverse_three, grad_second * (1.0 + scale_f) * gains[2:3]
    )
    gmid_ref[...] = grad_middle
    gate_a = jnp.tanh(mod[1:2])
    unit_two, inverse_two = normalize(attn_ref[...])
    weighted_mid = grad_middle * live
    sum_two = jnp.sum(weighted_mid * unit_two, axis=0, keepdims=True)
    sums_ref[1:2, :] = sum_two * gains[1:2] * (1.0 - gate_a * gate_a)
    sums_ref[5:6, :] = sum_two * gate_a
    sums_ref[0:1, :] = jnp.zeros((1, D), F32)
    sums_ref[4:5, :] = jnp.zeros((1, D), F32)
    gattn_ref[...] = norm_back(unit_two, inverse_two, weighted_mid * gate_a * gains[1:2]).astype(BF16)
    send.drain()


def ffn_call(second_in, w_f, middle, attn, cot, mod_rows, gains, live, cid):
    S = jax.ShapeDtypeStruct
    vm = pl.BlockSpec(memory_space=VMEM)
    any_ = pl.BlockSpec(memory_space=pl.ANY)
    return pl.pallas_call(
        ffn_kernel,
        out_shape=[
            S((128, D), BF16),
            S((128, D), F32),
            S((128, D), BF16),
            S((8, D), F32),
            S((2, D, D), BF16),
        ],
        in_specs=[vm, any_] + [vm] * 6,
        out_specs=[vm] * 5,
        scratch_shapes=[
            VMEM((2, D, D), BF16),
            VMEM((4, 128, D), BF16),
            VMEM((4, 128, D), BF16),
            VMEM((2, 4, 128, 512), BF16),
            VMEM((2, 4, 128, 512), F32),
            VMEM((2, 4, 128, 512), F32),
            VMEM((2, 4, 128, 1024), BF16),
            VMEM((4, 128, D), BF16),
            VMEM((4, 128, D), BF16),
            VMEM((2, 64, D), BF16),
            VMEM((2, 64, D), BF16),
            VMEM((2, 128, D), BF16),
            VMEM((2, 128, D), BF16),
            VMEM((D, 512), BF16),
            VMEM((128, D), BF16),
            pltpu.SemaphoreType.DMA,
        ]
        + dma_sems(20),
        compiler_params=pltpu.CompilerParams(
            collective_id=cid, has_side_effects=True, vmem_limit_bytes=56 * 2**20
        ),
        name="ffn",
    )(second_in, w_f, middle, attn, cot, mod_rows, gains, live)


def pick(array, index):
    return lax.dynamic_index_in_dim(array, index, 0, keepdims=False)


def dot(spec, a, b):
    return jnp.einsum(spec, a, b, preferred_element_type=F32)


def on_device(
    hidden,
    condition,
    caption,
    lengths,
    frames,
    widths,
    caption_lens,
    cotangent,
    ada_weight,
    ada_bias,
    norm_gains,
    qkv_weight,
    head_gains,
    caption_weight,
    head_gate,
    out_weight,
    ffn_weight,
    down_weight,
):
    S = jax.ShapeDtypeStruct
    dp = lax.axis_index("dp")
    t = lax.axis_index("tensor")
    z = t // 2
    xl = t % 2
    def head_tiles(rows):
        return jnp.concatenate([rows, rows], axis=-1)

    head_scales = head_gains.astype(F32)
    hg2 = jnp.pad(head_tiles(head_scales), ((0, 5), (0, 0)))
    gate_values = jnp.tanh(lax.dynamic_slice_in_dim(head_gate.astype(F32), z * 6, 6, 0))
    gate_tile = jnp.pad(
        jnp.repeat(gate_values[jnp.array([0, 1, 3, 4, 2, 5])].reshape(3, 2), 64, axis=1),
        ((0, 5), (0, 0)),
    )
    (
        w_a,
        w_f,
        first_rel,
        resid_b,
        cot,
        q8,
        kk,
        vv,
        qr,
        kr,
        tk,
        tv,
        tkr,
        other_rel,
        lse,
        cw,
        attn,
        middle,
        second_in,
        mod8,
        gains8,
        got1,
        cos_t,
        sin_t,
        live128,
    ) = attention_call(
        [
            hidden[:, 0],
            cotangent[:, 0],
            condition[:, 0],
            norm_gains,
            ada_bias[None],
            ada_weight,
            qkv_weight,
            out_weight.T,
            ffn_weight,
            down_weight.T,
            caption_weight,
            caption[:, 0],
            hg2,
            gate_tile,
            lengths,
            frames,
            widths,
            caption_lens,
        ],
        1,
    )
    w_f = w_f.reshape(2, D, D)
    w_a = w_a.reshape(2, D, 768)
    perm = jnp.array([0, 2, 3, 1])[(jnp.arange(4) - z) % 4]

    def nat(v):
        return v[perm].reshape((512,) + v.shape[2:])

    def heads_of(v):
        v = jnp.stack([nat(v[i]) for i in range(3)]) if v.ndim == 4 else v
        v = v.reshape(3, v.shape[1], 2, 64)
        return jnp.stack([v[0, :, 0], v[0, :, 1], v[2, :, 0], v[1, :, 0], v[1, :, 1], v[2, :, 1]], axis=1)

    mod_rows, gains = mod8[:4], gains8[:4]
    scale_attn = mod_rows[0]
    units = got1[:, 0:2, :64].reshape(32, 64)
    first_all = nat(first_rel)
    resid = resid_b.astype(F32)
    w_q = w_a[:, :, :192]
    w_k = jnp.concatenate([w_a[:, :, 256:384], w_a[:, :, 192:256]], axis=2)
    w_v = w_a[:, :, 384:576]
    w_o = jnp.concatenate([w_a[:, :, 640:768], w_a[:, :, 576:640]], axis=2)
    unit_one, inverse_one = normalize(resid)
    query_unit, query_inverse = normalize(heads_of(qr))
    key_unit, key_inverse = normalize(heads_of(kr))
    text_unit, text_inverse = normalize(heads_of(tkr))
    queries, keys, values = heads_of(q8) * 8.0, heads_of(kk), heads_of(vv)
    text_keys, text_values = heads_of(tk), heads_of(tv)
    other = heads_of(other_rel)
    cos64, sin64 = nat(cos_t), nat(sin_t)
    cosine, sine_table = cos64[:, :32], -sin64[:, :32]
    lse_n = nat(lse)
    horder = jnp.array([0, 1, 4, 2, 3, 5])
    length = pick(lengths[:, 0], xl)
    text_len = pick(caption_lens[:, 0], xl)
    cap = pick(caption[:, 0], xl)
    key_live = jnp.arange(512) < length
    text_live = jnp.arange(256) < text_len
    scaling = 0.125

    def reprob(keyset, live, lses):
        sc = dot("qhd,khd->hqk", queries, keyset) * scaling
        sc = jnp.where(live[None, None], sc, NEGATIVE)
        return jnp.exp(sc - lses.T[:, :, None])

    probs = reprob(keys, key_live, lse_n[:, :6][:, horder])
    text_probs = reprob(text_keys, text_live, lse_n[:, 8:14][:, horder])
    comb0 = jnp.concatenate([nat(cw[0])[:, 128:256], nat(cw[0])[:, 64:128]], axis=1)
    comb1 = jnp.concatenate([nat(cw[1])[:, 128:256], nat(cw[1])[:, 64:128]], axis=1)
    combined = jnp.stack([comb0, comb1], axis=1)
    hs = (512, 6, HD)
    ts = (256, 6, HD)
    layer_out, grad_middle, grad_attn_in, ffn_sums, f_grad = ffn_call(
        second_in,
        w_f,
        middle,
        attn,
        cot.reshape(128, D),
        mod8,
        gains8,
        live128,
        6,
    )
    grad_top = cot.reshape(128, D).astype(F32)
    grad_one = z_gather(grad_attn_in, 10)
    grad_combined = dot("sd,xdk->sxk", grad_one, w_o).astype(BF16)
    out_grad = dot("sd,sxk->xdk", grad_one, combined)
    grad_heads = grad_combined.reshape(hs)
    gate_local = jnp.sum(grad_heads.astype(F32) * other, axis=(0, 2)) * (
        1.0 - gate_values * gate_values
    )
    grad_text_heads = (gate_values[None, :, None] * grad_heads.astype(F32)).astype(BF16)

    def back(p, grad, vals):
        grad_values = dot("hqk,qhd->khd", p.astype(BF16), grad)
        grad_probs = dot("qhd,khd->hqk", grad, vals)
        grad_scores = p * (grad_probs - jnp.sum(p * grad_probs, axis=-1, keepdims=True))
        return grad_values, grad_scores.astype(BF16)

    grad_values, grad_scores = back(probs, grad_heads, values)
    grad_text_values, grad_text_scores = back(text_probs, grad_text_heads, text_values)
    grad_query = (
        dot("hqk,khd->qhd", grad_scores, keys) + dot("hqk,khd->qhd", grad_text_scores, text_keys)
    ) * scaling
    grad_keys = dot("hqk,qhd->khd", grad_scores, queries) * scaling
    grad_text_keys = dot("hqk,qhd->khd", grad_text_scores, queries) * scaling
    grad_query_rot = rotate_back(grad_query, cosine, sine_table)
    grad_key_rot = rotate_back(grad_keys, cosine, sine_table)
    head_query = jnp.sum(grad_query_rot * query_unit, axis=(0, 1))
    head_key = jnp.sum(grad_key_rot * key_unit, axis=(0, 1))
    head_text = jnp.sum(grad_text_keys * text_unit, axis=(0, 1))
    shape = (512, 2, 192)
    grad_q = norm_back(query_unit, query_inverse, grad_query_rot * head_scales[0])
    grad_k = norm_back(key_unit, key_inverse, grad_key_rot * head_scales[1])
    grad_q = grad_q.astype(BF16).reshape(shape)
    grad_k = grad_k.astype(BF16).reshape(shape)
    grad_v = grad_values.astype(BF16).reshape(shape)
    grad_tk = norm_back(text_unit, text_inverse, grad_text_keys * head_scales[2])
    grad_tk = grad_tk.astype(BF16).reshape(256, 2, 192)
    grad_tv = grad_text_values.astype(BF16).reshape(256, 2, 192)
    grad_first = z_scatter(
        (
            dot("sxk,xdk->sd", grad_q, w_q)
            + dot("sxk,xdk->sd", grad_k, w_k)
            + dot("sxk,xdk->sd", grad_v, w_v)
        ).astype(BF16),
        11,
    )
    scale_attn_grad = jnp.sum(grad_first * unit_one * gains[0], axis=0)
    gain_one = jnp.sum(grad_first * (1.0 + scale_attn) * unit_one, axis=0)
    grad_hidden = grad_middle + norm_back(
        unit_one, inverse_one, grad_first * (1.0 + scale_attn) * gains[0]
    )
    d_grad = jnp.concatenate(
        [
            dot("sd,sxk->xdk", first_all, grad_q).astype(BF16),
            dot("sd,sxk->xdk", first_all, grad_k).astype(BF16),
            dot("sd,sxk->xdk", first_all, grad_v).astype(BF16),
            out_grad.astype(BF16),
        ],
        axis=2,
    )
    c_grad = jnp.concatenate(
        [
            dot("td,txk->xdk", cap, grad_tk).astype(BF16),
            dot("td,txk->xdk", cap, grad_tv).astype(BF16),
        ],
        axis=2,
    )
    d_out = plane_scatter(d_grad, 12)
    f_out = plane_scatter(f_grad, 17)
    c_out = plane_scatter(c_grad, 13)
    out_half = layer_out.reshape(2, 64, D)
    grad_half = grad_hidden.reshape(2, 64, D)
    out_got, grad_got = kernel_call(
        swap_kernel,
        [out_half, grad_half],
        [S((2, 64, D), BF16), S((2, 64, D), F32)],
        14,
        dma_sems(2),
        name="swap_back",
    )
    mine = jnp.arange(2)[:, None, None] == xl
    layer_final = jnp.where(mine, pick(out_half, xl)[None], pick(out_got, 1 - xl)[None])
    grad_final = jnp.where(mine, pick(grad_half, xl)[None], pick(grad_got, 1 - xl)[None])

    mod_grad = jnp.concatenate([scale_attn_grad[None], ffn_sums[1:4]])
    mod_msg = jnp.pad(mod_grad.reshape(8, 6, 128), ((0, 0), (0, 2), (0, 0)))
    gain_grad = jnp.concatenate([gain_one[None], ffn_sums[5:8]])
    gain_part = jnp.pad(
        jnp.transpose(gain_grad.reshape(4, 16, 96), (1, 0, 2)), ((0, 0), (0, 0), (0, 32))
    )
    gate_part = lax.dynamic_update_slice_in_dim(jnp.zeros((64,), F32), gate_local, z * 6, 0)
    head_part = jnp.concatenate([head_query, head_key, head_text, gate_part]).reshape(2, 128)
    head_part = jnp.broadcast_to(jnp.pad(head_part, ((0, 2), (0, 0)))[None], (16, 4, 128))
    gain_msg = jnp.concatenate([gain_part, head_part], axis=1)
    g_all, gain_out, bias_all = kernel_call(
        small_kernel,
        [mod_msg, gain_msg],
        [S((16, 2, 8, 128), F32), S((8, 128), F32), S((8, 8, 128), F32)],
        15,
        [VMEM((8, 8, 128), F32), VMEM((16, 8, 128), F32), VMEM((8, 8, 128), F32)]
        + dma_sems(7)
        + dma_sems(15)
        + dma_sems(15)
        + dma_sems(7)
        + dma_sems(7),
        name="small_sums",
    )
    g_items = g_all[:, :, :6].reshape(32, 768)
    ada_grad = jnp.einsum("mc,mk->ck", units, g_items, precision=lax.Precision.HIGHEST)
    bias_block = pick(bias_all, dp // 2)[:6].reshape(2, 384)
    bias_grad = pick(bias_block, dp % 2)
    heads = gain_out[4:6].reshape(256)
    return (
        layer_final[:, None],
        grad_final[:, None],
        ada_grad,
        bias_grad,
        gain_out[:4, :96],
        jnp.stack([d_out[:, :192], d_out[:, 192:384], d_out[:, 384:576]]),
        heads[:192].reshape(3, 64),
        jnp.stack([c_out[:, :192], c_out[:, 192:]]),
        heads[192:216],
        d_out[:, 576:768].T,
        jnp.stack([f_out[:, :512], f_out[:, 512:1024]]),
        f_out[:, 1024:].T,
    )


def solution(mesh):
    return jax.shard_map(
        on_device,
        mesh=mesh,
        in_specs=(
            P(None, "dp", "tensor", None),
            P(None, "dp", None),
            P(None, "dp", None, None),
            P(None, "dp"),
            P(None, "dp"),
            P(None, "dp"),
            P(None, "dp"),
            P(None, "dp", "tensor", None),
            P("dp", "tensor"),
            P("dp"),
            P(None, "dp"),
            P(None, "dp", "tensor"),
            P(),
            P(None, "dp", "tensor"),
            P(),
            P("tensor", "dp"),
            P(None, "dp", "tensor"),
            P("tensor", "dp"),
        ),
        out_specs=(
            P(None, "dp", "tensor", None),
            P(None, "dp", "tensor", None),
            P("dp", "tensor"),
            P("dp"),
            P(None, "dp"),
            P(None, "dp", "tensor"),
            P(),
            P(None, "dp", "tensor"),
            P(),
            P("tensor", "dp"),
            P(None, "dp", "tensor"),
            P("tensor", "dp"),
        ),
        check_vma=False,
    )
```

```python
import functools

import jax
import jax.numpy as jnp
from jax import lax
from jax.experimental import pallas as pl
from jax.experimental.pallas import tpu as pltpu
from jax.sharding import PartitionSpec as P

D = 1536
H = 24
HD = 64
EPSILON = 1e-05
NEGATIVE = -1e30
MESH = pl.DeviceIdType.MESH
VMEM = pltpu.VMEM
F32 = jnp.float32
BF16 = jnp.bfloat16


def coords():
    dp = lax.axis_index("dp")
    t = lax.axis_index("tensor")
    return dp // 8, t % 2, (dp // 2) % 4, t // 2, dp % 2


def device_of(x, y, z, c):
    return ((x // 2) * 8 + y * 2 + c, z * 2 + x % 2)


def greet(devices):
    barrier = pltpu.get_barrier_semaphore()
    for device in devices:
        pl.semaphore_signal(barrier, inc=1, device_id=device, device_id_type=MESH)
    pl.semaphore_wait(barrier, len(devices))


class Sender:
    def __init__(self, send_sem, recv_sem):
        self.send_sem = send_sem
        self.recv_sem = recv_sem
        self.copies = []

    def __call__(self, src, dst, device):
        k = len(self.copies)
        copy = pltpu.make_async_remote_copy(
            src_ref=src,
            dst_ref=dst,
            send_sem=self.send_sem.at[k],
            recv_sem=self.recv_sem.at[k],
            device_id=device,
            device_id_type=MESH,
        )
        copy.start()
        self.copies.append(copy)
        return copy

    def drain(self):
        for copy in self.copies:
            copy.wait_send()


def dma_sems(n):
    return [pltpu.SemaphoreType.DMA((n,)), pltpu.SemaphoreType.DMA((n,))]


def kernel_call(body, inputs, out_shape, cid, scratch, in_space=VMEM, out_space=VMEM, name=None):
    single = not isinstance(out_shape, (tuple, list))
    spec = pl.BlockSpec(memory_space=out_space)
    return pl.pallas_call(
        body,
        out_shape=out_shape,
        in_specs=[pl.BlockSpec(memory_space=in_space)] * len(inputs),
        out_specs=spec if single else [spec] * len(out_shape),
        scratch_shapes=scratch,
        compiler_params=pltpu.CompilerParams(
            collective_id=cid, has_side_effects=True, vmem_limit_bytes=56 * 2**20
        ),
        name=name,
    )(*inputs)


def mod_kernel(msg_ref, ada_ref, bias_ref, got1, got3, sent, got2, s1, r1, s2, r2, s3, r3):
    dp = lax.axis_index("dp")
    t = lax.axis_index("tensor")
    dp_peers = [((dp + k) % 16, t) for k in range(1, 16)]
    t_peers = [(dp, (t + k) % 8) for k in range(1, 8)]
    greet(dp_peers + t_peers)
    first = Sender(s1, r1)
    for peer in dp_peers:
        first(msg_ref.at[peer[0]], got1.at[dp], peer)
    got1[dp] = msg_ref[dp]
    for copy in first.copies:
        copy.wait_recv()
    rows = got1[...].reshape(128, 128).astype(BF16)
    part = jnp.dot(rows, ada_ref[...], preferred_element_type=F32) + bias_ref[...]
    sent[...] = part.reshape(16, 8, 768)
    second = Sender(s2, r2)
    for peer in dp_peers:
        second(sent.at[peer[0]], got2.at[dp], peer)
    got2[dp] = sent[dp]
    for copy in second.copies:
        copy.wait_recv()
    got3[t] = jnp.sum(got2[...], axis=0)
    third = Sender(s3, r3)
    for peer in t_peers:
        third(got3.at[t], got3.at[t], peer)
    for copy in third.copies:
        copy.wait_recv()
    for sender in (first, second, third):
        sender.drain()


def hidden_kernel(hid_ref, cot_ref, all_ref, cot_out, ss, rs):
    xh, xl, y, z, c = coords()
    pair = device_of(2 * xh + 1 - xl, y, z, c)
    right = device_of(2 * xh + xl, y, (z + 1) % 4, c)
    left = device_of(2 * xh + xl, y, (z + 3) % 4, c)
    greet([pair, right, left])
    send = Sender(ss, rs)
    swap = send(hid_ref.at[1 - xl], all_ref.at[z, xl], pair)
    all_ref[z, xl] = hid_ref[xl]
    cot_swap = send(cot_ref.at[1 - xl], cot_out.at[xl], pair)
    cot_out[xl] = cot_ref[xl]
    swap.wait_recv()
    zl = (z + 3) % 4
    zr = (z + 1) % 4
    to_right = send(all_ref.at[z], all_ref.at[z], right)
    to_left = send(all_ref.at[z], all_ref.at[z], left)
    to_right.wait_recv()
    on_right = send(all_ref.at[zl, 0], all_ref.at[zl, 0], right)
    to_left.wait_recv()
    on_left = send(all_ref.at[zr, 1], all_ref.at[zr, 1], left)
    on_right.wait_recv()
    on_left.wait_recv()
    cot_swap.wait_recv()
    send.drain()


def swap_kernel(out_ref, grad_ref, out_got, grad_got, ss, rs):
    xh, xl, y, z, c = coords()
    pair = device_of(2 * xh + 1 - xl, y, z, c)
    greet([pair])
    send = Sender(ss, rs)
    a = send(out_ref.at[1 - xl], out_got.at[xl], pair)
    b = send(grad_ref.at[1 - xl], grad_got.at[xl], pair)
    a.wait_recv()
    b.wait_recv()
    send.drain()


def z_gather_kernel(x_ref, all_ref, ss, rs):
    xh, xl, y, z, c = coords()
    right = device_of(2 * xh + xl, y, (z + 1) % 4, c)
    left = device_of(2 * xh + xl, y, (z + 3) % 4, c)
    greet([left, right])
    send = Sender(ss, rs)
    to_right = send(x_ref, all_ref.at[z], right)
    to_left = send(x_ref, all_ref.at[z], left)
    all_ref[z] = x_ref[...]
    zl = (z + 3) % 4
    zr = (z + 1) % 4
    lower, upper = pl.ds(0, 64), pl.ds(64, 64)
    to_right.wait_recv()
    on_right = send(all_ref.at[zl, lower], all_ref.at[zl, lower], right)
    to_left.wait_recv()
    on_left = send(all_ref.at[zr, upper], all_ref.at[zr, upper], left)
    on_right.wait_recv()
    on_left.wait_recv()
    send.drain()


def z_scatter_kernel(x_ref, sum_ref, relay_r, relay_l, sum_r, sum_l, got_r, got_l, ss, rs):
    xh, xl, y, z, c = coords()
    right = device_of(2 * xh + xl, y, (z + 1) % 4, c)
    left = device_of(2 * xh + xl, y, (z + 3) % 4, c)
    greet([left, right])
    send = Sender(ss, rs)
    zl = (z + 3) % 4
    zr = (z + 1) % 4
    zo = (z + 2) % 4
    lower, upper = pl.ds(0, 64), pl.ds(64, 64)
    relay1 = send(x_ref.at[zo, lower], relay_r, right)
    relay2 = send(x_ref.at[zo, upper], relay_l, left)
    near1 = send(x_ref.at[zr, upper], got_r.at[upper], right)
    near2 = send(x_ref.at[zl, lower], got_l.at[lower], left)
    relay1.wait_recv()
    sum_r[...] = (relay_r[...].astype(F32) + x_ref[zr, lower].astype(F32)).astype(BF16)
    far1 = send(sum_r, got_r.at[lower], right)
    relay2.wait_recv()
    sum_l[...] = (relay_l[...].astype(F32) + x_ref[zl, upper].astype(F32)).astype(BF16)
    far2 = send(sum_l, got_l.at[upper], left)
    for copy in (near1, near2, far1, far2):
        copy.wait_recv()
    sum_ref[...] = x_ref[z].astype(F32) + got_r[...].astype(F32) + got_l[...].astype(F32)
    send.drain()


def z_gather(x, cid):
    return kernel_call(
        z_gather_kernel,
        [x],
        jax.ShapeDtypeStruct((4, 128, D), BF16),
        cid,
        dma_sems(4),
        name="z_gather%d" % cid,
    ).reshape(512, D)


def z_scatter(x, cid):
    half = VMEM((64, D), BF16)
    full = VMEM((128, D), BF16)
    return kernel_call(
        z_scatter_kernel,
        [x.reshape(4, 128, D)],
        jax.ShapeDtypeStruct((128, D), F32),
        cid,
        [half, half, half, half, full, full] + dma_sems(6),
        name="z_scatter%d" % cid,
    )


def plane_peers():
    xh, xl, y, z, c = coords()
    x = 2 * xh + xl
    xr, xq = (x + 1) % 4, (x + 3) % 4
    yr, yq = (y + 1) % 4, (y + 3) % 4
    peers = [
        device_of(xr, y, z, c),
        device_of(xq, y, z, c),
        device_of(x, yr, z, c),
        device_of(x, yq, z, c),
        device_of(x, y, z, 1 - c),
    ]
    return x, y, c, xr, xq, yr, yq, peers


def plane_gather_kernel(rows, cols, w_ref, all_ref, ss, rs, local_sem):
    x, y, c, xr, xq, yr, yq, peers = plane_peers()
    go_xr, go_xq, go_yr, go_yq, sibling = peers
    greet(peers)
    send = Sender(ss, rs)
    half = rows // 2
    top, low = pl.ds(0, half), pl.ds(half, half)

    def at(xx, yy, *rest):
        return all_ref.at[(xx % 2, xx // 2, yy, c) + rest]

    def same(ref, device):
        return send(ref, ref, device)

    local = pltpu.make_async_copy(w_ref, at(x, y), local_sem)
    local.start()
    a_r = send(w_ref.at[top], at(x, y, top), go_xr)
    a_l = send(w_ref.at[top], at(x, y, top), go_xq)
    b_r = send(w_ref.at[low], at(x, y, low), go_yr)
    b_l = send(w_ref.at[low], at(x, y, low), go_yq)
    own = send(w_ref, at(x, y), sibling)
    if rows == 96:
        left_half, right_half = pl.ds(0, cols // 2), pl.ds(cols // 2, cols // 2)
        qa = [(top, left_half), (top, right_half)]
        qb = [(low, left_half), (low, right_half)]
    else:
        q = half // 2
        qa = [(pl.ds(0, q),), (pl.ds(q, q),)]
        qb = [(pl.ds(2 * q, q),), (pl.ds(3 * q, q),)]
    a_r.wait_recv()
    f1 = same(at(xq, y, *qa[0]), go_xr)
    a_l.wait_recv()
    f2 = same(at(xr, y, *qa[1]), go_xq)
    b_r.wait_recv()
    f3 = same(at(x, yq, *qb[0]), go_yr)
    b_l.wait_recv()
    f4 = same(at(x, yr, *qb[1]), go_yq)
    for copy in (f1, f2, f3, f4):
        copy.wait_recv()
    local.wait()
    every = slice(None)
    block = all_ref.at[:, :, y, c, top]
    g_r = same(block, go_yr)
    g_l = same(block, go_yq)
    block = all_ref.at[x % 2, x // 2, :, c, low]
    h_r = same(block, go_xr)
    h_l = same(block, go_xq)
    g_r.wait_recv()
    f1 = same(all_ref.at[0, :, yq, c, top], go_yr)
    g_l.wait_recv()
    f2 = same(all_ref.at[1, :, yr, c, top], go_yq)
    h_r.wait_recv()
    f3 = same(all_ref.at[xq % 2, xq // 2, pl.ds(0, 2), c, low], go_xr)
    h_l.wait_recv()
    f4 = same(all_ref.at[xr % 2, xr // 2, pl.ds(2, 2), c, low], go_xq)
    for copy in (f1, f2, f3, f4):
        copy.wait_recv()
    late = []
    for k in range(1, 4):
        xx = (x + k) % 4
        late.append(same(all_ref.at[xx % 2, xx // 2, :, c], sibling))
    for k in range(1, 4):
        late.append(same(at(x, (y + k) % 4), sibling))
    for copy in late:
        copy.wait_recv()
    own.wait_recv()
    send.drain()


def plane_gather(w, cid):
    rows, cols = w.shape
    return kernel_call(
        functools.partial(plane_gather_kernel, rows, cols),
        [w],
        jax.ShapeDtypeStruct((2, 2, 4, 2, rows, cols), BF16),
        cid,
        dma_sems(24) + [pltpu.SemaphoreType.DMA],
        pl.ANY,
        pl.ANY,
        name="plane_gather%d" % cid,
    ).reshape(2, 16 * rows, cols)


def add_low(a, b):
    return (a.astype(F32) + b.astype(F32)).astype(BF16)


def plane_scatter_kernel(rows, cols, g_ref, out_ref, sib, ra, rb, ga, gb, pa, pb, qa, qb, ss, rs):
    x, y, c, xr, xq, yr, yq, peers = plane_peers()
    go_xr, go_xq, go_yr, go_yq, sibling = peers
    greet(peers)
    send = Sender(ss, rs)
    half = rows // 2
    top, low = pl.ds(0, half), pl.ds(half, half)
    xo, yo = (x + 2) % 4, (y + 2) % 4
    parts = []
    for k in range(4):
        parts.append(
            send(g_ref.at[k % 2, k // 2, :, 1 - c], sib.at[k % 2, k // 2], sibling)
        )
    for k in range(4):
        parts[k].wait_recv()

        def add_sibling(j, carry, k=k):
            sib[k % 2, k // 2, j] = add_low(sib[k % 2, k // 2, j], g_ref[k % 2, k // 2, j, c])
            return carry

        lax.fori_loop(0, 4, add_sibling, 0)
    t1 = send(sib.at[0, :, yo, top], ra.at[0], go_yr)
    t2 = send(sib.at[1, :, yo, top], ra.at[1], go_yq)
    l1 = send(sib.at[xo % 2, xo // 2, pl.ds(0, 2), low], rb.at[0], go_xr)
    l2 = send(sib.at[xo % 2, xo // 2, pl.ds(2, 2), low], rb.at[1], go_xq)
    t1.wait_recv()
    for j in range(2):
        sib[0, j, yr, top] = add_low(sib[0, j, yr, top], ra[0, j])
    t2.wait_recv()
    for j in range(2):
        sib[1, j, yq, top] = add_low(sib[1, j, yq, top], ra[1, j])
    t3 = send(sib.at[:, :, yr, top], ga.at[0], go_yr)
    t4 = send(sib.at[:, :, yq, top], ga.at[1], go_yq)
    l1.wait_recv()
    for j in range(2):
        sib[xr % 2, xr // 2, j, low] = add_low(sib[xr % 2, xr // 2, j, low], rb[0, j])
    l2.wait_recv()
    for j in range(2):
        sib[xq % 2, xq // 2, 2 + j, low] = add_low(sib[xq % 2, xq // 2, 2 + j, low], rb[1, j])
    l3 = send(sib.at[xr % 2, xr // 2, :, low], gb.at[0], go_xr)
    l4 = send(sib.at[xq % 2, xq // 2, :, low], gb.at[1], go_xq)
    t3.wait_recv()
    t4.wait_recv()
    for i in range(2):
        for j in range(2):
            total = (
                sib[i, j, y, top].astype(F32) + ga[0, i, j].astype(F32) + ga[1, i, j].astype(F32)
            )
            pa[i, j] = total.astype(BF16)
    q = half // 2
    q0, q1 = pl.ds(0, q), pl.ds(q, q)
    if rows == 96:
        q0 = (slice(None), pl.ds(0, cols // 2))
        q1 = (slice(None), pl.ds(cols // 2, cols // 2))
        shape0 = (half, cols // 2)
    else:
        q0, q1 = (pl.ds(0, q),), (pl.ds(q, q),)
        shape0 = (q, cols)
    e1 = send(pa.at[(xo % 2, xo // 2) + q0], qa.at[0], go_xr)
    e2 = send(pa.at[(xo % 2, xo // 2) + q1], qa.at[1], go_xq)
    l3.wait_recv()
    l4.wait_recv()
    for j in range(4):
        total = (
            sib[x % 2, x // 2, j, low].astype(F32) + gb[0, j].astype(F32) + gb[1, j].astype(F32)
        )
        pb[j] = total.astype(BF16)
    m1 = send(pb.at[(yo,) + q0], qb.at[0], go_yr)
    m2 = send(pb.at[(yo,) + q1], qb.at[1], go_yq)
    e1.wait_recv()
    ir = (xr % 2, xr // 2)
    iq = (xq % 2, xq // 2)
    pa[ir + q0] = add_low(pa[ir + q0], qa[0])
    e2.wait_recv()
    pa[iq + q1] = add_low(pa[iq + q1], qa[1])
    e3 = send(pa.at[ir], ga.at[0, 0, 0], go_xr)
    e4 = send(pa.at[iq], ga.at[1, 0, 0], go_xq)
    m1.wait_recv()
    pb[(yr,) + q0] = add_low(pb[(yr,) + q0], qb[0])
    m2.wait_recv()
    pb[(yq,) + q1] = add_low(pb[(yq,) + q1], qb[1])
    m3 = send(pb.at[yr], gb.at[0, 0], go_yr)
    m4 = send(pb.at[yq], gb.at[1, 0], go_yq)
    e3.wait_recv()
    e4.wait_recv()
    out_ref[top] = (
        pa[x % 2, x // 2].astype(F32) + ga[0, 0, 0].astype(F32) + ga[1, 0, 0].astype(F32)
    )
    m3.wait_recv()
    m4.wait_recv()
    out_ref[low] = pb[y].astype(F32) + gb[0, 0].astype(F32) + gb[1, 0].astype(F32)
    send.drain()


def plane_scatter(g, cid):
    _, total_rows, cols = g.shape
    rows = total_rows // 16
    half = rows // 2
    quarter = (half, cols // 2) if rows == 96 else (half // 2, cols)
    return kernel_call(
        functools.partial(plane_scatter_kernel, rows, cols),
        [g.reshape(2, 2, 4, 2, rows, cols)],
        jax.ShapeDtypeStruct((rows, cols), F32),
        cid,
        [
            VMEM((2, 2, 4, rows, cols), BF16),
            VMEM((2, 2, half, cols), BF16),
            VMEM((2, 2, half, cols), BF16),
            VMEM((2, 2, 2, half, cols), BF16),
            VMEM((2, 4, half, cols), BF16),
            VMEM((2, 2, half, cols), BF16),
            VMEM((4, half, cols), BF16),
            VMEM((2,) + quarter, BF16),
            VMEM((2,) + quarter, BF16),
        ]
        + dma_sems(20),
        name="plane_scatter%d" % cid,
    )


def small_kernel(mod_ref, gain_ref, g_all, gain_out, bias_all, gt, gg, gsum, s1, r1, s2, r2, s3, r3, s4, r4, s5, r5):
    dp = lax.axis_index("dp")
    t = lax.axis_index("tensor")
    dp_peers = [((dp + k) % 16, t) for k in range(1, 16)]
    t_peers = [(dp, (t + k) % 8) for k in range(1, 8)]
    greet(dp_peers + t_peers)
    first = Sender(s1, r1)
    for peer in t_peers:
        first(mod_ref.at[peer[1]], gt.at[t], peer)
    gains = Sender(s2, r2)
    for peer in dp_peers:
        gains(gain_ref.at[peer[0]], gg.at[dp], peer)
    gt[t] = mod_ref[t]
    gg[dp] = gain_ref[dp]
    for copy in first.copies:
        copy.wait_recv()
    g_all[dp, 0] = gt[0] + gt[2] + gt[4] + gt[6]
    g_all[dp, 1] = gt[1] + gt[3] + gt[5] + gt[7]
    second = Sender(s3, r3)
    for peer in dp_peers:
        second(g_all.at[dp], g_all.at[dp], peer)
    for copy in gains.copies:
        copy.wait_recv()
    gsum[t] = jnp.sum(gg[...], axis=0)
    third = Sender(s4, r4)
    for peer in t_peers:
        third(gsum.at[t], gsum.at[t], peer)
    for copy in second.copies:
        copy.wait_recv()
    bias_all[t] = jnp.sum(g_all[...], axis=(0, 1))
    fourth = Sender(s5, r5)
    for peer in t_peers:
        fourth(bias_all.at[t], bias_all.at[t], peer)
    for copy in third.copies:
        copy.wait_recv()
    gain_out[...] = jnp.sum(gsum[...], axis=0)
    for copy in fourth.copies:
        copy.wait_recv()
    for sender in (first, gains, second, third, fourth):
        sender.drain()


def normalize(values):
    inverse = lax.rsqrt(jnp.mean(values * values, axis=-1, keepdims=True) + EPSILON)
    return (values * inverse, inverse)


def norm_back(unit_values, inverse, gradient):
    return inverse * (
        gradient - unit_values * jnp.mean(gradient * unit_values, axis=-1, keepdims=True)
    )


def swish(values):
    return values * jax.nn.sigmoid(values)


def rope_tables(length, frames, width, total, head_size):
    position = jnp.arange(total, dtype=jnp.int32)
    per_frame = (length + frames - 1) // frames
    frame_pos = position // per_frame
    within = position - frame_pos * per_frame
    row_pos = within // width
    col_pos = within - row_pos * width
    half_size = head_size // 2
    time_pairs = head_size // 8
    space_pairs = (half_size - time_pairs) // 2
    pair = jnp.arange(half_size, dtype=jnp.int32)
    in_row = pair >= time_pairs
    in_col = pair >= time_pairs + space_pairs
    offset = jnp.where(in_col, time_pairs + space_pairs, jnp.where(in_row, time_pairs, 0))
    group_size = jnp.where(in_row, space_pairs, time_pairs)
    freq = 10000.0 ** (-(pair - offset).astype(jnp.float32) / group_size.astype(jnp.float32))
    chosen = jnp.where(
        in_col[None, :],
        col_pos[:, None],
        jnp.where(in_row[None, :], row_pos[:, None], frame_pos[:, None]),
    )
    angle = chosen.astype(jnp.float32) * freq[None, :]
    return (jnp.cos(angle), jnp.sin(angle))


def rotate(values, cosine, sine_table):
    half_size = values.shape[-1] // 2
    first_half = values[..., :half_size]
    second_half = values[..., half_size:]
    cos_rows = cosine[:, None, :]
    sin_rows = sine_table[:, None, :]
    return jnp.concatenate(
        [
            first_half * cos_rows - second_half * sin_rows,
            first_half * sin_rows + second_half * cos_rows,
        ],
        axis=-1,
    )


def rotate_back(gradient, cosine, sine_table):
    return rotate(gradient, cosine, -sine_table)


def z_ring():
    xh, xl, y, z, c = coords()
    x = 2 * xh + xl
    return z, device_of(x, y, (z + 1) % 4, c), device_of(x, y, (z + 3) % 4, c)


class ZGather:
    def __init__(self, send, own, every, right, left):
        self.send, self.every, self.right, self.left = send, every, right, left
        self.from_left = send(own, every.at[1], right)
        self.from_right = send(own, every.at[2], left)

    def near(self):
        self.from_left.wait_recv()
        every = self.every
        half = every.shape[1] // 2
        lower, upper = pl.ds(0, half), pl.ds(half, half)
        self.far_low = self.send(every.at[1, lower], every.at[3, lower], self.right)
        self.from_right.wait_recv()
        self.far_up = self.send(every.at[2, upper], every.at[3, upper], self.left)

    def far(self):
        self.far_low.wait_recv()
        self.far_up.wait_recv()


class ZScatter:
    def __init__(self, send, part, relay, got, right, left):
        self.send, self.part, self.relay, self.got = send, part, relay, got
        self.right, self.left = right, left
        half = part.shape[1] // 2
        self.lower, self.upper = pl.ds(0, half), pl.ds(half, half)

    def near(self):
        part, got = self.part, self.got
        self.near_r = self.send(part.at[2, self.upper], got.at[0, self.upper], self.right)
        self.near_l = self.send(part.at[1, self.lower], got.at[1, self.lower], self.left)

    def far(self):
        part, relay = self.part, self.relay
        self.relay_r = self.send(part.at[3, self.lower], relay.at[0], self.right)
        self.relay_l = self.send(part.at[3, self.upper], relay.at[1], self.left)

    def pass_on(self):
        part, relay, got = self.part, self.relay, self.got
        self.relay_r.wait_recv()
        part[2, self.lower] = add_low(part[2, self.lower], relay[0])
        self.last_r = self.send(part.at[2, self.lower], got.at[0, self.lower], self.right)
        self.relay_l.wait_recv()
        part[1, self.upper] = add_low(part[1, self.upper], relay[1])
        self.last_l = self.send(part.at[1, self.upper], got.at[1, self.upper], self.left)

    def total(self):
        for copy in (self.near_r, self.near_l, self.last_r, self.last_l):
            copy.wait_recv()
        got = self.got
        return self.part[0].astype(F32) + got[0].astype(F32) + got[1].astype(F32)


def mm(a, b):
    return lax.dot_general(a, b, (((1,), (0,)), ((), ())), preferred_element_type=F32)


def mm_t(a, b):
    return lax.dot_general(a, b, (((1,), (1,)), ((), ())), preferred_element_type=F32)


def tile(j, size=256):
    return pl.ds(pl.multiple_of(j * size, size), size)


def transpose_into(src, dst):
    def column(j, carry):
        cols = tile(j, 128)
        for slot in range(4):
            dst[cols, slot * 128 : (slot + 1) * 128] = src[slot, :, cols].T
        return carry

    lax.fori_loop(0, D // 128, column, 0)


class PlaneGather:
    def __init__(self, send, shard, every):
        self.send, self.shard, self.every = send, shard, every
        rows, cols = shard.shape
        half = rows // 2
        self.top, self.low = pl.ds(0, half), pl.ds(half, half)
        if rows == 96:
            left, right = pl.ds(0, cols // 2), pl.ds(cols // 2, cols // 2)
            self.qa = [(self.top, left), (self.top, right)]
            self.qb = [(self.low, left), (self.low, right)]
        else:
            q = half // 2
            self.qa = [(pl.ds(0, q),), (pl.ds(q, q),)]
            self.qb = [(pl.ds(2 * q, q),), (pl.ds(3 * q, q),)]
        self.late = []

    def at(self, xx, yy, *rest):
        return self.every.at[(xx % 2, xx // 2, yy, self.c) + rest]

    def same(self, ref, device):
        return self.send(ref, ref, device)

    def to_sibling(self, ref):
        self.late.append(self.send(ref, ref, self.sibling))

    def start(self, local_sem):
        x, y, c, xr, xq, yr, yq, peers = plane_peers()
        self.x, self.y, self.c = x, y, c
        self.xr, self.xq, self.yr, self.yq = xr, xq, yr, yq
        self.go_xr, self.go_xq, self.go_yr, self.go_yq, self.sibling = peers
        shard, top, low = self.shard, self.top, self.low
        self.a_r = self.send(shard.at[top], self.at(x, y, top), self.go_xr)
        self.a_l = self.send(shard.at[top], self.at(x, y, top), self.go_xq)
        self.b_r = self.send(shard.at[low], self.at(x, y, low), self.go_yr)
        self.b_l = self.send(shard.at[low], self.at(x, y, low), self.go_yq)
        self.late.append(self.send(shard, self.at(x, y), self.sibling))
        self.local = pltpu.make_async_copy(shard, self.at(x, y), local_sem)
        self.local.start()

    def step2(self):
        x, y = self.x, self.y
        self.a_r.wait_recv()
        self.f1 = self.same(self.at(self.xq, y, *self.qa[0]), self.go_xr)
        self.a_l.wait_recv()
        self.f2 = self.same(self.at(self.xr, y, *self.qa[1]), self.go_xq)
        self.b_r.wait_recv()
        self.f3 = self.same(self.at(x, self.yq, *self.qb[0]), self.go_yr)
        self.b_l.wait_recv()
        self.f4 = self.same(self.at(x, self.yr, *self.qb[1]), self.go_yq)

    def step3(self):
        x, y, c = self.x, self.y, self.c
        every, top, low = self.every, self.top, self.low
        self.local.wait()
        self.f1.wait_recv()
        self.f2.wait_recv()
        block = every.at[:, :, y, c, top]
        self.g_r = self.same(block, self.go_yr)
        self.g_l = self.same(block, self.go_yq)
        self.f3.wait_recv()
        self.f4.wait_recv()
        block = every.at[x % 2, x // 2, :, c, low]
        self.h_r = self.same(block, self.go_xr)
        self.h_l = self.same(block, self.go_xq)
        for k in range(1, 4):
            self.to_sibling(self.at((x + k) % 4, y, top))
            self.to_sibling(self.at(x, (y + k) % 4, low))

    def step4(self):
        c, every, top, low = self.c, self.every, self.top, self.low
        xr, xq, yr, yq = self.xr, self.xq, self.yr, self.yq
        self.g_r.wait_recv()
        self.f1 = self.same(every.at[0, :, yq, c, top], self.go_yr)
        self.g_l.wait_recv()
        self.f2 = self.same(every.at[1, :, yr, c, top], self.go_yq)
        self.h_r.wait_recv()
        self.f3 = self.same(every.at[xq % 2, xq // 2, pl.ds(0, 2), c, low], self.go_xr)
        self.h_l.wait_recv()
        self.f4 = self.same(every.at[xr % 2, xr // 2, pl.ds(2, 2), c, low], self.go_xq)
        self.to_sibling(every.at[:, :, yq, c, top])
        self.to_sibling(every.at[:, :, yr, c, top])
        self.to_sibling(every.at[xq % 2, xq // 2, :, c, low])
        self.to_sibling(every.at[xr % 2, xr // 2, :, c, low])

    def step5(self):
        c, every, top, low = self.c, self.every, self.top, self.low
        xo, yo = (self.x + 2) % 4, (self.y + 2) % 4
        for copy in (self.f1, self.f2, self.f3, self.f4):
            copy.wait_recv()
        self.to_sibling(every.at[:, :, yo, c, top])
        self.to_sibling(every.at[xo % 2, xo // 2, :, c, low])

    def finish(self):
        for copy in self.late:
            copy.wait_recv()


OFFSETS = (0, 3, 1, 2)


def lanes(shape):
    return lax.broadcasted_iota(jnp.int32, shape, len(shape) - 1)


def head_block():
    row = lax.broadcasted_iota(jnp.int32, (128, 128), 0) // 64
    col = lax.broadcasted_iota(jnp.int32, (128, 128), 1) // 64
    return jnp.where(row == col, 1.0 / 64.0, 0.0).astype(BF16)


def head_mean(values, block):
    high = values.astype(BF16)
    low = (values - high.astype(F32)).astype(BF16)
    return mm(high, block) + mm(low, block)


def swap_quarters(values):
    second = (lanes(values.shape) % 64) >= 32
    return jnp.where(second, pltpu.roll(values, 32, 1), pltpu.roll(values, 96, 1))


def pick_scalar(ref, xl):
    return jnp.where(xl == 0, ref[0, 0], ref[1, 0])


def key_bias(total, z, length):
    lane = lanes((1, total))
    if total == 512:
        slot = lane // 128
        block = jnp.where(slot == 0, z, jnp.where(slot == 1, z + 3, jnp.where(slot == 2, z + 1, z + 2)))
        position = (block % 4) * 128 + lane % 128
    else:
        position = lane
    return jnp.where(position < length, 0.0, NEGATIVE)


def fill_rope(cos_ref, sin_ref, z, length, frames, width):
    lane = lanes((128, 128))
    pair = lane % 32
    offset = jnp.where(pair >= 20, 20, jnp.where(pair >= 8, 8, 0))
    size = jnp.where(pair >= 8, 12.0, 8.0)
    freq = jnp.exp((pair - offset).astype(F32) / size * (-9.210340371976184))
    sign = jnp.where(lane % 64 >= 32, 1.0, -1.0)
    ones = jnp.ones((128, 128), F32)
    count = ones * length.astype(F32)
    frame_count = ones * frames.astype(F32)
    row_size = ones * width.astype(F32)
    per_frame = jnp.floor((count + frame_count - 0.5) / frame_count)
    row = lax.broadcasted_iota(jnp.int32, (128, 128), 0).astype(F32)
    for slot in range(4):
        start = (((z + OFFSETS[slot]) % 4) * 128).astype(F32)
        position = row + start
        frame = jnp.floor((position + 0.5) / per_frame)
        within = position - frame * per_frame
        row_pos = jnp.floor((within + 0.5) / row_size)
        col_pos = within - row_pos * row_size
        chosen = jnp.where(pair >= 20, col_pos, jnp.where(pair >= 8, row_pos, frame))
        angle = chosen * freq
        cos_ref[slot] = jnp.cos(angle)
        sin_ref[slot] = jnp.sin(angle) * sign


def attention_kernel(
    hid_ref,
    cot_ref,
    cond_ref,
    gain_in,
    bias_in,
    ada_ref,
    qkv_ref,
    out_t_ref,
    ffn_w_ref,
    down_t_ref,
    cap_w_ref,
    cap_hbm,
    hg_ref,
    gate_ref,
    len_ref,
    frame_ref,
    width_ref,
    tlen_ref,
    w_a,
    w_f,
    first,
    resid_ref,
    cot_out,
    q8,
    kk,
    vv,
    qr,
    kr,
    tk,
    tv,
    tkr,
    other_ref,
    lse_ref,
    cw,
    attn_ref,
    mid_ref,
    second_ref,
    mod_ref,
    gains_ref,
    got1,
    cos_ref,
    sin_ref,
    live_ref,
    cap_flip,
    sh_a,
    sh_f,
    sh_c,
    w_c,
    cap,
    hid_all,
    hid_own,
    msg,
    sent2,
    got2,
    got3,
    mixed,
    text_acc,
    part,
    relay,
    got,
    local_sems,
    ss,
    rs,
):
    dp = lax.axis_index("dp")
    t = lax.axis_index("tensor")
    xh, xl, y, z, c = coords()
    _, right, left = z_ring()
    pair = device_of(2 * xh + 1 - xl, y, z, c)
    dp_peers = [((dp + k) % 16, t) for k in range(1, 16)]
    t_peers = [(dp, (t + k) % 8) for k in range(1, 8)]
    outer_x = device_of((2 * xh + xl + 3 - 2 * xl) % 4, y, z, c)
    barrier = pltpu.get_barrier_semaphore()
    everyone = dp_peers + t_peers + [outer_x]
    for device in everyone:
        pl.semaphore_signal(barrier, inc=1, device_id=device, device_id_type=MESH)
    load_cap = pltpu.make_async_copy(cap_hbm.at[xl], cap, local_sems.at[0])
    load_cap.start()
    qs, ks, vs = qkv_ref[0], qkv_ref[1], qkv_ref[2]
    os = out_t_ref[...]
    sh_a[...] = jnp.concatenate(
        [
            qs,
            ks[:, 128:192],
            ks[:, 0:128],
            vs,
            os[:, 128:192],
            os[:, 0:128],
        ],
        axis=1,
    )
    ck, cv = cap_w_ref[0], cap_w_ref[1]
    sh_c[...] = jnp.concatenate([ck, cv[:, 128:192], cv[:, 0:128]], axis=1)
    unit = swish(cond_ref[...].astype(F32)).astype(BF16).astype(F32)
    msg[...] = jnp.zeros((16, 8, 128), F32)
    gain_rows = gain_in[...].astype(F32)
    for d in range(16):
        msg[d, 0:2, 0:64] = unit[:, d * 64 : (d + 1) * 64]
        msg[d, 4:8, 0:96] = gain_rows
    pl.semaphore_wait(barrier, len(everyone))

    send = Sender(ss, rs)
    swap = send(hid_ref.at[1 - xl], hid_own.at[xl], pair)
    cot_swap = send(cot_ref.at[1 - xl], cot_out.at[xl], pair)
    round1 = [send(msg.at[p[0]], got1.at[dp], p) for p in dp_peers]
    ga = PlaneGather(send, sh_a, w_a)
    gc = PlaneGather(send, sh_c, w_c)
    gf = PlaneGather(send, sh_f, w_f)
    ga.start(local_sems.at[1])
    hid_own[xl] = hid_ref[xl]
    cot_out[xl] = cot_ref[xl]
    got1[dp] = msg[dp]
    sh_f[:, 0:512] = ffn_w_ref[0]
    sh_f[:, 512:1024] = ffn_w_ref[1]
    sh_f[:, 1024:1536] = down_t_ref[...]
    length = pick_scalar(len_ref, xl)
    text_len = pick_scalar(tlen_ref, xl)
    swap.wait_recv()
    tokens = ZGather(send, hid_own, hid_all, right, left)
    hid_all[0] = hid_own[...]
    gc.start(local_sems.at[2])
    for copy in round1:
        copy.wait_recv()
    rows = got1[...].reshape(128, 128)[:, :64].astype(BF16)
    bias = bias_in[...].astype(F32)
    here = t == dp // 2
    low_bias = jnp.where(jnp.logical_and(here, dp % 2 == 0), 1.0, 0.0)
    high_bias = jnp.where(jnp.logical_and(here, dp % 2 == 1), 1.0, 0.0)
    terms = mm(rows, ada_ref[...])
    terms = terms + jnp.concatenate([bias * low_bias, bias * high_bias], axis=1)
    sent2[...] = jnp.zeros((16, 16, 128), F32)
    for d in range(16):
        for j in range(6):
            sent2[d, 2 * j : 2 * j + 2, :] = terms[8 * d : 8 * d + 2, 128 * j : 128 * j + 128]
    round2 = [send(sent2.at[p[0]], got2.at[dp], p) for p in dp_peers]
    got2[dp] = sent2[dp]
    ga.step2()
    fill_rope(cos_ref, sin_ref, z, length, pick_scalar(frame_ref, xl), pick_scalar(width_ref, xl))
    gc.step2()
    ga.step3()
    tokens.near()
    load_cap.wait()

    def flip_caption(j, carry):
        rows = tile(j, 128)
        cap_flip[rows, 0:128] = cap[0:128, rows].T
        cap_flip[rows, 128:256] = cap[128:256, rows].T
        return carry

    lax.fori_loop(0, 32, flip_caption, 0)
    for copy in round2:
        copy.wait_recv()
    got3[t] = jnp.sum(got2[...], axis=0)
    round3 = [send(got3.at[t], got3.at[t], p) for p in t_peers]
    for d in range(16):
        gains_ref[0:4, d * 96 : (d + 1) * 96] = got1[d, 4:8, 0:96]
    gains_ref[4:8, :] = jnp.zeros((4, D), F32)
    slot_row = lax.broadcasted_iota(jnp.int32, (128, 128), 0) + z * 128
    live_ref[...] = jnp.where(slot_row < length, 1.0, 0.0)
    gc.step3()
    ga.step4()
    gf.start(local_sems.at[3])
    for copy in round3:
        copy.wait_recv()
    for i in range(4):
        for h in range(2):
            block = got3[2 * i + h]
            for j in range(6):
                lo = h * 768 + j * 128
                mod_ref[i : i + 1, lo : lo + 128] = jnp.where(
                    xl == 0, block[2 * j : 2 * j + 1], block[2 * j + 1 : 2 * j + 2]
                )
    mod_ref[4:8, :] = jnp.zeros((4, D), F32)
    factor = gains_ref[0:1, :] * (1.0 + mod_ref[0:1, :])
    tokens.far()

    def scale_rows(slot, carry):
        unit_rows, _ = normalize(hid_all[slot].reshape(128, D).astype(F32))
        first[slot] = (unit_rows * factor).astype(BF16)
        return carry

    lax.fori_loop(0, 4, scale_rows, 0)
    resid_ref[...] = hid_all[0].reshape(128, D)
    gc.step4()
    ga.step5()
    gf.step2()
    ga.finish()

    x_rows = first[...].reshape(512, D)
    low_head = lanes((512, 128)) < 64
    w_flat = w_a

    def project(xx, cols):
        w_cols = w_flat[xx, :, :, :, :, cols].reshape(D, cols.stop - cols.start)
        return mm(x_rows, w_cols)

    for xx in range(2):
        p = project(xx, slice(0, 256))
        qr[xx] = p[:, :128].reshape(4, 128, 128)
        mixed[0, xx] = p[:, 128:]
        p = project(xx, slice(256, 512))
        kr[xx] = p[:, :128].reshape(4, 128, 128)
        vv[xx] = p[:, 128:].astype(BF16).reshape(4, 128, 128)
        mixed[1, xx] = project(xx, slice(512, 640))
    x0, x1 = mixed[0, 0], mixed[0, 1]
    qr[2] = jnp.where(low_head, x0, pltpu.roll(x1, 64, 1)).reshape(4, 128, 128)
    kr[2] = jnp.where(low_head, pltpu.roll(x0, 64, 1), x1).reshape(4, 128, 128)
    x0, x1 = mixed[1, 0], mixed[1, 1]
    vv[2] = jnp.where(low_head, x0, pltpu.roll(x1, 64, 1)).astype(BF16).reshape(4, 128, 128)
    gc.step5()
    gf.step3()
    block = head_block()
    cos = cos_ref[...].reshape(512, 128)
    sin = sin_ref[...].reshape(512, 128)

    def turned(raw, gain):
        raw = raw.reshape(512, 128)
        v = raw * lax.rsqrt(head_mean(raw * raw, block) + EPSILON) * gain
        return v * cos + swap_quarters(v) * sin

    for p in range(3):
        q = turned(qr[p], hg_ref[0:1, :]).astype(BF16)
        q8[p] = (q.astype(F32) * 0.125).astype(BF16).reshape(4, 128, 128)
        kk[p] = turned(kr[p], hg_ref[1:2, :]).astype(BF16).reshape(4, 128, 128)
    gc.finish()
    text_acc[...] = jnp.zeros((2, 256, 384), F32)

    def text_step(i, carry):
        xx = i // 8
        j = i % 8
        w_cols = w_c[xx, j // 4, j % 4].reshape(512, 384)
        text_acc[xx] += mm(cap[:, tile(j, 512)], w_cols)
        return carry

    lax.fori_loop(0, 16, text_step, 0)
    gf.step4()
    low_text = lanes((256, 128)) < 64
    for xx in range(2):
        tkr[xx] = text_acc[xx, :, 0:128]
        tv[xx] = text_acc[xx, :, 256:384].astype(BF16)
    x0, x1 = text_acc[0, :, 128:256], text_acc[1, :, 128:256]
    tkr[2] = jnp.where(low_text, x0, pltpu.roll(x1, 64, 1))
    tv[2] = jnp.where(low_text, pltpu.roll(x0, 64, 1), x1).astype(BF16)
    for p in range(3):
        raw = tkr[p]
        tk[p] = (raw * lax.rsqrt(head_mean(raw * raw, block) + EPSILON) * hg_ref[2:3, :]).astype(BF16)

    self_bias = key_bias(512, z, length)
    text_bias = key_bias(256, z, text_len)
    lse_ref[...] = jnp.zeros((4, 128, 128), F32)

    def attend(p):
        def rows_step(b, carry):
            slots = pl.ds(b * 2, 2)
            q = q8[p, slots].reshape(256, 128)
            low_rows = lanes((256, 128)) < 64
            own = jnp.zeros((256, 128), F32)
            other = jnp.zeros((256, 128), F32)
            for head in range(2):
                keep = low_rows if head == 0 else jnp.logical_not(low_rows)
                qm = jnp.where(keep, q, jnp.zeros_like(q))
                for text in range(2):
                    k = tk[p] if text else kk[p].reshape(512, 128)
                    v = tv[p] if text else vv[p].reshape(512, 128)
                    scores = mm_t(qm, k) + (text_bias if text else self_bias)
                    top = jnp.max(scores, axis=-1, keepdims=True)
                    e = jnp.exp(scores - top)
                    total = jnp.sum(e, axis=-1, keepdims=True)
                    probs = (e * (1.0 / total)).astype(BF16)
                    mix = jnp.where(keep, mm(probs, v), 0.0)
                    lane = p * 2 + head + 8 * text
                    lse_ref[slots, :, lane : lane + 1] = (top + jnp.log(total)).reshape(2, 128, 1)
                    if text:
                        other = other + mix
                    else:
                        own = own + mix
            other_ref[p, slots] = other.reshape(2, 128, 128)
            both = own + gate_ref[p : p + 1, :] * other
            if p < 2:
                cw[p, slots, :, 128:256] = both.astype(BF16).reshape(2, 128, 128)
            else:
                moved = pltpu.roll(both, 64, 1)
                zero = jnp.zeros_like(both)
                cw[0, slots, :, 0:128] = jnp.where(low_rows, zero, moved).astype(BF16).reshape(2, 128, 128)
                cw[1, slots, :, 0:128] = jnp.where(low_rows, zero, both).astype(BF16).reshape(2, 128, 128)
            return carry

        lax.fori_loop(0, 2, rows_step, 0)

    attend(0)
    gf.step5()
    attend(1)
    attend(2)

    def out_rows(lo, count):
        n = count * 128
        a0 = cw[0, lo : lo + count].reshape(n, 256)
        a1 = cw[1, lo : lo + count].reshape(n, 256)
        for xb in range(2):
            cols = slice(xb * 768, xb * 768 + 768)
            b0 = w_a[0, xb, :, :, :, 512:768].reshape(768, 256)
            b1 = w_a[1, xb, :, :, :, 512:768].reshape(768, 256)
            total = mm_t(a0, b0) + mm_t(a1, b1)
            part[lo : lo + count, :, cols] = total.astype(BF16).reshape(count, 128, 768)

    sums = ZScatter(send, part, relay, got, right, left)
    out_rows(1, 2)
    sums.near()
    out_rows(3, 1)
    sums.far()
    out_rows(0, 1)
    sums.pass_on()
    attn = sums.total()
    attn_ref[...] = attn
    unit_two, _ = normalize(attn)
    live = live_ref[...][:, :1]
    middle = resid_ref[...].astype(F32) + live * jnp.tanh(mod_ref[1:2, :]) * unit_two * gains_ref[1:2, :]
    mid_ref[...] = middle
    unit_three, _ = normalize(middle)
    second_ref[...] = (unit_three * gains_ref[2:3, :] * (1.0 + mod_ref[2:3, :])).astype(BF16)
    cot_swap.wait_recv()
    gf.finish()
    send.drain()


def attention_call(args, cid):
    S = jax.ShapeDtypeStruct
    vm = pl.BlockSpec(memory_space=VMEM)
    sm = pl.BlockSpec(memory_space=pltpu.SMEM)
    any_ = pl.BlockSpec(memory_space=pl.ANY)
    pair = (3, 4, 128, 128)
    outs = [
        S((2, 2, 4, 2, 96, 768), BF16),
        S((2, 2, 4, 2, 96, D), BF16),
        S((4, 128, D), BF16),
        S((128, D), BF16),
        S((2, 64, D), BF16),
        S(pair, BF16),
        S(pair, BF16),
        S(pair, BF16),
        S(pair, F32),
        S(pair, F32),
        S((3, 256, 128), BF16),
        S((3, 256, 128), BF16),
        S((3, 256, 128), F32),
        S(pair, F32),
        S((4, 128, 128), F32),
        S((2, 4, 128, 256), BF16),
        S((128, D), F32),
        S((128, D), F32),
        S((128, D), BF16),
        S((8, D), F32),
        S((8, D), F32),
        S((16, 8, 128), F32),
        S((4, 128, 128), F32),
        S((4, 128, 128), F32),
        S((128, 128), F32),
        S((4096, 256), BF16),
    ]
    return pl.pallas_call(
        attention_kernel,
        out_shape=outs,
        in_specs=[vm] * 11 + [any_] + [vm] * 2 + [sm] * 4,
        out_specs=[vm, any_] + [vm] * (len(outs) - 2),
        scratch_shapes=[
            VMEM((96, 768), BF16),
            VMEM((96, D), BF16),
            VMEM((256, 384), BF16),
            VMEM((2, 2, 4, 2, 256, 384), BF16),
            VMEM((256, 4096), BF16),
            VMEM((4, 2, 64, D), BF16),
            VMEM((2, 64, D), BF16),
            VMEM((16, 8, 128), F32),
            VMEM((16, 16, 128), F32),
            VMEM((16, 16, 128), F32),
            VMEM((8, 16, 128), F32),
            VMEM((2, 2, 512, 128), F32),
            VMEM((2, 256, 384), F32),
            VMEM((4, 128, D), BF16),
            VMEM((2, 64, D), BF16),
            VMEM((2, 128, D), BF16),
            pltpu.SemaphoreType.DMA((4,)),
        ]
        + dma_sems(160),
        compiler_params=pltpu.CompilerParams(
            collective_id=cid, has_side_effects=True, vmem_limit_bytes=56 * 2**20
        ),
        name="attention",
    )(*args)


def ffn_kernel(
    x_ref,
    w_hbm,
    mid_ref,
    attn_ref,
    cot_ref,
    mod_ref,
    gain_ref,
    live_ref,
    out_ref,
    gmid_ref,
    gattn_ref,
    sums_ref,
    dw_ref,
    w,
    x_all,
    g_all,
    act,
    dgate,
    dup,
    gpre,
    part1,
    part2,
    relay1,
    relay2,
    got1,
    got2,
    flip,
    own_g,
    w_sem,
    ss,
    rs,
):
    z, right, left = z_ring()
    load = pltpu.make_async_copy(w_hbm, w, w_sem)
    load.start()
    greet([right, left])
    send = Sender(ss, rs)
    one = ZGather(send, x_ref, x_all, right, left)
    x_all[0] = x_ref[...]
    load.wait()

    def pre(lo, count):
        rows = count * 128
        x = x_all[lo : lo + count].reshape(rows, D)
        for xx in range(2):

            def column(j, carry, xx=xx):
                g = mm(x, w[xx, :, tile(j)])
                u = mm(x, w[xx, :, tile(j + 2)])
                s = jax.nn.sigmoid(g)
                gs = g * s
                act[xx, lo : lo + count, :, tile(j)] = (gs * u).astype(BF16).reshape(count, 128, 256)
                dgate[xx, lo : lo + count, :, tile(j)] = (u * s * (1.0 + g * (1.0 - s))).reshape(count, 128, 256)
                dup[xx, lo : lo + count, :, tile(j)] = gs.reshape(count, 128, 256)
                return carry

            lax.fori_loop(0, 2, column, 0)

    def down(lo, count):
        rows = count * 128
        a0 = act[0, lo : lo + count].reshape(rows, 512)
        a1 = act[1, lo : lo + count].reshape(rows, 512)

        def column(j, carry):
            cols = tile(j)
            total = mm_t(a0, w[0, cols, 1024:1536]) + mm_t(a1, w[1, cols, 1024:1536])
            part1[lo : lo + count, :, cols] = total.astype(BF16).reshape(count, 128, 256)
            return carry

        lax.fori_loop(0, D // 256, column, 0)

    sum1 = ZScatter(send, part1, relay1, got1, right, left)
    pre(0, 1)
    one.near()
    pre(1, 2)
    down(1, 2)
    sum1.near()
    one.far()
    pre(3, 1)
    down(3, 1)
    sum1.far()
    down(0, 1)
    transpose_into(x_all, flip)
    sum1.pass_on()
    ffn_total = sum1.total()

    live = live_ref[...][:, :1]
    mod = mod_ref[...]
    gains = gain_ref[...]
    gate_f = jnp.tanh(mod[3:4])
    middle = mid_ref[...]
    unit_four, inverse_four = normalize(ffn_total)
    out_ref[...] = (middle + live * gate_f * unit_four * gains[3:4]).astype(BF16)
    grad_top = cot_ref[...].astype(F32)
    weighted = grad_top * live
    part_four = jnp.sum(weighted * unit_four, axis=0, keepdims=True)
    own_g[...] = norm_back(unit_four, inverse_four, weighted * gate_f * gains[3:4]).astype(BF16)
    two = ZGather(send, own_g, g_all, right, left)
    g_all[0] = own_g[...]
    sums_ref[3:4, :] = part_four * gains[3:4] * (1.0 - gate_f * gate_f)
    sums_ref[7:8, :] = part_four * gate_f

    def back(lo, count):
        rows = count * 128
        g = g_all[lo : lo + count].reshape(rows, D)
        for xx in range(2):

            def column(j, carry, xx=xx):
                ga = mm(g, w[xx, :, tile(j + 4)])
                dg = dgate[xx, lo : lo + count, :, tile(j)].reshape(rows, 256)
                du = dup[xx, lo : lo + count, :, tile(j)].reshape(rows, 256)
                gpre[xx, lo : lo + count, :, tile(j)] = (ga * dg).astype(BF16).reshape(count, 128, 256)
                gpre[xx, lo : lo + count, :, tile(j + 2)] = (ga * du).astype(BF16).reshape(count, 128, 256)
                return carry

            lax.fori_loop(0, 2, column, 0)

    def back_in(lo, count):
        rows = count * 128
        a0 = gpre[0, lo : lo + count].reshape(rows, 1024)
        a1 = gpre[1, lo : lo + count].reshape(rows, 1024)

        def column(j, carry):
            cols = tile(j)
            total = mm_t(a0, w[0, cols, 0:1024]) + mm_t(a1, w[1, cols, 0:1024])
            part2[lo : lo + count, :, cols] = total.astype(BF16).reshape(count, 128, 256)
            return carry

        lax.fori_loop(0, D // 256, column, 0)

    sum2 = ZScatter(send, part2, relay2, got2, right, left)
    back(0, 1)
    two.near()
    back(1, 2)
    back_in(1, 2)
    sum2.near()
    two.far()
    back(3, 1)
    back_in(3, 1)
    sum2.far()
    back_in(0, 1)

    def weight_grad(right_of, first, count):
        def column(i, carry):
            xx = i // count
            j = i % count
            b = right_of(xx, j).reshape(512, 256)
            for r in range(0, D, 512):
                dw_ref[xx, r : r + 512, tile(j + first)] = mm(flip[r : r + 512, :], b).astype(BF16)
            return carry

        lax.fori_loop(0, 2 * count, column, 0)

    weight_grad(lambda xx, j: gpre[xx, :, :, tile(j)], 0, 4)
    sum2.pass_on()
    transpose_into(g_all, flip)
    weight_grad(lambda xx, j: act[xx, :, :, tile(j)], 4, 2)
    grad_second = sum2.total()

    scale_f = mod[2:3]
    unit_three, inverse_three = normalize(middle)
    sum_three = jnp.sum(grad_second * unit_three, axis=0, keepdims=True)
    sums_ref[2:3, :] = sum_three * gains[2:3]
    sums_ref[6:7, :] = sum_three * (1.0 + scale_f)
    grad_middle = grad_top + norm_back(
        unit_three, inverse_three, grad_second * (1.0 + scale_f) * gains[2:3]
    )
    gmid_ref[...] = grad_middle
    gate_a = jnp.tanh(mod[1:2])
    unit_two, inverse_two = normalize(attn_ref[...])
    weighted_mid = grad_middle * live
    sum_two = jnp.sum(weighted_mid * unit_two, axis=0, keepdims=True)
    sums_ref[1:2, :] = sum_two * gains[1:2] * (1.0 - gate_a * gate_a)
    sums_ref[5:6, :] = sum_two * gate_a
    sums_ref[0:1, :] = jnp.zeros((1, D), F32)
    sums_ref[4:5, :] = jnp.zeros((1, D), F32)
    gattn_ref[...] = norm_back(unit_two, inverse_two, weighted_mid * gate_a * gains[1:2]).astype(BF16)
    send.drain()


def ffn_call(second_in, w_f, middle, attn, cot, mod_rows, gains, live, cid):
    S = jax.ShapeDtypeStruct
    vm = pl.BlockSpec(memory_space=VMEM)
    any_ = pl.BlockSpec(memory_space=pl.ANY)
    return pl.pallas_call(
        ffn_kernel,
        out_shape=[
            S((128, D), BF16),
            S((128, D), F32),
            S((128, D), BF16),
            S((8, D), F32),
            S((2, D, D), BF16),
        ],
        in_specs=[vm, any_] + [vm] * 6,
        out_specs=[vm] * 5,
        scratch_shapes=[
            VMEM((2, D, D), BF16),
            VMEM((4, 128, D), BF16),
            VMEM((4, 128, D), BF16),
            VMEM((2, 4, 128, 512), BF16),
            VMEM((2, 4, 128, 512), F32),
            VMEM((2, 4, 128, 512), F32),
            VMEM((2, 4, 128, 1024), BF16),
            VMEM((4, 128, D), BF16),
            VMEM((4, 128, D), BF16),
            VMEM((2, 64, D), BF16),
            VMEM((2, 64, D), BF16),
            VMEM((2, 128, D), BF16),
            VMEM((2, 128, D), BF16),
            VMEM((D, 512), BF16),
            VMEM((128, D), BF16),
            pltpu.SemaphoreType.DMA,
        ]
        + dma_sems(20),
        compiler_params=pltpu.CompilerParams(
            collective_id=cid, has_side_effects=True, vmem_limit_bytes=56 * 2**20
        ),
        name="ffn",
    )(second_in, w_f, middle, attn, cot, mod_rows, gains, live)


def pick(array, index):
    return lax.dynamic_index_in_dim(array, index, 0, keepdims=False)


def dot(spec, a, b):
    return jnp.einsum(spec, a, b, preferred_element_type=F32)


class PlaneScatter:
    def __init__(self, send, grads, own, bufs):
        self.send, self.grads, self.own = send, grads, own
        self.sib, self.ra, self.rb, self.ga, self.gb, self.qa, self.qb = bufs
        rows, cols = self.sib.shape[3:]
        self.rows, self.cols = rows, cols
        self.half = half = rows // 2
        self.top, self.low = pl.ds(0, half), pl.ds(half, half)
        if rows == 96:
            self.q0 = (slice(None), pl.ds(0, cols // 2))
            self.q1 = (slice(None), pl.ds(cols // 2, cols // 2))
        else:
            q = half // 2
            self.q0, self.q1 = (pl.ds(0, q),), (pl.ds(q, q),)

    def start(self):
        self.where = plane_peers()
        x, y, c, xr, xq, yr, yq, peers = self.where
        self.go_xr, self.go_xq, self.go_yr, self.go_yq, sibling = peers
        self.parts = [
            self.send(
                self.grads.at[k % 2, k // 2]
                if callable(self.own)
                else self.grads.at[k % 2, k // 2, :, 1 - c],
                self.sib.at[k % 2, k // 2],
                sibling,
            )
            for k in range(4)
        ]
        if isinstance(self.own, tuple):
            self.loads = []
            self.load(0)
            self.load(1)

    def load(self, k):
        copy = pltpu.make_async_copy(
            self.grads.at[k % 2, k // 2, :, self.where[2]], self.own[0].at[k % 2], self.own[1].at[k]
        )
        copy.start()
        self.loads.append(copy)

    def step1(self):
        x, y, c, xr, xq, yr, yq, _ = self.where
        sib, own, send = self.sib, self.own, self.send
        for k in range(4):
            if isinstance(own, tuple):
                self.loads[k].wait()
            self.parts[k].wait_recv()

            def add_sibling(j, carry, k=k):
                if callable(own):
                    mine = own(k % 2, k // 2, j)
                elif own is not None:
                    mine = own[0][k % 2, j]
                else:
                    mine = self.grads[k % 2, k // 2, j, c]
                sib[k % 2, k // 2, j] = add_low(sib[k % 2, k // 2, j], mine)
                return carry

            lax.fori_loop(0, 4, add_sibling, 0)
            if isinstance(own, tuple) and k < 2:
                self.load(k + 2)
        xo, yo = (x + 2) % 4, (y + 2) % 4
        self.t1 = send(sib.at[0, :, yo, self.top], self.ra.at[pl.ds(0, 2)], self.go_yr)
        self.t2 = send(sib.at[1, :, yo, self.top], self.ra.at[pl.ds(2, 2)], self.go_yq)
        self.l1 = send(sib.at[xo % 2, xo // 2, pl.ds(0, 2), self.low], self.rb.at[pl.ds(0, 2)], self.go_xr)
        self.l2 = send(sib.at[xo % 2, xo // 2, pl.ds(2, 2), self.low], self.rb.at[pl.ds(2, 2)], self.go_xq)

    def step2(self):
        x, y, c, xr, xq, yr, yq, _ = self.where
        sib, send, top, low = self.sib, self.send, self.top, self.low
        ra, rb = self.ra, self.rb
        self.t1.wait_recv()
        for j in range(2):
            sib[0, j, yr, top] = add_low(sib[0, j, yr, top], ra[j])
        self.t3 = send(sib.at[:, :, yr, top], self.ga.at[0], self.go_yr)
        self.t2.wait_recv()
        for j in range(2):
            sib[1, j, yq, top] = add_low(sib[1, j, yq, top], ra[2 + j])
        self.t4 = send(sib.at[:, :, yq, top], self.ga.at[1], self.go_yq)
        self.l1.wait_recv()
        for j in range(2):
            sib[xr % 2, xr // 2, j, low] = add_low(sib[xr % 2, xr // 2, j, low], rb[j])
        self.l3 = send(sib.at[xr % 2, xr // 2, :, low], self.gb.at[0], self.go_xr)
        self.l2.wait_recv()
        for j in range(2):
            sib[xq % 2, xq // 2, 2 + j, low] = add_low(sib[xq % 2, xq // 2, 2 + j, low], rb[2 + j])
        self.l4 = send(sib.at[xq % 2, xq // 2, :, low], self.gb.at[1], self.go_xq)

    def step3(self):
        x, y, c, xr, xq, yr, yq, _ = self.where
        sib, send, ga, gb, pa, pb = self.sib, self.send, self.ga, self.gb, self.ra, self.rb
        xo, yo = (x + 2) % 4, (y + 2) % 4
        self.t3.wait_recv()
        self.t4.wait_recv()
        for i in range(2):
            for j in range(2):
                total = sib[i, j, y, self.top].astype(F32) + ga[0, i, j].astype(F32)
                pa[2 * j + i] = (total + ga[1, i, j].astype(F32)).astype(BF16)
        self.e1 = send(pa.at[(xo,) + self.q0], self.qa.at[0], self.go_xr)
        self.e2 = send(pa.at[(xo,) + self.q1], self.qa.at[1], self.go_xq)
        self.l3.wait_recv()
        self.l4.wait_recv()
        for j in range(4):
            total = sib[x % 2, x // 2, j, self.low].astype(F32) + gb[0, j].astype(F32)
            pb[j] = (total + gb[1, j].astype(F32)).astype(BF16)
        self.m1 = send(pb.at[(yo,) + self.q0], self.qb.at[0], self.go_yr)
        self.m2 = send(pb.at[(yo,) + self.q1], self.qb.at[1], self.go_yq)

    def step4(self):
        x, y, c, xr, xq, yr, yq, _ = self.where
        send, ga, gb, pa, pb, q0, q1 = self.send, self.ga, self.gb, self.ra, self.rb, self.q0, self.q1
        self.e1.wait_recv()
        pa[(xr,) + q0] = add_low(pa[(xr,) + q0], self.qa[0])
        self.e2.wait_recv()
        pa[(xq,) + q1] = add_low(pa[(xq,) + q1], self.qa[1])
        self.e3 = send(pa.at[xr], ga.at[0, 0, 0], self.go_xr)
        self.e4 = send(pa.at[xq], ga.at[1, 0, 0], self.go_xq)
        self.m1.wait_recv()
        pb[(yr,) + q0] = add_low(pb[(yr,) + q0], self.qb[0])
        self.m2.wait_recv()
        pb[(yq,) + q1] = add_low(pb[(yq,) + q1], self.qb[1])
        self.m3 = send(pb.at[yr], gb.at[0, 0], self.go_yr)
        self.m4 = send(pb.at[yq], gb.at[1, 0], self.go_yq)

    def finish(self):
        x, y = self.where[:2]
        ga, gb, pa, pb = self.ga, self.gb, self.ra, self.rb
        self.e3.wait_recv()
        self.e4.wait_recv()
        top = pa[x].astype(F32) + ga[0, 0, 0].astype(F32) + ga[1, 0, 0].astype(F32)
        self.m3.wait_recv()
        self.m4.wait_recv()
        low = pb[y].astype(F32) + gb[0, 0].astype(F32) + gb[1, 0].astype(F32)
        return top, low


def scatter_bufs(rows, cols):
    half = rows // 2
    quarter = (half, cols // 2) if rows == 96 else (half // 2, cols)
    return [
        VMEM((2, 2, 4, rows, cols), BF16),
        VMEM((4, half, cols), BF16),
        VMEM((4, half, cols), BF16),
        VMEM((2, 2, 2, half, cols), BF16),
        VMEM((2, 4, half, cols), BF16),
        VMEM((2,) + quarter, BF16),
        VMEM((2,) + quarter, BF16),
    ]


def mm_rows(a, b):
    return lax.dot_general(a, b, (((0,), (0,)), ((), ())), preferred_element_type=F32)


def back_kernel(
    gattn_ref,
    dw_f,
    w_a,
    first,
    resid_ref,
    q8,
    kk,
    vv,
    qr,
    kr,
    tk,
    tv,
    tkr,
    other_ref,
    lse_ref,
    cw,
    mod_ref,
    gains_ref,
    cos_ref,
    sin_ref,
    gmid_ref,
    out_ref,
    sums_ref,
    cap_flip,
    hg_ref,
    gate_ref,
    len_ref,
    tlen_ref,
    d_out,
    f_out,
    c_out,
    layer_final,
    hidden_final,
    g_all,
    gain_out,
    bias_all,
    own_f,
    flip,
    grad_all,
    gc,
    gq,
    gk,
    gv,
    gtk,
    gtv,
    gpack,
    tpack,
    dw_a,
    dw_c,
    part,
    relay,
    got,
    hid_grad,
    mod_msg,
    gain_msg,
    got_mod,
    got_gain,
    gain_sum,
    sf0, sf1, sf2, sf3, sf4, sf5, sf6,
    sa0, sa1, sa2, sa3, sa4, sa5, sa6,
    sc0, sc1, sc2, sc3, sc4, sc5, sc6,
    local_sems,
    ss,
    rs,
):
    dp = lax.axis_index("dp")
    t = lax.axis_index("tensor")
    xh, xl, y, z, c = coords()
    _, right, left = z_ring()
    pair = device_of(2 * xh + 1 - xl, y, z, c)
    dp_peers = [((dp + k) % 16, t) for k in range(1, 16)]
    t_peers = [(dp, (t + k) % 8) for k in range(1, 8)]
    outer_x = device_of((2 * xh + xl + 3 - 2 * xl) % 4, y, z, c)
    greet(dp_peers + t_peers + [outer_x])
    send = Sender(ss, rs)
    tokens = ZGather(send, gattn_ref, grad_all, right, left)

    def caption_own(xx, xb, yb):
        return mm(cap_flip[tile(2 * (4 * xb + yb) + c)], tpack[xx])

    scat_f = PlaneScatter(send, dw_f, (own_f, local_sems), (sf0, sf1, sf2, sf3, sf4, sf5, sf6))
    scat_a = PlaneScatter(send, dw_a, None, (sa0, sa1, sa2, sa3, sa4, sa5, sa6))
    scat_c = PlaneScatter(send, dw_c, caption_own, (sc0, sc1, sc2, sc3, sc4, sc5, sc6))
    scat_f.start()
    out_swap = send(out_ref.at[1 - xl], layer_final.at[xl], pair)
    layer_final[xl] = out_ref[xl]
    grad_all[0] = gattn_ref[...]
    length = pick_scalar(len_ref, xl)
    text_len = pick_scalar(tlen_ref, xl)
    self_bias = key_bias(512, z, length)
    text_bias = key_bias(256, z, text_len)
    block = head_block()
    low_row = lanes((1, 128)) < 64
    def head_grads(lo, count):
        n = count * 128
        g = grad_all[lo : lo + count].reshape(n, D)
        low_lane = lanes((n, 128)) < 64
        tiles = []
        for xx in range(2):
            w_cols = w_a[xx, :, :, :, :, 512:768].reshape(D, 256)
            o = mm(g, w_cols)
            gc[xx, lo : lo + count] = o[:, 128:].astype(BF16).reshape(count, 128, 128)
            tiles.append(o[:, :128])
        both = jnp.where(low_lane, pltpu.roll(tiles[0], 64, 1), tiles[1])
        gc[2, lo : lo + count] = both.astype(BF16).reshape(count, 128, 128)

    head_grads(0, 1)
    tokens.near()
    head_grads(1, 2)
    tokens.far()
    head_grads(3, 1)
    scat_f.step1()

    gtk[...] = jnp.zeros((3, 256, 128), F32)
    gtv[...] = jnp.zeros((3, 256, 128), F32)
    gk[...] = jnp.zeros((3, 512, 128), F32)
    gv[...] = jnp.zeros((3, 512, 128), F32)

    def back_rows(p, text, b):
        slots = pl.ds(b * 2, 2)
        rows = tile(b, 256)
        q = q8[p, slots].reshape(256, 128)
        g = gc[p, slots].reshape(256, 128)
        if text:
            g = (g.astype(F32) * gate_ref[p : p + 1, :]).astype(BF16)
        k = tk[p] if text else kk[p].reshape(512, 128)
        v = tv[p] if text else vv[p].reshape(512, 128)
        low_rows = lanes((256, 128)) < 64
        grad_q = jnp.zeros((256, 128), F32)
        for head in range(2):
            keep = low_rows if head == 0 else jnp.logical_not(low_rows)
            qm = jnp.where(keep, q, jnp.zeros_like(q))
            gm = jnp.where(keep, g, jnp.zeros_like(g))
            lane = p * 2 + head + 8 * text
            lse = lse_ref[slots, :, lane : lane + 1].reshape(256, 1)
            scores = mm_t(qm, k) + (text_bias if text else self_bias)
            probs = jnp.exp(scores - lse)
            grad_probs = mm_t(gm, v)
            delta = jnp.sum(probs * grad_probs, axis=-1, keepdims=True)
            grad_scores = (probs * (grad_probs - delta)).astype(BF16)
            grad_q = grad_q + jnp.where(keep, mm(grad_scores, k), 0.0)
            to_v, to_k = (gtv, gtk) if text else (gv, gk)
            to_v[p] += mm_rows(probs.astype(BF16), gm)
            to_k[p] += mm_rows(grad_scores, qm)
        if text:
            gq[p, rows] = grad_q
        else:
            gq[p, rows] += grad_q

    def over_rows(p, text):
        def step(b, carry):
            back_rows(p, text, b)
            return carry

        lax.fori_loop(0, 2, step, 0)

    def unit_of(raw):
        inverse = lax.rsqrt(head_mean(raw * raw, block) + EPSILON)
        return raw * inverse, inverse

    def back_head(unit, inverse, grad):
        return inverse * (grad - unit * head_mean(grad * unit, block))

    for p in range(3):
        over_rows(p, True)
    scat_f.step2()
    low_text = lanes((256, 128)) < 64
    head_rows = []
    rows = []
    text_row = jnp.zeros((1, 128), F32)
    grads_k, grads_v = [], []
    for p in range(3):
        unit, inverse = unit_of(tkr[p])
        gtk_p = gtk[p]
        text_row = text_row + jnp.sum(gtk_p * unit, axis=0, keepdims=True)
        grads_k.append(back_head(unit, inverse, gtk_p * hg_ref[2:3, :]))
        grads_v.append(gtv[p])
    for xx in range(2):
        tpack[xx, :, 0:128] = grads_k[xx].astype(BF16)
        tpack[xx, :, 256:384] = grads_v[xx].astype(BF16)
    tpack[0, :, 128:256] = jnp.where(low_text, grads_k[2], pltpu.roll(grads_v[2], 64, 1)).astype(BF16)
    tpack[1, :, 128:256] = jnp.where(low_text, pltpu.roll(grads_k[2], 64, 1), grads_v[2]).astype(BF16)

    def caption_grad(i, carry):
        xx = i // 8
        j = i % 8
        grad = mm(cap_flip[tile(2 * j + 1 - c)], tpack[xx])
        dw_c[xx, j // 4, j % 4] = grad.astype(BF16)
        return carry

    lax.fori_loop(0, 16, caption_grad, 0)
    scat_c.start()
    scat_f.step3()

    over_rows(0, False)
    scat_f.step4()
    over_rows(1, False)
    scat_c.step1()
    over_rows(2, False)
    scat_c.step2()

    cos = cos_ref[...].reshape(512, 128)
    sin = sin_ref[...].reshape(512, 128)
    low_head = lanes((512, 128)) < 64
    query_row = jnp.zeros((1, 128), F32)
    key_row = jnp.zeros((1, 128), F32)
    gate_rows = []
    raws = [[], []]
    for p in range(3):
        for i in range(2):
            grad = (gq[p] * 0.125) if i == 0 else gk[p]
            raw = (qr if i == 0 else kr)[p].reshape(512, 128)
            turned = grad * cos - swap_quarters(grad) * sin
            unit, inverse = unit_of(raw)
            row = jnp.sum(turned * unit, axis=0, keepdims=True)
            if i == 0:
                query_row = query_row + row
            else:
                key_row = key_row + row
            result = back_head(unit, inverse, turned * hg_ref[i : i + 1, :])
            if p < 2:
                gpack[p, :, (0 if i == 0 else 256) : (128 if i == 0 else 384)] = result.astype(BF16)
            else:
                raws[i] = result
        gate_rows.append(
            jnp.sum(
                gc[p].reshape(512, 128).astype(F32) * other_ref[p].reshape(512, 128),
                axis=0,
                keepdims=True,
            )
        )
    gpack[0, :, 128:256] = jnp.where(low_head, raws[0], pltpu.roll(raws[1], 64, 1)).astype(BF16)
    gpack[1, :, 128:256] = jnp.where(low_head, pltpu.roll(raws[0], 64, 1), raws[1]).astype(BF16)
    for xx in range(2):
        gpack[xx, :, 384:512] = gv[xx].astype(BF16)
    gpack[0, :, 512:640] = jnp.where(low_head, gv[2], 0.0).astype(BF16)
    gpack[1, :, 512:640] = jnp.where(low_head, pltpu.roll(gv[2], 64, 1), 0.0).astype(BF16)

    def first_rows(lo, count):
        n = count * 128
        a0 = gpack[0, lo * 128 : lo * 128 + n]
        a1 = gpack[1, lo * 128 : lo * 128 + n]
        for xb in range(2):
            cols = slice(xb * 768, xb * 768 + 768)
            b0 = w_a[0, xb, :, :, :, 0:640].reshape(768, 640)
            b1 = w_a[1, xb, :, :, :, 0:640].reshape(768, 640)
            total = mm_t(a0, b0) + mm_t(a1, b1)
            part[lo : lo + count, :, cols] = total.astype(BF16).reshape(count, 128, 768)

    sums = ZScatter(send, part, relay, got, right, left)
    first_rows(1, 2)
    sums.near()
    first_rows(3, 1)
    sums.far()
    first_rows(0, 1)
    scat_c.step3()

    def flip_rows(src):
        transpose_into(src, flip)

    flip_rows(grad_all)
    for xx in range(2):
        b = cw[xx].reshape(512, 256)

        def out_grad(j, carry, xx=xx, b=b):
            dw_a[xx, j // 2, (j % 2) * 2 : (j % 2) * 2 + 2, :, :, 512:768] = (
                mm(flip[tile(j, 384)], b).astype(BF16).reshape(2, 2, 96, 256)
            )
            return carry

        for j in range(4):
            out_grad(j, 0)
    sums.pass_on()
    flip_rows(first)
    for xx in range(2):
        for j in range(4):
            a = flip[j * 384 : j * 384 + 384]
            at = (xx, j // 2, slice((j % 2) * 2, (j % 2) * 2 + 2))
            dw_a[at + (slice(None), slice(None), slice(0, 512))] = (
                mm(a, gpack[xx, :, 0:512]).astype(BF16).reshape(2, 2, 96, 512)
            )
            last = at + (slice(None), slice(None), slice(512, 640))
            old = dw_a[last].reshape(384, 128).astype(F32)
            dw_a[last] = (
                (mm(a, gpack[xx, :, 512:640]) + old).astype(BF16).reshape(2, 2, 96, 128)
            )
    scat_a.start()
    scat_c.step4()
    grad_first = sums.total()

    unit_one, inverse_one = normalize(resid_ref[...].astype(F32))
    scale = 1.0 + mod_ref[0:1, :]
    gain = gains_ref[0:1, :]
    row_sum = jnp.sum(grad_first * unit_one, axis=0, keepdims=True)
    sums_0 = row_sum * gain
    sums_4 = row_sum * scale
    hid_grad[...] = (
        gmid_ref[...] + norm_back(unit_one, inverse_one, grad_first * scale * gain)
    ).reshape(2, 64, D)
    grad_swap = send(hid_grad.at[1 - xl], hidden_final.at[xl], pair)
    hidden_final[xl] = hid_grad[xl]
    mod_msg[...] = jnp.zeros((8, 8, 128), F32)
    gain_msg[...] = jnp.zeros((16, 8, 128), F32)
    for i in range(4):
        row = sums_0 if i == 0 else sums_ref[i : i + 1, :]
        for h in range(2):
            for j in range(6):
                lo = h * 768 + j * 128
                mod_msg[2 * i + h, j : j + 1, :] = row[:, lo : lo + 128]
    folded = [
        row + pltpu.roll(row, 64, 1) for row in (query_row, key_row, text_row)
    ]
    first_line = jnp.where(low_row, folded[0], folded[1])
    lane = lanes((1, 128))
    second_line = jnp.where(low_row, folded[2], 0.0)
    gate_row = gate_ref[...]
    for p in range(3):
        slope = 1.0 - gate_row[p : p + 1, :] * gate_row[p : p + 1, :]
        values = gate_rows[p] * slope
        for head in range(2):
            keep = low_row if head == 0 else jnp.logical_not(low_row)
            value = jnp.sum(jnp.where(keep, values, 0.0), axis=1, keepdims=True)
            index = (0, 1, 3, 4, 2, 5)[2 * p + head]
            second_line = second_line + jnp.where(lane == 64 + z * 6 + index, value, 0.0)
    gain_rows = jnp.concatenate([sums_4, sums_ref[5:8, :]], axis=0)
    for d in range(16):
        gain_msg[d, 0:4, 0:96] = gain_rows[:, d * 96 : (d + 1) * 96]
        gain_msg[d, 4:5, :] = first_line
        gain_msg[d, 5:6, :] = second_line
    to_t = [send(mod_msg.at[q[1]], got_mod.at[t], q) for q in t_peers]
    to_dp = [send(gain_msg.at[q[0]], got_gain.at[dp], q) for q in dp_peers]
    got_mod[t] = mod_msg[t]
    got_gain[dp] = gain_msg[dp]
    scat_a.step1()
    for copy in to_t:
        copy.wait_recv()
    g_all[dp, 0] = got_mod[0] + got_mod[2] + got_mod[4] + got_mod[6]
    g_all[dp, 1] = got_mod[1] + got_mod[3] + got_mod[5] + got_mod[7]
    to_all = [send(g_all.at[dp], g_all.at[dp], q) for q in dp_peers]
    for copy in to_dp:
        copy.wait_recv()
    gain_sum[t] = jnp.sum(got_gain[...], axis=0)
    to_rest = [send(gain_sum.at[t], gain_sum.at[t], q) for q in t_peers]
    scat_a.step2()
    top, low = scat_c.finish()
    c_out[0:128, :] = top
    c_out[128:256, :] = low
    for copy in to_all:
        copy.wait_recv()
    bias_all[t] = jnp.sum(g_all[...], axis=(0, 1))
    to_bias = [send(bias_all.at[t], bias_all.at[t], q) for q in t_peers]
    for copy in to_rest:
        copy.wait_recv()
    gain_out[...] = jnp.sum(gain_sum[...], axis=0)
    scat_a.step3()
    top, low = scat_f.finish()
    f_out[0:48, :] = top
    f_out[48:96, :] = low
    scat_a.step4()
    for copy in to_bias:
        copy.wait_recv()
    out_swap.wait_recv()
    grad_swap.wait_recv()
    top, low = scat_a.finish()
    d_out[0:48, :] = top
    d_out[48:96, :] = low
    send.drain()


def back_call(args, cid):
    S = jax.ShapeDtypeStruct
    vm = pl.BlockSpec(memory_space=VMEM)
    sm = pl.BlockSpec(memory_space=pltpu.SMEM)
    any_ = pl.BlockSpec(memory_space=pl.ANY)
    outs = [
        S((96, 768), F32),
        S((96, D), F32),
        S((256, 384), F32),
        S((2, 64, D), BF16),
        S((2, 64, D), F32),
        S((16, 2, 8, 128), F32),
        S((8, 128), F32),
        S((8, 8, 128), F32),
    ]
    return pl.pallas_call(
        back_kernel,
        out_shape=outs,
        in_specs=[vm, any_] + [vm] * 24 + [sm, sm],
        out_specs=[vm] * len(outs),
        scratch_shapes=[
            VMEM((2, 4, 96, D), BF16),
            VMEM((D, 512), BF16),
            VMEM((4, 128, D), BF16),
            VMEM((3, 4, 128, 128), BF16),
            VMEM((3, 512, 128), F32),
            VMEM((3, 512, 128), F32),
            VMEM((3, 512, 128), F32),
            VMEM((3, 256, 128), F32),
            VMEM((3, 256, 128), F32),
            VMEM((2, 512, 640), BF16),
            VMEM((2, 256, 384), BF16),
            VMEM((2, 2, 4, 2, 96, 768), BF16),
            VMEM((2, 2, 4, 256, 384), BF16),
            VMEM((4, 128, D), BF16),
            VMEM((2, 64, D), BF16),
            VMEM((2, 128, D), BF16),
            VMEM((2, 64, D), F32),
            VMEM((8, 8, 128), F32),
            VMEM((16, 8, 128), F32),
            VMEM((8, 8, 128), F32),
            VMEM((16, 8, 128), F32),
            VMEM((8, 8, 128), F32),
        ]
        + scatter_bufs(96, D)
        + scatter_bufs(96, 768)
        + scatter_bufs(256, 384)
        + [pltpu.SemaphoreType.DMA((4,))]
        + dma_sems(140),
        compiler_params=pltpu.CompilerParams(
            collective_id=cid, has_side_effects=True, vmem_limit_bytes=62 * 2**20
        ),
        name="attention_back",
    )(*args)


def on_device(
    hidden,
    condition,
    caption,
    lengths,
    frames,
    widths,
    caption_lens,
    cotangent,
    ada_weight,
    ada_bias,
    norm_gains,
    qkv_weight,
    head_gains,
    caption_weight,
    head_gate,
    out_weight,
    ffn_weight,
    down_weight,
):
    S = jax.ShapeDtypeStruct
    dp = lax.axis_index("dp")
    t = lax.axis_index("tensor")
    z = t // 2
    xl = t % 2
    def head_tiles(rows):
        return jnp.concatenate([rows, rows], axis=-1)

    head_scales = head_gains.astype(F32)
    hg2 = jnp.pad(head_tiles(head_scales), ((0, 5), (0, 0)))
    gate_values = jnp.tanh(lax.dynamic_slice_in_dim(head_gate.astype(F32), z * 6, 6, 0))
    gate_tile = jnp.pad(
        jnp.repeat(gate_values[jnp.array([0, 1, 3, 4, 2, 5])].reshape(3, 2), 64, axis=1),
        ((0, 5), (0, 0)),
    )
    (
        w_a,
        w_f,
        first_rel,
        resid_b,
        cot,
        q8,
        kk,
        vv,
        qr,
        kr,
        tk,
        tv,
        tkr,
        other_rel,
        lse,
        cw,
        attn,
        middle,
        second_in,
        mod8,
        gains8,
        got1,
        cos_t,
        sin_t,
        live128,
        cap_flip,
    ) = attention_call(
        [
            hidden[:, 0],
            cotangent[:, 0],
            condition[:, 0],
            norm_gains,
            ada_bias[None],
            ada_weight,
            qkv_weight,
            out_weight.T,
            ffn_weight,
            down_weight.T,
            caption_weight,
            caption[:, 0],
            hg2,
            gate_tile,
            lengths,
            frames,
            widths,
            caption_lens,
        ],
        1,
    )
    layer_out, grad_middle, grad_attn_in, ffn_sums, f_grad = ffn_call(
        second_in,
        w_f.reshape(2, D, D),
        middle,
        attn,
        cot.reshape(128, D),
        mod8,
        gains8,
        live128,
        6,
    )
    d_out, f_out, c_out, layer_final, grad_final, g_all, gain_out, bias_all = back_call(
        [
            grad_attn_in,
            f_grad.reshape(2, 2, 4, 2, 96, D),
            w_a,
            first_rel,
            resid_b,
            q8,
            kk,
            vv,
            qr,
            kr,
            tk,
            tv,
            tkr,
            other_rel,
            lse,
            cw,
            mod8,
            gains8,
            cos_t,
            sin_t,
            grad_middle,
            layer_out.reshape(2, 64, D),
            ffn_sums,
            cap_flip,
            hg2,
            gate_tile,
            lengths,
            caption_lens,
        ],
        3,
    )
    units = got1[:, 0:2, :64].reshape(32, 64)
    g_items = g_all[:, :, :6].reshape(32, 768)
    ada_grad = jnp.einsum("mc,mk->ck", units, g_items, precision=lax.Precision.HIGHEST)
    bias_block = pick(bias_all, dp // 2)[:6].reshape(2, 384)
    bias_grad = pick(bias_block, dp % 2)
    heads = gain_out[4:6].reshape(256)
    return (
        layer_final[:, None],
        grad_final[:, None],
        ada_grad,
        bias_grad,
        gain_out[:4, :96],
        jnp.stack(
            [
                d_out[:, :192],
                jnp.concatenate([d_out[:, 256:384], d_out[:, 192:256]], axis=1),
                d_out[:, 384:576],
            ]
        ),
        heads[:192].reshape(3, 64),
        jnp.stack(
            [c_out[:, :192], jnp.concatenate([c_out[:, 256:384], c_out[:, 192:256]], axis=1)]
        ),
        heads[192:216],
        jnp.concatenate([d_out[:, 640:768], d_out[:, 576:640]], axis=1).T,
        jnp.stack([f_out[:, :512], f_out[:, 512:1024]]),
        f_out[:, 1024:].T,
    )


def solution(mesh):
    return jax.shard_map(
        on_device,
        mesh=mesh,
        in_specs=(
            P(None, "dp", "tensor", None),
            P(None, "dp", None),
            P(None, "dp", None, None),
            P(None, "dp"),
            P(None, "dp"),
            P(None, "dp"),
            P(None, "dp"),
            P(None, "dp", "tensor", None),
            P("dp", "tensor"),
            P("dp"),
            P(None, "dp"),
            P(None, "dp", "tensor"),
            P(),
            P(None, "dp", "tensor"),
            P(),
            P("tensor", "dp"),
            P(None, "dp", "tensor"),
            P("tensor", "dp"),
        ),
        out_specs=(
            P(None, "dp", "tensor", None),
            P(None, "dp", "tensor", None),
            P("dp", "tensor"),
            P("dp"),
            P(None, "dp"),
            P(None, "dp", "tensor"),
            P(),
            P(None, "dp", "tensor"),
            P(),
            P("tensor", "dp"),
            P(None, "dp", "tensor"),
            P("tensor", "dp"),
        ),
        check_vma=False,
    )
```

```python
import jax
import jax.numpy as jnp
from jax import lax
from jax.experimental import pallas as pl
from jax.experimental.pallas import tpu as pltpu
from jax.sharding import PartitionSpec as P

D = 1536
H = 24
HD = 64
EPSILON = 1e-05
NEGATIVE = -1e30
MESH = pl.DeviceIdType.MESH
VMEM = pltpu.VMEM
F32 = jnp.float32
BF16 = jnp.bfloat16


def coords():
    dp = lax.axis_index("dp")
    t = lax.axis_index("tensor")
    return dp // 8, t % 2, (dp // 2) % 4, t // 2, dp % 2


def device_of(x, y, z, c):
    return ((x // 2) * 8 + y * 2 + c, z * 2 + x % 2)


def greet_signal(devices):
    barrier = pltpu.get_barrier_semaphore()
    for device in devices:
        pl.semaphore_signal(barrier, inc=1, device_id=device, device_id_type=MESH)


def greet_wait(devices):
    pl.semaphore_wait(pltpu.get_barrier_semaphore(), len(devices))


def greet(devices):
    greet_signal(devices)
    greet_wait(devices)


class Sender:
    def __init__(self, send_sem, recv_sem):
        self.send_sem = send_sem
        self.recv_sem = recv_sem
        self.copies = []

    def __call__(self, src, dst, device):
        k = len(self.copies)
        copy = pltpu.make_async_remote_copy(
            src_ref=src,
            dst_ref=dst,
            send_sem=self.send_sem.at[k],
            recv_sem=self.recv_sem.at[k],
            device_id=device,
            device_id_type=MESH,
        )
        copy.start()
        self.copies.append(copy)
        return copy

    def drain(self):
        for copy in self.copies:
            copy.wait_send()


def dma_sems(n):
    return [pltpu.SemaphoreType.DMA((n,)), pltpu.SemaphoreType.DMA((n,))]


def plane_peers():
    xh, xl, y, z, c = coords()
    x = 2 * xh + xl
    xr, xq = (x + 1) % 4, (x + 3) % 4
    yr, yq = (y + 1) % 4, (y + 3) % 4
    peers = [
        device_of(xr, y, z, c),
        device_of(xq, y, z, c),
        device_of(x, yr, z, c),
        device_of(x, yq, z, c),
        device_of(x, y, z, 1 - c),
    ]
    return x, y, c, xr, xq, yr, yq, peers


def add_low(a, b):
    return (a.astype(F32) + b.astype(F32)).astype(BF16)


def normalize(values):
    inverse = lax.rsqrt(jnp.mean(values * values, axis=-1, keepdims=True) + EPSILON)
    return (values * inverse, inverse)


def norm_back(unit_values, inverse, gradient):
    return inverse * (
        gradient - unit_values * jnp.mean(gradient * unit_values, axis=-1, keepdims=True)
    )


def swish(values):
    return values * jax.nn.sigmoid(values)


def z_ring():
    xh, xl, y, z, c = coords()
    x = 2 * xh + xl
    return z, device_of(x, y, (z + 1) % 4, c), device_of(x, y, (z + 3) % 4, c)


class ZGather:
    def __init__(self, send, own, every, right, left):
        self.send, self.every, self.right, self.left = send, every, right, left
        half = every.shape[1] // 2
        self.lower, self.upper = pl.ds(0, half), pl.ds(half, half)
        self.a_low = send(own.at[self.lower], every.at[1, self.lower], right)
        self.b_up = send(own.at[self.upper], every.at[2, self.upper], left)
        self.a_up = send(own.at[self.upper], every.at[1, self.upper], right)
        self.b_low = send(own.at[self.lower], every.at[2, self.lower], left)

    def near(self):
        every, lower, upper = self.every, self.lower, self.upper
        self.a_low.wait_recv()
        self.far_low = self.send(every.at[1, lower], every.at[3, lower], self.right)
        self.b_up.wait_recv()
        self.far_up = self.send(every.at[2, upper], every.at[3, upper], self.left)
        self.a_up.wait_recv()
        self.b_low.wait_recv()

    def far(self):
        self.far_low.wait_recv()
        self.far_up.wait_recv()


class ZScatter:
    def __init__(self, send, part, relay, got, right, left):
        self.send, self.part, self.relay, self.got = send, part, relay, got
        self.right, self.left = right, left
        self.lower, self.upper = pl.ds(0, 64), pl.ds(64, 64)
        self.waits = []

    def near(self):
        part, got = self.part, self.got
        self.waits.append(self.send(part.at[2, self.upper], got.at[0, self.upper], self.right))
        self.waits.append(self.send(part.at[1, self.lower], got.at[1, self.lower], self.left))

    def far(self):
        part, relay = self.part, self.relay
        self.relays = []
        for i in range(2):
            rows, low, up = pl.ds(32 * i, 32), pl.ds(32 * i, 32), pl.ds(64 + 32 * i, 32)
            self.relays.append(
                (
                    self.send(part.at[3, low], relay.at[0, rows], self.right),
                    self.send(part.at[3, up], relay.at[1, rows], self.left),
                )
            )

    def pass_on(self):
        part, relay, got = self.part, self.relay, self.got
        for i in range(2):
            rows, low, up = pl.ds(32 * i, 32), pl.ds(32 * i, 32), pl.ds(64 + 32 * i, 32)
            self.relays[i][0].wait_recv()
            part[2, low] = add_low(part[2, low], relay[0, rows])
            self.waits.append(self.send(part.at[2, low], got.at[0, low], self.right))
            self.relays[i][1].wait_recv()
            part[1, up] = add_low(part[1, up], relay[1, rows])
            self.waits.append(self.send(part.at[1, up], got.at[1, up], self.left))

    def total(self):
        for copy in self.waits:
            copy.wait_recv()
        got = self.got
        return self.part[0].astype(F32) + got[0].astype(F32) + got[1].astype(F32)


def mm(a, b):
    return lax.dot_general(a, b, (((1,), (0,)), ((), ())), preferred_element_type=F32)


def mm_t(a, b):
    return lax.dot_general(a, b, (((1,), (1,)), ((), ())), preferred_element_type=F32)


def tile(j, size=256):
    return pl.ds(pl.multiple_of(j * size, size), size)


def transpose_into(src, dst):
    def column(j, carry):
        cols = tile(j, 128)
        for slot in range(4):
            dst[cols, slot * 128 : (slot + 1) * 128] = src[slot, :, cols].T
        return carry

    lax.fori_loop(0, D // 128, column, 0)


class PlaneGather:
    def __init__(self, send, shard, every):
        self.send, self.shard, self.every = send, shard, every
        rows, cols = shard.shape
        half = rows // 2
        self.top, self.low = pl.ds(0, half), pl.ds(half, half)
        if rows == 96:
            left, right = pl.ds(0, cols // 2), pl.ds(cols // 2, cols // 2)
            self.qa = [(self.top, left), (self.top, right)]
            self.qb = [(self.low, left), (self.low, right)]
        else:
            q = half // 2
            self.qa = [(pl.ds(0, q),), (pl.ds(q, q),)]
            self.qb = [(pl.ds(2 * q, q),), (pl.ds(3 * q, q),)]
        self.late = []

    def at(self, xx, yy, *rest):
        return self.every.at[(xx % 2, xx // 2, yy, self.c) + rest]

    def same(self, ref, device):
        return self.send(ref, ref, device)

    def to_sibling(self, ref):
        self.late.append(self.send(ref, ref, self.sibling))

    def start(self, local_sem):
        x, y, c, xr, xq, yr, yq, peers = plane_peers()
        self.x, self.y, self.c = x, y, c
        self.xr, self.xq, self.yr, self.yq = xr, xq, yr, yq
        self.go_xr, self.go_xq, self.go_yr, self.go_yq, self.sibling = peers
        shard, top, low = self.shard, self.top, self.low
        self.a_r = self.send(shard.at[top], self.at(x, y, top), self.go_xr)
        self.a_l = self.send(shard.at[top], self.at(x, y, top), self.go_xq)
        self.b_r = self.send(shard.at[low], self.at(x, y, low), self.go_yr)
        self.b_l = self.send(shard.at[low], self.at(x, y, low), self.go_yq)
        self.late.append(self.send(shard, self.at(x, y), self.sibling))
        self.local = pltpu.make_async_copy(shard, self.at(x, y), local_sem)
        self.local.start()

    def step2(self):
        x, y = self.x, self.y
        self.a_r.wait_recv()
        self.f1 = self.same(self.at(self.xq, y, *self.qa[0]), self.go_xr)
        self.a_l.wait_recv()
        self.f2 = self.same(self.at(self.xr, y, *self.qa[1]), self.go_xq)
        self.b_r.wait_recv()
        self.f3 = self.same(self.at(x, self.yq, *self.qb[0]), self.go_yr)
        self.b_l.wait_recv()
        self.f4 = self.same(self.at(x, self.yr, *self.qb[1]), self.go_yq)

    def step3(self):
        x, y, c = self.x, self.y, self.c
        every, top, low = self.every, self.top, self.low
        self.local.wait()
        self.f1.wait_recv()
        self.f2.wait_recv()
        block = every.at[:, :, y, c, top]
        self.g_r = self.same(block, self.go_yr)
        self.g_l = self.same(block, self.go_yq)
        self.f3.wait_recv()
        self.f4.wait_recv()
        block = every.at[x % 2, x // 2, :, c, low]
        self.h_r = self.same(block, self.go_xr)
        self.h_l = self.same(block, self.go_xq)
        for k in range(1, 4):
            self.to_sibling(self.at((x + k) % 4, y, top))
            self.to_sibling(self.at(x, (y + k) % 4, low))

    def step4(self):
        c, every, top, low = self.c, self.every, self.top, self.low
        xr, xq, yr, yq = self.xr, self.xq, self.yr, self.yq
        self.g_r.wait_recv()
        self.f1 = self.same(every.at[0, :, yq, c, top], self.go_yr)
        self.g_l.wait_recv()
        self.f2 = self.same(every.at[1, :, yr, c, top], self.go_yq)
        self.h_r.wait_recv()
        self.f3 = self.same(every.at[xq % 2, xq // 2, pl.ds(0, 2), c, low], self.go_xr)
        self.h_l.wait_recv()
        self.f4 = self.same(every.at[xr % 2, xr // 2, pl.ds(2, 2), c, low], self.go_xq)
        self.to_sibling(every.at[:, :, yq, c, top])
        self.to_sibling(every.at[:, :, yr, c, top])
        self.to_sibling(every.at[xq % 2, xq // 2, :, c, low])
        self.to_sibling(every.at[xr % 2, xr // 2, :, c, low])

    def step5(self):
        c, every, top, low = self.c, self.every, self.top, self.low
        xo, yo = (self.x + 2) % 4, (self.y + 2) % 4
        for copy in (self.f1, self.f2, self.f3, self.f4):
            copy.wait_recv()
        self.to_sibling(every.at[:, :, yo, c, top])
        self.to_sibling(every.at[xo % 2, xo // 2, :, c, low])

    def finish(self):
        for copy in self.late:
            copy.wait_recv()


OFFSETS = (0, 3, 1, 2)


def lanes(shape):
    return lax.broadcasted_iota(jnp.int32, shape, len(shape) - 1)


def head_block():
    row = lax.broadcasted_iota(jnp.int32, (128, 128), 0) // 64
    col = lax.broadcasted_iota(jnp.int32, (128, 128), 1) // 64
    return jnp.where(row == col, 1.0 / 64.0, 0.0).astype(BF16)


def head_mean(values, block):
    high = values.astype(BF16)
    low = (values - high.astype(F32)).astype(BF16)
    return mm(high, block) + mm(low, block)


def swap_quarters(values):
    second = (lanes(values.shape) % 64) >= 32
    return jnp.where(second, pltpu.roll(values, 32, 1), pltpu.roll(values, 96, 1))


GAIN_ROW, GATE_ROW, LENGTH_ROW, FRAMES_ROW, WIDTH_ROW, TEXT_ROW, BIAS_ROW = 0, 3, 6, 7, 8, 9, 10


def key_bias(total, z, length):
    lane = lanes((1, total))
    if total == 512:
        slot = lane // 128
        block = jnp.where(slot == 0, z, jnp.where(slot == 1, z + 3, jnp.where(slot == 2, z + 1, z + 2)))
        position = (block % 4) * 128 + lane % 128
    else:
        position = lane
    return jnp.where(position.astype(F32) < length[:, :1], 0.0, NEGATIVE)


def fill_rope(cos_ref, sin_ref, z, length, frames, width):
    lane = lanes((128, 128))
    pair = lane % 32
    offset = jnp.where(pair >= 20, 20, jnp.where(pair >= 8, 8, 0))
    size = jnp.where(pair >= 8, 12.0, 8.0)
    freq = jnp.exp((pair - offset).astype(F32) / size * (-9.210340371976184))
    sign = jnp.where(lane % 64 >= 32, 1.0, -1.0)
    row_size = width
    per_frame = jnp.floor((length + frames - 0.5) / frames)
    row = lax.broadcasted_iota(jnp.int32, (128, 128), 0).astype(F32)
    for slot in range(4):
        start = (((z + OFFSETS[slot]) % 4) * 128).astype(F32)
        position = row + start
        frame = jnp.floor((position + 0.5) / per_frame)
        within = position - frame * per_frame
        row_pos = jnp.floor((within + 0.5) / row_size)
        col_pos = within - row_pos * row_size
        chosen = jnp.where(pair >= 20, col_pos, jnp.where(pair >= 8, row_pos, frame))
        angle = chosen * freq
        cos_ref[slot] = jnp.cos(angle)
        sin_ref[slot] = jnp.sin(angle) * sign


def attention_kernel(
    hid_ref,
    cot_ref,
    cap_hbm,
    cond_ref,
    gain_in,
    ada_ref,
    qkv_ref,
    out_w_ref,
    ffn_w_ref,
    down_t_ref,
    cap_t_ref,
    bias_ref,
    head_gain_ref,
    head_gate_ref,
    len_ref,
    frame_ref,
    width_ref,
    tlen_ref,
    w_f,
    w_a_out,
    cap_flip_out,
    first_flip_out,
    q8_out,
    kk_out,
    vv_out,
    qr_out,
    kr_out,
    tkr_out,
    other_out,
    lse_out,
    cw_out,
    cos_out,
    sin_out,
    resid_out,
    tk_out,
    tv_out,
    attn_out,
    mid_out,
    second_out,
    cot_out,
    mod_ref,
    gains_ref,
    got1,
    live_ref,
    facts,
    w_a,
    cap_flip,
    first_flip,
    q8,
    kk,
    vv,
    qr,
    kr,
    tkr,
    other_ref,
    lse_ref,
    cw,
    cos_ref,
    sin_ref,
    resid_ref,
    tk,
    tv,
    attn_ref,
    mid_ref,
    second_ref,
    first,
    own_ref,
    sh_a,
    sh_f,
    sh_c,
    w_c,
    cap,
    hid_all,
    hid_own,
    msg,
    sent2,
    got2,
    got3,
    mixed,
    part,
    relay,
    got,
    local_sems,
    ss,
    rs,
):
    dp = lax.axis_index("dp")
    t = lax.axis_index("tensor")
    xh, xl, y, z, c = coords()
    _, right, left = z_ring()
    pair = device_of(2 * xh + 1 - xl, y, z, c)
    dp_peers = [((dp + k) % 16, t) for k in range(1, 16)]
    t_peers = [(dp, (t + k) % 8) for k in range(1, 8)]
    outer_x = device_of((2 * xh + xl + 3 - 2 * xl) % 4, y, z, c)
    everyone = dp_peers + t_peers + [outer_x]
    greet_signal(everyone)
    load_cap = pltpu.make_async_copy(cap_hbm.at[xl], cap, local_sems.at[0])
    load_cap.start()
    load_hid = pltpu.make_async_copy(hid_ref.at[xl], hid_own.at[xl], local_sems.at[4])
    load_hid.start()
    flushes = []

    def flush(src, dst):
        copy = pltpu.make_async_copy(src, dst, local_sems.at[5 + len(flushes)])
        copy.start()
        flushes.append(copy)

    flush(cot_ref.at[xl], cot_out.at[xl])
    facts[...] = jnp.zeros((16, 128), F32)
    for i in range(3):
        gain = head_gain_ref[i : i + 1, :].astype(F32)
        facts[i : i + 1, 0:64] = gain
        facts[i : i + 1, 64:128] = gain
        facts[BIAS_ROW + i : BIAS_ROW + i + 1, :] = bias_ref[:, i * 128 : i * 128 + 128].astype(F32)
    gates = jnp.tanh(head_gate_ref[...].astype(F32))
    gate_lane = lanes((1, 24))
    low_row = lanes((1, 128)) < 64
    for p in range(3):
        a, b = [
            jnp.sum(jnp.where(gate_lane == z * 6 + h, gates, 0.0), axis=1, keepdims=True)
            for h in ((0, 1), (3, 4), (2, 5))[p]
        ]
        facts[GATE_ROW + p : GATE_ROW + p + 1, :] = jnp.where(low_row, a, b)
    for i, ref in enumerate((len_ref, frame_ref, width_ref, tlen_ref)):
        count = jnp.where(xl == 0, ref[:, 0:1], ref[:, 1:2]).astype(F32)
        facts[LENGTH_ROW + i : LENGTH_ROW + i + 1, :] = jnp.broadcast_to(count, (1, 128))
    unit = swish(cond_ref[...].astype(F32)).astype(BF16).astype(F32)
    msg[...] = jnp.zeros((16, 8, 128), F32)
    gain_rows = gain_in[...].astype(F32)
    for d in range(16):
        msg[d, 0:2, 0:64] = unit[:, d * 64 : (d + 1) * 64]
        msg[d, 4:8, 0:96] = gain_rows
    qs, ks, vs = qkv_ref[0], qkv_ref[1], qkv_ref[2]
    os = out_w_ref[...].T
    sh_a[...] = jnp.concatenate(
        [qs, ks[:, 128:192], ks[:, 0:128], vs, os[:, 128:192], os[:, 0:128]],
        axis=1,
    )
    ck, cv = cap_t_ref[0].T, cap_t_ref[1].T
    sh_c[...] = jnp.concatenate([ck, cv[:, 128:192], cv[:, 0:128]], axis=1)
    greet_wait(everyone)

    send = Sender(ss, rs)
    swap = send(hid_ref.at[1 - xl], hid_own.at[xl], pair)
    near_r1 = send(hid_ref.at[xl], hid_all.at[1, xl], right)
    near_l1 = send(hid_ref.at[xl], hid_all.at[2, xl], left)
    round1 = [send(msg.at[p[0]], got1.at[dp], p) for p in dp_peers]
    ga = PlaneGather(send, sh_a, w_a)
    gc = PlaneGather(send, sh_c, w_c)
    gf = PlaneGather(send, sh_f, w_f)
    ga.start(local_sems.at[1])
    gc.start(local_sems.at[2])
    got1[dp] = msg[dp]
    sh_f[:, 0:512] = ffn_w_ref[0]
    sh_f[:, 512:1024] = ffn_w_ref[1]
    sh_f[:, 1024:1536] = down_t_ref[...]
    length = facts[LENGTH_ROW : LENGTH_ROW + 1, :]
    text_len = facts[TEXT_ROW : TEXT_ROW + 1, :]
    for copy in round1:
        copy.wait_recv()
    rows = got1[...].reshape(128, 128)[:, :64].astype(BF16)
    here = t == dp // 2
    low_bias = jnp.where(jnp.logical_and(here, dp % 2 == 0), 1.0, 0.0)
    high_bias = jnp.where(jnp.logical_and(here, dp % 2 == 1), 1.0, 0.0)
    terms = mm(rows, ada_ref[...])
    bias = [facts[BIAS_ROW + j : BIAS_ROW + j + 1, :] for j in range(3)]
    bias = [row * low_bias for row in bias] + [row * high_bias for row in bias]
    for d in range(16):
        for j in range(6):
            sent2[d, 2 * j : 2 * j + 2, :] = terms[8 * d : 8 * d + 2, 128 * j : 128 * j + 128] + bias[j]
    round2 = [send(sent2.at[p[0]], got2.at[dp], p) for p in dp_peers]
    got2[dp] = sent2[dp]
    load_hid.wait()
    swap.wait_recv()
    near_r2 = send(hid_own.at[1 - xl], hid_all.at[1, 1 - xl], right)
    near_l2 = send(hid_own.at[1 - xl], hid_all.at[2, 1 - xl], left)
    hid_all[0] = hid_own[...]
    ga.step2()
    gf.start(local_sems.at[3])
    gc.step2()
    for copy in round2:
        copy.wait_recv()
    got3[t] = jnp.sum(got2[...], axis=0)
    round3 = [send(got3.at[t], got3.at[t], p) for p in t_peers]
    ga.step3()
    fill_rope(
        cos_ref,
        sin_ref,
        z,
        length,
        facts[FRAMES_ROW : FRAMES_ROW + 1, :],
        facts[WIDTH_ROW : WIDTH_ROW + 1, :],
    )
    flush(cos_ref, cos_out)
    flush(sin_ref, sin_out)
    near_r1.wait_recv()
    near_r2.wait_recv()
    far_r = send(hid_all.at[1, 0], hid_all.at[3, 0], right)
    near_l1.wait_recv()
    near_l2.wait_recv()
    far_l = send(hid_all.at[2, 1], hid_all.at[3, 1], left)
    gf.step2()
    cot_swap = send(cot_ref.at[1 - xl], cot_out.at[xl], pair)
    for d in range(16):
        gains_ref[0:4, d * 96 : (d + 1) * 96] = got1[d, 4:8, 0:96]
    gains_ref[4:8, :] = jnp.zeros((4, D), F32)
    slot_row = lax.broadcasted_iota(jnp.int32, (128, 128), 0) + z * 128
    live_ref[...] = jnp.where(slot_row.astype(F32) < length, 1.0, 0.0)
    for copy in round3:
        copy.wait_recv()
    for i in range(4):
        for h in range(2):
            block = got3[2 * i + h]
            for j in range(6):
                lo = h * 768 + j * 128
                mod_ref[i : i + 1, lo : lo + 128] = jnp.where(
                    xl == 0, block[2 * j : 2 * j + 1], block[2 * j + 1 : 2 * j + 2]
                )
    mod_ref[4:8, :] = jnp.zeros((4, D), F32)
    factor = gains_ref[0:1, :] * (1.0 + mod_ref[0:1, :])

    def scale_rows(slot, carry):
        unit_rows, _ = normalize(hid_all[slot].reshape(128, D).astype(F32))
        first[slot] = (unit_rows * factor).astype(BF16)
        return carry

    lax.fori_loop(0, 3, scale_rows, 0)
    far_r.wait_recv()
    far_l.wait_recv()
    scale_rows(3, 0)
    resid_ref[...] = hid_all[0].reshape(128, D)
    flush(resid_ref, resid_out)
    ga.step4()
    gc.step3()
    transpose_into(first, first_flip)
    flush(first_flip, first_flip_out)
    ga.step5()
    load_cap.wait()

    def flip_caption(j, carry):
        rows = tile(j, 128)
        cap_flip[rows, 0:128] = cap[0:128, rows].T
        cap_flip[rows, 128:256] = cap[128:256, rows].T
        return carry

    lax.fori_loop(0, 8, flip_caption, 0)
    ga.finish()
    flush(w_a, w_a_out)

    x_rows = first[...].reshape(512, D)
    low_head = lanes((512, 128)) < 64

    def project(xx, cols):
        w_cols = w_a[xx, :, :, :, :, cols].reshape(D, cols.stop - cols.start)
        return mm(x_rows, w_cols)

    for xx in range(2):
        p = project(xx, slice(0, 256))
        qr[xx] = p[:, :128].reshape(4, 128, 128)
        mixed[0, xx] = p[:, 128:]
        p = project(xx, slice(256, 512))
        kr[xx] = p[:, :128].reshape(4, 128, 128)
        vv[xx] = p[:, 128:].astype(BF16).reshape(4, 128, 128)
        mixed[1, xx] = project(xx, slice(512, 640))
    x0, x1 = mixed[0, 0], mixed[0, 1]
    qr[2] = jnp.where(low_head, x0, pltpu.roll(x1, 64, 1)).reshape(4, 128, 128)
    kr[2] = jnp.where(low_head, pltpu.roll(x0, 64, 1), x1).reshape(4, 128, 128)
    x0, x1 = mixed[1, 0], mixed[1, 1]
    vv[2] = jnp.where(low_head, x0, pltpu.roll(x1, 64, 1)).astype(BF16).reshape(4, 128, 128)
    block = head_block()
    cos = cos_ref[...].reshape(512, 128)
    sin = sin_ref[...].reshape(512, 128)

    def turned(raw, gain):
        raw = raw.reshape(512, 128)
        v = raw * lax.rsqrt(head_mean(raw * raw, block) + EPSILON) * gain
        return v * cos + swap_quarters(v) * sin

    for p in range(3):
        q = turned(qr[p], facts[GAIN_ROW : GAIN_ROW + 1, :]).astype(BF16)
        q8[p] = (q.astype(F32) * 0.125).astype(BF16).reshape(4, 128, 128)
        k = turned(kr[p], facts[GAIN_ROW + 1 : GAIN_ROW + 2, :])
        kk[p] = k.astype(BF16).reshape(4, 128, 128)
    for src, dst in ((q8, q8_out), (kk, kk_out), (vv, vv_out), (qr, qr_out), (kr, kr_out)):
        flush(src, dst)

    self_bias = key_bias(512, z, length)
    text_bias = key_bias(256, z, text_len)
    lse_ref[...] = jnp.zeros((4, 128, 128), F32)

    def attend_rows(p, text, b):
        slots = pl.ds(b * 2, 2)
        q = q8[p, slots].reshape(256, 128)
        k = tk[p] if text else kk[p].reshape(512, 128)
        v = tv[p] if text else vv[p].reshape(512, 128)
        low_rows = lanes((256, 128)) < 64
        mix = jnp.zeros((256, 128), F32)
        for head in range(2):
            keep = low_rows if head == 0 else jnp.logical_not(low_rows)
            qm = jnp.where(keep, q, jnp.zeros_like(q))
            scores = mm_t(qm, k) + (text_bias if text else self_bias)
            top = jnp.max(scores, axis=-1, keepdims=True)
            e = jnp.exp(scores - top)
            total = jnp.sum(e, axis=-1, keepdims=True)
            probs = (e * (1.0 / total)).astype(BF16)
            mix = mix + jnp.where(keep, mm(probs, v), 0.0)
            lane = p * 2 + head + 8 * text
            lse_ref[slots, :, lane : lane + 1] = (top + jnp.log(total)).reshape(2, 128, 1)
        if not text:
            own_ref[p, slots] = mix.reshape(2, 128, 128)
            return
        other_ref[p, slots] = mix.reshape(2, 128, 128)
        both = own_ref[p, slots].reshape(256, 128) + facts[GATE_ROW + p : GATE_ROW + p + 1, :] * mix
        if p < 2:
            cw[p, slots, :, 128:256] = both.astype(BF16).reshape(2, 128, 128)
        else:
            moved = pltpu.roll(both, 64, 1)
            zero = jnp.zeros_like(both)
            cw[0, slots, :, 0:128] = jnp.where(low_rows, zero, moved).astype(BF16).reshape(2, 128, 128)
            cw[1, slots, :, 0:128] = jnp.where(low_rows, zero, both).astype(BF16).reshape(2, 128, 128)

    def attend(p, text):
        def step(b, carry):
            attend_rows(p, text, b)
            return carry

        lax.fori_loop(0, 2, step, 0)

    attend(0, False)
    gc.step4()
    gf.step3()
    attend(1, False)
    attend(2, False)
    gc.step5()
    lax.fori_loop(8, 32, flip_caption, 0)
    flush(cap_flip, cap_flip_out)
    gc.finish()
    low_text = lanes((256, 128)) < 64
    sides = []
    for xx in range(2):
        total = mm(cap[:, 0:2048], w_c[xx, 0].reshape(2048, 384))
        total = total + mm(cap[:, 2048:4096], w_c[xx, 1].reshape(2048, 384))
        tkr[xx] = total[:, 0:128]
        tv[xx] = total[:, 256:384].astype(BF16)
        sides.append(total[:, 128:256])
    x0, x1 = sides
    tkr[2] = jnp.where(low_text, x0, pltpu.roll(x1, 64, 1))
    tv[2] = jnp.where(low_text, pltpu.roll(x0, 64, 1), x1).astype(BF16)
    flush(tv, tv_out)
    for p in range(3):
        raw = tkr[p]
        gain = facts[GAIN_ROW + 2 : GAIN_ROW + 3, :]
        tk[p] = (raw * lax.rsqrt(head_mean(raw * raw, block) + EPSILON) * gain).astype(BF16)
    flush(tkr, tkr_out)
    flush(tk, tk_out)
    for p in range(3):
        attend(p, True)
    flush(lse_ref, lse_out)
    flush(other_ref, other_out)
    flush(cw, cw_out)

    def out_rows(lo, count):
        n = count * 128
        a0 = cw[0, lo : lo + count].reshape(n, 256)
        a1 = cw[1, lo : lo + count].reshape(n, 256)
        for xb in range(2):
            cols = slice(xb * 768, xb * 768 + 768)
            b0 = w_a[0, xb, :, :, :, 512:768].reshape(768, 256)
            b1 = w_a[1, xb, :, :, :, 512:768].reshape(768, 256)
            total = mm_t(a0, b0) + mm_t(a1, b1)
            part[lo : lo + count, :, cols] = total.astype(BF16).reshape(count, 128, 768)

    sums = ZScatter(send, part, relay, got, right, left)
    out_rows(3, 1)
    sums.far()
    out_rows(1, 2)
    sums.near()
    out_rows(0, 1)
    gf.step4()
    sums.pass_on()
    gf.step5()
    attn = sums.total()
    attn_ref[...] = attn
    flush(attn_ref, attn_out)
    unit_two, _ = normalize(attn)
    live = live_ref[...][:, :1]
    middle = resid_ref[...].astype(F32) + live * jnp.tanh(mod_ref[1:2, :]) * unit_two * gains_ref[1:2, :]
    mid_ref[...] = middle
    flush(mid_ref, mid_out)
    unit_three, _ = normalize(middle)
    second_ref[...] = (unit_three * gains_ref[2:3, :] * (1.0 + mod_ref[2:3, :])).astype(BF16)
    flush(second_ref, second_out)
    cot_swap.wait_recv()
    gf.finish()
    send.drain()
    for copy in flushes:
        copy.wait()


def attention_call(args, cid):
    S = jax.ShapeDtypeStruct
    vm = pl.BlockSpec(memory_space=VMEM)
    any_ = pl.BlockSpec(memory_space=pl.ANY)
    pair = (3, 4, 128, 128)
    saved = [
        ((2, 2, 4, 2, 96, 768), BF16),
        ((4096, 256), BF16),
        ((D, 512), BF16),
        (pair, BF16),
        (pair, BF16),
        (pair, BF16),
        (pair, F32),
        (pair, F32),
        ((3, 256, 128), F32),
        (pair, F32),
        ((4, 128, 128), F32),
        ((2, 4, 128, 256), BF16),
        ((4, 128, 128), F32),
        ((4, 128, 128), F32),
        ((128, D), BF16),
        ((3, 256, 128), BF16),
        ((3, 256, 128), BF16),
        ((128, D), F32),
        ((128, D), F32),
        ((128, D), BF16),
    ]
    outs = [
        ((8, D), F32),
        ((8, D), F32),
        ((16, 8, 128), F32),
        ((128, 128), F32),
        ((16, 128), F32),
    ]
    return pl.pallas_call(
        attention_kernel,
        out_shape=[S((2, 2, 4, 2, 96, D), BF16)]
        + [S(*o) for o in saved]
        + [S((2, 64, D), BF16)]
        + [S(*o) for o in outs],
        in_specs=[any_] * 3 + [vm] * 15,
        out_specs=[any_] * (2 + len(saved)) + [vm] * len(outs),
        scratch_shapes=[VMEM(*o) for o in saved]
        + [
            VMEM((4, 128, D), BF16),
            VMEM(pair, F32),
            VMEM((96, 768), BF16),
            VMEM((96, D), BF16),
            VMEM((256, 384), BF16),
            VMEM((2, 2, 4, 2, 256, 384), BF16),
            VMEM((256, 4096), BF16),
            VMEM((4, 2, 64, D), BF16),
            VMEM((2, 64, D), BF16),
            VMEM((16, 8, 128), F32),
            VMEM((16, 16, 128), F32),
            VMEM((16, 16, 128), F32),
            VMEM((8, 16, 128), F32),
            VMEM((2, 2, 512, 128), F32),
            VMEM((4, 128, D), BF16),
            VMEM((2, 64, D), BF16),
            VMEM((2, 128, D), BF16),
            pltpu.SemaphoreType.DMA((28,)),
        ]
        + dma_sems(160),
        compiler_params=pltpu.CompilerParams(
            collective_id=cid, has_side_effects=True, vmem_limit_bytes=58 * 2**20
        ),
        name="attention",
    )(*args)


def ffn_kernel(
    x_ref,
    w_hbm,
    mid_in,
    attn_in,
    cot_in,
    mod_ref,
    gain_ref,
    live_ref,
    out_out,
    gmid_out,
    gattn_out,
    dw_half,
    sums_ref,
    mid_ref,
    attn_ref,
    cot_ref,
    out_ref,
    gmid_ref,
    gattn_ref,
    w,
    dw_ref,
    dw_got,
    x_all,
    g_all,
    act,
    dgate,
    dup,
    gpre,
    part1,
    part2,
    relay1,
    relay2,
    got1,
    got2,
    flip,
    flip_g,
    own_g,
    w_sem,
    out_sems,
    ss,
    rs,
):
    z, right, left = z_ring()
    load = pltpu.make_async_copy(w_hbm, w, w_sem)
    load.start()
    loads = []
    for src, dst in ((x_ref, x_all.at[0]), (mid_in, mid_ref), (attn_in, attn_ref), (cot_in, cot_ref)):
        copy = pltpu.make_async_copy(src, dst, out_sems.at[4 + len(loads)])
        copy.start()
        loads.append(copy)
    stores = []

    def store(src, dst):
        copy = pltpu.make_async_copy(src, dst, out_sems.at[8 + len(stores)])
        copy.start()
        stores.append(copy)

    xh, xl, y, _, c = coords()
    sibling = device_of(2 * xh + xl, y, z, 1 - c)
    greet([right, left, sibling])
    send = Sender(ss, rs)
    one = ZGather(send, x_ref, x_all, right, left)
    for copy in loads:
        copy.wait()
    load.wait()

    def pre(lo, count):
        rows = count * 128
        x = x_all[lo : lo + count].reshape(rows, D)
        for xx in range(2):

            def column(j, carry, xx=xx):
                g = mm(x, w[xx, :, tile(j)])
                u = mm(x, w[xx, :, tile(j + 2)])
                s = jax.nn.sigmoid(g)
                gs = g * s
                act[xx, lo : lo + count, :, tile(j)] = (gs * u).astype(BF16).reshape(count, 128, 256)
                dgate[xx, lo : lo + count, :, tile(j)] = (u * s * (1.0 + g * (1.0 - s))).reshape(count, 128, 256)
                dup[xx, lo : lo + count, :, tile(j)] = gs.reshape(count, 128, 256)
                return carry

            lax.fori_loop(0, 2, column, 0)

    def down(lo, count):
        rows = count * 128
        a0 = act[0, lo : lo + count].reshape(rows, 512)
        a1 = act[1, lo : lo + count].reshape(rows, 512)

        def column(j, carry):
            cols = tile(j)
            total = mm_t(a0, w[0, cols, 1024:1536]) + mm_t(a1, w[1, cols, 1024:1536])
            part1[lo : lo + count, :, cols] = total.astype(BF16).reshape(count, 128, 256)
            return carry

        lax.fori_loop(0, D // 256, column, 0)

    sum1 = ZScatter(send, part1, relay1, got1, right, left)
    pre(0, 1)
    one.near()
    pre(1, 2)
    down(1, 2)
    sum1.near()
    one.far()
    pre(3, 1)
    down(3, 1)
    sum1.far()
    down(0, 1)
    transpose_into(x_all, flip)
    sum1.pass_on()
    ffn_total = sum1.total()

    live = live_ref[...][:, :1]
    mod = mod_ref[...]
    gains = gain_ref[...]
    gate_f = jnp.tanh(mod[3:4])
    middle = mid_ref[...]
    unit_four, inverse_four = normalize(ffn_total)
    out_ref[...] = (middle + live * gate_f * unit_four * gains[3:4]).astype(BF16)
    store(out_ref, out_out)
    grad_top = cot_ref[...].astype(F32)
    weighted = grad_top * live
    part_four = jnp.sum(weighted * unit_four, axis=0, keepdims=True)
    own_g[...] = norm_back(unit_four, inverse_four, weighted * gate_f * gains[3:4]).astype(BF16)
    two = ZGather(send, own_g, g_all, right, left)
    g_all[0] = own_g[...]
    sums_ref[3:4, :] = part_four * gains[3:4] * (1.0 - gate_f * gate_f)
    sums_ref[7:8, :] = part_four * gate_f

    def back(lo, count):
        rows = count * 128
        g = g_all[lo : lo + count].reshape(rows, D)
        for xx in range(2):

            def column(j, carry, xx=xx):
                ga = mm(g, w[xx, :, tile(j + 4)])
                dg = dgate[xx, lo : lo + count, :, tile(j)].reshape(rows, 256)
                du = dup[xx, lo : lo + count, :, tile(j)].reshape(rows, 256)
                gpre[xx, lo : lo + count, :, tile(j)] = (ga * dg).astype(BF16).reshape(count, 128, 256)
                gpre[xx, lo : lo + count, :, tile(j + 2)] = (ga * du).astype(BF16).reshape(count, 128, 256)
                return carry

            lax.fori_loop(0, 2, column, 0)

    def back_in(lo, count):
        rows = count * 128
        a0 = gpre[0, lo : lo + count].reshape(rows, 1024)
        a1 = gpre[1, lo : lo + count].reshape(rows, 1024)

        def column(j, carry):
            cols = tile(j)
            total = mm_t(a0, w[0, cols, 0:1024]) + mm_t(a1, w[1, cols, 0:1024])
            part2[lo : lo + count, :, cols] = total.astype(BF16).reshape(count, 128, 256)
            return carry

        lax.fori_loop(0, D // 256, column, 0)

    def weight_grad(xx):
        def column(j, carry):
            b = gpre[xx, :, :, tile(j)].reshape(512, 256)
            for xb in range(2):
                grad = mm(flip[xb * 768 : xb * 768 + 768, :], b)
                dw_ref[xx, xb, :, :, :, tile(j)] = grad.astype(BF16).reshape(4, 2, 96, 256)
            return carry

        lax.fori_loop(0, 4, column, 0)

        def down_column(j, carry):
            b = act[xx, :, :, tile(j)].reshape(512, 256)
            for xb in range(2):
                grad = mm(flip_g[xb * 768 : xb * 768 + 768, :], b)
                dw_ref[xx, xb, :, :, :, tile(j + 4)] = grad.astype(BF16).reshape(4, 2, 96, 256)
            return carry

        lax.fori_loop(0, 2, down_column, 0)
        return [
            send(dw_ref.at[xx, xb, :, 1 - c], dw_got.at[xx, xb], sibling) for xb in range(2)
        ]

    def add_sibling(xx, copies):
        for xb in range(2):
            copies[xb].wait_recv()

            def add(j, carry, xb=xb):
                dw_got[xx, xb, j] = add_low(dw_got[xx, xb, j], dw_ref[xx, xb, j, c])
                return carry

            lax.fori_loop(0, 4, add, 0)
            store(dw_got.at[xx, xb], dw_half.at[xx, xb])

    sum2 = ZScatter(send, part2, relay2, got2, right, left)
    back(0, 1)
    two.near()
    back(1, 2)
    back_in(1, 2)
    sum2.near()
    two.far()
    back(3, 1)
    back_in(3, 1)
    sum2.far()
    back_in(0, 1)
    transpose_into(g_all, flip_g)
    to_sibling0 = weight_grad(0)
    sum2.pass_on()
    to_sibling1 = weight_grad(1)
    add_sibling(0, to_sibling0)
    grad_second = sum2.total()

    scale_f = mod[2:3]
    unit_three, inverse_three = normalize(middle)
    sum_three = jnp.sum(grad_second * unit_three, axis=0, keepdims=True)
    sums_ref[2:3, :] = sum_three * gains[2:3]
    sums_ref[6:7, :] = sum_three * (1.0 + scale_f)
    grad_middle = grad_top + norm_back(
        unit_three, inverse_three, grad_second * (1.0 + scale_f) * gains[2:3]
    )
    gmid_ref[...] = grad_middle
    store(gmid_ref, gmid_out)
    gate_a = jnp.tanh(mod[1:2])
    unit_two, inverse_two = normalize(attn_ref[...])
    weighted_mid = grad_middle * live
    sum_two = jnp.sum(weighted_mid * unit_two, axis=0, keepdims=True)
    sums_ref[1:2, :] = sum_two * gains[1:2] * (1.0 - gate_a * gate_a)
    sums_ref[5:6, :] = sum_two * gate_a
    sums_ref[0:1, :] = jnp.zeros((1, D), F32)
    sums_ref[4:5, :] = jnp.zeros((1, D), F32)
    gattn_ref[...] = norm_back(unit_two, inverse_two, weighted_mid * gate_a * gains[1:2]).astype(BF16)
    store(gattn_ref, gattn_out)
    add_sibling(1, to_sibling1)
    send.drain()
    for copy in stores:
        copy.wait()


def ffn_call(second_in, w_f, middle, attn, cot, mod_rows, gains, live, cid):
    S = jax.ShapeDtypeStruct
    vm = pl.BlockSpec(memory_space=VMEM)
    any_ = pl.BlockSpec(memory_space=pl.ANY)
    return pl.pallas_call(
        ffn_kernel,
        out_shape=[
            S((128, D), BF16),
            S((128, D), F32),
            S((128, D), BF16),
            S((2, 2, 4, 96, D), BF16),
            S((8, D), F32),
        ],
        in_specs=[any_] * 5 + [vm] * 3,
        out_specs=[any_] * 4 + [vm],
        scratch_shapes=[
            VMEM((128, D), F32),
            VMEM((128, D), F32),
            VMEM((128, D), BF16),
            VMEM((128, D), BF16),
            VMEM((128, D), F32),
            VMEM((128, D), BF16),
            VMEM((2, D, D), BF16),
            VMEM((2, 2, 4, 2, 96, D), BF16),
            VMEM((2, 2, 4, 96, D), BF16),
            VMEM((4, 128, D), BF16),
            VMEM((4, 128, D), BF16),
            VMEM((2, 4, 128, 512), BF16),
            VMEM((2, 4, 128, 512), F32),
            VMEM((2, 4, 128, 512), F32),
            VMEM((2, 4, 128, 1024), BF16),
            VMEM((4, 128, D), BF16),
            VMEM((4, 128, D), BF16),
            VMEM((2, 64, D), BF16),
            VMEM((2, 64, D), BF16),
            VMEM((2, 128, D), BF16),
            VMEM((2, 128, D), BF16),
            VMEM((D, 512), BF16),
            VMEM((D, 512), BF16),
            VMEM((128, D), BF16),
            pltpu.SemaphoreType.DMA,
            pltpu.SemaphoreType.DMA((16,)),
        ]
        + dma_sems(40),
        compiler_params=pltpu.CompilerParams(
            collective_id=cid, has_side_effects=True, vmem_limit_bytes=56 * 2**20
        ),
        name="ffn",
    )(second_in, w_f, middle, attn, cot, mod_rows, gains, live)


def pick(array, index):
    return lax.dynamic_index_in_dim(array, index, 0, keepdims=False)


def dot(spec, a, b):
    return jnp.einsum(spec, a, b, preferred_element_type=F32)


class PlaneScatter:
    def __init__(self, send, grads, own, bufs):
        self.send, self.grads, self.own = send, grads, own
        self.sib, self.ra, self.rb, self.ga, self.gb, self.qa, self.qb = bufs
        rows, cols = self.sib.shape[3:]
        self.rows, self.cols = rows, cols
        self.half = half = rows // 2
        self.top, self.low = pl.ds(0, half), pl.ds(half, half)
        if rows == 96:
            self.q0 = (slice(None), pl.ds(0, cols // 2))
            self.q1 = (slice(None), pl.ds(cols // 2, cols // 2))
        else:
            q = half // 2
            self.q0, self.q1 = (pl.ds(0, q),), (pl.ds(q, q),)

    def setup(self):
        self.where = plane_peers()
        self.go_xr, self.go_xq, self.go_yr, self.go_yq, self.sibling = self.where[7]
        self.parts = {}

    def to_sibling(self, k):
        block = self.grads.at[k % 2, k // 2]
        if self.own is None:
            block = self.grads.at[k % 2, k // 2, :, 1 - self.where[2]]
        self.parts[k] = self.send(block, self.sib.at[k % 2, k // 2], self.sibling)

    def add(self):
        c, sib, own, grads = self.where[2], self.sib, self.own, self.grads
        for k in self.parts:
            self.parts[k].wait_recv()

            def add_sibling(j, carry, k=k):
                if own is None:
                    mine = grads[k % 2, k // 2, j, c]
                else:
                    mine = own(k % 2, k // 2, j)
                sib[k % 2, k // 2, j] = add_low(sib[k % 2, k // 2, j], mine)
                return carry

            lax.fori_loop(0, 4, add_sibling, 0)

    def first(self):
        x, y, c, xr, xq, yr, yq, _ = self.where
        sib, send = self.sib, self.send
        xo, yo = (x + 2) % 4, (y + 2) % 4
        self.t1 = send(sib.at[0, :, yo, self.top], self.ra.at[pl.ds(0, 2)], self.go_yr)
        self.t2 = send(sib.at[1, :, yo, self.top], self.ra.at[pl.ds(2, 2)], self.go_yq)
        self.l1 = send(sib.at[xo % 2, xo // 2, pl.ds(0, 2), self.low], self.rb.at[pl.ds(0, 2)], self.go_xr)
        self.l2 = send(sib.at[xo % 2, xo // 2, pl.ds(2, 2), self.low], self.rb.at[pl.ds(2, 2)], self.go_xq)

    def step2(self):
        x, y, c, xr, xq, yr, yq, _ = self.where
        sib, send, top, low = self.sib, self.send, self.top, self.low
        ra, rb = self.ra, self.rb
        self.t1.wait_recv()
        for j in range(2):
            sib[0, j, yr, top] = add_low(sib[0, j, yr, top], ra[j])
        self.t3 = send(sib.at[:, :, yr, top], self.ga.at[0], self.go_yr)
        self.t2.wait_recv()
        for j in range(2):
            sib[1, j, yq, top] = add_low(sib[1, j, yq, top], ra[2 + j])
        self.t4 = send(sib.at[:, :, yq, top], self.ga.at[1], self.go_yq)
        self.l1.wait_recv()
        for j in range(2):
            sib[xr % 2, xr // 2, j, low] = add_low(sib[xr % 2, xr // 2, j, low], rb[j])
        self.l3 = send(sib.at[xr % 2, xr // 2, :, low], self.gb.at[0], self.go_xr)
        self.l2.wait_recv()
        for j in range(2):
            sib[xq % 2, xq // 2, 2 + j, low] = add_low(sib[xq % 2, xq // 2, 2 + j, low], rb[2 + j])
        self.l4 = send(sib.at[xq % 2, xq // 2, :, low], self.gb.at[1], self.go_xq)

    def step3(self):
        x, y, c, xr, xq, yr, yq, _ = self.where
        sib, send, ga, gb, pa, pb = self.sib, self.send, self.ga, self.gb, self.ra, self.rb
        xo, yo = (x + 2) % 4, (y + 2) % 4
        self.t3.wait_recv()
        self.t4.wait_recv()
        for i in range(2):
            for j in range(2):
                total = sib[i, j, y, self.top].astype(F32) + ga[0, i, j].astype(F32)
                pa[2 * j + i] = (total + ga[1, i, j].astype(F32)).astype(BF16)
        self.e1 = send(pa.at[(xo,) + self.q0], self.qa.at[0], self.go_xr)
        self.e2 = send(pa.at[(xo,) + self.q1], self.qa.at[1], self.go_xq)
        self.l3.wait_recv()
        self.l4.wait_recv()
        for j in range(4):
            total = sib[x % 2, x // 2, j, self.low].astype(F32) + gb[0, j].astype(F32)
            pb[j] = (total + gb[1, j].astype(F32)).astype(BF16)
        self.m1 = send(pb.at[(yo,) + self.q0], self.qb.at[0], self.go_yr)
        self.m2 = send(pb.at[(yo,) + self.q1], self.qb.at[1], self.go_yq)

    def step4(self):
        x, y, c, xr, xq, yr, yq, _ = self.where
        send, ga, gb, pa, pb, q0, q1 = self.send, self.ga, self.gb, self.ra, self.rb, self.q0, self.q1
        self.e1.wait_recv()
        pa[(xr,) + q0] = add_low(pa[(xr,) + q0], self.qa[0])
        self.e2.wait_recv()
        pa[(xq,) + q1] = add_low(pa[(xq,) + q1], self.qa[1])
        self.e3 = send(pa.at[xr], ga.at[0, 0, 0], self.go_xr)
        self.e4 = send(pa.at[xq], ga.at[1, 0, 0], self.go_xq)
        self.m1.wait_recv()
        pb[(yr,) + q0] = add_low(pb[(yr,) + q0], self.qb[0])
        self.m2.wait_recv()
        pb[(yq,) + q1] = add_low(pb[(yq,) + q1], self.qb[1])
        self.m3 = send(pb.at[yr], gb.at[0, 0], self.go_yr)
        self.m4 = send(pb.at[yq], gb.at[1, 0], self.go_yq)

    def finish(self):
        x, y = self.where[:2]
        ga, gb, pa, pb = self.ga, self.gb, self.ra, self.rb
        self.e3.wait_recv()
        self.e4.wait_recv()
        top = pa[x].astype(F32) + ga[0, 0, 0].astype(F32) + ga[1, 0, 0].astype(F32)
        self.m3.wait_recv()
        self.m4.wait_recv()
        low = pb[y].astype(F32) + gb[0, 0].astype(F32) + gb[1, 0].astype(F32)
        return top, low


def scatter_bufs(rows, cols):
    half = rows // 2
    quarter = (half, cols // 2) if rows == 96 else (half // 2, cols)
    return [
        VMEM((2, 2, 4, rows, cols), BF16),
        VMEM((4, half, cols), BF16),
        VMEM((4, half, cols), BF16),
        VMEM((2, 2, 2, half, cols), BF16),
        VMEM((2, 4, half, cols), BF16),
        VMEM((2,) + quarter, BF16),
        VMEM((2,) + quarter, BF16),
    ]


def mm_rows(a, b):
    return lax.dot_general(a, b, (((0,), (0,)), ((), ())), preferred_element_type=F32)


def back_kernel(
    sib_in,
    w_a_in,
    cap_flip_in,
    first_flip_in,
    q8_in,
    kk_in,
    vv_in,
    qr_in,
    kr_in,
    tkr_in,
    other_in,
    lse_in,
    cw_in,
    cos_in,
    sin_in,
    resid_in,
    tk_in,
    tv_in,
    gmid_in,
    gattn_in,
    out_ref,
    mod_ref,
    gains_ref,
    sums_ref,
    facts,
    d_final,
    f_final,
    c_final,
    layer_final,
    hidden_final,
    g_all,
    gain_out,
    bias_all,
    sib_f,
    w_a,
    cap_flip,
    first_flip,
    q8,
    kk,
    vv,
    qr,
    kr,
    tkr,
    other_ref,
    lse_ref,
    cw,
    cos_ref,
    sin_ref,
    resid_ref,
    tk,
    tv,
    gmid_ref,
    d_out,
    f_out,
    c_out,
    flip,
    grad_all,
    gc,
    gq,
    gk,
    gv,
    gtk,
    gtv,
    gpack,
    tpack,
    dw_a,
    dw_c,
    part,
    relay,
    got,
    hid_grad,
    mod_msg,
    gain_msg,
    got_mod,
    got_gain,
    gain_sum,
    sf1, sf2, sf3, sf4, sf5, sf6,
    sa0, sa1, sa2, sa3, sa4, sa5, sa6,
    sc0, sc1, sc2, sc3, sc4, sc5, sc6,
    local_sems,
    ss,
    rs,
):
    dp = lax.axis_index("dp")
    t = lax.axis_index("tensor")
    xh, xl, y, z, c = coords()
    _, right, left = z_ring()
    pair = device_of(2 * xh + 1 - xl, y, z, c)
    dp_peers = [((dp + k) % 16, t) for k in range(1, 16)]
    t_peers = [(dp, (t + k) % 8) for k in range(1, 8)]
    outer_x = device_of((2 * xh + xl + 3 - 2 * xl) % 4, y, z, c)
    everyone = dp_peers + t_peers + [outer_x]
    greet_signal(everyone)
    loads = []
    for src, dst in (
        (sib_in, sib_f),
        (w_a_in, w_a),
        (q8_in, q8),
        (gattn_in, grad_all.at[0]),
        (tk_in, tk),
        (tv_in, tv),
        (kk_in, kk),
        (vv_in, vv),
        (lse_in, lse_ref),
        (tkr_in, tkr),
        (cap_flip_in, cap_flip),
        (cw_in, cw),
        (qr_in, qr),
        (kr_in, kr),
        (cos_in, cos_ref),
        (sin_in, sin_ref),
        (other_in, other_ref),
        (first_flip_in, first_flip),
        (resid_in, resid_ref),
        (gmid_in, gmid_ref),
    ):
        copy = pltpu.make_async_copy(src, dst, local_sems.at[len(loads)])
        copy.start()
        loads.append(copy)
    greet_wait(everyone)
    send = Sender(ss, rs)
    tokens = ZGather(send, gattn_in, grad_all, right, left)

    def caption_own(xx, xb, yb):
        return mm(cap_flip[tile(2 * (4 * xb + yb) + c)], tpack[xx])

    scat_f = PlaneScatter(send, None, None, (sib_f, sf1, sf2, sf3, sf4, sf5, sf6))
    scat_a = PlaneScatter(send, dw_a, None, (sa0, sa1, sa2, sa3, sa4, sa5, sa6))
    scat_c = PlaneScatter(send, dw_c, caption_own, (sc0, sc1, sc2, sc3, sc4, sc5, sc6))
    for scatter in (scat_f, scat_a, scat_c):
        scatter.setup()
    loads[0].wait()
    scat_f.first()
    stores = []

    def store(src, dst):
        copy = pltpu.make_async_copy(src, dst, local_sems.at[len(loads) + len(stores)])
        copy.start()
        stores.append(copy)

    store(out_ref.at[xl], layer_final.at[xl])
    self_bias = key_bias(512, z, facts[LENGTH_ROW : LENGTH_ROW + 1, :])
    text_bias = key_bias(256, z, facts[TEXT_ROW : TEXT_ROW + 1, :])
    block = head_block()
    low_row = lanes((1, 128)) < 64
    gtk[...] = jnp.zeros((3, 256, 128), F32)
    gtv[...] = jnp.zeros((3, 256, 128), F32)
    gk[...] = jnp.zeros((3, 512, 128), F32)
    gv[...] = jnp.zeros((3, 512, 128), F32)
    for copy in loads[1:4]:
        copy.wait()

    def head_grads(lo, count):
        n = count * 128
        g = grad_all[lo : lo + count].reshape(n, D)
        low_lane = lanes((n, 128)) < 64
        tiles = []
        for xx in range(2):
            w_cols = w_a[xx, :, :, :, :, 512:768].reshape(D, 256)
            o = mm(g, w_cols)
            gc[xx, lo : lo + count] = o[:, 128:].astype(BF16).reshape(count, 128, 128)
            tiles.append(o[:, :128])
        both = jnp.where(low_lane, pltpu.roll(tiles[0], 64, 1), tiles[1])
        gc[2, lo : lo + count] = both.astype(BF16).reshape(count, 128, 128)

    head_grads(0, 1)
    tokens.near()
    head_grads(1, 2)
    scat_f.step2()
    tokens.far()
    head_grads(3, 1)
    for copy in loads[4:]:
        copy.wait()

    def back_rows(p, text, b):
        slots = pl.ds(b * 2, 2)
        rows = tile(b, 256)
        q = q8[p, slots].reshape(256, 128)
        g = gc[p, slots].reshape(256, 128)
        if text:
            g = (g.astype(F32) * facts[GATE_ROW + p : GATE_ROW + p + 1, :]).astype(BF16)
        k = tk[p] if text else kk[p].reshape(512, 128)
        v = tv[p] if text else vv[p].reshape(512, 128)
        low_rows = lanes((256, 128)) < 64
        grad_q = jnp.zeros((256, 128), F32)
        for head in range(2):
            keep = low_rows if head == 0 else jnp.logical_not(low_rows)
            qm = jnp.where(keep, q, jnp.zeros_like(q))
            gm = jnp.where(keep, g, jnp.zeros_like(g))
            lane = p * 2 + head + 8 * text
            lse = lse_ref[slots, :, lane : lane + 1].reshape(256, 1)
            scores = mm_t(qm, k) + (text_bias if text else self_bias)
            probs = jnp.exp(scores - lse)
            grad_probs = mm_t(gm, v)
            delta = jnp.sum(probs * grad_probs, axis=-1, keepdims=True)
            grad_scores = (probs * (grad_probs - delta)).astype(BF16)
            grad_q = grad_q + jnp.where(keep, mm(grad_scores, k), 0.0)
            to_v, to_k = (gtv, gtk) if text else (gv, gk)
            to_v[p] += mm_rows(probs.astype(BF16), gm)
            to_k[p] += mm_rows(grad_scores, qm)
        if text:
            gq[p, rows] = grad_q
        else:
            gq[p, rows] += grad_q

    def over_rows(p, text):
        def step(b, carry):
            back_rows(p, text, b)
            return carry

        lax.fori_loop(0, 2, step, 0)

    def unit_of(raw):
        inverse = lax.rsqrt(head_mean(raw * raw, block) + EPSILON)
        return raw * inverse, inverse

    def back_head(unit, inverse, grad):
        return inverse * (grad - unit * head_mean(grad * unit, block))

    for p in range(3):
        over_rows(p, True)
    low_text = lanes((256, 128)) < 64
    text_row = jnp.zeros((1, 128), F32)
    grads_k = []
    for p in range(3):
        unit, inverse = unit_of(tkr[p])
        gtk_p = gtk[p]
        text_row = text_row + jnp.sum(gtk_p * unit, axis=0, keepdims=True)
        grads_k.append(back_head(unit, inverse, gtk_p * facts[GAIN_ROW + 2 : GAIN_ROW + 3, :]))
    for xx in range(2):
        tpack[xx, :, 0:128] = grads_k[xx].astype(BF16)
        tpack[xx, :, 256:384] = gtv[xx].astype(BF16)
    tpack[0, :, 128:256] = jnp.where(low_text, grads_k[2], pltpu.roll(gtv[2], 64, 1)).astype(BF16)
    tpack[1, :, 128:256] = jnp.where(low_text, pltpu.roll(grads_k[2], 64, 1), gtv[2]).astype(BF16)

    def caption_grad(i, carry):
        xx = i // 8
        j = i % 8
        grad = mm(cap_flip[tile(2 * j + 1 - c)], tpack[xx])
        dw_c[xx, j // 4, j % 4] = grad.astype(BF16)
        return carry

    lax.fori_loop(0, 8, caption_grad, 0)
    scat_c.to_sibling(0)
    scat_c.to_sibling(2)
    lax.fori_loop(8, 16, caption_grad, 0)
    scat_c.to_sibling(1)
    scat_c.to_sibling(3)
    scat_f.step3()
    transpose_into(grad_all, flip)
    for xx in range(2):
        b = cw[xx].reshape(512, 256)
        for xb in range(2):
            grad = mm(flip[xb * 768 : xb * 768 + 768], b)
            dw_a[xx, xb, :, :, :, 512:768] = grad.astype(BF16).reshape(4, 2, 96, 256)
    scat_c.add()
    scat_c.first()
    scat_f.step4()

    over_rows(0, False)
    scat_c.step2()
    over_rows(1, False)
    over_rows(2, False)
    out_swap = send(out_ref.at[1 - xl], layer_final.at[xl], pair)
    top, low = scat_f.finish()
    f_out[0:48, :] = top
    f_out[48:96, :] = low
    store(f_out, f_final)

    cos = cos_ref[...].reshape(512, 128)
    sin = sin_ref[...].reshape(512, 128)
    low_head = lanes((512, 128)) < 64
    query_row = jnp.zeros((1, 128), F32)
    key_row = jnp.zeros((1, 128), F32)
    raws = [[], []]
    for p in range(3):
        for i in range(2):
            grad = (gq[p] * 0.125) if i == 0 else gk[p]
            raw = (qr if i == 0 else kr)[p].reshape(512, 128)
            turned = grad * cos - swap_quarters(grad) * sin
            unit, inverse = unit_of(raw)
            row = jnp.sum(turned * unit, axis=0, keepdims=True)
            if i == 0:
                query_row = query_row + row
            else:
                key_row = key_row + row
            result = back_head(unit, inverse, turned * facts[GAIN_ROW + i : GAIN_ROW + i + 1, :])
            if p < 2:
                gpack[p, :, (0 if i == 0 else 256) : (128 if i == 0 else 384)] = result.astype(BF16)
            else:
                raws[i] = result
    gpack[0, :, 128:256] = jnp.where(low_head, raws[0], pltpu.roll(raws[1], 64, 1)).astype(BF16)
    gpack[1, :, 128:256] = jnp.where(low_head, pltpu.roll(raws[0], 64, 1), raws[1]).astype(BF16)
    for xx in range(2):
        gpack[xx, :, 384:512] = gv[xx].astype(BF16)
    gpack[0, :, 512:640] = jnp.where(low_head, gv[2], 0.0).astype(BF16)
    gpack[1, :, 512:640] = jnp.where(low_head, pltpu.roll(gv[2], 64, 1), 0.0).astype(BF16)

    def first_rows(lo, count):
        n = count * 128
        a0 = gpack[0, lo * 128 : lo * 128 + n]
        a1 = gpack[1, lo * 128 : lo * 128 + n]
        for xb in range(2):
            cols = slice(xb * 768, xb * 768 + 768)
            b0 = w_a[0, xb, :, :, :, 0:640].reshape(768, 640)
            b1 = w_a[1, xb, :, :, :, 0:640].reshape(768, 640)
            total = mm_t(a0, b0) + mm_t(a1, b1)
            part[lo : lo + count, :, cols] = total.astype(BF16).reshape(count, 128, 768)

    sums = ZScatter(send, part, relay, got, right, left)
    first_rows(3, 1)
    sums.far()
    first_rows(1, 2)
    sums.near()
    for xx in range(2):
        for xb in range(2):
            a = first_flip[xb * 768 : xb * 768 + 768]
            grad = mm(a, gpack[xx, :, 0:512])
            dw_a[xx, xb, :, :, :, 0:512] = grad.astype(BF16).reshape(4, 2, 96, 512)
            last = (xx, xb, slice(None), slice(None), slice(None), slice(512, 640))
            old = dw_a[last].reshape(768, 128).astype(F32)
            grad = mm(a, gpack[xx, :, 512:640]) + old
            dw_a[last] = grad.astype(BF16).reshape(4, 2, 96, 128)
            scat_a.to_sibling(xx + 2 * xb)
        if xx == 0:
            sums.pass_on()
    first_rows(0, 1)
    scat_c.step3()
    scat_a.add()
    scat_a.first()
    grad_first = sums.total()

    unit_one, inverse_one = normalize(resid_ref[...].astype(F32))
    scale = 1.0 + mod_ref[0:1, :]
    gain = gains_ref[0:1, :]
    row_sum = jnp.sum(grad_first * unit_one, axis=0, keepdims=True)
    sums_0 = row_sum * gain
    sums_4 = row_sum * scale
    hid_grad[...] = (
        (gmid_ref[...] + norm_back(unit_one, inverse_one, grad_first * scale * gain))
        .astype(BF16)
        .reshape(2, 64, D)
    )
    grad_swap = send(hid_grad.at[1 - xl], hidden_final.at[xl], pair)
    store(hid_grad.at[xl], hidden_final.at[xl])
    mod_msg[...] = jnp.zeros((8, 8, 128), F32)
    gain_msg[...] = jnp.zeros((16, 8, 128), F32)
    for i in range(4):
        row = sums_0 if i == 0 else sums_ref[i : i + 1, :]
        for h in range(2):
            for j in range(6):
                lo = h * 768 + j * 128
                mod_msg[2 * i + h, j : j + 1, :] = row[:, lo : lo + 128]
    folded = [row + pltpu.roll(row, 64, 1) for row in (query_row, key_row, text_row)]
    first_line = jnp.where(low_row, folded[0], folded[1])
    lane = lanes((1, 128))
    second_line = jnp.where(low_row, folded[2], 0.0)
    for p in range(3):
        gate_row = facts[GATE_ROW + p : GATE_ROW + p + 1, :]
        products = gc[p].reshape(512, 128).astype(F32) * other_ref[p].reshape(512, 128)
        values = jnp.sum(products, axis=0, keepdims=True) * (1.0 - gate_row * gate_row)
        for head in range(2):
            keep = low_row if head == 0 else jnp.logical_not(low_row)
            value = jnp.sum(jnp.where(keep, values, 0.0), axis=1, keepdims=True)
            index = (0, 1, 3, 4, 2, 5)[2 * p + head]
            second_line = second_line + jnp.where(lane == 64 + z * 6 + index, value, 0.0)
    gain_rows = jnp.concatenate([sums_4, sums_ref[5:8, :]], axis=0)
    for d in range(16):
        gain_msg[d, 0:4, 0:96] = gain_rows[:, d * 96 : (d + 1) * 96]
        gain_msg[d, 4:5, :] = first_line
        gain_msg[d, 5:6, :] = second_line
    to_t = [send(mod_msg.at[q[1]], got_mod.at[t], q) for q in t_peers]
    to_dp = [send(gain_msg.at[q[0]], got_gain.at[dp], q) for q in dp_peers]
    got_mod[t] = mod_msg[t]
    got_gain[dp] = gain_msg[dp]
    scat_a.step2()
    scat_c.step4()
    for copy in to_t:
        copy.wait_recv()
    g_all[dp, 0] = got_mod[0] + got_mod[2] + got_mod[4] + got_mod[6]
    g_all[dp, 1] = got_mod[1] + got_mod[3] + got_mod[5] + got_mod[7]
    to_all = [send(g_all.at[dp], g_all.at[dp], q) for q in dp_peers]
    for copy in to_dp:
        copy.wait_recv()
    gain_sum[t] = jnp.sum(got_gain[...], axis=0)
    to_rest = [send(gain_sum.at[t], gain_sum.at[t], q) for q in t_peers]
    for copy in to_all:
        copy.wait_recv()
    bias_all[t] = jnp.sum(g_all[...], axis=(0, 1))
    to_bias = [send(bias_all.at[t], bias_all.at[t], q) for q in t_peers]
    scat_a.step3()
    top, low = scat_c.finish()
    c_out[0:128, :] = top
    c_out[128:256, :] = low
    store(c_out, c_final)
    for copy in to_rest:
        copy.wait_recv()
    gain_out[...] = jnp.sum(gain_sum[...], axis=0)
    for copy in to_bias:
        copy.wait_recv()
    scat_a.step4()
    out_swap.wait_recv()
    grad_swap.wait_recv()
    top, low = scat_a.finish()
    d_out[0:48, :] = top
    d_out[48:96, :] = low
    store(d_out, d_final)
    send.drain()
    for copy in stores:
        copy.wait()


def back_call(args, cid):
    S = jax.ShapeDtypeStruct
    vm = pl.BlockSpec(memory_space=VMEM)
    any_ = pl.BlockSpec(memory_space=pl.ANY)
    loaded = args[:19]
    outs = [
        S((96, 768), F32),
        S((96, D), F32),
        S((256, 384), F32),
        S((2, 64, D), BF16),
        S((2, 64, D), BF16),
        S((16, 2, 8, 128), F32),
        S((8, 128), F32),
        S((8, 8, 128), F32),
    ]
    return pl.pallas_call(
        back_kernel,
        out_shape=outs,
        in_specs=[any_] * 21 + [vm] * 4,
        out_specs=[any_] * 5 + [vm] * 3,
        scratch_shapes=[VMEM(a.shape, a.dtype) for a in loaded]
        + [
            VMEM((96, 768), F32),
            VMEM((96, D), F32),
            VMEM((256, 384), F32),
            VMEM((D, 512), BF16),
            VMEM((4, 128, D), BF16),
            VMEM((3, 4, 128, 128), BF16),
            VMEM((3, 512, 128), F32),
            VMEM((3, 512, 128), F32),
            VMEM((3, 512, 128), F32),
            VMEM((3, 256, 128), F32),
            VMEM((3, 256, 128), F32),
            VMEM((2, 512, 640), BF16),
            VMEM((2, 256, 384), BF16),
            VMEM((2, 2, 4, 2, 96, 768), BF16),
            VMEM((2, 2, 4, 256, 384), BF16),
            VMEM((4, 128, D), BF16),
            VMEM((2, 64, D), BF16),
            VMEM((2, 128, D), BF16),
            VMEM((2, 64, D), BF16),
            VMEM((8, 8, 128), F32),
            VMEM((16, 8, 128), F32),
            VMEM((8, 8, 128), F32),
            VMEM((16, 8, 128), F32),
            VMEM((8, 8, 128), F32),
        ]
        + scatter_bufs(96, D)[1:]
        + scatter_bufs(96, 768)
        + scatter_bufs(256, 384)
        + [pltpu.SemaphoreType.DMA((28,))]
        + dma_sems(140),
        compiler_params=pltpu.CompilerParams(
            collective_id=cid, has_side_effects=True, vmem_limit_bytes=62 * 2**20
        ),
        name="attention_back",
    )(*args)


def final_kernel(
    d_in,
    f_in,
    c_in,
    layer_in,
    hidden_in,
    g_in,
    gain_hbm,
    bias_hbm,
    got_in,
    layer,
    hidden,
    ada,
    bias,
    gains,
    qkv,
    heads,
    cap,
    gate,
    out_w,
    ffn,
    down,
    d_ref,
    f_ref,
    c_ref,
    hidden_half,
    g_all,
    gain_in,
    bias_in,
    got1,
    units,
    items,
    sems,
):
    dp = lax.axis_index("dp")
    loads = []
    for src, dst in (
        (layer_in, layer),
        (hidden_in, hidden_half),
        (got_in, got1),
        (g_in, g_all),
        (gain_hbm, gain_in),
        (bias_hbm, bias_in),
        (d_in, d_ref),
        (f_in, f_ref),
        (c_in, c_ref),
    ):
        copy = pltpu.make_async_copy(src, dst, sems.at[len(loads)])
        copy.start()
        loads.append(copy)
    for copy in loads[1:]:
        copy.wait()
    hidden[...] = hidden_half[...].astype(F32)
    qkv[0] = d_ref[:, 0:192]
    qkv[1, :, 0:128] = d_ref[:, 256:384]
    qkv[1, :, 128:192] = d_ref[:, 192:256]
    qkv[2] = d_ref[:, 384:576]
    out_w[0:128, :] = d_ref[:, 640:768].T
    out_w[128:192, :] = d_ref[:, 576:640].T
    ffn[0] = f_ref[:, 0:512]
    ffn[1] = f_ref[:, 512:1024]
    down[...] = f_ref[:, 1024:1536]
    cap[0] = c_ref[:, 0:192].T
    cap[1, 0:128, :] = c_ref[:, 256:384].T
    cap[1, 128:192, :] = c_ref[:, 192:256].T
    for d in range(16):
        units[2 * d : 2 * d + 2, :] = got1[d, 0:2, 0:64]
        for j in range(6):
            items[2 * d : 2 * d + 2, j * 128 : j * 128 + 128] = jnp.concatenate(
                [g_all[d, 0, j : j + 1, :], g_all[d, 1, j : j + 1, :]], axis=0
            )
    unit_rows = units[...].astype(BF16)
    high = items[...].astype(BF16)
    low = (items[...] - high.astype(F32)).astype(BF16)
    ada[...] = mm_rows(unit_rows, high) + mm_rows(unit_rows, low)
    rows = bias_in[dp // 2]
    half = jnp.where(dp % 2 == 0, rows[0:3], rows[3:6])
    for j in range(3):
        bias[:, j * 128 : j * 128 + 128] = half[j : j + 1]
    gains[...] = gain_in[0:4, 0:96]
    heads[0:1, :] = gain_in[4:5, 0:64]
    heads[1:2, :] = gain_in[4:5, 64:128]
    heads[2:3, :] = gain_in[5:6, 0:64]
    gate[...] = gain_in[5:6, 64:88]
    loads[0].wait()


def final_call(args):
    S = jax.ShapeDtypeStruct
    vm = pl.BlockSpec(memory_space=VMEM)
    outs = [
        S((2, 64, D), BF16),
        S((2, 64, D), F32),
        S((64, 768), F32),
        S((1, 384), F32),
        S((4, 96), F32),
        S((3, 96, 192), F32),
        S((3, 64), F32),
        S((2, 192, 256), F32),
        S((1, 24), F32),
        S((192, 96), F32),
        S((2, 96, 512), F32),
        S((96, 512), F32),
    ]
    return pl.pallas_call(
        final_kernel,
        out_shape=outs,
        in_specs=[pl.BlockSpec(memory_space=pl.ANY)] * len(args),
        out_specs=[pl.BlockSpec(memory_space=pl.ANY)] + [vm] * (len(outs) - 1),
        scratch_shapes=[VMEM(a.shape, a.dtype) for a in args[:3] + args[4:]]
        + [VMEM((32, 64), F32), VMEM((32, 768), F32), pltpu.SemaphoreType.DMA((9,))],
        compiler_params=pltpu.CompilerParams(vmem_limit_bytes=32 * 2**20),
        name="final_layout",
    )(*args)


def on_device(
    hidden,
    condition,
    caption,
    lengths,
    frames,
    widths,
    caption_lens,
    cotangent,
    ada_weight,
    ada_bias,
    norm_gains,
    qkv_weight,
    head_gains,
    caption_weight,
    head_gate,
    out_weight,
    ffn_weight,
    down_weight,
):
    (
        w_f,
        w_a,
        cap_flip,
        first_flip,
        q8,
        kk,
        vv,
        qr,
        kr,
        tkr,
        other,
        lse,
        cw,
        cos_t,
        sin_t,
        resid,
        tk,
        tv,
        attn,
        middle,
        second_in,
        cot,
        mod_rows,
        gains,
        got1,
        live,
        facts,
    ) = attention_call(
        [
            hidden[:, 0],
            cotangent[:, 0],
            caption[:, 0],
            condition[:, 0],
            norm_gains,
            ada_weight,
            qkv_weight,
            out_weight,
            ffn_weight,
            down_weight.T,
            jnp.transpose(caption_weight, (0, 2, 1)),
            ada_bias[None],
            head_gains,
            head_gate[None],
            lengths.T,
            frames.T,
            widths.T,
            caption_lens.T,
        ],
        1,
    )
    layer_out, grad_middle, grad_attn_in, dw_half, ffn_sums = ffn_call(
        second_in,
        w_f.reshape(2, D, D),
        middle,
        attn,
        cot.reshape(128, D),
        mod_rows,
        gains,
        live,
        2,
    )
    d_out, f_out, c_out, layer_final, hidden_final, g_all, gain_out, bias_all = back_call(
        [
            dw_half,
            w_a,
            cap_flip,
            first_flip,
            q8,
            kk,
            vv,
            qr,
            kr,
            tkr,
            other,
            lse,
            cw,
            cos_t,
            sin_t,
            resid,
            tk,
            tv,
            grad_middle,
            grad_attn_in,
            layer_out.reshape(2, 64, D),
            mod_rows,
            gains,
            ffn_sums,
            facts,
        ],
        3,
    )
    (
        layer,
        grad_hidden,
        ada,
        bias,
        norm,
        qkv,
        heads,
        cap,
        gate,
        out_w,
        ffn,
        down,
    ) = final_call(
        [d_out, f_out, c_out, layer_final, hidden_final, g_all, gain_out, bias_all, got1]
    )
    return (
        layer[:, None],
        grad_hidden[:, None],
        ada,
        bias[0],
        norm,
        qkv,
        heads,
        jnp.transpose(cap, (0, 2, 1)),
        gate[0],
        out_w,
        ffn,
        down.T,
    )


def solution(mesh):
    return jax.shard_map(
        on_device,
        mesh=mesh,
        in_specs=(
            P(None, "dp", "tensor", None),
            P(None, "dp", None),
            P(None, "dp", None, None),
            P(None, "dp"),
            P(None, "dp"),
            P(None, "dp"),
            P(None, "dp"),
            P(None, "dp", "tensor", None),
            P("dp", "tensor"),
            P("dp"),
            P(None, "dp"),
            P(None, "dp", "tensor"),
            P(),
            P(None, "dp", "tensor"),
            P(),
            P("tensor", "dp"),
            P(None, "dp", "tensor"),
            P("tensor", "dp"),
        ),
        out_specs=(
            P(None, "dp", "tensor", None),
            P(None, "dp", "tensor", None),
            P("dp", "tensor"),
            P("dp"),
            P(None, "dp"),
            P(None, "dp", "tensor"),
            P(),
            P(None, "dp", "tensor"),
            P(),
            P("tensor", "dp"),
            P(None, "dp", "tensor"),
            P("tensor", "dp"),
        ),
        check_vma=False,
    )
```

```python
import jax
import jax.numpy as jnp
from jax import lax
from jax.experimental import pallas as pl
from jax.experimental.pallas import tpu as pltpu
from jax.sharding import PartitionSpec as P

D = 1536
H = 24
HD = 64
EPSILON = 1e-05
NEGATIVE = -1e30
MESH = pl.DeviceIdType.MESH
VMEM = pltpu.VMEM
F32 = jnp.float32
BF16 = jnp.bfloat16


def coords():
    dp = lax.axis_index("dp")
    t = lax.axis_index("tensor")
    return dp // 8, t % 2, (dp // 2) % 4, t // 2, dp % 2


def device_of(x, y, z, c):
    return ((x // 2) * 8 + y * 2 + c, z * 2 + x % 2)


def greet_signal(devices):
    barrier = pltpu.get_barrier_semaphore()
    for device in devices:
        pl.semaphore_signal(barrier, inc=1, device_id=device, device_id_type=MESH)


def greet_wait(devices):
    pl.semaphore_wait(pltpu.get_barrier_semaphore(), len(devices))


def greet(devices):
    greet_signal(devices)
    greet_wait(devices)


class Sender:
    def __init__(self, send_sem, recv_sem):
        self.send_sem = send_sem
        self.recv_sem = recv_sem
        self.copies = []

    def __call__(self, src, dst, device):
        k = len(self.copies)
        copy = pltpu.make_async_remote_copy(
            src_ref=src,
            dst_ref=dst,
            send_sem=self.send_sem.at[k],
            recv_sem=self.recv_sem.at[k],
            device_id=device,
            device_id_type=MESH,
        )
        copy.start()
        self.copies.append(copy)
        return copy

    def drain(self):
        for copy in self.copies:
            copy.wait_send()


def dma_sems(n):
    return [pltpu.SemaphoreType.DMA((n,)), pltpu.SemaphoreType.DMA((n,))]


def plane_peers():
    xh, xl, y, z, c = coords()
    x = 2 * xh + xl
    xr, xq = (x + 1) % 4, (x + 3) % 4
    yr, yq = (y + 1) % 4, (y + 3) % 4
    peers = [
        device_of(xr, y, z, c),
        device_of(xq, y, z, c),
        device_of(x, yr, z, c),
        device_of(x, yq, z, c),
        device_of(x, y, z, 1 - c),
        device_of((x + 2) % 4, y, z, c),
        device_of(x, (y + 2) % 4, z, c),
    ]
    return x, y, c, xr, xq, yr, yq, peers


def add_low(a, b):
    return (a.astype(F32) + b.astype(F32)).astype(BF16)


def normalize(values):
    inverse = lax.rsqrt(jnp.mean(values * values, axis=-1, keepdims=True) + EPSILON)
    return (values * inverse, inverse)


def norm_back(unit_values, inverse, gradient):
    return inverse * (
        gradient - unit_values * jnp.mean(gradient * unit_values, axis=-1, keepdims=True)
    )


def swish(values):
    return values * jax.nn.sigmoid(values)


def z_ring():
    xh, xl, y, z, c = coords()
    x = 2 * xh + xl
    return z, device_of(x, y, (z + 1) % 4, c), device_of(x, y, (z + 3) % 4, c)


class ZGather:
    def __init__(self, send, own, every, right, left):
        self.send, self.every, self.right, self.left = send, every, right, left
        half = every.shape[1] // 2
        self.lower, self.upper = pl.ds(0, half), pl.ds(half, half)
        self.a_low = send(own.at[self.lower], every.at[1, self.lower], right)
        self.b_up = send(own.at[self.upper], every.at[2, self.upper], left)
        self.a_up = send(own.at[self.upper], every.at[1, self.upper], right)
        self.b_low = send(own.at[self.lower], every.at[2, self.lower], left)

    def near(self):
        every, lower, upper = self.every, self.lower, self.upper
        self.a_low.wait_recv()
        self.far_low = self.send(every.at[1, lower], every.at[3, lower], self.right)
        self.b_up.wait_recv()
        self.far_up = self.send(every.at[2, upper], every.at[3, upper], self.left)
        self.a_up.wait_recv()
        self.b_low.wait_recv()

    def far(self):
        self.far_low.wait_recv()
        self.far_up.wait_recv()


class ZScatter:
    def __init__(self, send, part, relay, got, right, left):
        self.send, self.part, self.relay, self.got = send, part, relay, got
        self.right, self.left = right, left
        self.lower, self.upper = pl.ds(0, 64), pl.ds(64, 64)
        self.waits = []

    def near(self):
        part, got = self.part, self.got
        self.waits.append(self.send(part.at[2, self.upper], got.at[0, self.upper], self.right))
        self.waits.append(self.send(part.at[1, self.lower], got.at[1, self.lower], self.left))

    def far(self):
        part, relay = self.part, self.relay
        self.relays = []
        for i in range(2):
            rows, low, up = pl.ds(32 * i, 32), pl.ds(32 * i, 32), pl.ds(64 + 32 * i, 32)
            self.relays.append(
                (
                    self.send(part.at[3, low], relay.at[0, rows], self.right),
                    self.send(part.at[3, up], relay.at[1, rows], self.left),
                )
            )

    def pass_on(self):
        part, relay, got = self.part, self.relay, self.got
        for i in range(2):
            rows, low, up = pl.ds(32 * i, 32), pl.ds(32 * i, 32), pl.ds(64 + 32 * i, 32)
            self.relays[i][0].wait_recv()
            part[2, low] = add_low(part[2, low], relay[0, rows])
            self.waits.append(self.send(part.at[2, low], got.at[0, low], self.right))
            self.relays[i][1].wait_recv()
            part[1, up] = add_low(part[1, up], relay[1, rows])
            self.waits.append(self.send(part.at[1, up], got.at[1, up], self.left))

    def total(self):
        for copy in self.waits:
            copy.wait_recv()
        got = self.got
        return self.part[0].astype(F32) + got[0].astype(F32) + got[1].astype(F32)


def mm(a, b):
    return lax.dot_general(a, b, (((1,), (0,)), ((), ())), preferred_element_type=F32)


def mm_t(a, b):
    return lax.dot_general(a, b, (((1,), (1,)), ((), ())), preferred_element_type=F32)


def tile(j, size=256):
    return pl.ds(pl.multiple_of(j * size, size), size)


def transpose_into(src, dst):
    def column(j, carry):
        cols = tile(j, 128)
        for slot in range(4):
            dst[cols, slot * 128 : (slot + 1) * 128] = src[slot, :, cols].T
        return carry

    lax.fori_loop(0, D // 128, column, 0)


class PlaneGather:
    def __init__(self, send, shard, every):
        self.send, self.shard, self.every = send, shard, every
        rows, cols = shard.shape
        half = rows // 2
        self.top, self.low = pl.ds(0, half), pl.ds(half, half)
        self.late = []

    def at(self, xx, yy, *rest):
        return self.every.at[(xx % 2, xx // 2, yy, self.c) + rest]

    def same(self, ref, device):
        return self.send(ref, ref, device)

    def to_sibling(self, ref):
        self.late.append(self.send(ref, ref, self.sibling))

    def start(self, local_sem):
        x, y, c, xr, xq, yr, yq, peers = plane_peers()
        self.x, self.y, self.c = x, y, c
        self.xr, self.xq, self.yr, self.yq = xr, xq, yr, yq
        self.go_xr, self.go_xq, self.go_yr, self.go_yq, self.sibling, go_xo, go_yo = peers
        shard, top, low = self.shard, self.top, self.low
        self.a_r = self.send(shard.at[top], self.at(x, y, top), self.go_xr)
        self.a_l = self.send(shard.at[top], self.at(x, y, top), self.go_xq)
        self.b_r = self.send(shard.at[low], self.at(x, y, low), self.go_yr)
        self.b_l = self.send(shard.at[low], self.at(x, y, low), self.go_yq)
        self.a_o = self.send(shard.at[top], self.at(x, y, top), go_xo)
        self.b_o = self.send(shard.at[low], self.at(x, y, low), go_yo)
        self.late.append(self.send(shard, self.at(x, y), self.sibling))
        self.local = pltpu.make_async_copy(shard, self.at(x, y), local_sem)
        self.local.start()

    def step3(self):
        x, y, c = self.x, self.y, self.c
        every, top, low = self.every, self.top, self.low
        self.local.wait()
        for copy in (self.a_r, self.a_l, self.a_o):
            copy.wait_recv()
        block = every.at[:, :, y, c, top]
        self.g_r = self.same(block, self.go_yr)
        self.g_l = self.same(block, self.go_yq)
        for copy in (self.b_r, self.b_l, self.b_o):
            copy.wait_recv()
        block = every.at[x % 2, x // 2, :, c, low]
        self.h_r = self.same(block, self.go_xr)
        self.h_l = self.same(block, self.go_xq)
        for k in range(1, 4):
            self.to_sibling(self.at((x + k) % 4, y, top))
            self.to_sibling(self.at(x, (y + k) % 4, low))

    def step4(self):
        c, every, top, low = self.c, self.every, self.top, self.low
        xr, xq, yr, yq = self.xr, self.xq, self.yr, self.yq
        self.g_r.wait_recv()
        self.f1 = self.same(every.at[0, :, yq, c, top], self.go_yr)
        self.g_l.wait_recv()
        self.f2 = self.same(every.at[1, :, yr, c, top], self.go_yq)
        self.h_r.wait_recv()
        self.f3 = self.same(every.at[xq % 2, xq // 2, pl.ds(0, 2), c, low], self.go_xr)
        self.h_l.wait_recv()
        self.f4 = self.same(every.at[xr % 2, xr // 2, pl.ds(2, 2), c, low], self.go_xq)
        self.to_sibling(every.at[:, :, yq, c, top])
        self.to_sibling(every.at[:, :, yr, c, top])
        self.to_sibling(every.at[xq % 2, xq // 2, :, c, low])
        self.to_sibling(every.at[xr % 2, xr // 2, :, c, low])

    def step5(self):
        c, every, top, low = self.c, self.every, self.top, self.low
        xo, yo = (self.x + 2) % 4, (self.y + 2) % 4
        for copy in (self.f1, self.f2, self.f3, self.f4):
            copy.wait_recv()
        self.to_sibling(every.at[:, :, yo, c, top])
        self.to_sibling(every.at[xo % 2, xo // 2, :, c, low])

    def finish(self):
        for copy in self.late:
            copy.wait_recv()


OFFSETS = (0, 3, 1, 2)


def lanes(shape):
    return lax.broadcasted_iota(jnp.int32, shape, len(shape) - 1)


def head_block():
    row = lax.broadcasted_iota(jnp.int32, (128, 128), 0) // 64
    col = lax.broadcasted_iota(jnp.int32, (128, 128), 1) // 64
    return jnp.where(row == col, 1.0 / 64.0, 0.0).astype(BF16)


def head_mean(values, block):
    high = values.astype(BF16)
    low = (values - high.astype(F32)).astype(BF16)
    return mm(high, block) + mm(low, block)


def swap_quarters(values):
    second = (lanes(values.shape) % 64) >= 32
    return jnp.where(second, pltpu.roll(values, 32, 1), pltpu.roll(values, 96, 1))


GAIN_ROW, GATE_ROW, LENGTH_ROW, FRAMES_ROW, WIDTH_ROW, TEXT_ROW, BIAS_ROW = 0, 3, 6, 7, 8, 9, 10


def key_bias(total, z, length):
    lane = lanes((1, total))
    if total == 512:
        slot = lane // 128
        block = jnp.where(slot == 0, z, jnp.where(slot == 1, z + 3, jnp.where(slot == 2, z + 1, z + 2)))
        position = (block % 4) * 128 + lane % 128
    else:
        position = lane
    return jnp.where(position.astype(F32) < length[:, :1], 0.0, NEGATIVE)


def fill_rope(cos_ref, sin_ref, z, length, frames, width):
    lane = lanes((128, 128))
    pair = lane % 32
    offset = jnp.where(pair >= 20, 20, jnp.where(pair >= 8, 8, 0))
    size = jnp.where(pair >= 8, 12.0, 8.0)
    freq = jnp.exp((pair - offset).astype(F32) / size * (-9.210340371976184))
    sign = jnp.where(lane % 64 >= 32, 1.0, -1.0)
    row_size = width
    per_frame = jnp.floor((length + frames - 0.5) / frames)
    row = lax.broadcasted_iota(jnp.int32, (128, 128), 0).astype(F32)
    for slot in range(4):
        start = (((z + OFFSETS[slot]) % 4) * 128).astype(F32)
        position = row + start
        frame = jnp.floor((position + 0.5) / per_frame)
        within = position - frame * per_frame
        row_pos = jnp.floor((within + 0.5) / row_size)
        col_pos = within - row_pos * row_size
        chosen = jnp.where(pair >= 20, col_pos, jnp.where(pair >= 8, row_pos, frame))
        angle = chosen * freq
        cos_ref[slot] = jnp.cos(angle)
        sin_ref[slot] = jnp.sin(angle) * sign


def attention_kernel(
    hid_ref,
    cot_ref,
    cap_hbm,
    cond_ref,
    gain_in,
    ada_ref,
    qkv_ref,
    out_w_ref,
    ffn_w_ref,
    down_t_ref,
    cap_t_ref,
    bias_ref,
    head_gain_ref,
    head_gate_ref,
    len_ref,
    frame_ref,
    width_ref,
    tlen_ref,
    w_f,
    w_a_out,
    cap_flip_out,
    first_flip_out,
    q8_out,
    kk_out,
    vv_out,
    qr_out,
    kr_out,
    tkr_out,
    other_out,
    lse_out,
    cw_out,
    cos_out,
    sin_out,
    resid_out,
    tk_out,
    tv_out,
    attn_out,
    mid_out,
    second_out,
    cot_out,
    mod_ref,
    gains_ref,
    got1,
    live_ref,
    facts,
    w_a,
    cap_flip,
    first_flip,
    q8,
    kk,
    vv,
    qr,
    kr,
    tkr,
    other_ref,
    lse_ref,
    cw,
    cos_ref,
    sin_ref,
    resid_ref,
    tk,
    tv,
    attn_ref,
    mid_ref,
    second_ref,
    first,
    own_ref,
    sh_a,
    sh_f,
    sh_c,
    w_c,
    cap,
    hid_all,
    hid_own,
    msg,
    sent2,
    got2,
    got3,
    mixed,
    part,
    relay,
    got,
    local_sems,
    ss,
    rs,
):
    dp = lax.axis_index("dp")
    t = lax.axis_index("tensor")
    xh, xl, y, z, c = coords()
    _, right, left = z_ring()
    pair = device_of(2 * xh + 1 - xl, y, z, c)
    dp_peers = [((dp + k) % 16, t) for k in range(1, 16)]
    t_peers = [(dp, (t + k) % 8) for k in range(1, 8)]
    outer_x = device_of((2 * xh + xl + 3 - 2 * xl) % 4, y, z, c)
    everyone = dp_peers + t_peers + [outer_x]
    greet_signal(everyone)
    load_cap = pltpu.make_async_copy(cap_hbm.at[xl], cap, local_sems.at[0])
    load_cap.start()
    load_hid = pltpu.make_async_copy(hid_ref.at[xl], hid_own.at[xl], local_sems.at[4])
    load_hid.start()
    flushes = []

    def flush(src, dst):
        copy = pltpu.make_async_copy(src, dst, local_sems.at[5 + len(flushes)])
        copy.start()
        flushes.append(copy)

    flush(cot_ref.at[xl], cot_out.at[xl])
    facts[...] = jnp.zeros((16, 128), F32)
    for i in range(3):
        gain = head_gain_ref[i : i + 1, :].astype(F32)
        facts[i : i + 1, 0:64] = gain
        facts[i : i + 1, 64:128] = gain
        facts[BIAS_ROW + i : BIAS_ROW + i + 1, :] = bias_ref[:, i * 128 : i * 128 + 128].astype(F32)
    gates = jnp.tanh(head_gate_ref[...].astype(F32))
    gate_lane = lanes((1, 24))
    low_row = lanes((1, 128)) < 64
    for p in range(3):
        a, b = [
            jnp.sum(jnp.where(gate_lane == z * 6 + h, gates, 0.0), axis=1, keepdims=True)
            for h in ((0, 1), (3, 4), (2, 5))[p]
        ]
        facts[GATE_ROW + p : GATE_ROW + p + 1, :] = jnp.where(low_row, a, b)
    for i, ref in enumerate((len_ref, frame_ref, width_ref, tlen_ref)):
        count = jnp.where(xl == 0, ref[:, 0:1], ref[:, 1:2]).astype(F32)
        facts[LENGTH_ROW + i : LENGTH_ROW + i + 1, :] = jnp.broadcast_to(count, (1, 128))
    unit = swish(cond_ref[...].astype(F32)).astype(BF16).astype(F32)
    msg[...] = jnp.zeros((16, 8, 128), F32)
    gain_rows = gain_in[...].astype(F32)
    for d in range(16):
        msg[d, 0:2, 0:64] = unit[:, d * 64 : (d + 1) * 64]
        msg[d, 4:8, 0:96] = gain_rows
    qs, ks, vs = qkv_ref[0], qkv_ref[1], qkv_ref[2]
    os = out_w_ref[...].T
    sh_a[...] = jnp.concatenate(
        [qs, ks[:, 128:192], ks[:, 0:128], vs, os[:, 128:192], os[:, 0:128]],
        axis=1,
    )
    ck, cv = cap_t_ref[0].T, cap_t_ref[1].T
    sh_c[...] = jnp.concatenate([ck, cv[:, 128:192], cv[:, 0:128]], axis=1)
    greet_wait(everyone)

    send = Sender(ss, rs)
    round1 = [send(msg.at[p[0]], got1.at[dp], p) for p in dp_peers]
    swap = send(hid_ref.at[1 - xl], hid_own.at[xl], pair)
    near_r1 = send(hid_ref.at[xl], hid_all.at[1, xl], right)
    near_l1 = send(hid_ref.at[xl], hid_all.at[2, xl], left)
    ga = PlaneGather(send, sh_a, w_a)
    gc = PlaneGather(send, sh_c, w_c)
    gf = PlaneGather(send, sh_f, w_f)
    ga.start(local_sems.at[1])
    got1[dp] = msg[dp]
    sh_f[:, 0:512] = ffn_w_ref[0]
    sh_f[:, 512:1024] = ffn_w_ref[1]
    sh_f[:, 1024:1536] = down_t_ref[...]
    length = facts[LENGTH_ROW : LENGTH_ROW + 1, :]
    text_len = facts[TEXT_ROW : TEXT_ROW + 1, :]
    for copy in round1:
        copy.wait_recv()
    rows = got1[...].reshape(128, 128)[:, :64].astype(BF16)
    here = t == dp // 2
    low_bias = jnp.where(jnp.logical_and(here, dp % 2 == 0), 1.0, 0.0)
    high_bias = jnp.where(jnp.logical_and(here, dp % 2 == 1), 1.0, 0.0)
    terms = mm(rows, ada_ref[...])
    bias = [facts[BIAS_ROW + j : BIAS_ROW + j + 1, :] for j in range(3)]
    bias = [row * low_bias for row in bias] + [row * high_bias for row in bias]
    for d in range(16):
        for j in range(6):
            sent2[d, 2 * j : 2 * j + 2, :] = terms[8 * d : 8 * d + 2, 128 * j : 128 * j + 128] + bias[j]
    round2 = [send(sent2.at[p[0]], got2.at[dp], p) for p in dp_peers]
    got2[dp] = sent2[dp]
    load_hid.wait()
    swap.wait_recv()
    near_r2 = send(hid_own.at[1 - xl], hid_all.at[1, 1 - xl], right)
    near_l2 = send(hid_own.at[1 - xl], hid_all.at[2, 1 - xl], left)
    hid_all[0] = hid_own[...]
    for copy in round2:
        copy.wait_recv()
    got3[t] = jnp.sum(got2[...], axis=0)
    round3 = [send(got3.at[t], got3.at[t], p) for p in t_peers]
    ga.step3()
    gc.start(local_sems.at[2])
    fill_rope(
        cos_ref,
        sin_ref,
        z,
        length,
        facts[FRAMES_ROW : FRAMES_ROW + 1, :],
        facts[WIDTH_ROW : WIDTH_ROW + 1, :],
    )
    flush(cos_ref, cos_out)
    flush(sin_ref, sin_out)
    near_r1.wait_recv()
    near_r2.wait_recv()
    far_r = send(hid_all.at[1, 0], hid_all.at[3, 0], right)
    near_l1.wait_recv()
    near_l2.wait_recv()
    far_l = send(hid_all.at[2, 1], hid_all.at[3, 1], left)
    for d in range(16):
        gains_ref[0:4, d * 96 : (d + 1) * 96] = got1[d, 4:8, 0:96]
    gains_ref[4:8, :] = jnp.zeros((4, D), F32)
    slot_row = lax.broadcasted_iota(jnp.int32, (128, 128), 0) + z * 128
    live_ref[...] = jnp.where(slot_row.astype(F32) < length, 1.0, 0.0)
    for copy in round3:
        copy.wait_recv()
    for i in range(4):
        for h in range(2):
            block = got3[2 * i + h]
            for j in range(6):
                lo = h * 768 + j * 128
                mod_ref[i : i + 1, lo : lo + 128] = jnp.where(
                    xl == 0, block[2 * j : 2 * j + 1], block[2 * j + 1 : 2 * j + 2]
                )
    mod_ref[4:8, :] = jnp.zeros((4, D), F32)
    factor = gains_ref[0:1, :] * (1.0 + mod_ref[0:1, :])

    def scale_rows(slot, carry):
        unit_rows, _ = normalize(hid_all[slot].reshape(128, D).astype(F32))
        first[slot] = (unit_rows * factor).astype(BF16)
        return carry

    load_cap.wait()

    def flip_caption(j, carry):
        rows = tile(j, 128)
        cap_flip[rows, 0:128] = cap[0:128, rows].T
        cap_flip[rows, 128:256] = cap[128:256, rows].T
        return carry

    lax.fori_loop(0, 3, scale_rows, 0)
    ga.step4()
    far_r.wait_recv()
    far_l.wait_recv()
    scale_rows(3, 0)
    resid_ref[...] = hid_all[0].reshape(128, D)
    flush(resid_ref, resid_out)
    gc.step3()
    gf.start(local_sems.at[3])
    transpose_into(first, first_flip)
    flush(first_flip, first_flip_out)
    lax.fori_loop(0, 32, flip_caption, 0)
    flush(cap_flip, cap_flip_out)
    ga.step5()
    ga.finish()
    flush(w_a, w_a_out)

    x_rows = first[...].reshape(512, D)
    low_head = lanes((512, 128)) < 64

    def project(xx, cols):
        w_cols = w_a[xx, :, :, :, :, cols].reshape(D, cols.stop - cols.start)
        return mm(x_rows, w_cols)

    def project_side(xx, carry):
        p = project(xx, slice(0, 256))
        qr[xx] = p[:, :128].reshape(4, 128, 128)
        mixed[0, xx] = p[:, 128:]
        p = project(xx, slice(256, 512))
        kr[xx] = p[:, :128].reshape(4, 128, 128)
        vv[xx] = p[:, 128:].astype(BF16).reshape(4, 128, 128)
        mixed[1, xx] = project(xx, slice(512, 640))
        return carry

    lax.fori_loop(0, 2, project_side, 0)
    x0, x1 = mixed[0, 0], mixed[0, 1]
    qr[2] = jnp.where(low_head, x0, pltpu.roll(x1, 64, 1)).reshape(4, 128, 128)
    kr[2] = jnp.where(low_head, pltpu.roll(x0, 64, 1), x1).reshape(4, 128, 128)
    x0, x1 = mixed[1, 0], mixed[1, 1]
    vv[2] = jnp.where(low_head, x0, pltpu.roll(x1, 64, 1)).astype(BF16).reshape(4, 128, 128)
    block = head_block()
    cos = cos_ref[...].reshape(512, 128)
    sin = sin_ref[...].reshape(512, 128)

    def turned(raw, gain):
        raw = raw.reshape(512, 128)
        v = raw * lax.rsqrt(head_mean(raw * raw, block) + EPSILON) * gain
        return v * cos + swap_quarters(v) * sin

    for p in range(3):
        q = turned(qr[p], facts[GAIN_ROW : GAIN_ROW + 1, :]).astype(BF16)
        q8[p] = (q.astype(F32) * 0.125).astype(BF16).reshape(4, 128, 128)
        k = turned(kr[p], facts[GAIN_ROW + 1 : GAIN_ROW + 2, :])
        kk[p] = k.astype(BF16).reshape(4, 128, 128)
    for src, dst in ((q8, q8_out), (kk, kk_out), (vv, vv_out), (qr, qr_out), (kr, kr_out)):
        flush(src, dst)

    self_bias = key_bias(512, z, length)
    text_bias = key_bias(256, z, text_len)
    lse_ref[...] = jnp.zeros((4, 128, 128), F32)

    def attend_rows(p, text, b):
        slots = pl.ds(b * 2, 2)
        q = q8[p, slots].reshape(256, 128)
        k = tk[p] if text else kk[p].reshape(512, 128)
        v = tv[p] if text else vv[p].reshape(512, 128)
        low_rows = lanes((256, 128)) < 64
        mix = jnp.zeros((256, 128), F32)
        for head in range(2):
            keep = low_rows if head == 0 else jnp.logical_not(low_rows)
            qm = jnp.where(keep, q, jnp.zeros_like(q))
            scores = mm_t(qm, k) + (text_bias if text else self_bias)
            top = jnp.max(scores, axis=-1, keepdims=True)
            e = jnp.exp(scores - top)
            total = jnp.sum(e, axis=-1, keepdims=True)
            probs = (e * (1.0 / total)).astype(BF16)
            mix = mix + jnp.where(keep, mm(probs, v), 0.0)
            here = lanes((256, 128)) == p * 2 + head + 8 * text
            old = lse_ref[slots].reshape(256, 128)
            lse_ref[slots] = jnp.where(here, top + jnp.log(total), old).reshape(2, 128, 128)
        if not text:
            own_ref[p, slots] = mix.reshape(2, 128, 128)
            return
        other_ref[p, slots] = mix.reshape(2, 128, 128)
        gate = facts[pl.ds(GATE_ROW + p, 1), :]
        both = own_ref[p, slots].reshape(256, 128) + gate * mix
        own_ref[p, slots] = both.reshape(2, 128, 128)

    def attend(lo, hi, text):
        def step(i, carry):
            attend_rows(i // 2, text, i % 2)
            return carry

        lax.fori_loop(2 * lo, 2 * hi, step, 0)

    attend(0, 1, False)
    gc.step4()
    gf.step3()
    cot_swap = send(cot_ref.at[1 - xl], cot_out.at[xl], pair)
    attend(1, 3, False)
    gc.step5()
    gc.finish()
    low_text = lanes((256, 128)) < 64

    def text_side(xx, carry):
        total = mm(cap[:, 0:2048], w_c[xx, 0].reshape(2048, 384))
        total = total + mm(cap[:, 2048:4096], w_c[xx, 1].reshape(2048, 384))
        tkr[xx] = total[:, 0:128]
        tv[xx] = total[:, 256:384].astype(BF16)
        mixed[0, xx, 0:256, :] = total[:, 128:256]
        return carry

    lax.fori_loop(0, 2, text_side, 0)
    x0, x1 = mixed[0, 0, 0:256, :], mixed[0, 1, 0:256, :]
    tkr[2] = jnp.where(low_text, x0, pltpu.roll(x1, 64, 1))
    tv[2] = jnp.where(low_text, pltpu.roll(x0, 64, 1), x1).astype(BF16)
    flush(tv, tv_out)
    for p in range(3):
        raw = tkr[p]
        gain = facts[GAIN_ROW + 2 : GAIN_ROW + 3, :]
        tk[p] = (raw * lax.rsqrt(head_mean(raw * raw, block) + EPSILON) * gain).astype(BF16)
    flush(tkr, tkr_out)
    flush(tk, tk_out)
    attend(0, 3, True)
    for p in range(2):
        cw[p, :, :, 128:256] = own_ref[p].astype(BF16)
    both = own_ref[2].reshape(512, 128)
    zero = jnp.zeros_like(both)
    moved = pltpu.roll(both, 64, 1)
    cw[0, :, :, 0:128] = jnp.where(low_head, zero, moved).astype(BF16).reshape(4, 128, 128)
    cw[1, :, :, 0:128] = jnp.where(low_head, zero, both).astype(BF16).reshape(4, 128, 128)
    flush(lse_ref, lse_out)
    flush(other_ref, other_out)
    flush(cw, cw_out)

    def out_rows(lo, count):
        n = count * 128
        a0 = cw[0, lo : lo + count].reshape(n, 256)
        a1 = cw[1, lo : lo + count].reshape(n, 256)
        def column(xb, carry):
            b0 = w_a[0, xb, :, :, :, 512:768].reshape(768, 256)
            b1 = w_a[1, xb, :, :, :, 512:768].reshape(768, 256)
            total = mm_t(a0, b0) + mm_t(a1, b1)
            part[lo : lo + count, :, tile(xb, 768)] = total.astype(BF16).reshape(count, 128, 768)
            return carry

        lax.fori_loop(0, 2, column, 0)

    sums = ZScatter(send, part, relay, got, right, left)
    out_rows(3, 1)
    sums.far()
    out_rows(1, 2)
    sums.near()
    out_rows(0, 1)
    gf.step4()
    sums.pass_on()
    gf.step5()
    attn = sums.total()
    attn_ref[...] = attn
    flush(attn_ref, attn_out)
    unit_two, _ = normalize(attn)
    live = live_ref[...][:, :1]
    middle = resid_ref[...].astype(F32) + live * jnp.tanh(mod_ref[1:2, :]) * unit_two * gains_ref[1:2, :]
    mid_ref[...] = middle
    flush(mid_ref, mid_out)
    unit_three, _ = normalize(middle)
    second_ref[...] = (unit_three * gains_ref[2:3, :] * (1.0 + mod_ref[2:3, :])).astype(BF16)
    flush(second_ref, second_out)
    cot_swap.wait_recv()
    gf.finish()
    send.drain()
    for copy in flushes:
        copy.wait()


def attention_call(args, cid):
    S = jax.ShapeDtypeStruct
    vm = pl.BlockSpec(memory_space=VMEM)
    any_ = pl.BlockSpec(memory_space=pl.ANY)
    pair = (3, 4, 128, 128)
    saved = [
        ((2, 2, 4, 2, 96, 768), BF16),
        ((4096, 256), BF16),
        ((D, 512), BF16),
        (pair, BF16),
        (pair, BF16),
        (pair, BF16),
        (pair, F32),
        (pair, F32),
        ((3, 256, 128), F32),
        (pair, F32),
        ((4, 128, 128), F32),
        ((2, 4, 128, 256), BF16),
        ((4, 128, 128), F32),
        ((4, 128, 128), F32),
        ((128, D), BF16),
        ((3, 256, 128), BF16),
        ((3, 256, 128), BF16),
        ((128, D), F32),
        ((128, D), F32),
        ((128, D), BF16),
    ]
    outs = [
        ((8, D), F32),
        ((8, D), F32),
        ((16, 8, 128), F32),
        ((128, 128), F32),
        ((16, 128), F32),
    ]
    return pl.pallas_call(
        attention_kernel,
        out_shape=[S((2, 2, 4, 2, 96, D), BF16)]
        + [S(*o) for o in saved]
        + [S((2, 64, D), BF16)]
        + [S(*o) for o in outs],
        in_specs=[any_] * 3 + [vm] * 15,
        out_specs=[any_] * (2 + len(saved)) + [vm] * len(outs),
        scratch_shapes=[VMEM(*o) for o in saved]
        + [
            VMEM((4, 128, D), BF16),
            VMEM(pair, F32),
            VMEM((96, 768), BF16),
            VMEM((96, D), BF16),
            VMEM((256, 384), BF16),
            VMEM((2, 2, 4, 2, 256, 384), BF16),
            VMEM((256, 4096), BF16),
            VMEM((4, 2, 64, D), BF16),
            VMEM((2, 64, D), BF16),
            VMEM((16, 8, 128), F32),
            VMEM((16, 16, 128), F32),
            VMEM((16, 16, 128), F32),
            VMEM((8, 16, 128), F32),
            VMEM((2, 2, 512, 128), F32),
            VMEM((4, 128, D), BF16),
            VMEM((2, 64, D), BF16),
            VMEM((2, 128, D), BF16),
            pltpu.SemaphoreType.DMA((28,)),
        ]
        + dma_sems(160),
        compiler_params=pltpu.CompilerParams(
            collective_id=cid, has_side_effects=True, vmem_limit_bytes=58 * 2**20
        ),
        name="attention",
    )(*args)


def ffn_kernel(
    x_ref,
    w_hbm,
    mid_in,
    attn_in,
    cot_in,
    mod_ref,
    gain_ref,
    live_ref,
    out_out,
    gmid_out,
    gattn_out,
    dw_half,
    sums_ref,
    mid_ref,
    attn_ref,
    cot_ref,
    out_ref,
    gmid_ref,
    gattn_ref,
    w,
    dw_ref,
    dw_got,
    x_all,
    g_all,
    act,
    dgate,
    dup,
    gpre,
    part1,
    part2,
    relay1,
    relay2,
    got1,
    got2,
    flip,
    flip_g,
    own_g,
    w_sem,
    out_sems,
    ss,
    rs,
):
    z, right, left = z_ring()
    load = pltpu.make_async_copy(w_hbm, w, w_sem)
    load.start()
    loads = []
    for src, dst in ((x_ref, x_all.at[0]), (mid_in, mid_ref), (attn_in, attn_ref), (cot_in, cot_ref)):
        copy = pltpu.make_async_copy(src, dst, out_sems.at[4 + len(loads)])
        copy.start()
        loads.append(copy)
    stores = []

    def store(src, dst):
        copy = pltpu.make_async_copy(src, dst, out_sems.at[8 + len(stores)])
        copy.start()
        stores.append(copy)

    xh, xl, y, _, c = coords()
    sibling = device_of(2 * xh + xl, y, z, 1 - c)
    greet([right, left, sibling])
    send = Sender(ss, rs)
    one = ZGather(send, x_ref, x_all, right, left)
    for copy in loads:
        copy.wait()
    load.wait()

    def pre(lo, count):
        rows = count * 128
        x = x_all[lo : lo + count].reshape(rows, D)

        def column(i, carry):
            xx, j = i // 2, i % 2
            g = mm(x, w[xx, :, tile(j)])
            u = mm(x, w[xx, :, tile(j + 2)])
            s = jax.nn.sigmoid(g)
            gs = g * s
            act[xx, lo : lo + count, :, tile(j)] = (gs * u).astype(BF16).reshape(count, 128, 256)
            dgate[xx, lo : lo + count, :, tile(j)] = (u * s * (1.0 + g * (1.0 - s))).reshape(count, 128, 256)
            dup[xx, lo : lo + count, :, tile(j)] = gs.reshape(count, 128, 256)
            return carry

        lax.fori_loop(0, 4, column, 0)

    def down(lo, count):
        rows = count * 128
        a0 = act[0, lo : lo + count].reshape(rows, 512)
        a1 = act[1, lo : lo + count].reshape(rows, 512)

        def column(j, carry):
            cols = tile(j)
            total = mm_t(a0, w[0, cols, 1024:1536]) + mm_t(a1, w[1, cols, 1024:1536])
            part1[lo : lo + count, :, cols] = total.astype(BF16).reshape(count, 128, 256)
            return carry

        lax.fori_loop(0, D // 256, column, 0)

    sum1 = ZScatter(send, part1, relay1, got1, right, left)
    pre(0, 1)
    one.near()
    pre(1, 2)
    down(1, 2)
    sum1.near()
    one.far()
    pre(3, 1)
    down(3, 1)
    sum1.far()
    down(0, 1)
    transpose_into(x_all, flip)
    sum1.pass_on()
    ffn_total = sum1.total()

    live = live_ref[...][:, :1]
    mod = mod_ref[...]
    gains = gain_ref[...]
    gate_f = jnp.tanh(mod[3:4])
    middle = mid_ref[...]
    unit_four, inverse_four = normalize(ffn_total)
    out_ref[...] = (middle + live * gate_f * unit_four * gains[3:4]).astype(BF16)
    store(out_ref, out_out)
    grad_top = cot_ref[...].astype(F32)
    weighted = grad_top * live
    part_four = jnp.sum(weighted * unit_four, axis=0, keepdims=True)
    own_g[...] = norm_back(unit_four, inverse_four, weighted * gate_f * gains[3:4]).astype(BF16)
    two = ZGather(send, own_g, g_all, right, left)
    g_all[0] = own_g[...]
    sums_ref[3:4, :] = part_four * gains[3:4] * (1.0 - gate_f * gate_f)
    sums_ref[7:8, :] = part_four * gate_f

    def back(lo, count):
        rows = count * 128
        g = g_all[lo : lo + count].reshape(rows, D)

        def column(i, carry):
            xx, j = i // 2, i % 2
            ga = mm(g, w[xx, :, tile(j + 4)])
            dg = dgate[xx, lo : lo + count, :, tile(j)].reshape(rows, 256)
            du = dup[xx, lo : lo + count, :, tile(j)].reshape(rows, 256)
            gpre[xx, lo : lo + count, :, tile(j)] = (ga * dg).astype(BF16).reshape(count, 128, 256)
            gpre[xx, lo : lo + count, :, tile(j + 2)] = (ga * du).astype(BF16).reshape(count, 128, 256)
            return carry

        lax.fori_loop(0, 4, column, 0)

    def back_in(lo, count):
        rows = count * 128
        a0 = gpre[0, lo : lo + count].reshape(rows, 1024)
        a1 = gpre[1, lo : lo + count].reshape(rows, 1024)

        def column(j, carry):
            cols = tile(j)
            total = mm_t(a0, w[0, cols, 0:1024]) + mm_t(a1, w[1, cols, 0:1024])
            part2[lo : lo + count, :, cols] = total.astype(BF16).reshape(count, 128, 256)
            return carry

        lax.fori_loop(0, D // 256, column, 0)

    def weight_grad(xx):
        def column(i, carry):
            j, xb = i // 2, i % 2
            b = gpre[xx, :, :, tile(j)].reshape(512, 256)
            grad = mm(flip[tile(xb, 768), :], b)
            dw_ref[xx, xb, :, :, :, tile(j)] = grad.astype(BF16).reshape(4, 2, 96, 256)
            return carry

        lax.fori_loop(0, 8, column, 0)

        def down_column(i, carry):
            j, xb = i // 2, i % 2
            b = act[xx, :, :, tile(j)].reshape(512, 256)
            grad = mm(flip_g[tile(xb, 768), :], b)
            dw_ref[xx, xb, :, :, :, tile(j + 4)] = grad.astype(BF16).reshape(4, 2, 96, 256)
            return carry

        lax.fori_loop(0, 4, down_column, 0)
        return [
            send(dw_ref.at[xx, xb, :, 1 - c], dw_got.at[xx, xb], sibling) for xb in range(2)
        ]

    def add_sibling(xx, copies):
        for xb in range(2):
            copies[xb].wait_recv()

            def add(j, carry, xb=xb):
                dw_got[xx, xb, j] = add_low(dw_got[xx, xb, j], dw_ref[xx, xb, j, c])
                return carry

            lax.fori_loop(0, 4, add, 0)
            store(dw_got.at[xx, xb], dw_half.at[xx, xb])

    sum2 = ZScatter(send, part2, relay2, got2, right, left)
    back(0, 1)
    two.near()
    back(1, 2)
    back_in(1, 2)
    sum2.near()
    two.far()
    back(3, 1)
    back_in(3, 1)
    sum2.far()
    back_in(0, 1)
    transpose_into(g_all, flip_g)
    to_sibling0 = weight_grad(0)
    sum2.pass_on()
    to_sibling1 = weight_grad(1)
    add_sibling(0, to_sibling0)
    grad_second = sum2.total()

    scale_f = mod[2:3]
    unit_three, inverse_three = normalize(middle)
    sum_three = jnp.sum(grad_second * unit_three, axis=0, keepdims=True)
    sums_ref[2:3, :] = sum_three * gains[2:3]
    sums_ref[6:7, :] = sum_three * (1.0 + scale_f)
    grad_middle = grad_top + norm_back(
        unit_three, inverse_three, grad_second * (1.0 + scale_f) * gains[2:3]
    )
    gmid_ref[...] = grad_middle
    store(gmid_ref, gmid_out)
    gate_a = jnp.tanh(mod[1:2])
    unit_two, inverse_two = normalize(attn_ref[...])
    weighted_mid = grad_middle * live
    sum_two = jnp.sum(weighted_mid * unit_two, axis=0, keepdims=True)
    sums_ref[1:2, :] = sum_two * gains[1:2] * (1.0 - gate_a * gate_a)
    sums_ref[5:6, :] = sum_two * gate_a
    sums_ref[0:1, :] = jnp.zeros((1, D), F32)
    sums_ref[4:5, :] = jnp.zeros((1, D), F32)
    gattn_ref[...] = norm_back(unit_two, inverse_two, weighted_mid * gate_a * gains[1:2]).astype(BF16)
    store(gattn_ref, gattn_out)
    add_sibling(1, to_sibling1)
    send.drain()
    for copy in stores:
        copy.wait()


def ffn_call(second_in, w_f, middle, attn, cot, mod_rows, gains, live, cid):
    S = jax.ShapeDtypeStruct
    vm = pl.BlockSpec(memory_space=VMEM)
    any_ = pl.BlockSpec(memory_space=pl.ANY)
    return pl.pallas_call(
        ffn_kernel,
        out_shape=[
            S((128, D), BF16),
            S((128, D), F32),
            S((128, D), BF16),
            S((2, 2, 4, 96, D), BF16),
            S((8, D), F32),
        ],
        in_specs=[any_] * 5 + [vm] * 3,
        out_specs=[any_] * 4 + [vm],
        scratch_shapes=[
            VMEM((128, D), F32),
            VMEM((128, D), F32),
            VMEM((128, D), BF16),
            VMEM((128, D), BF16),
            VMEM((128, D), F32),
            VMEM((128, D), BF16),
            VMEM((2, D, D), BF16),
            VMEM((2, 2, 4, 2, 96, D), BF16),
            VMEM((2, 2, 4, 96, D), BF16),
            VMEM((4, 128, D), BF16),
            VMEM((4, 128, D), BF16),
            VMEM((2, 4, 128, 512), BF16),
            VMEM((2, 4, 128, 512), F32),
            VMEM((2, 4, 128, 512), F32),
            VMEM((2, 4, 128, 1024), BF16),
            VMEM((4, 128, D), BF16),
            VMEM((4, 128, D), BF16),
            VMEM((2, 64, D), BF16),
            VMEM((2, 64, D), BF16),
            VMEM((2, 128, D), BF16),
            VMEM((2, 128, D), BF16),
            VMEM((D, 512), BF16),
            VMEM((D, 512), BF16),
            VMEM((128, D), BF16),
            pltpu.SemaphoreType.DMA,
            pltpu.SemaphoreType.DMA((16,)),
        ]
        + dma_sems(40),
        compiler_params=pltpu.CompilerParams(
            collective_id=cid, has_side_effects=True, vmem_limit_bytes=56 * 2**20
        ),
        name="ffn",
    )(second_in, w_f, middle, attn, cot, mod_rows, gains, live)


def pick(array, index):
    return lax.dynamic_index_in_dim(array, index, 0, keepdims=False)


def dot(spec, a, b):
    return jnp.einsum(spec, a, b, preferred_element_type=F32)


class PlaneScatter:
    def __init__(self, send, grads, own, bufs):
        self.send, self.grads, self.own = send, grads, own
        self.sib, self.ra, self.rb, self.ga, self.gb, self.ha, self.hb = bufs
        rows, cols = self.sib.shape[3:]
        self.rows, self.cols = rows, cols
        self.half = half = rows // 2
        self.top, self.low = pl.ds(0, half), pl.ds(half, half)
    def setup(self):
        self.where = plane_peers()
        self.go_xr, self.go_xq, self.go_yr, self.go_yq, self.sibling, self.go_xo, self.go_yo = self.where[7]
        self.parts = {}

    def to_sibling(self, k):
        block = self.grads.at[k % 2, k // 2]
        if self.own is None:
            block = self.grads.at[k % 2, k // 2, :, 1 - self.where[2]]
        self.parts[k] = self.send(block, self.sib.at[k % 2, k // 2], self.sibling)

    def add(self):
        c, sib, own, grads = self.where[2], self.sib, self.own, self.grads
        for k in self.parts:
            self.parts[k].wait_recv()

            def add_sibling(j, carry, k=k):
                if own is None:
                    mine = grads[k % 2, k // 2, j, c]
                else:
                    mine = own(k % 2, k // 2, j)
                sib[k % 2, k // 2, j] = add_low(sib[k % 2, k // 2, j], mine)
                return carry

            lax.fori_loop(0, 4, add_sibling, 0)

    def first(self):
        x, y, c, xr, xq, yr, yq, _ = self.where
        sib, send = self.sib, self.send
        xo, yo = (x + 2) % 4, (y + 2) % 4
        self.t1 = send(sib.at[0, :, yo, self.top], self.ra.at[pl.ds(0, 2)], self.go_yr)
        self.t2 = send(sib.at[1, :, yo, self.top], self.ra.at[pl.ds(2, 2)], self.go_yq)
        self.l1 = send(sib.at[xo % 2, xo // 2, pl.ds(0, 2), self.low], self.rb.at[pl.ds(0, 2)], self.go_xr)
        self.l2 = send(sib.at[xo % 2, xo // 2, pl.ds(2, 2), self.low], self.rb.at[pl.ds(2, 2)], self.go_xq)

    def step2(self):
        x, y, c, xr, xq, yr, yq, _ = self.where
        sib, send, top, low = self.sib, self.send, self.top, self.low
        ra, rb = self.ra, self.rb
        self.t1.wait_recv()
        for j in range(2):
            sib[0, j, yr, top] = add_low(sib[0, j, yr, top], ra[j])
        self.t3 = send(sib.at[:, :, yr, top], self.ga.at[0], self.go_yr)
        self.t2.wait_recv()
        for j in range(2):
            sib[1, j, yq, top] = add_low(sib[1, j, yq, top], ra[2 + j])
        self.t4 = send(sib.at[:, :, yq, top], self.ga.at[1], self.go_yq)
        self.l1.wait_recv()
        for j in range(2):
            sib[xr % 2, xr // 2, j, low] = add_low(sib[xr % 2, xr // 2, j, low], rb[j])
        self.l3 = send(sib.at[xr % 2, xr // 2, :, low], self.gb.at[0], self.go_xr)
        self.l2.wait_recv()
        for j in range(2):
            sib[xq % 2, xq // 2, 2 + j, low] = add_low(sib[xq % 2, xq // 2, 2 + j, low], rb[2 + j])
        self.l4 = send(sib.at[xq % 2, xq // 2, :, low], self.gb.at[1], self.go_xq)

    def step3(self):
        x, y, c, xr, xq, yr, yq, _ = self.where
        sib, send, ga, gb, pa, pb = self.sib, self.send, self.ga, self.gb, self.ra, self.rb
        xo, yo = (x + 2) % 4, (y + 2) % 4
        self.t3.wait_recv()
        self.t4.wait_recv()
        for i in range(2):
            for j in range(2):
                total = sib[i, j, y, self.top].astype(F32) + ga[0, i, j].astype(F32)
                pa[2 * j + i] = (total + ga[1, i, j].astype(F32)).astype(BF16)
        ha, hb = self.ha, self.hb
        self.last_a = [
            send(pa.at[xr], ha.at[0], self.go_xr),
            send(pa.at[xq], ha.at[1], self.go_xq),
            send(pa.at[xo], ha.at[2], self.go_xo),
        ]
        self.l3.wait_recv()
        self.l4.wait_recv()
        for j in range(4):
            total = sib[x % 2, x // 2, j, self.low].astype(F32) + gb[0, j].astype(F32)
            pb[j] = (total + gb[1, j].astype(F32)).astype(BF16)
        self.last_b = [
            send(pb.at[yr], hb.at[0], self.go_yr),
            send(pb.at[yq], hb.at[1], self.go_yq),
            send(pb.at[yo], hb.at[2], self.go_yo),
        ]

    def finish(self):
        x, y = self.where[:2]
        results = []
        for copies, mine, got in (
            (self.last_a, self.ra[x], self.ha),
            (self.last_b, self.rb[y], self.hb),
        ):
            for copy in copies:
                copy.wait_recv()
            total = mine.astype(F32) + got[0].astype(F32)
            results.append(total + got[1].astype(F32) + got[2].astype(F32))
        return results


def scatter_bufs(rows, cols):
    half = rows // 2
    return [
        VMEM((2, 2, 4, rows, cols), BF16),
        VMEM((4, half, cols), BF16),
        VMEM((4, half, cols), BF16),
        VMEM((2, 2, 2, half, cols), BF16),
        VMEM((2, 4, half, cols), BF16),
        VMEM((3, half, cols), BF16),
        VMEM((3, half, cols), BF16),
    ]


def mm_rows(a, b):
    return lax.dot_general(a, b, (((0,), (0,)), ((), ())), preferred_element_type=F32)


def back_kernel(
    sib_in,
    w_a_in,
    cap_flip_in,
    first_flip_in,
    q8_in,
    kk_in,
    vv_in,
    qr_in,
    kr_in,
    tkr_in,
    other_in,
    lse_in,
    cw_in,
    cos_in,
    sin_in,
    resid_in,
    tk_in,
    tv_in,
    gmid_in,
    gattn_in,
    out_ref,
    mod_ref,
    gains_ref,
    sums_ref,
    facts,
    d_final,
    f_final,
    c_final,
    layer_final,
    hidden_final,
    g_all,
    gain_out,
    sib_f,
    w_a,
    cap_flip,
    first_flip,
    q8,
    kk,
    vv,
    qr,
    kr,
    tkr,
    other_ref,
    lse_ref,
    cw,
    cos_ref,
    sin_ref,
    resid_ref,
    tk,
    tv,
    gmid_ref,
    d_out,
    f_out,
    c_out,
    flip,
    grad_all,
    gc,
    gq,
    gk,
    gv,
    gtk,
    gtv,
    gpack,
    tpack,
    dw_a,
    dw_c,
    part,
    relay,
    got,
    hid_grad,
    mod_msg,
    gain_msg,
    got_mod,
    got_gain,
    gain_sum,
    sf1, sf2, sf3, sf4, sf5, sf6,
    sa0, sa1, sa2, sa3, sa4, sa5, sa6,
    sc0, sc1, sc2, sc3, sc4, sc5, sc6,
    local_sems,
    ss,
    rs,
):
    dp = lax.axis_index("dp")
    t = lax.axis_index("tensor")
    xh, xl, y, z, c = coords()
    _, right, left = z_ring()
    pair = device_of(2 * xh + 1 - xl, y, z, c)
    dp_peers = [((dp + k) % 16, t) for k in range(1, 16)]
    t_peers = [(dp, (t + k) % 8) for k in range(1, 8)]
    outer_x = device_of((2 * xh + xl + 3 - 2 * xl) % 4, y, z, c)
    everyone = dp_peers + t_peers + [outer_x]
    greet_signal(everyone)
    loads = []
    for src, dst in (
        (sib_in, sib_f),
        (w_a_in, w_a),
        (q8_in, q8),
        (gattn_in, grad_all.at[0]),
        (tk_in, tk),
        (tv_in, tv),
        (kk_in, kk),
        (vv_in, vv),
        (lse_in, lse_ref),
        (tkr_in, tkr),
        (cap_flip_in, cap_flip),
        (cw_in, cw),
        (qr_in, qr),
        (kr_in, kr),
        (cos_in, cos_ref),
        (sin_in, sin_ref),
        (other_in, other_ref),
        (first_flip_in, first_flip),
        (resid_in, resid_ref),
        (gmid_in, gmid_ref),
    ):
        copy = pltpu.make_async_copy(src, dst, local_sems.at[len(loads)])
        copy.start()
        loads.append(copy)
    greet_wait(everyone)
    send = Sender(ss, rs)
    tokens = ZGather(send, gattn_in, grad_all, right, left)

    def caption_own(xx, xb, yb):
        return mm(cap_flip[tile(2 * (4 * xb + yb) + c)], tpack[xx])

    scat_f = PlaneScatter(send, None, None, (sib_f, sf1, sf2, sf3, sf4, sf5, sf6))
    scat_a = PlaneScatter(send, dw_a, None, (sa0, sa1, sa2, sa3, sa4, sa5, sa6))
    scat_c = PlaneScatter(send, dw_c, caption_own, (sc0, sc1, sc2, sc3, sc4, sc5, sc6))
    for scatter in (scat_f, scat_a, scat_c):
        scatter.setup()
    loads[0].wait()
    scat_f.first()
    stores = []

    def store(src, dst):
        copy = pltpu.make_async_copy(src, dst, local_sems.at[len(loads) + len(stores)])
        copy.start()
        stores.append(copy)

    store(out_ref.at[xl], layer_final.at[xl])
    out_swap = send(out_ref.at[1 - xl], layer_final.at[xl], pair)
    self_bias = key_bias(512, z, facts[LENGTH_ROW : LENGTH_ROW + 1, :])
    text_bias = key_bias(256, z, facts[TEXT_ROW : TEXT_ROW + 1, :])
    block = head_block()
    low_row = lanes((1, 128)) < 64
    gtk[...] = jnp.zeros((3, 256, 128), F32)
    gtv[...] = jnp.zeros((3, 256, 128), F32)
    gk[...] = jnp.zeros((3, 512, 128), F32)
    gv[...] = jnp.zeros((3, 512, 128), F32)
    for copy in loads[1:4]:
        copy.wait()

    def head_grads(lo, count):
        n = count * 128
        g = grad_all[lo : lo + count].reshape(n, D)
        low_lane = lanes((n, 128)) < 64
        tiles = []
        for xx in range(2):
            w_cols = w_a[xx, :, :, :, :, 512:768].reshape(D, 256)
            o = mm(g, w_cols)
            gc[xx, lo : lo + count] = o[:, 128:].astype(BF16).reshape(count, 128, 128)
            tiles.append(o[:, :128])
        both = jnp.where(low_lane, pltpu.roll(tiles[0], 64, 1), tiles[1])
        gc[2, lo : lo + count] = both.astype(BF16).reshape(count, 128, 128)

    def back_rows(p, lo, count, kinds):
        n = count * 128
        q = q8[p, lo : lo + count].reshape(n, 128)
        low_rows = lanes((n, 128)) < 64
        grad_q = jnp.zeros((n, 128), F32)
        for text in kinds:
            g = gc[p, lo : lo + count].reshape(n, 128)
            if text:
                g = (g.astype(F32) * facts[pl.ds(GATE_ROW + p, 1), :]).astype(BF16)
            k = tk[p] if text else kk[p].reshape(512, 128)
            v = tv[p] if text else vv[p].reshape(512, 128)
            to_v, to_k = (gtv, gtk) if text else (gv, gk)
            for head in range(2):
                keep = low_rows if head == 0 else jnp.logical_not(low_rows)
                qm = jnp.where(keep, q, jnp.zeros_like(q))
                gm = jnp.where(keep, g, jnp.zeros_like(g))
                here = lanes((n, 128)) == p * 2 + head + 8 * text
                kept = lse_ref[lo : lo + count].reshape(n, 128)
                lse = jnp.sum(jnp.where(here, kept, 0.0), axis=-1, keepdims=True)
                scores = mm_t(qm, k) + (text_bias if text else self_bias)
                probs = jnp.exp(scores - lse)
                grad_probs = mm_t(gm, v)
                delta = jnp.sum(probs * grad_probs, axis=-1, keepdims=True)
                grad_scores = (probs * (grad_probs - delta)).astype(BF16)
                grad_q = grad_q + jnp.where(keep, mm(grad_scores, k), 0.0)
                to_v[p] += mm_rows(probs.astype(BF16), gm)
                to_k[p] += mm_rows(grad_scores, qm)
        if 1 in kinds:
            gq[p, lo * 128 : lo * 128 + n] = grad_q
        else:
            gq[p, lo * 128 : lo * 128 + n] += grad_q

    def over_pairs(lo, count, kinds):
        def step(p, carry):
            back_rows(p, lo, count, kinds)
            return carry

        lax.fori_loop(0, 3, step, 0)

    head_grads(0, 1)
    for copy in loads[4:]:
        copy.wait()
    over_pairs(0, 1, (0, 1))
    tokens.near()
    head_grads(1, 2)
    scat_f.step2()
    over_pairs(1, 2, (1,))
    tokens.far()
    head_grads(3, 1)
    over_pairs(3, 1, (1,))

    def unit_of(raw):
        inverse = lax.rsqrt(head_mean(raw * raw, block) + EPSILON)
        return raw * inverse, inverse

    def back_head(unit, inverse, grad):
        return inverse * (grad - unit * head_mean(grad * unit, block))

    low_text = lanes((256, 128)) < 64
    text_row = jnp.zeros((1, 128), F32)
    grads_k = []
    for p in range(3):
        unit, inverse = unit_of(tkr[p])
        gtk_p = gtk[p]
        text_row = text_row + jnp.sum(gtk_p * unit, axis=0, keepdims=True)
        grads_k.append(back_head(unit, inverse, gtk_p * facts[GAIN_ROW + 2 : GAIN_ROW + 3, :]))
    for xx in range(2):
        tpack[xx, :, 0:128] = grads_k[xx].astype(BF16)
        tpack[xx, :, 256:384] = gtv[xx].astype(BF16)
    tpack[0, :, 128:256] = jnp.where(low_text, grads_k[2], pltpu.roll(gtv[2], 64, 1)).astype(BF16)
    tpack[1, :, 128:256] = jnp.where(low_text, pltpu.roll(grads_k[2], 64, 1), gtv[2]).astype(BF16)

    def caption_grad(i, carry):
        xx = i // 8
        j = i % 8
        grad = mm(cap_flip[tile(2 * j + 1 - c)], tpack[xx])
        dw_c[xx, j // 4, j % 4] = grad.astype(BF16)
        return carry

    lax.fori_loop(0, 8, caption_grad, 0)
    scat_c.to_sibling(0)
    scat_c.to_sibling(2)
    lax.fori_loop(8, 16, caption_grad, 0)
    scat_c.to_sibling(1)
    scat_c.to_sibling(3)
    transpose_into(grad_all, flip)
    over_pairs(1, 2, (0,))
    scat_f.step3()
    over_pairs(3, 1, (0,))
    scat_c.add()
    scat_c.first()
    cos = cos_ref[...].reshape(512, 128)
    sin = sin_ref[...].reshape(512, 128)
    low_head = lanes((512, 128)) < 64
    query_row = jnp.zeros((1, 128), F32)
    key_row = jnp.zeros((1, 128), F32)
    raws = [[], []]
    for p in range(3):
        for i in range(2):
            grad = (gq[p] * 0.125) if i == 0 else gk[p]
            raw = (qr if i == 0 else kr)[p].reshape(512, 128)
            turned = grad * cos - swap_quarters(grad) * sin
            unit, inverse = unit_of(raw)
            row = jnp.sum(turned * unit, axis=0, keepdims=True)
            if i == 0:
                query_row = query_row + row
            else:
                key_row = key_row + row
            result = back_head(unit, inverse, turned * facts[GAIN_ROW + i : GAIN_ROW + i + 1, :])
            if p < 2:
                gpack[p, :, (0 if i == 0 else 256) : (128 if i == 0 else 384)] = result.astype(BF16)
            else:
                raws[i] = result
    gpack[0, :, 128:256] = jnp.where(low_head, raws[0], pltpu.roll(raws[1], 64, 1)).astype(BF16)
    gpack[1, :, 128:256] = jnp.where(low_head, pltpu.roll(raws[0], 64, 1), raws[1]).astype(BF16)
    for xx in range(2):
        gpack[xx, :, 384:512] = gv[xx].astype(BF16)
    gpack[0, :, 512:640] = jnp.where(low_head, gv[2], 0.0).astype(BF16)
    gpack[1, :, 512:640] = jnp.where(low_head, pltpu.roll(gv[2], 64, 1), 0.0).astype(BF16)

    def first_rows(lo, count):
        n = count * 128
        a0 = gpack[0, lo * 128 : lo * 128 + n]
        a1 = gpack[1, lo * 128 : lo * 128 + n]
        def column(xb, carry):
            b0 = w_a[0, xb, :, :, :, 0:640].reshape(768, 640)
            b1 = w_a[1, xb, :, :, :, 0:640].reshape(768, 640)
            total = mm_t(a0, b0) + mm_t(a1, b1)
            part[lo : lo + count, :, tile(xb, 768)] = total.astype(BF16).reshape(count, 128, 768)
            return carry

        lax.fori_loop(0, 2, column, 0)

    def weight_grad(i, carry):
        xx, xb = i // 2, i % 2
        a = first_flip[tile(xb, 768)]
        g = flip[tile(xb, 768)]
        b = cw[xx].reshape(512, 256)
        grad = mm(a, gpack[xx, :, 0:512])
        dw_a[xx, xb, :, :, :, 0:512] = grad.astype(BF16).reshape(4, 2, 96, 512)
        grad = mm(g, b)
        last = grad[:, 0:128] + mm(a, gpack[xx, :, 512:640])
        dw_a[xx, xb, :, :, :, 512:640] = last.astype(BF16).reshape(4, 2, 96, 128)
        dw_a[xx, xb, :, :, :, 640:768] = grad[:, 128:256].astype(BF16).reshape(4, 2, 96, 128)
        return carry

    for xx in range(2):
        lax.fori_loop(2 * xx, 2 * xx + 2, weight_grad, 0)
        scat_a.to_sibling(xx)
        scat_a.to_sibling(xx + 2)
    scat_c.step2()
    sums = ZScatter(send, part, relay, got, right, left)
    first_rows(3, 1)
    sums.far()
    first_rows(1, 2)
    sums.near()
    scat_a.add()
    scat_a.first()
    first_rows(0, 1)
    sums.pass_on()
    scat_c.step3()
    scat_a.step2()
    top, low = scat_f.finish()
    f_out[0:48, :] = top
    f_out[48:96, :] = low
    store(f_out, f_final)

    grad_first = sums.total()

    unit_one, inverse_one = normalize(resid_ref[...].astype(F32))
    scale = 1.0 + mod_ref[0:1, :]
    gain = gains_ref[0:1, :]
    row_sum = jnp.sum(grad_first * unit_one, axis=0, keepdims=True)
    sums_0 = row_sum * gain
    sums_4 = row_sum * scale
    hid_grad[...] = (
        (gmid_ref[...] + norm_back(unit_one, inverse_one, grad_first * scale * gain))
        .astype(BF16)
        .reshape(2, 64, D)
    )
    grad_swap = send(hid_grad.at[1 - xl], hidden_final.at[xl], pair)
    store(hid_grad.at[xl], hidden_final.at[xl])
    mod_msg[...] = jnp.zeros((8, 8, 128), F32)
    gain_msg[...] = jnp.zeros((16, 16, 128), F32)
    for i in range(4):
        row = sums_0 if i == 0 else sums_ref[i : i + 1, :]
        for h in range(2):
            for j in range(6):
                lo = h * 768 + j * 128
                mod_msg[2 * i + h, j : j + 1, :] = row[:, lo : lo + 128]
    folded = [row + pltpu.roll(row, 64, 1) for row in (query_row, key_row, text_row)]
    first_line = jnp.where(low_row, folded[0], folded[1])
    lane = lanes((1, 128))
    second_line = jnp.where(low_row, folded[2], 0.0)
    for p in range(3):
        gate_row = facts[GATE_ROW + p : GATE_ROW + p + 1, :]
        products = gc[p].reshape(512, 128).astype(F32) * other_ref[p].reshape(512, 128)
        values = jnp.sum(products, axis=0, keepdims=True) * (1.0 - gate_row * gate_row)
        for head in range(2):
            keep = low_row if head == 0 else jnp.logical_not(low_row)
            value = jnp.sum(jnp.where(keep, values, 0.0), axis=1, keepdims=True)
            index = (0, 1, 3, 4, 2, 5)[2 * p + head]
            second_line = second_line + jnp.where(lane == 64 + z * 6 + index, value, 0.0)
    gain_rows = jnp.concatenate([sums_4, sums_ref[5:8, :]], axis=0)
    mod_rows = [sums_0] + [sums_ref[i : i + 1, :] for i in range(1, 4)]
    for d in range(16):
        for j in range(3):
            lo = (d % 4) * 384 + j * 128
            gain_msg[d, 8 + j : 9 + j, :] = mod_rows[d // 4][:, lo : lo + 128]
        gain_msg[d, 0:4, 0:96] = gain_rows[:, d * 96 : (d + 1) * 96]
        gain_msg[d, 4:5, :] = first_line
        gain_msg[d, 5:6, :] = second_line
    to_t = [send(mod_msg.at[q[1]], got_mod.at[t], q) for q in t_peers]
    to_dp = [send(gain_msg.at[q[0]], got_gain.at[dp], q) for q in dp_peers]
    got_mod[t] = mod_msg[t]
    got_gain[dp] = gain_msg[dp]
    scat_a.step3()
    for copy in to_t:
        copy.wait_recv()
    g_all[dp, 0] = got_mod[0] + got_mod[2] + got_mod[4] + got_mod[6]
    g_all[dp, 1] = got_mod[1] + got_mod[3] + got_mod[5] + got_mod[7]
    to_all = [send(g_all.at[dp], g_all.at[dp], q) for q in dp_peers]
    for copy in to_dp:
        copy.wait_recv()
    gain_sum[t] = jnp.sum(got_gain[...], axis=0)
    to_rest = [send(gain_sum.at[t], gain_sum.at[t], q) for q in t_peers]
    top, low = scat_a.finish()
    d_out[0:48, :] = top
    d_out[48:96, :] = low
    store(d_out, d_final)
    for copy in to_all + to_rest:
        copy.wait_recv()
    gain_out[...] = jnp.sum(gain_sum[...], axis=0)
    top, low = scat_c.finish()
    c_out[0:128, :] = top
    c_out[128:256, :] = low
    store(c_out, c_final)
    out_swap.wait_recv()
    grad_swap.wait_recv()
    send.drain()
    for copy in stores:
        copy.wait()


def back_call(args, cid):
    S = jax.ShapeDtypeStruct
    vm = pl.BlockSpec(memory_space=VMEM)
    any_ = pl.BlockSpec(memory_space=pl.ANY)
    loaded = args[:19]
    outs = [
        S((96, 768), F32),
        S((96, D), F32),
        S((256, 384), F32),
        S((2, 64, D), BF16),
        S((2, 64, D), BF16),
        S((16, 2, 8, 128), F32),
        S((16, 128), F32),
    ]
    return pl.pallas_call(
        back_kernel,
        out_shape=outs,
        in_specs=[any_] * 21 + [vm] * 4,
        out_specs=[any_] * 5 + [vm] * 2,
        scratch_shapes=[VMEM(a.shape, a.dtype) for a in loaded]
        + [
            VMEM((96, 768), F32),
            VMEM((96, D), F32),
            VMEM((256, 384), F32),
            VMEM((D, 512), BF16),
            VMEM((4, 128, D), BF16),
            VMEM((3, 4, 128, 128), BF16),
            VMEM((3, 512, 128), F32),
            VMEM((3, 512, 128), F32),
            VMEM((3, 512, 128), F32),
            VMEM((3, 256, 128), F32),
            VMEM((3, 256, 128), F32),
            VMEM((2, 512, 640), BF16),
            VMEM((2, 256, 384), BF16),
            VMEM((2, 2, 4, 2, 96, 768), BF16),
            VMEM((2, 2, 4, 256, 384), BF16),
            VMEM((4, 128, D), BF16),
            VMEM((2, 64, D), BF16),
            VMEM((2, 128, D), BF16),
            VMEM((2, 64, D), BF16),
            VMEM((8, 8, 128), F32),
            VMEM((16, 16, 128), F32),
            VMEM((8, 8, 128), F32),
            VMEM((16, 16, 128), F32),
            VMEM((8, 16, 128), F32),
        ]
        + scatter_bufs(96, D)[1:]
        + scatter_bufs(96, 768)
        + scatter_bufs(256, 384)
        + [pltpu.SemaphoreType.DMA((28,))]
        + dma_sems(140),
        compiler_params=pltpu.CompilerParams(
            collective_id=cid, has_side_effects=True, vmem_limit_bytes=62 * 2**20
        ),
        name="attention_back",
    )(*args)


def final_kernel(
    d_in,
    f_in,
    c_in,
    layer_in,
    hidden_in,
    g_in,
    gain_hbm,
    got_in,
    layer,
    hidden,
    ada,
    bias,
    gains,
    qkv,
    heads,
    cap,
    gate,
    out_w,
    ffn,
    down,
    d_ref,
    f_ref,
    c_ref,
    hidden_half,
    g_all,
    gain_in,
    got1,
    units,
    items,
    sems,
):
    loads = []
    for src, dst in (
        (layer_in, layer),
        (hidden_in, hidden_half),
        (got_in, got1),
        (g_in, g_all),
        (gain_hbm, gain_in),
        (d_in, d_ref),
        (f_in, f_ref),
        (c_in, c_ref),
    ):
        copy = pltpu.make_async_copy(src, dst, sems.at[len(loads)])
        copy.start()
        loads.append(copy)
    for copy in loads:
        copy.wait()
    hidden[...] = hidden_half[...].astype(F32)
    qkv[0] = d_ref[:, 0:192]
    qkv[1, :, 0:128] = d_ref[:, 256:384]
    qkv[1, :, 128:192] = d_ref[:, 192:256]
    qkv[2] = d_ref[:, 384:576]
    out_w[0:128, :] = d_ref[:, 640:768].T
    out_w[128:192, :] = d_ref[:, 576:640].T
    ffn[0] = f_ref[:, 0:512]
    ffn[1] = f_ref[:, 512:1024]
    down[...] = f_ref[:, 1024:1536]
    cap[0] = c_ref[:, 0:192].T
    cap[1, 0:128, :] = c_ref[:, 256:384].T
    cap[1, 128:192, :] = c_ref[:, 192:256].T
    for d in range(16):
        units[2 * d : 2 * d + 2, :] = got1[d, 0:2, 0:64]
        for j in range(6):
            items[2 * d : 2 * d + 2, j * 128 : j * 128 + 128] = jnp.concatenate(
                [g_all[d, 0, j : j + 1, :], g_all[d, 1, j : j + 1, :]], axis=0
            )
    unit_rows = units[...].astype(BF16)
    high = items[...].astype(BF16)
    low = (items[...] - high.astype(F32)).astype(BF16)
    ada[...] = mm_rows(unit_rows, high) + mm_rows(unit_rows, low)
    for j in range(3):
        bias[:, j * 128 : j * 128 + 128] = gain_in[8 + j : 9 + j, :]
    gains[...] = gain_in[0:4, 0:96]
    heads[0:1, :] = gain_in[4:5, 0:64]
    heads[1:2, :] = gain_in[4:5, 64:128]
    heads[2:3, :] = gain_in[5:6, 0:64]
    gate[...] = gain_in[5:6, 64:88]


def final_call(args):
    S = jax.ShapeDtypeStruct
    vm = pl.BlockSpec(memory_space=VMEM)
    outs = [
        S((2, 64, D), BF16),
        S((2, 64, D), F32),
        S((64, 768), F32),
        S((1, 384), F32),
        S((4, 96), F32),
        S((3, 96, 192), F32),
        S((3, 64), F32),
        S((2, 192, 256), F32),
        S((1, 24), F32),
        S((192, 96), F32),
        S((2, 96, 512), F32),
        S((96, 512), F32),
    ]
    return pl.pallas_call(
        final_kernel,
        out_shape=outs,
        in_specs=[pl.BlockSpec(memory_space=pl.ANY)] * len(args),
        out_specs=[vm] * len(outs),
        scratch_shapes=[VMEM(a.shape, a.dtype) for a in args[:3] + args[4:]]
        + [VMEM((32, 64), F32), VMEM((32, 768), F32), pltpu.SemaphoreType.DMA((8,))],
        compiler_params=pltpu.CompilerParams(vmem_limit_bytes=62 * 2**20),
        name="final_layout",
    )(*args)


def on_device(
    hidden,
    condition,
    caption,
    lengths,
    frames,
    widths,
    caption_lens,
    cotangent,
    ada_weight,
    ada_bias,
    norm_gains,
    qkv_weight,
    head_gains,
    caption_weight,
    head_gate,
    out_weight,
    ffn_weight,
    down_weight,
):
    (
        w_f,
        w_a,
        cap_flip,
        first_flip,
        q8,
        kk,
        vv,
        qr,
        kr,
        tkr,
        other,
        lse,
        cw,
        cos_t,
        sin_t,
        resid,
        tk,
        tv,
        attn,
        middle,
        second_in,
        cot,
        mod_rows,
        gains,
        got1,
        live,
        facts,
    ) = attention_call(
        [
            hidden[:, 0],
            cotangent[:, 0],
            caption[:, 0],
            condition[:, 0],
            norm_gains,
            ada_weight,
            qkv_weight,
            out_weight,
            ffn_weight,
            down_weight.T,
            jnp.transpose(caption_weight, (0, 2, 1)),
            ada_bias[None],
            head_gains,
            head_gate[None],
            lengths.T,
            frames.T,
            widths.T,
            caption_lens.T,
        ],
        1,
    )
    layer_out, grad_middle, grad_attn_in, dw_half, ffn_sums = ffn_call(
        second_in,
        w_f.reshape(2, D, D),
        middle,
        attn,
        cot.reshape(128, D),
        mod_rows,
        gains,
        live,
        2,
    )
    d_out, f_out, c_out, layer_final, hidden_final, g_all, gain_out = back_call(
        [
            dw_half,
            w_a,
            cap_flip,
            first_flip,
            q8,
            kk,
            vv,
            qr,
            kr,
            tkr,
            other,
            lse,
            cw,
            cos_t,
            sin_t,
            resid,
            tk,
            tv,
            grad_middle,
            grad_attn_in,
            layer_out.reshape(2, 64, D),
            mod_rows,
            gains,
            ffn_sums,
            facts,
        ],
        3,
    )
    (
        layer,
        grad_hidden,
        ada,
        bias,
        norm,
        qkv,
        heads,
        cap,
        gate,
        out_w,
        ffn,
        down,
    ) = final_call(
        [d_out, f_out, c_out, layer_final, hidden_final, g_all, gain_out, got1]
    )
    return (
        layer[:, None],
        grad_hidden[:, None],
        ada,
        bias[0],
        norm,
        qkv,
        heads,
        jnp.transpose(cap, (0, 2, 1)),
        gate[0],
        out_w,
        ffn,
        down.T,
    )


def solution(mesh):
    return jax.shard_map(
        on_device,
        mesh=mesh,
        in_specs=(
            P(None, "dp", "tensor", None),
            P(None, "dp", None),
            P(None, "dp", None, None),
            P(None, "dp"),
            P(None, "dp"),
            P(None, "dp"),
            P(None, "dp"),
            P(None, "dp", "tensor", None),
            P("dp", "tensor"),
            P("dp"),
            P(None, "dp"),
            P(None, "dp", "tensor"),
            P(),
            P(None, "dp", "tensor"),
            P(),
            P("tensor", "dp"),
            P(None, "dp", "tensor"),
            P("tensor", "dp"),
        ),
        out_specs=(
            P(None, "dp", "tensor", None),
            P(None, "dp", "tensor", None),
            P("dp", "tensor"),
            P("dp"),
            P(None, "dp"),
            P(None, "dp", "tensor"),
            P(),
            P(None, "dp", "tensor"),
            P(),
            P("tensor", "dp"),
            P(None, "dp", "tensor"),
            P("tensor", "dp"),
        ),
        check_vma=False,
    )
```

```python
import jax
import jax.numpy as jnp
from jax import lax
from jax.experimental import pallas as pl
from jax.experimental.pallas import tpu as pltpu
from jax.sharding import PartitionSpec as P

D = 1536
H = 24
HD = 64
EPSILON = 1e-05
NEGATIVE = -1e30
MESH = pl.DeviceIdType.MESH
VMEM = pltpu.VMEM
F32 = jnp.float32
BF16 = jnp.bfloat16


def coords():
    dp = lax.axis_index("dp")
    t = lax.axis_index("tensor")
    return dp // 8, t % 2, (dp // 2) % 4, t // 2, dp % 2


def device_of(x, y, z, c):
    return ((x // 2) * 8 + y * 2 + c, z * 2 + x % 2)


def greet_signal(devices):
    barrier = pltpu.get_barrier_semaphore()
    for device in devices:
        pl.semaphore_signal(barrier, inc=1, device_id=device, device_id_type=MESH)


def greet_wait(devices):
    pl.semaphore_wait(pltpu.get_barrier_semaphore(), len(devices))


def greet(devices):
    greet_signal(devices)
    greet_wait(devices)


class Sender:
    def __init__(self, send_sem, recv_sem):
        self.send_sem = send_sem
        self.recv_sem = recv_sem
        self.copies = []

    def __call__(self, src, dst, device):
        k = len(self.copies)
        copy = pltpu.make_async_remote_copy(
            src_ref=src,
            dst_ref=dst,
            send_sem=self.send_sem.at[k],
            recv_sem=self.recv_sem.at[k],
            device_id=device,
            device_id_type=MESH,
        )
        copy.start()
        self.copies.append(copy)
        return copy

    def drain(self):
        for copy in self.copies:
            copy.wait_send()


def dma_sems(n):
    return [pltpu.SemaphoreType.DMA((n,)), pltpu.SemaphoreType.DMA((n,))]


def plane_peers():
    xh, xl, y, z, c = coords()
    x = 2 * xh + xl
    xr, xq = (x + 1) % 4, (x + 3) % 4
    yr, yq = (y + 1) % 4, (y + 3) % 4
    peers = [
        device_of(xr, y, z, c),
        device_of(xq, y, z, c),
        device_of(x, yr, z, c),
        device_of(x, yq, z, c),
        device_of(x, y, z, 1 - c),
        device_of((x + 2) % 4, y, z, c),
        device_of(x, (y + 2) % 4, z, c),
    ]
    return x, y, c, xr, xq, yr, yq, peers


def add_low(a, b):
    return (a.astype(F32) + b.astype(F32)).astype(BF16)


def normalize(values):
    inverse = lax.rsqrt(jnp.mean(values * values, axis=-1, keepdims=True) + EPSILON)
    return (values * inverse, inverse)


def norm_back(unit_values, inverse, gradient):
    return inverse * (
        gradient - unit_values * jnp.mean(gradient * unit_values, axis=-1, keepdims=True)
    )


def swish(values):
    return values * jax.nn.sigmoid(values)


def z_ring():
    xh, xl, y, z, c = coords()
    x = 2 * xh + xl
    return z, device_of(x, y, (z + 1) % 4, c), device_of(x, y, (z + 3) % 4, c)


class ZGather:
    def __init__(self, send, own, every, right, left):
        self.send, self.every, self.right, self.left = send, every, right, left
        half = every.shape[1] // 2
        self.lower, self.upper = pl.ds(0, half), pl.ds(half, half)
        self.a_low = send(own.at[self.lower], every.at[1, self.lower], right)
        self.b_up = send(own.at[self.upper], every.at[2, self.upper], left)
        self.a_up = send(own.at[self.upper], every.at[1, self.upper], right)
        self.b_low = send(own.at[self.lower], every.at[2, self.lower], left)

    def near(self):
        every, lower, upper = self.every, self.lower, self.upper
        self.a_low.wait_recv()
        self.far_low = self.send(every.at[1, lower], every.at[3, lower], self.right)
        self.b_up.wait_recv()
        self.far_up = self.send(every.at[2, upper], every.at[3, upper], self.left)
        self.a_up.wait_recv()
        self.b_low.wait_recv()

    def far(self):
        self.far_low.wait_recv()
        self.far_up.wait_recv()


class ZScatter:
    def __init__(self, send, part, relay, got, right, left):
        self.send, self.part, self.relay, self.got = send, part, relay, got
        self.right, self.left = right, left
        self.lower, self.upper = pl.ds(0, 64), pl.ds(64, 64)
        self.waits = []

    def near(self):
        part, got = self.part, self.got
        self.waits.append(self.send(part.at[2, self.upper], got.at[0, self.upper], self.right))
        self.waits.append(self.send(part.at[1, self.lower], got.at[1, self.lower], self.left))

    def far(self):
        part, relay = self.part, self.relay
        self.relays = []
        for i in range(2):
            rows, low, up = pl.ds(32 * i, 32), pl.ds(32 * i, 32), pl.ds(64 + 32 * i, 32)
            self.relays.append(
                (
                    self.send(part.at[3, low], relay.at[0, rows], self.right),
                    self.send(part.at[3, up], relay.at[1, rows], self.left),
                )
            )

    def pass_on(self):
        part, relay, got = self.part, self.relay, self.got
        for i in range(2):
            rows, low, up = pl.ds(32 * i, 32), pl.ds(32 * i, 32), pl.ds(64 + 32 * i, 32)
            self.relays[i][0].wait_recv()
            part[2, low] = add_low(part[2, low], relay[0, rows])
            self.waits.append(self.send(part.at[2, low], got.at[0, low], self.right))
            self.relays[i][1].wait_recv()
            part[1, up] = add_low(part[1, up], relay[1, rows])
            self.waits.append(self.send(part.at[1, up], got.at[1, up], self.left))

    def total(self):
        for copy in self.waits:
            copy.wait_recv()
        got = self.got
        return self.part[0].astype(F32) + got[0].astype(F32) + got[1].astype(F32)


def mm(a, b):
    return lax.dot_general(a, b, (((1,), (0,)), ((), ())), preferred_element_type=F32)


def mm_t(a, b):
    return lax.dot_general(a, b, (((1,), (1,)), ((), ())), preferred_element_type=F32)


def tile(j, size=256):
    return pl.ds(pl.multiple_of(j * size, size), size)


def transpose_into(src, dst):
    def column(j, carry):
        cols = tile(j, 128)
        for slot in range(4):
            dst[cols, slot * 128 : (slot + 1) * 128] = src[slot, :, cols].T
        return carry

    lax.fori_loop(0, D // 128, column, 0)


class PlaneGather:
    def __init__(self, send, shard, every):
        self.send, self.shard, self.every = send, shard, every
        rows, cols = shard.shape
        half = rows // 2
        self.top, self.low = pl.ds(0, half), pl.ds(half, half)
        self.late = []

    def at(self, xx, yy, *rest):
        return self.every.at[(xx % 2, xx // 2, yy, self.c) + rest]

    def same(self, ref, device):
        return self.send(ref, ref, device)

    def to_sibling(self, ref):
        self.late.append(self.send(ref, ref, self.sibling))

    def start(self, local_sem):
        x, y, c, xr, xq, yr, yq, peers = plane_peers()
        self.x, self.y, self.c = x, y, c
        self.xr, self.xq, self.yr, self.yq = xr, xq, yr, yq
        self.go_xr, self.go_xq, self.go_yr, self.go_yq, self.sibling, go_xo, go_yo = peers
        shard, top, low = self.shard, self.top, self.low
        self.a_r = self.send(shard.at[top], self.at(x, y, top), self.go_xr)
        self.a_l = self.send(shard.at[top], self.at(x, y, top), self.go_xq)
        self.b_r = self.send(shard.at[low], self.at(x, y, low), self.go_yr)
        self.b_l = self.send(shard.at[low], self.at(x, y, low), self.go_yq)
        self.a_o = self.send(shard.at[top], self.at(x, y, top), go_xo)
        self.b_o = self.send(shard.at[low], self.at(x, y, low), go_yo)
        self.late.append(self.send(shard, self.at(x, y), self.sibling))
        self.local = pltpu.make_async_copy(shard, self.at(x, y), local_sem)
        self.local.start()

    def step3(self):
        x, y, c = self.x, self.y, self.c
        every, top, low = self.every, self.top, self.low
        self.local.wait()
        for copy in (self.a_r, self.a_l, self.a_o):
            copy.wait_recv()
        block = every.at[:, :, y, c, top]
        self.g_r = self.same(block, self.go_yr)
        self.g_l = self.same(block, self.go_yq)
        for copy in (self.b_r, self.b_l, self.b_o):
            copy.wait_recv()
        block = every.at[x % 2, x // 2, :, c, low]
        self.h_r = self.same(block, self.go_xr)
        self.h_l = self.same(block, self.go_xq)
        for k in range(1, 4):
            self.to_sibling(self.at((x + k) % 4, y, top))
            self.to_sibling(self.at(x, (y + k) % 4, low))

    def step4(self):
        c, every, top, low = self.c, self.every, self.top, self.low
        xr, xq, yr, yq = self.xr, self.xq, self.yr, self.yq
        self.g_r.wait_recv()
        self.f1 = self.same(every.at[0, :, yq, c, top], self.go_yr)
        self.g_l.wait_recv()
        self.f2 = self.same(every.at[1, :, yr, c, top], self.go_yq)
        self.h_r.wait_recv()
        self.f3 = self.same(every.at[xq % 2, xq // 2, pl.ds(0, 2), c, low], self.go_xr)
        self.h_l.wait_recv()
        self.f4 = self.same(every.at[xr % 2, xr // 2, pl.ds(2, 2), c, low], self.go_xq)
        self.to_sibling(every.at[:, :, yq, c, top])
        self.to_sibling(every.at[:, :, yr, c, top])
        self.to_sibling(every.at[xq % 2, xq // 2, :, c, low])
        self.to_sibling(every.at[xr % 2, xr // 2, :, c, low])

    def step5(self):
        c, every, top, low = self.c, self.every, self.top, self.low
        xo, yo = (self.x + 2) % 4, (self.y + 2) % 4
        for copy in (self.f1, self.f2, self.f3, self.f4):
            copy.wait_recv()
        self.to_sibling(every.at[:, :, yo, c, top])
        self.to_sibling(every.at[xo % 2, xo // 2, :, c, low])

    def finish(self):
        for copy in self.late:
            copy.wait_recv()


OFFSETS = (0, 3, 1, 2)


def lanes(shape):
    return lax.broadcasted_iota(jnp.int32, shape, len(shape) - 1)


def head_block():
    row = lax.broadcasted_iota(jnp.int32, (128, 128), 0) // 64
    col = lax.broadcasted_iota(jnp.int32, (128, 128), 1) // 64
    return jnp.where(row == col, 1.0 / 64.0, 0.0).astype(BF16)


def head_mean(values, block):
    high = values.astype(BF16)
    low = (values - high.astype(F32)).astype(BF16)
    return mm(high, block) + mm(low, block)


def swap_quarters(values):
    second = (lanes(values.shape) % 64) >= 32
    return jnp.where(second, pltpu.roll(values, 32, 1), pltpu.roll(values, 96, 1))


GAIN_ROW, GATE_ROW, LENGTH_ROW, FRAMES_ROW, WIDTH_ROW, TEXT_ROW, BIAS_ROW = 0, 3, 6, 7, 8, 9, 10


def key_bias(total, z, length):
    lane = lanes((1, total))
    if total == 512:
        slot = lane // 128
        block = jnp.where(slot == 0, z, jnp.where(slot == 1, z + 3, jnp.where(slot == 2, z + 1, z + 2)))
        position = (block % 4) * 128 + lane % 128
    else:
        position = lane
    return jnp.where(position.astype(F32) < length[:, :1], 0.0, NEGATIVE)


def fill_rope(cos_ref, sin_ref, z, length, frames, width):
    lane = lanes((128, 128))
    pair = lane % 32
    offset = jnp.where(pair >= 20, 20, jnp.where(pair >= 8, 8, 0))
    size = jnp.where(pair >= 8, 12.0, 8.0)
    freq = jnp.exp((pair - offset).astype(F32) / size * (-9.210340371976184))
    sign = jnp.where(lane % 64 >= 32, 1.0, -1.0)
    row_size = width
    per_frame = jnp.floor((length + frames - 0.5) / frames)
    row = lax.broadcasted_iota(jnp.int32, (128, 128), 0).astype(F32)
    for slot in range(4):
        start = (((z + OFFSETS[slot]) % 4) * 128).astype(F32)
        position = row + start
        frame = jnp.floor((position + 0.5) / per_frame)
        within = position - frame * per_frame
        row_pos = jnp.floor((within + 0.5) / row_size)
        col_pos = within - row_pos * row_size
        chosen = jnp.where(pair >= 20, col_pos, jnp.where(pair >= 8, row_pos, frame))
        angle = chosen * freq
        cos_ref[slot] = jnp.cos(angle)
        sin_ref[slot] = jnp.sin(angle) * sign


def attention_kernel(
    hid_ref,
    cot_ref,
    cap_hbm,
    cond_ref,
    gain_in,
    ada_ref,
    qkv_ref,
    out_w_ref,
    ffn_w_ref,
    down_t_ref,
    cap_t_ref,
    bias_ref,
    head_gain_ref,
    head_gate_ref,
    len_ref,
    frame_ref,
    width_ref,
    tlen_ref,
    w_f,
    w_a_out,
    cap_flip_out,
    first_flip_out,
    q8_out,
    kk_out,
    vv_out,
    qr_out,
    kr_out,
    tkr_out,
    other_out,
    lse_out,
    cw_out,
    cos_out,
    sin_out,
    resid_out,
    tk_out,
    tv_out,
    attn_out,
    mid_out,
    second_out,
    cot_out,
    mod_ref,
    gains_ref,
    got1,
    live_ref,
    facts,
    w_a,
    cap_flip,
    first_flip,
    q8,
    kk,
    vv,
    qr,
    kr,
    tkr,
    other_ref,
    lse_ref,
    cw,
    cos_ref,
    sin_ref,
    resid_ref,
    tk,
    tv,
    attn_ref,
    mid_ref,
    second_ref,
    first,
    own_ref,
    sh_a,
    sh_f,
    sh_c,
    w_c,
    cap,
    hid_all,
    hid_own,
    msg,
    sent2,
    got2,
    got3,
    mixed,
    part,
    relay,
    got,
    local_sems,
    ss,
    rs,
):
    dp = lax.axis_index("dp")
    t = lax.axis_index("tensor")
    xh, xl, y, z, c = coords()
    _, right, left = z_ring()
    pair = device_of(2 * xh + 1 - xl, y, z, c)
    dp_peers = [((dp + k) % 16, t) for k in range(1, 16)]
    t_peers = [(dp, (t + k) % 8) for k in range(1, 8)]
    outer_x = device_of((2 * xh + xl + 3 - 2 * xl) % 4, y, z, c)
    everyone = dp_peers + t_peers + [outer_x]
    greet_signal(everyone)
    load_cap = pltpu.make_async_copy(cap_hbm.at[xl], cap, local_sems.at[0])
    load_cap.start()
    load_hid = pltpu.make_async_copy(hid_ref.at[xl], hid_own.at[xl], local_sems.at[4])
    load_hid.start()
    flushes = []

    def flush(src, dst):
        copy = pltpu.make_async_copy(src, dst, local_sems.at[5 + len(flushes)])
        copy.start()
        flushes.append(copy)

    flush(cot_ref.at[xl], cot_out.at[xl])
    facts[...] = jnp.zeros((16, 128), F32)
    for i in range(3):
        gain = head_gain_ref[i : i + 1, :].astype(F32)
        facts[i : i + 1, 0:64] = gain
        facts[i : i + 1, 64:128] = gain
        facts[BIAS_ROW + i : BIAS_ROW + i + 1, :] = bias_ref[i * 128 : i * 128 + 128].astype(F32).reshape(1, 128)
    gates = jnp.tanh(head_gate_ref[...].astype(F32))
    gate_lane = lanes((1, 24))
    low_row = lanes((1, 128)) < 64
    for p in range(3):
        a, b = [
            jnp.sum(jnp.where(gate_lane == z * 6 + h, gates, 0.0), axis=1, keepdims=True)
            for h in ((0, 1), (3, 4), (2, 5))[p]
        ]
        facts[GATE_ROW + p : GATE_ROW + p + 1, :] = jnp.where(low_row, a, b)
    for i, ref in enumerate((len_ref, frame_ref, width_ref, tlen_ref)):
        count = jnp.where(xl == 0, ref[:, 0:1], ref[:, 1:2]).astype(F32)
        facts[LENGTH_ROW + i : LENGTH_ROW + i + 1, :] = jnp.broadcast_to(count, (1, 128))
    unit = swish(cond_ref[...].astype(F32)).astype(BF16).astype(F32)
    msg[...] = jnp.zeros((16, 8, 128), F32)
    gain_rows = gain_in[...].astype(F32)
    for d in range(16):
        msg[d, 0:2, 0:64] = unit[:, d * 64 : (d + 1) * 64]
        msg[d, 4:8, 0:96] = gain_rows
    qs, ks, vs = qkv_ref[0], qkv_ref[1], qkv_ref[2]
    os = out_w_ref[...].T
    sh_a[...] = jnp.concatenate(
        [qs, ks[:, 128:192], ks[:, 0:128], vs, os[:, 128:192], os[:, 0:128]],
        axis=1,
    )
    ck, cv = cap_t_ref[0].T, cap_t_ref[1].T
    sh_c[...] = jnp.concatenate([ck, cv[:, 128:192], cv[:, 0:128]], axis=1)
    greet_wait(everyone)

    send = Sender(ss, rs)
    round1 = [send(msg.at[p[0]], got1.at[dp], p) for p in dp_peers]
    swap = send(hid_ref.at[1 - xl], hid_own.at[xl], pair)
    near_r1 = send(hid_ref.at[xl], hid_all.at[1, xl], right)
    near_l1 = send(hid_ref.at[xl], hid_all.at[2, xl], left)
    ga = PlaneGather(send, sh_a, w_a)
    gc = PlaneGather(send, sh_c, w_c)
    gf = PlaneGather(send, sh_f, w_f)
    ga.start(local_sems.at[1])
    got1[dp] = msg[dp]
    sh_f[:, 0:512] = ffn_w_ref[0]
    sh_f[:, 512:1024] = ffn_w_ref[1]
    sh_f[:, 1024:1536] = down_t_ref[...]
    length = facts[LENGTH_ROW : LENGTH_ROW + 1, :]
    text_len = facts[TEXT_ROW : TEXT_ROW + 1, :]
    for copy in round1:
        copy.wait_recv()
    rows = got1[...].reshape(128, 128)[:, :64].astype(BF16)
    here = t == dp // 2
    low_bias = jnp.where(jnp.logical_and(here, dp % 2 == 0), 1.0, 0.0)
    high_bias = jnp.where(jnp.logical_and(here, dp % 2 == 1), 1.0, 0.0)
    terms = mm(rows, ada_ref[...])
    bias = [facts[BIAS_ROW + j : BIAS_ROW + j + 1, :] for j in range(3)]
    bias = [row * low_bias for row in bias] + [row * high_bias for row in bias]
    for d in range(16):
        for j in range(6):
            sent2[d, 2 * j : 2 * j + 2, :] = terms[8 * d : 8 * d + 2, 128 * j : 128 * j + 128] + bias[j]
    round2 = [send(sent2.at[p[0]], got2.at[dp], p) for p in dp_peers]
    got2[dp] = sent2[dp]
    load_hid.wait()
    swap.wait_recv()
    near_r2 = send(hid_own.at[1 - xl], hid_all.at[1, 1 - xl], right)
    near_l2 = send(hid_own.at[1 - xl], hid_all.at[2, 1 - xl], left)
    hid_all[0] = hid_own[...]
    for copy in round2:
        copy.wait_recv()
    got3[t] = jnp.sum(got2[...], axis=0)
    round3 = [send(got3.at[t], got3.at[t], p) for p in t_peers]
    ga.step3()
    gc.start(local_sems.at[2])
    fill_rope(
        cos_ref,
        sin_ref,
        z,
        length,
        facts[FRAMES_ROW : FRAMES_ROW + 1, :],
        facts[WIDTH_ROW : WIDTH_ROW + 1, :],
    )
    flush(cos_ref, cos_out)
    flush(sin_ref, sin_out)
    near_r1.wait_recv()
    near_r2.wait_recv()
    far_r = send(hid_all.at[1, 0], hid_all.at[3, 0], right)
    near_l1.wait_recv()
    near_l2.wait_recv()
    far_l = send(hid_all.at[2, 1], hid_all.at[3, 1], left)
    for d in range(16):
        gains_ref[0:4, d * 96 : (d + 1) * 96] = got1[d, 4:8, 0:96]
    gains_ref[4:8, :] = jnp.zeros((4, D), F32)
    slot_row = lax.broadcasted_iota(jnp.int32, (128, 128), 0) + z * 128
    live_ref[...] = jnp.where(slot_row.astype(F32) < length, 1.0, 0.0)
    for copy in round3:
        copy.wait_recv()
    for i in range(4):
        for h in range(2):
            block = got3[2 * i + h]
            for j in range(6):
                lo = h * 768 + j * 128
                mod_ref[i : i + 1, lo : lo + 128] = jnp.where(
                    xl == 0, block[2 * j : 2 * j + 1], block[2 * j + 1 : 2 * j + 2]
                )
    mod_ref[4:8, :] = jnp.zeros((4, D), F32)
    factor = gains_ref[0:1, :] * (1.0 + mod_ref[0:1, :])

    def scale_rows(slot, carry):
        unit_rows, _ = normalize(hid_all[slot].reshape(128, D).astype(F32))
        first[slot] = (unit_rows * factor).astype(BF16)
        return carry

    load_cap.wait()

    def flip_caption(j, carry):
        rows = tile(j, 128)
        cap_flip[rows, 0:128] = cap[0:128, rows].T
        cap_flip[rows, 128:256] = cap[128:256, rows].T
        return carry

    lax.fori_loop(0, 3, scale_rows, 0)
    ga.step4()
    gc.step3()
    gf.start(local_sems.at[3])
    far_r.wait_recv()
    far_l.wait_recv()
    scale_rows(3, 0)
    resid_ref[...] = hid_all[0].reshape(128, D)
    flush(resid_ref, resid_out)
    transpose_into(first, first_flip)
    flush(first_flip, first_flip_out)
    lax.fori_loop(0, 32, flip_caption, 0)
    flush(cap_flip, cap_flip_out)
    ga.step5()
    ga.finish()
    flush(w_a, w_a_out)

    x_rows = first[...].reshape(512, D)
    low_head = lanes((512, 128)) < 64

    def project(xx, cols):
        w_cols = w_a[xx, :, :, :, :, cols].reshape(D, cols.stop - cols.start)
        return mm(x_rows, w_cols)

    def project_side(xx, carry):
        p = project(xx, slice(0, 256))
        qr[xx] = p[:, :128].reshape(4, 128, 128)
        mixed[0, xx] = p[:, 128:]
        p = project(xx, slice(256, 512))
        kr[xx] = p[:, :128].reshape(4, 128, 128)
        vv[xx] = p[:, 128:].astype(BF16).reshape(4, 128, 128)
        mixed[1, xx] = project(xx, slice(512, 640))
        return carry

    lax.fori_loop(0, 2, project_side, 0)
    x0, x1 = mixed[0, 0], mixed[0, 1]
    qr[2] = jnp.where(low_head, x0, pltpu.roll(x1, 64, 1)).reshape(4, 128, 128)
    kr[2] = jnp.where(low_head, pltpu.roll(x0, 64, 1), x1).reshape(4, 128, 128)
    x0, x1 = mixed[1, 0], mixed[1, 1]
    vv[2] = jnp.where(low_head, x0, pltpu.roll(x1, 64, 1)).astype(BF16).reshape(4, 128, 128)
    block = head_block()
    cos = cos_ref[...].reshape(512, 128)
    sin = sin_ref[...].reshape(512, 128)

    def turned(raw, gain):
        raw = raw.reshape(512, 128)
        v = raw * lax.rsqrt(head_mean(raw * raw, block) + EPSILON) * gain
        return v * cos + swap_quarters(v) * sin

    for p in range(3):
        q = turned(qr[p], facts[GAIN_ROW : GAIN_ROW + 1, :]).astype(BF16)
        q8[p] = (q.astype(F32) * 0.125).astype(BF16).reshape(4, 128, 128)
        k = turned(kr[p], facts[GAIN_ROW + 1 : GAIN_ROW + 2, :])
        kk[p] = k.astype(BF16).reshape(4, 128, 128)
    for src, dst in ((q8, q8_out), (kk, kk_out), (vv, vv_out), (qr, qr_out), (kr, kr_out)):
        flush(src, dst)

    self_bias = key_bias(512, z, length)
    text_bias = key_bias(256, z, text_len)
    lse_ref[...] = jnp.zeros((4, 128, 128), F32)

    def attend_rows(p, text, b):
        slots = pl.ds(b * 2, 2)
        q = q8[p, slots].reshape(256, 128)
        k = tk[p] if text else kk[p].reshape(512, 128)
        v = tv[p] if text else vv[p].reshape(512, 128)
        low_rows = lanes((256, 128)) < 64
        mix = jnp.zeros((256, 128), F32)
        for head in range(2):
            keep = low_rows if head == 0 else jnp.logical_not(low_rows)
            qm = jnp.where(keep, q, jnp.zeros_like(q))
            scores = mm_t(qm, k) + (text_bias if text else self_bias)
            top = jnp.max(scores, axis=-1, keepdims=True)
            e = jnp.exp(scores - top)
            total = jnp.sum(e, axis=-1, keepdims=True)
            probs = (e * (1.0 / total)).astype(BF16)
            mix = mix + jnp.where(keep, mm(probs, v), 0.0)
            here = lanes((256, 128)) == p * 2 + head + 8 * text
            old = lse_ref[slots].reshape(256, 128)
            lse_ref[slots] = jnp.where(here, top + jnp.log(total), old).reshape(2, 128, 128)
        if not text:
            own_ref[p, slots] = mix.reshape(2, 128, 128)
            return
        other_ref[p, slots] = mix.reshape(2, 128, 128)
        gate = facts[pl.ds(GATE_ROW + p, 1), :]
        both = own_ref[p, slots].reshape(256, 128) + gate * mix
        own_ref[p, slots] = both.reshape(2, 128, 128)

    def attend(lo, hi, text):
        def step(i, carry):
            attend_rows(i // 2, text, i % 2)
            return carry

        lax.fori_loop(2 * lo, 2 * hi, step, 0)

    attend(0, 1, False)
    gc.step4()
    gf.step3()
    cot_swap = send(cot_ref.at[1 - xl], cot_out.at[xl], pair)
    attend(1, 3, False)
    gc.step5()
    gc.finish()
    low_text = lanes((256, 128)) < 64

    def text_side(xx, carry):
        total = mm(cap[:, 0:2048], w_c[xx, 0].reshape(2048, 384))
        total = total + mm(cap[:, 2048:4096], w_c[xx, 1].reshape(2048, 384))
        tkr[xx] = total[:, 0:128]
        tv[xx] = total[:, 256:384].astype(BF16)
        mixed[0, xx, 0:256, :] = total[:, 128:256]
        return carry

    lax.fori_loop(0, 2, text_side, 0)
    x0, x1 = mixed[0, 0, 0:256, :], mixed[0, 1, 0:256, :]
    tkr[2] = jnp.where(low_text, x0, pltpu.roll(x1, 64, 1))
    tv[2] = jnp.where(low_text, pltpu.roll(x0, 64, 1), x1).astype(BF16)
    flush(tv, tv_out)
    for p in range(3):
        raw = tkr[p]
        gain = facts[GAIN_ROW + 2 : GAIN_ROW + 3, :]
        tk[p] = (raw * lax.rsqrt(head_mean(raw * raw, block) + EPSILON) * gain).astype(BF16)
    flush(tkr, tkr_out)
    flush(tk, tk_out)
    attend(0, 3, True)
    for p in range(2):
        cw[p, :, :, 128:256] = own_ref[p].astype(BF16)
    both = own_ref[2].reshape(512, 128)
    zero = jnp.zeros_like(both)
    moved = pltpu.roll(both, 64, 1)
    cw[0, :, :, 0:128] = jnp.where(low_head, zero, moved).astype(BF16).reshape(4, 128, 128)
    cw[1, :, :, 0:128] = jnp.where(low_head, zero, both).astype(BF16).reshape(4, 128, 128)
    flush(lse_ref, lse_out)
    flush(other_ref, other_out)
    flush(cw, cw_out)

    def out_rows(lo, count):
        n = count * 128
        a0 = cw[0, lo : lo + count].reshape(n, 256)
        a1 = cw[1, lo : lo + count].reshape(n, 256)
        def column(xb, carry):
            b0 = w_a[0, xb, :, :, :, 512:768].reshape(768, 256)
            b1 = w_a[1, xb, :, :, :, 512:768].reshape(768, 256)
            total = mm_t(a0, b0) + mm_t(a1, b1)
            part[lo : lo + count, :, tile(xb, 768)] = total.astype(BF16).reshape(count, 128, 768)
            return carry

        lax.fori_loop(0, 2, column, 0)

    sums = ZScatter(send, part, relay, got, right, left)
    out_rows(3, 1)
    sums.far()
    out_rows(1, 2)
    sums.near()
    out_rows(0, 1)
    gf.step4()
    sums.pass_on()
    gf.step5()
    attn = sums.total()
    attn_ref[...] = attn
    flush(attn_ref, attn_out)
    unit_two, _ = normalize(attn)
    live = live_ref[...][:, :1]
    middle = resid_ref[...].astype(F32) + live * jnp.tanh(mod_ref[1:2, :]) * unit_two * gains_ref[1:2, :]
    mid_ref[...] = middle
    flush(mid_ref, mid_out)
    unit_three, _ = normalize(middle)
    second_ref[...] = (unit_three * gains_ref[2:3, :] * (1.0 + mod_ref[2:3, :])).astype(BF16)
    flush(second_ref, second_out)
    cot_swap.wait_recv()
    gf.finish()
    send.drain()
    for copy in flushes:
        copy.wait()


def attention_call(args, cid):
    S = jax.ShapeDtypeStruct
    vm = pl.BlockSpec(memory_space=VMEM)
    any_ = pl.BlockSpec(memory_space=pl.ANY)
    pair = (3, 4, 128, 128)
    saved = [
        ((2, 2, 4, 2, 96, 768), BF16),
        ((4096, 256), BF16),
        ((D, 512), BF16),
        (pair, BF16),
        (pair, BF16),
        (pair, BF16),
        (pair, F32),
        (pair, F32),
        ((3, 256, 128), F32),
        (pair, F32),
        ((4, 128, 128), F32),
        ((2, 4, 128, 256), BF16),
        ((4, 128, 128), F32),
        ((4, 128, 128), F32),
        ((128, D), BF16),
        ((3, 256, 128), BF16),
        ((3, 256, 128), BF16),
        ((128, D), F32),
        ((128, D), F32),
        ((128, D), BF16),
    ]
    outs = [
        ((8, D), F32),
        ((8, D), F32),
        ((16, 8, 128), F32),
        ((128, 128), F32),
        ((16, 128), F32),
    ]
    return pl.pallas_call(
        attention_kernel,
        out_shape=[S((2, 2, 4, 2, 96, D), BF16)]
        + [S(*o) for o in saved]
        + [S((2, 64, D), BF16)]
        + [S(*o) for o in outs],
        in_specs=[any_] * 3 + [vm] * 15,
        out_specs=[any_] * (2 + len(saved)) + [vm] * len(outs),
        scratch_shapes=[VMEM(*o) for o in saved]
        + [
            VMEM((4, 128, D), BF16),
            VMEM(pair, F32),
            VMEM((96, 768), BF16),
            VMEM((96, D), BF16),
            VMEM((256, 384), BF16),
            VMEM((2, 2, 4, 2, 256, 384), BF16),
            VMEM((256, 4096), BF16),
            VMEM((4, 2, 64, D), BF16),
            VMEM((2, 64, D), BF16),
            VMEM((16, 8, 128), F32),
            VMEM((16, 16, 128), F32),
            VMEM((16, 16, 128), F32),
            VMEM((8, 16, 128), F32),
            VMEM((2, 2, 512, 128), F32),
            VMEM((4, 128, D), BF16),
            VMEM((2, 64, D), BF16),
            VMEM((2, 128, D), BF16),
            pltpu.SemaphoreType.DMA((28,)),
        ]
        + dma_sems(160),
        compiler_params=pltpu.CompilerParams(
            collective_id=cid, has_side_effects=True, vmem_limit_bytes=58 * 2**20
        ),
        name="attention",
    )(*args)


def ffn_kernel(
    x_ref,
    w_hbm,
    mid_in,
    attn_in,
    cot_in,
    mod_ref,
    gain_ref,
    live_ref,
    out_out,
    gmid_out,
    gattn_out,
    dw_half,
    sums_ref,
    mid_ref,
    attn_ref,
    cot_ref,
    out_ref,
    gmid_ref,
    gattn_ref,
    w,
    dw_ref,
    dw_got,
    x_all,
    g_all,
    act,
    dgate,
    dup,
    gpre,
    part1,
    part2,
    relay1,
    relay2,
    got1,
    got2,
    flip,
    flip_g,
    own_g,
    w_sem,
    out_sems,
    ss,
    rs,
):
    z, right, left = z_ring()
    load = pltpu.make_async_copy(w_hbm, w, w_sem)
    load.start()
    loads = []
    for src, dst in ((x_ref, x_all.at[0]), (mid_in, mid_ref), (attn_in, attn_ref), (cot_in, cot_ref)):
        copy = pltpu.make_async_copy(src, dst, out_sems.at[4 + len(loads)])
        copy.start()
        loads.append(copy)
    stores = []

    def store(src, dst):
        copy = pltpu.make_async_copy(src, dst, out_sems.at[8 + len(stores)])
        copy.start()
        stores.append(copy)

    xh, xl, y, _, c = coords()
    sibling = device_of(2 * xh + xl, y, z, 1 - c)
    greet([right, left, sibling])
    send = Sender(ss, rs)
    one = ZGather(send, x_ref, x_all, right, left)
    for copy in loads:
        copy.wait()
    load.wait()

    def pre(lo, count):
        rows = count * 128
        x = x_all[lo : lo + count].reshape(rows, D)

        def column(i, carry):
            xx, j = i // 2, i % 2
            g = mm(x, w[xx, :, tile(j)])
            u = mm(x, w[xx, :, tile(j + 2)])
            s = jax.nn.sigmoid(g)
            gs = g * s
            act[xx, lo : lo + count, :, tile(j)] = (gs * u).astype(BF16).reshape(count, 128, 256)
            dgate[xx, lo : lo + count, :, tile(j)] = (u * s * (1.0 + g * (1.0 - s))).reshape(count, 128, 256)
            dup[xx, lo : lo + count, :, tile(j)] = gs.reshape(count, 128, 256)
            return carry

        lax.fori_loop(0, 4, column, 0)

    def down(lo, count):
        rows = count * 128
        a0 = act[0, lo : lo + count].reshape(rows, 512)
        a1 = act[1, lo : lo + count].reshape(rows, 512)

        def column(j, carry):
            cols = tile(j)
            total = mm_t(a0, w[0, cols, 1024:1536]) + mm_t(a1, w[1, cols, 1024:1536])
            part1[lo : lo + count, :, cols] = total.astype(BF16).reshape(count, 128, 256)
            return carry

        lax.fori_loop(0, D // 256, column, 0)

    sum1 = ZScatter(send, part1, relay1, got1, right, left)
    pre(0, 1)
    one.near()
    pre(1, 2)
    down(1, 2)
    sum1.near()
    one.far()
    pre(3, 1)
    down(3, 1)
    sum1.far()
    down(0, 1)
    transpose_into(x_all, flip)
    sum1.pass_on()
    ffn_total = sum1.total()

    live = live_ref[...][:, :1]
    mod = mod_ref[...]
    gains = gain_ref[...]
    gate_f = jnp.tanh(mod[3:4])
    middle = mid_ref[...]
    unit_four, inverse_four = normalize(ffn_total)
    out_ref[...] = (middle + live * gate_f * unit_four * gains[3:4]).astype(BF16)
    store(out_ref, out_out)
    grad_top = cot_ref[...].astype(F32)
    weighted = grad_top * live
    part_four = jnp.sum(weighted * unit_four, axis=0, keepdims=True)
    own_g[...] = norm_back(unit_four, inverse_four, weighted * gate_f * gains[3:4]).astype(BF16)
    two = ZGather(send, own_g, g_all, right, left)
    g_all[0] = own_g[...]
    sums_ref[3:4, :] = part_four * gains[3:4] * (1.0 - gate_f * gate_f)
    sums_ref[7:8, :] = part_four * gate_f

    def back(lo, count):
        rows = count * 128
        g = g_all[lo : lo + count].reshape(rows, D)

        def column(i, carry):
            xx, j = i // 2, i % 2
            ga = mm(g, w[xx, :, tile(j + 4)])
            dg = dgate[xx, lo : lo + count, :, tile(j)].reshape(rows, 256)
            du = dup[xx, lo : lo + count, :, tile(j)].reshape(rows, 256)
            gpre[xx, lo : lo + count, :, tile(j)] = (ga * dg).astype(BF16).reshape(count, 128, 256)
            gpre[xx, lo : lo + count, :, tile(j + 2)] = (ga * du).astype(BF16).reshape(count, 128, 256)
            return carry

        lax.fori_loop(0, 4, column, 0)

    def back_in(lo, count):
        rows = count * 128
        a0 = gpre[0, lo : lo + count].reshape(rows, 1024)
        a1 = gpre[1, lo : lo + count].reshape(rows, 1024)

        def column(j, carry):
            cols = tile(j)
            total = mm_t(a0, w[0, cols, 0:1024]) + mm_t(a1, w[1, cols, 0:1024])
            part2[lo : lo + count, :, cols] = total.astype(BF16).reshape(count, 128, 256)
            return carry

        lax.fori_loop(0, D // 256, column, 0)

    def weight_grad(xx):
        def column(i, carry):
            j, xb = i // 2, i % 2
            b = gpre[xx, :, :, tile(j)].reshape(512, 256)
            grad = mm(flip[tile(xb, 768), :], b)
            dw_ref[xx, xb, :, :, :, tile(j)] = grad.astype(BF16).reshape(4, 2, 96, 256)
            return carry

        lax.fori_loop(0, 8, column, 0)

        def down_column(i, carry):
            j, xb = i // 2, i % 2
            b = act[xx, :, :, tile(j)].reshape(512, 256)
            grad = mm(flip_g[tile(xb, 768), :], b)
            dw_ref[xx, xb, :, :, :, tile(j + 4)] = grad.astype(BF16).reshape(4, 2, 96, 256)
            return carry

        lax.fori_loop(0, 4, down_column, 0)
        return [
            send(dw_ref.at[xx, xb, :, 1 - c], dw_got.at[xx, xb], sibling) for xb in range(2)
        ]

    def add_sibling(xx, copies):
        for xb in range(2):
            copies[xb].wait_recv()

            def add(j, carry, xb=xb):
                dw_got[xx, xb, j] = add_low(dw_got[xx, xb, j], dw_ref[xx, xb, j, c])
                return carry

            lax.fori_loop(0, 4, add, 0)
            store(dw_got.at[xx, xb], dw_half.at[xx, xb])

    sum2 = ZScatter(send, part2, relay2, got2, right, left)
    back(0, 1)
    two.near()
    back(1, 2)
    back_in(1, 2)
    sum2.near()
    two.far()
    back(3, 1)
    back_in(3, 1)
    sum2.far()
    back_in(0, 1)
    transpose_into(g_all, flip_g)
    to_sibling0 = weight_grad(0)
    sum2.pass_on()
    to_sibling1 = weight_grad(1)
    add_sibling(0, to_sibling0)
    grad_second = sum2.total()

    scale_f = mod[2:3]
    unit_three, inverse_three = normalize(middle)
    sum_three = jnp.sum(grad_second * unit_three, axis=0, keepdims=True)
    sums_ref[2:3, :] = sum_three * gains[2:3]
    sums_ref[6:7, :] = sum_three * (1.0 + scale_f)
    grad_middle = grad_top + norm_back(
        unit_three, inverse_three, grad_second * (1.0 + scale_f) * gains[2:3]
    )
    gmid_ref[...] = grad_middle
    store(gmid_ref, gmid_out)
    gate_a = jnp.tanh(mod[1:2])
    unit_two, inverse_two = normalize(attn_ref[...])
    weighted_mid = grad_middle * live
    sum_two = jnp.sum(weighted_mid * unit_two, axis=0, keepdims=True)
    sums_ref[1:2, :] = sum_two * gains[1:2] * (1.0 - gate_a * gate_a)
    sums_ref[5:6, :] = sum_two * gate_a
    sums_ref[0:1, :] = jnp.zeros((1, D), F32)
    sums_ref[4:5, :] = jnp.zeros((1, D), F32)
    gattn_ref[...] = norm_back(unit_two, inverse_two, weighted_mid * gate_a * gains[1:2]).astype(BF16)
    store(gattn_ref, gattn_out)
    add_sibling(1, to_sibling1)
    send.drain()
    for copy in stores:
        copy.wait()


def ffn_call(second_in, w_f, middle, attn, cot, mod_rows, gains, live, cid):
    S = jax.ShapeDtypeStruct
    vm = pl.BlockSpec(memory_space=VMEM)
    any_ = pl.BlockSpec(memory_space=pl.ANY)
    return pl.pallas_call(
        ffn_kernel,
        out_shape=[
            S((128, D), BF16),
            S((128, D), F32),
            S((128, D), BF16),
            S((2, 2, 4, 96, D), BF16),
            S((8, D), F32),
        ],
        in_specs=[any_] * 5 + [vm] * 3,
        out_specs=[any_] * 4 + [vm],
        scratch_shapes=[
            VMEM((128, D), F32),
            VMEM((128, D), F32),
            VMEM((128, D), BF16),
            VMEM((128, D), BF16),
            VMEM((128, D), F32),
            VMEM((128, D), BF16),
            VMEM((2, D, D), BF16),
            VMEM((2, 2, 4, 2, 96, D), BF16),
            VMEM((2, 2, 4, 96, D), BF16),
            VMEM((4, 128, D), BF16),
            VMEM((4, 128, D), BF16),
            VMEM((2, 4, 128, 512), BF16),
            VMEM((2, 4, 128, 512), F32),
            VMEM((2, 4, 128, 512), F32),
            VMEM((2, 4, 128, 1024), BF16),
            VMEM((4, 128, D), BF16),
            VMEM((4, 128, D), BF16),
            VMEM((2, 64, D), BF16),
            VMEM((2, 64, D), BF16),
            VMEM((2, 128, D), BF16),
            VMEM((2, 128, D), BF16),
            VMEM((D, 512), BF16),
            VMEM((D, 512), BF16),
            VMEM((128, D), BF16),
            pltpu.SemaphoreType.DMA,
            pltpu.SemaphoreType.DMA((16,)),
        ]
        + dma_sems(40),
        compiler_params=pltpu.CompilerParams(
            collective_id=cid, has_side_effects=True, vmem_limit_bytes=56 * 2**20
        ),
        name="ffn",
    )(second_in, w_f, middle, attn, cot, mod_rows, gains, live)


def pick(array, index):
    return lax.dynamic_index_in_dim(array, index, 0, keepdims=False)


def dot(spec, a, b):
    return jnp.einsum(spec, a, b, preferred_element_type=F32)


class PlaneScatter:
    def __init__(self, send, grads, own, bufs):
        self.send, self.grads, self.own = send, grads, own
        self.sib, self.ra, self.rb, self.ga, self.gb, self.ha, self.hb = bufs
        rows, cols = self.sib.shape[3:]
        self.rows, self.cols = rows, cols
        self.half = half = rows // 2
        self.top, self.low = pl.ds(0, half), pl.ds(half, half)
    def setup(self):
        self.where = plane_peers()
        self.go_xr, self.go_xq, self.go_yr, self.go_yq, self.sibling, self.go_xo, self.go_yo = self.where[7]
        self.parts = {}

    def to_sibling(self, k):
        block = self.grads.at[k % 2, k // 2]
        if self.own is None:
            block = self.grads.at[k % 2, k // 2, :, 1 - self.where[2]]
        self.parts[k] = self.send(block, self.sib.at[k % 2, k // 2], self.sibling)

    def add(self):
        c, sib, own, grads = self.where[2], self.sib, self.own, self.grads
        for k in self.parts:
            self.parts[k].wait_recv()

            def add_sibling(j, carry, k=k):
                if own is None:
                    mine = grads[k % 2, k // 2, j, c]
                else:
                    mine = own(k % 2, k // 2, j)
                sib[k % 2, k // 2, j] = add_low(sib[k % 2, k // 2, j], mine)
                return carry

            lax.fori_loop(0, 4, add_sibling, 0)

    def first(self):
        x, y, c, xr, xq, yr, yq, _ = self.where
        sib, send = self.sib, self.send
        xo, yo = (x + 2) % 4, (y + 2) % 4
        self.t1 = send(sib.at[0, :, yo, self.top], self.ra.at[pl.ds(0, 2)], self.go_yr)
        self.t2 = send(sib.at[1, :, yo, self.top], self.ra.at[pl.ds(2, 2)], self.go_yq)
        self.l1 = send(sib.at[xo % 2, xo // 2, pl.ds(0, 2), self.low], self.rb.at[pl.ds(0, 2)], self.go_xr)
        self.l2 = send(sib.at[xo % 2, xo // 2, pl.ds(2, 2), self.low], self.rb.at[pl.ds(2, 2)], self.go_xq)

    def step2(self):
        x, y, c, xr, xq, yr, yq, _ = self.where
        sib, send, top, low = self.sib, self.send, self.top, self.low
        ra, rb = self.ra, self.rb
        self.t1.wait_recv()
        for j in range(2):
            sib[0, j, yr, top] = add_low(sib[0, j, yr, top], ra[j])
        self.t3 = send(sib.at[:, :, yr, top], self.ga.at[0], self.go_yr)
        self.t2.wait_recv()
        for j in range(2):
            sib[1, j, yq, top] = add_low(sib[1, j, yq, top], ra[2 + j])
        self.t4 = send(sib.at[:, :, yq, top], self.ga.at[1], self.go_yq)
        self.l1.wait_recv()
        for j in range(2):
            sib[xr % 2, xr // 2, j, low] = add_low(sib[xr % 2, xr // 2, j, low], rb[j])
        self.l3 = send(sib.at[xr % 2, xr // 2, :, low], self.gb.at[0], self.go_xr)
        self.l2.wait_recv()
        for j in range(2):
            sib[xq % 2, xq // 2, 2 + j, low] = add_low(sib[xq % 2, xq // 2, 2 + j, low], rb[2 + j])
        self.l4 = send(sib.at[xq % 2, xq // 2, :, low], self.gb.at[1], self.go_xq)

    def step3(self):
        x, y, c, xr, xq, yr, yq, _ = self.where
        sib, send, ga, gb, pa, pb = self.sib, self.send, self.ga, self.gb, self.ra, self.rb
        xo, yo = (x + 2) % 4, (y + 2) % 4
        self.t3.wait_recv()
        self.t4.wait_recv()
        for i in range(2):
            for j in range(2):
                total = sib[i, j, y, self.top].astype(F32) + ga[0, i, j].astype(F32)
                pa[2 * j + i] = (total + ga[1, i, j].astype(F32)).astype(BF16)
        ha, hb = self.ha, self.hb
        self.last_a = [
            send(pa.at[xr], ha.at[0], self.go_xr),
            send(pa.at[xq], ha.at[1], self.go_xq),
            send(pa.at[xo], ha.at[2], self.go_xo),
        ]
        self.l3.wait_recv()
        self.l4.wait_recv()
        for j in range(4):
            total = sib[x % 2, x // 2, j, self.low].astype(F32) + gb[0, j].astype(F32)
            pb[j] = (total + gb[1, j].astype(F32)).astype(BF16)
        self.last_b = [
            send(pb.at[yr], hb.at[0], self.go_yr),
            send(pb.at[yq], hb.at[1], self.go_yq),
            send(pb.at[yo], hb.at[2], self.go_yo),
        ]

    def finish(self):
        x, y = self.where[:2]
        results = []
        for copies, mine, got in (
            (self.last_a, self.ra[x], self.ha),
            (self.last_b, self.rb[y], self.hb),
        ):
            for copy in copies:
                copy.wait_recv()
            total = mine.astype(F32) + got[0].astype(F32)
            results.append(total + got[1].astype(F32) + got[2].astype(F32))
        return results


def scatter_bufs(rows, cols):
    half = rows // 2
    return [
        VMEM((2, 2, 4, rows, cols), BF16),
        VMEM((4, half, cols), BF16),
        VMEM((4, half, cols), BF16),
        VMEM((2, 2, 2, half, cols), BF16),
        VMEM((2, 4, half, cols), BF16),
        VMEM((3, half, cols), BF16),
        VMEM((3, half, cols), BF16),
    ]


def mm_rows(a, b):
    return lax.dot_general(a, b, (((0,), (0,)), ((), ())), preferred_element_type=F32)


def back_kernel(
    sib_in,
    w_a_in,
    cap_flip_in,
    first_flip_in,
    q8_in,
    kk_in,
    vv_in,
    qr_in,
    kr_in,
    tkr_in,
    other_in,
    lse_in,
    cw_in,
    cos_in,
    sin_in,
    resid_in,
    tk_in,
    tv_in,
    gmid_in,
    gattn_in,
    out_ref,
    mod_ref,
    gains_ref,
    sums_ref,
    facts,
    d_final,
    f_final,
    c_final,
    layer_final,
    hidden_final,
    g_all,
    gain_out,
    sib_f,
    w_a,
    cap_flip,
    first_flip,
    q8,
    kk,
    vv,
    qr,
    kr,
    tkr,
    other_ref,
    lse_ref,
    cw,
    cos_ref,
    sin_ref,
    resid_ref,
    tk,
    tv,
    gmid_ref,
    d_out,
    f_out,
    c_out,
    flip,
    grad_all,
    gc,
    gq,
    gk,
    gv,
    gtk,
    gtv,
    gpack,
    tpack,
    dw_a,
    dw_c,
    part,
    relay,
    got,
    hid_grad,
    mod_msg,
    gain_msg,
    got_mod,
    got_gain,
    gain_sum,
    sf1, sf2, sf3, sf4, sf5, sf6,
    sa0, sa1, sa2, sa3, sa4, sa5, sa6,
    sc0, sc1, sc2, sc3, sc4, sc5, sc6,
    local_sems,
    ss,
    rs,
):
    dp = lax.axis_index("dp")
    t = lax.axis_index("tensor")
    xh, xl, y, z, c = coords()
    _, right, left = z_ring()
    pair = device_of(2 * xh + 1 - xl, y, z, c)
    dp_peers = [((dp + k) % 16, t) for k in range(1, 16)]
    t_peers = [(dp, (t + k) % 8) for k in range(1, 8)]
    outer_x = device_of((2 * xh + xl + 3 - 2 * xl) % 4, y, z, c)
    everyone = dp_peers + t_peers + [outer_x]
    greet_signal(everyone)
    loads = []
    for src, dst in (
        (sib_in, sib_f),
        (w_a_in, w_a),
        (q8_in, q8),
        (gattn_in, grad_all.at[0]),
        (tk_in, tk),
        (tv_in, tv),
        (kk_in, kk),
        (vv_in, vv),
        (lse_in, lse_ref),
        (tkr_in, tkr),
        (cap_flip_in, cap_flip),
        (cw_in, cw),
        (qr_in, qr),
        (kr_in, kr),
        (cos_in, cos_ref),
        (sin_in, sin_ref),
        (other_in, other_ref),
        (first_flip_in, first_flip),
        (resid_in, resid_ref),
        (gmid_in, gmid_ref),
    ):
        copy = pltpu.make_async_copy(src, dst, local_sems.at[len(loads)])
        copy.start()
        loads.append(copy)
    greet_wait(everyone)
    send = Sender(ss, rs)
    tokens = ZGather(send, gattn_in, grad_all, right, left)

    def caption_own(xx, xb, yb):
        return mm(cap_flip[tile(2 * (4 * xb + yb) + c)], tpack[xx])

    scat_f = PlaneScatter(send, None, None, (sib_f, sf1, sf2, sf3, sf4, sf5, sf6))
    scat_a = PlaneScatter(send, dw_a, None, (sa0, sa1, sa2, sa3, sa4, sa5, sa6))
    scat_c = PlaneScatter(send, dw_c, caption_own, (sc0, sc1, sc2, sc3, sc4, sc5, sc6))
    for scatter in (scat_f, scat_a, scat_c):
        scatter.setup()
    loads[0].wait()
    scat_f.first()
    stores = []

    def store(src, dst):
        copy = pltpu.make_async_copy(src, dst, local_sems.at[len(loads) + len(stores)])
        copy.start()
        stores.append(copy)

    store(out_ref.at[xl], layer_final.at[xl])
    out_swap = send(out_ref.at[1 - xl], layer_final.at[xl], pair)
    self_bias = key_bias(512, z, facts[LENGTH_ROW : LENGTH_ROW + 1, :])
    text_bias = key_bias(256, z, facts[TEXT_ROW : TEXT_ROW + 1, :])
    block = head_block()
    low_row = lanes((1, 128)) < 64
    gtk[...] = jnp.zeros((3, 256, 128), F32)
    gtv[...] = jnp.zeros((3, 256, 128), F32)
    gk[...] = jnp.zeros((3, 512, 128), F32)
    gv[...] = jnp.zeros((3, 512, 128), F32)
    for copy in loads[1:4]:
        copy.wait()

    def head_grads(lo, count):
        n = count * 128
        g = grad_all[lo : lo + count].reshape(n, D)
        low_lane = lanes((n, 128)) < 64
        tiles = []
        for xx in range(2):
            w_cols = w_a[xx, :, :, :, :, 512:768].reshape(D, 256)
            o = mm(g, w_cols)
            gc[xx, lo : lo + count] = o[:, 128:].astype(BF16).reshape(count, 128, 128)
            tiles.append(o[:, :128])
        both = jnp.where(low_lane, pltpu.roll(tiles[0], 64, 1), tiles[1])
        gc[2, lo : lo + count] = both.astype(BF16).reshape(count, 128, 128)

    def back_rows(p, lo, count, kinds):
        n = count * 128
        q = q8[p, lo : lo + count].reshape(n, 128)
        low_rows = lanes((n, 128)) < 64
        grad_q = jnp.zeros((n, 128), F32)
        for text in kinds:
            g = gc[p, lo : lo + count].reshape(n, 128)
            if text:
                g = (g.astype(F32) * facts[pl.ds(GATE_ROW + p, 1), :]).astype(BF16)
            k = tk[p] if text else kk[p].reshape(512, 128)
            v = tv[p] if text else vv[p].reshape(512, 128)
            to_v, to_k = (gtv, gtk) if text else (gv, gk)
            for head in range(2):
                keep = low_rows if head == 0 else jnp.logical_not(low_rows)
                qm = jnp.where(keep, q, jnp.zeros_like(q))
                gm = jnp.where(keep, g, jnp.zeros_like(g))
                here = lanes((n, 128)) == p * 2 + head + 8 * text
                kept = lse_ref[lo : lo + count].reshape(n, 128)
                lse = jnp.sum(jnp.where(here, kept, 0.0), axis=-1, keepdims=True)
                scores = mm_t(qm, k) + (text_bias if text else self_bias)
                probs = jnp.exp(scores - lse)
                grad_probs = mm_t(gm, v)
                delta = jnp.sum(probs * grad_probs, axis=-1, keepdims=True)
                grad_scores = (probs * (grad_probs - delta)).astype(BF16)
                grad_q = grad_q + jnp.where(keep, mm(grad_scores, k), 0.0)
                to_v[p] += mm_rows(probs.astype(BF16), gm)
                to_k[p] += mm_rows(grad_scores, qm)
        if 1 in kinds:
            gq[p, lo * 128 : lo * 128 + n] = grad_q
        else:
            gq[p, lo * 128 : lo * 128 + n] += grad_q

    def over_pairs(lo, count, kinds):
        def step(p, carry):
            back_rows(p, lo, count, kinds)
            return carry

        lax.fori_loop(0, 3, step, 0)

    head_grads(0, 1)
    for copy in loads[4:]:
        copy.wait()
    over_pairs(0, 1, (0, 1))
    tokens.near()
    head_grads(1, 2)
    scat_f.step2()
    over_pairs(1, 2, (1,))
    tokens.far()
    head_grads(3, 1)
    over_pairs(3, 1, (1,))

    def unit_of(raw):
        inverse = lax.rsqrt(head_mean(raw * raw, block) + EPSILON)
        return raw * inverse, inverse

    def back_head(unit, inverse, grad):
        return inverse * (grad - unit * head_mean(grad * unit, block))

    low_text = lanes((256, 128)) < 64
    text_row = jnp.zeros((1, 128), F32)
    grads_k = []
    for p in range(3):
        unit, inverse = unit_of(tkr[p])
        gtk_p = gtk[p]
        text_row = text_row + jnp.sum(gtk_p * unit, axis=0, keepdims=True)
        grads_k.append(back_head(unit, inverse, gtk_p * facts[GAIN_ROW + 2 : GAIN_ROW + 3, :]))
    for xx in range(2):
        tpack[xx, :, 0:128] = grads_k[xx].astype(BF16)
        tpack[xx, :, 256:384] = gtv[xx].astype(BF16)
    tpack[0, :, 128:256] = jnp.where(low_text, grads_k[2], pltpu.roll(gtv[2], 64, 1)).astype(BF16)
    tpack[1, :, 128:256] = jnp.where(low_text, pltpu.roll(grads_k[2], 64, 1), gtv[2]).astype(BF16)

    def caption_grad(i, carry):
        xx = i // 8
        j = i % 8
        grad = mm(cap_flip[tile(2 * j + 1 - c)], tpack[xx])
        dw_c[xx, j // 4, j % 4] = grad.astype(BF16)
        return carry

    lax.fori_loop(0, 8, caption_grad, 0)
    scat_c.to_sibling(0)
    scat_c.to_sibling(2)
    lax.fori_loop(8, 16, caption_grad, 0)
    scat_c.to_sibling(1)
    scat_c.to_sibling(3)
    transpose_into(grad_all, flip)
    over_pairs(1, 2, (0,))
    scat_f.step3()
    scat_c.add()
    scat_c.first()
    over_pairs(3, 1, (0,))
    cos = cos_ref[...].reshape(512, 128)
    sin = sin_ref[...].reshape(512, 128)
    low_head = lanes((512, 128)) < 64
    query_row = jnp.zeros((1, 128), F32)
    key_row = jnp.zeros((1, 128), F32)
    raws = [[], []]
    for p in range(3):
        for i in range(2):
            grad = (gq[p] * 0.125) if i == 0 else gk[p]
            raw = (qr if i == 0 else kr)[p].reshape(512, 128)
            turned = grad * cos - swap_quarters(grad) * sin
            unit, inverse = unit_of(raw)
            row = jnp.sum(turned * unit, axis=0, keepdims=True)
            if i == 0:
                query_row = query_row + row
            else:
                key_row = key_row + row
            result = back_head(unit, inverse, turned * facts[GAIN_ROW + i : GAIN_ROW + i + 1, :])
            if p < 2:
                gpack[p, :, (0 if i == 0 else 256) : (128 if i == 0 else 384)] = result.astype(BF16)
            else:
                raws[i] = result
    gpack[0, :, 128:256] = jnp.where(low_head, raws[0], pltpu.roll(raws[1], 64, 1)).astype(BF16)
    gpack[1, :, 128:256] = jnp.where(low_head, pltpu.roll(raws[0], 64, 1), raws[1]).astype(BF16)
    for xx in range(2):
        gpack[xx, :, 384:512] = gv[xx].astype(BF16)
    gpack[0, :, 512:640] = jnp.where(low_head, gv[2], 0.0).astype(BF16)
    gpack[1, :, 512:640] = jnp.where(low_head, pltpu.roll(gv[2], 64, 1), 0.0).astype(BF16)

    def first_rows(lo, count):
        n = count * 128
        a0 = gpack[0, lo * 128 : lo * 128 + n]
        a1 = gpack[1, lo * 128 : lo * 128 + n]
        def column(xb, carry):
            b0 = w_a[0, xb, :, :, :, 0:640].reshape(768, 640)
            b1 = w_a[1, xb, :, :, :, 0:640].reshape(768, 640)
            total = mm_t(a0, b0) + mm_t(a1, b1)
            part[lo : lo + count, :, tile(xb, 768)] = total.astype(BF16).reshape(count, 128, 768)
            return carry

        lax.fori_loop(0, 2, column, 0)

    def weight_grad(i, carry):
        xx, xb = i // 2, i % 2
        a = first_flip[tile(xb, 768)]
        g = flip[tile(xb, 768)]
        b = cw[xx].reshape(512, 256)
        grad = mm(a, gpack[xx, :, 0:512])
        dw_a[xx, xb, :, :, :, 0:512] = grad.astype(BF16).reshape(4, 2, 96, 512)
        grad = mm(g, b)
        last = grad[:, 0:128] + mm(a, gpack[xx, :, 512:640])
        dw_a[xx, xb, :, :, :, 512:640] = last.astype(BF16).reshape(4, 2, 96, 128)
        dw_a[xx, xb, :, :, :, 640:768] = grad[:, 128:256].astype(BF16).reshape(4, 2, 96, 128)
        return carry

    for xx in range(2):
        lax.fori_loop(2 * xx, 2 * xx + 2, weight_grad, 0)
        scat_a.to_sibling(xx)
        scat_a.to_sibling(xx + 2)
    scat_c.step2()
    sums = ZScatter(send, part, relay, got, right, left)
    first_rows(3, 1)
    sums.far()
    first_rows(1, 2)
    sums.near()
    scat_a.add()
    scat_a.first()
    first_rows(0, 1)
    sums.pass_on()
    scat_c.step3()
    scat_a.step2()
    top, low = scat_f.finish()
    f_out[0:48, :] = top
    f_out[48:96, :] = low
    store(f_out, f_final)

    grad_first = sums.total()

    unit_one, inverse_one = normalize(resid_ref[...].astype(F32))
    scale = 1.0 + mod_ref[0:1, :]
    gain = gains_ref[0:1, :]
    row_sum = jnp.sum(grad_first * unit_one, axis=0, keepdims=True)
    sums_0 = row_sum * gain
    sums_4 = row_sum * scale
    hid_grad[...] = (
        (gmid_ref[...] + norm_back(unit_one, inverse_one, grad_first * scale * gain))
        .astype(BF16)
        .reshape(2, 64, D)
    )
    grad_swap = send(hid_grad.at[1 - xl], hidden_final.at[xl], pair)
    store(hid_grad.at[xl], hidden_final.at[xl])
    mod_msg[...] = jnp.zeros((8, 8, 128), F32)
    gain_msg[...] = jnp.zeros((16, 16, 128), F32)
    for i in range(4):
        row = sums_0 if i == 0 else sums_ref[i : i + 1, :]
        for h in range(2):
            for j in range(6):
                lo = h * 768 + j * 128
                mod_msg[2 * i + h, j : j + 1, :] = row[:, lo : lo + 128]
    folded = [row + pltpu.roll(row, 64, 1) for row in (query_row, key_row, text_row)]
    first_line = jnp.where(low_row, folded[0], folded[1])
    lane = lanes((1, 128))
    second_line = jnp.where(low_row, folded[2], 0.0)
    for p in range(3):
        gate_row = facts[GATE_ROW + p : GATE_ROW + p + 1, :]
        products = gc[p].reshape(512, 128).astype(F32) * other_ref[p].reshape(512, 128)
        values = jnp.sum(products, axis=0, keepdims=True) * (1.0 - gate_row * gate_row)
        for head in range(2):
            keep = low_row if head == 0 else jnp.logical_not(low_row)
            value = jnp.sum(jnp.where(keep, values, 0.0), axis=1, keepdims=True)
            index = (0, 1, 3, 4, 2, 5)[2 * p + head]
            second_line = second_line + jnp.where(lane == 64 + z * 6 + index, value, 0.0)
    gain_rows = jnp.concatenate([sums_4, sums_ref[5:8, :]], axis=0)
    mod_rows = [sums_0] + [sums_ref[i : i + 1, :] for i in range(1, 4)]
    for d in range(16):
        for j in range(3):
            lo = (d % 4) * 384 + j * 128
            gain_msg[d, 8 + j : 9 + j, :] = mod_rows[d // 4][:, lo : lo + 128]
        gain_msg[d, 0:4, 0:96] = gain_rows[:, d * 96 : (d + 1) * 96]
        gain_msg[d, 4:5, :] = first_line
        gain_msg[d, 5:6, :] = second_line
    to_t = [send(mod_msg.at[q[1]], got_mod.at[t], q) for q in t_peers]
    to_dp = [send(gain_msg.at[q[0]], got_gain.at[dp], q) for q in dp_peers]
    got_mod[t] = mod_msg[t]
    got_gain[dp] = gain_msg[dp]
    scat_a.step3()
    for copy in to_t:
        copy.wait_recv()
    g_all[dp, 0] = got_mod[0] + got_mod[2] + got_mod[4] + got_mod[6]
    g_all[dp, 1] = got_mod[1] + got_mod[3] + got_mod[5] + got_mod[7]
    to_all = [send(g_all.at[dp], g_all.at[dp], q) for q in dp_peers]
    for copy in to_dp:
        copy.wait_recv()
    gain_sum[t] = jnp.sum(got_gain[...], axis=0)
    to_rest = [send(gain_sum.at[t], gain_sum.at[t], q) for q in t_peers]
    top, low = scat_a.finish()
    d_out[0:48, :] = top
    d_out[48:96, :] = low
    store(d_out, d_final)
    for copy in to_all + to_rest:
        copy.wait_recv()
    gain_out[...] = jnp.sum(gain_sum[...], axis=0)
    top, low = scat_c.finish()
    c_out[0:128, :] = top
    c_out[128:256, :] = low
    store(c_out, c_final)
    out_swap.wait_recv()
    grad_swap.wait_recv()
    send.drain()
    for copy in stores:
        copy.wait()


def back_call(args, cid):
    S = jax.ShapeDtypeStruct
    vm = pl.BlockSpec(memory_space=VMEM)
    any_ = pl.BlockSpec(memory_space=pl.ANY)
    loaded = args[:19]
    outs = [
        S((96, 768), F32),
        S((96, D), F32),
        S((256, 384), F32),
        S((2, 64, D), BF16),
        S((2, 64, D), BF16),
        S((16, 2, 8, 128), F32),
        S((16, 128), F32),
    ]
    return pl.pallas_call(
        back_kernel,
        out_shape=outs,
        in_specs=[any_] * 21 + [vm] * 4,
        out_specs=[any_] * 5 + [vm] * 2,
        scratch_shapes=[VMEM(a.shape, a.dtype) for a in loaded]
        + [
            VMEM((96, 768), F32),
            VMEM((96, D), F32),
            VMEM((256, 384), F32),
            VMEM((D, 512), BF16),
            VMEM((4, 128, D), BF16),
            VMEM((3, 4, 128, 128), BF16),
            VMEM((3, 512, 128), F32),
            VMEM((3, 512, 128), F32),
            VMEM((3, 512, 128), F32),
            VMEM((3, 256, 128), F32),
            VMEM((3, 256, 128), F32),
            VMEM((2, 512, 640), BF16),
            VMEM((2, 256, 384), BF16),
            VMEM((2, 2, 4, 2, 96, 768), BF16),
            VMEM((2, 2, 4, 256, 384), BF16),
            VMEM((4, 128, D), BF16),
            VMEM((2, 64, D), BF16),
            VMEM((2, 128, D), BF16),
            VMEM((2, 64, D), BF16),
            VMEM((8, 8, 128), F32),
            VMEM((16, 16, 128), F32),
            VMEM((8, 8, 128), F32),
            VMEM((16, 16, 128), F32),
            VMEM((8, 16, 128), F32),
        ]
        + scatter_bufs(96, D)[1:]
        + scatter_bufs(96, 768)
        + scatter_bufs(256, 384)
        + [pltpu.SemaphoreType.DMA((28,))]
        + dma_sems(140),
        compiler_params=pltpu.CompilerParams(
            collective_id=cid, has_side_effects=True, vmem_limit_bytes=62 * 2**20
        ),
        name="attention_back",
    )(*args)


def final_kernel(
    d_in,
    f_in,
    c_in,
    layer_in,
    hidden_in,
    g_in,
    gain_hbm,
    got_in,
    layer,
    hidden,
    ada,
    bias,
    gains,
    qkv,
    heads,
    cap,
    gate,
    out_w,
    ffn,
    down,
    d_ref,
    f_ref,
    c_ref,
    hidden_half,
    g_all,
    gain_in,
    got1,
    units,
    items,
    sems,
):
    loads = []
    for src, dst in (
        (layer_in, layer),
        (hidden_in, hidden_half),
        (got_in, got1),
        (g_in, g_all),
        (gain_hbm, gain_in),
        (d_in, d_ref),
        (f_in, f_ref),
        (c_in, c_ref),
    ):
        copy = pltpu.make_async_copy(src, dst, sems.at[len(loads)])
        copy.start()
        loads.append(copy)
    for copy in loads:
        copy.wait()
    hidden[...] = hidden_half[...].astype(F32)
    qkv[0] = d_ref[:, 0:192]
    qkv[1, :, 0:128] = d_ref[:, 256:384]
    qkv[1, :, 128:192] = d_ref[:, 192:256]
    qkv[2] = d_ref[:, 384:576]
    out_w[0:128, :] = d_ref[:, 640:768].T
    out_w[128:192, :] = d_ref[:, 576:640].T
    ffn[0] = f_ref[:, 0:512]
    ffn[1] = f_ref[:, 512:1024]
    down[...] = f_ref[:, 1024:1536]
    cap[0] = c_ref[:, 0:192].T
    cap[1, 0:128, :] = c_ref[:, 256:384].T
    cap[1, 128:192, :] = c_ref[:, 192:256].T
    for d in range(16):
        units[2 * d : 2 * d + 2, :] = got1[d, 0:2, 0:64]
        for j in range(6):
            items[2 * d : 2 * d + 2, j * 128 : j * 128 + 128] = jnp.concatenate(
                [g_all[d, 0, j : j + 1, :], g_all[d, 1, j : j + 1, :]], axis=0
            )
    unit_rows = units[...].astype(BF16)
    high = items[...].astype(BF16)
    low = (items[...] - high.astype(F32)).astype(BF16)
    ada[...] = mm_rows(unit_rows, high) + mm_rows(unit_rows, low)
    for j in range(3):
        bias[j * 128 : j * 128 + 128] = gain_in[8 + j : 9 + j, :].reshape(128)
    gains[...] = gain_in[0:4, 0:96]
    heads[0:1, :] = gain_in[4:5, 0:64]
    heads[1:2, :] = gain_in[4:5, 64:128]
    heads[2:3, :] = gain_in[5:6, 0:64]
    gate[...] = gain_in[5:6, 64:88]


def final_call(args):
    S = jax.ShapeDtypeStruct
    vm = pl.BlockSpec(memory_space=VMEM)
    outs = [
        S((2, 64, D), BF16),
        S((2, 64, D), F32),
        S((64, 768), F32),
        S((384,), F32),
        S((4, 96), F32),
        S((3, 96, 192), F32),
        S((3, 64), F32),
        S((2, 192, 256), F32),
        S((1, 24), F32),
        S((192, 96), F32),
        S((2, 96, 512), F32),
        S((96, 512), F32),
    ]
    return pl.pallas_call(
        final_kernel,
        out_shape=outs,
        in_specs=[pl.BlockSpec(memory_space=pl.ANY)] * len(args),
        out_specs=[vm] * len(outs),
        scratch_shapes=[VMEM(a.shape, a.dtype) for a in args[:3] + args[4:]]
        + [VMEM((32, 64), F32), VMEM((32, 768), F32), pltpu.SemaphoreType.DMA((8,))],
        compiler_params=pltpu.CompilerParams(vmem_limit_bytes=62 * 2**20),
        name="final_layout",
    )(*args)


def on_device(
    hidden,
    condition,
    caption,
    lengths,
    frames,
    widths,
    caption_lens,
    cotangent,
    ada_weight,
    ada_bias,
    norm_gains,
    qkv_weight,
    head_gains,
    caption_weight,
    head_gate,
    out_weight,
    ffn_weight,
    down_weight,
):
    (
        w_f,
        w_a,
        cap_flip,
        first_flip,
        q8,
        kk,
        vv,
        qr,
        kr,
        tkr,
        other,
        lse,
        cw,
        cos_t,
        sin_t,
        resid,
        tk,
        tv,
        attn,
        middle,
        second_in,
        cot,
        mod_rows,
        gains,
        got1,
        live,
        facts,
    ) = attention_call(
        [
            hidden[:, 0],
            cotangent[:, 0],
            caption[:, 0],
            condition[:, 0],
            norm_gains,
            ada_weight,
            qkv_weight,
            out_weight,
            ffn_weight,
            down_weight.T,
            jnp.transpose(caption_weight, (0, 2, 1)),
            ada_bias,
            head_gains,
            head_gate[None],
            lengths.T,
            frames.T,
            widths.T,
            caption_lens.T,
        ],
        1,
    )
    layer_out, grad_middle, grad_attn_in, dw_half, ffn_sums = ffn_call(
        second_in,
        w_f.reshape(2, D, D),
        middle,
        attn,
        cot.reshape(128, D),
        mod_rows,
        gains,
        live,
        2,
    )
    d_out, f_out, c_out, layer_final, hidden_final, g_all, gain_out = back_call(
        [
            dw_half,
            w_a,
            cap_flip,
            first_flip,
            q8,
            kk,
            vv,
            qr,
            kr,
            tkr,
            other,
            lse,
            cw,
            cos_t,
            sin_t,
            resid,
            tk,
            tv,
            grad_middle,
            grad_attn_in,
            layer_out.reshape(2, 64, D),
            mod_rows,
            gains,
            ffn_sums,
            facts,
        ],
        3,
    )
    (
        layer,
        grad_hidden,
        ada,
        bias,
        norm,
        qkv,
        heads,
        cap,
        gate,
        out_w,
        ffn,
        down,
    ) = final_call(
        [d_out, f_out, c_out, layer_final, hidden_final, g_all, gain_out, got1]
    )
    return (
        layer[:, None],
        grad_hidden[:, None],
        ada,
        bias,
        norm,
        qkv,
        heads,
        jnp.transpose(cap, (0, 2, 1)),
        gate[0],
        out_w,
        ffn,
        down.T,
    )


def solution(mesh):
    return jax.shard_map(
        on_device,
        mesh=mesh,
        in_specs=(
            P(None, "dp", "tensor", None),
            P(None, "dp", None),
            P(None, "dp", None, None),
            P(None, "dp"),
            P(None, "dp"),
            P(None, "dp"),
            P(None, "dp"),
            P(None, "dp", "tensor", None),
            P("dp", "tensor"),
            P("dp"),
            P(None, "dp"),
            P(None, "dp", "tensor"),
            P(),
            P(None, "dp", "tensor"),
            P(),
            P("tensor", "dp"),
            P(None, "dp", "tensor"),
            P("tensor", "dp"),
        ),
        out_specs=(
            P(None, "dp", "tensor", None),
            P(None, "dp", "tensor", None),
            P("dp", "tensor"),
            P("dp"),
            P(None, "dp"),
            P(None, "dp", "tensor"),
            P(),
            P(None, "dp", "tensor"),
            P(),
            P("tensor", "dp"),
            P(None, "dp", "tensor"),
            P("tensor", "dp"),
        ),
        check_vma=False,
    )
```
